128 devices in a mesh: mp: 16 (over z, y_hi, core), dp: 8 (over y_lo, x).
Axes of the slice: x: 4, y: 4 (y_hi: 2, y_lo: 2; y = y_hi * 2 + y_lo), z: 4, core: 2. Of those that a mesh axis runs over, the one named last changes fastest.
Arguments:
- inputs: bfloat16 [16384, 512], P('dp', 'mp'), may hold values from -45 to 45
- out_grad: bfloat16 [16384, 512], P('dp', 'mp'), may hold values from -6 to 6
- shape_pick: int32 [8], P('dp'), may hold values from 0 to 1, as said below
- filters: bfloat16 [24, 2048], replicated, may hold values from -0.125 to 0.125
- stu_gain: bfloat16 [512], P('mp'), may hold values from 0.25 to 1.75
- stu_weight: bfloat16 [27, 512, 512], P(None, 'mp'), may hold values from -0.0546875 to 0.0546875
- mlp_gain_a: bfloat16 [512], P('mp'), may hold values from 0.25 to 1.75
- gate_a: bfloat16 [512, 2048], P(None, 'mp'), may hold values from -0.25 to 0.25
- up_a: bfloat16 [512, 2048], P(None, 'mp'), may hold values from -0.25 to 0.25
- down_a: bfloat16 [2048, 512], P('mp'), may hold values from -0.125 to 0.125
- attn_gain: bfloat16 [512], P('mp'), may hold values from 0.25 to 1.75
- qkv_weight: bfloat16 [512, 1536], P(None, 'mp'), may hold values from -0.25 to 0.25
- out_weight: bfloat16 [512, 512], P('mp'), may hold values from -3 to 3
- mlp_gain_b: bfloat16 [512], P('mp'), may hold values from 0.25 to 1.75
- gate_b: bfloat16 [512, 2048], P(None, 'mp'), may hold values from -0.25 to 0.25
- up_b: bfloat16 [512, 2048], P(None, 'mp'), may hold values from -0.25 to 0.25
- down_b: bfloat16 [2048, 512], P('mp'), may hold values from -0.125 to 0.125
Outputs:
- output: bfloat16 [16384, 512], P('dp', 'mp')
- input_grad: float32 [16384, 512], P('dp', 'mp')
- stu_gain_grad: float32 [512], P('mp')
- stu_weight_grad: float32 [27, 512, 512], P(None, 'mp')
- mlp_gain_a_grad: float32 [512], P('mp')
- gate_a_grad: float32 [512, 2048], P(None, 'mp')
- up_a_grad: float32 [512, 2048], P(None, 'mp')
- down_a_grad: float32 [2048, 512], P('mp')
- attn_gain_grad: float32 [512], P('mp')
- qkv_weight_grad: float32 [512, 1536], P(None, 'mp')
- out_weight_grad: float32 [512, 512], P('mp')
- mlp_gain_b_grad: float32 [512], P('mp')
- gate_b_grad: float32 [512, 2048], P(None, 'mp')
- up_b_grad: float32 [512, 2048], P(None, 'mp')
- down_b_grad: float32 [2048, 512], P('mp')
The draws below stay inside these ranges and needn't reach their ends.
Inputs may be any that keep to these rules, and one draw needn't show every extreme that they name: `shape_pick`: 1 makes the sequence one row of 2048 tokens, 0 two rows of 1024 tokens; both occur in every draw.
All inputs are finite; a program needn't handle non-finite values.
Results may differ from the reference program's by a relative error of at most 0.04.
Values may be sent and summed in bfloat16 or wider, within the bound.
A program may use at most 128 MiB of HBM per device.

```python
import math
import jax
import jax.numpy as jnp
from jax import lax

D = 512
FF = 2048
K = 24
LAGS = 3
H = 8
HD = 64
LONG = 2048
SEQUENCES = 8
TOKENS = 16384


def draw_inputs(key, part):
    key = jax.random.fold_in(key, 11)
    base_key, row_key, col_key = jax.random.split(key, 3)
    row_scale = jnp.exp(jax.random.uniform(row_key, (TOKENS, 1), jnp.float32, math.log(0.5), math.log(3.0)))
    col_scale = jnp.exp(jnp.linspace(math.log(0.6), math.log(1.8), D)).astype(jnp.float32)[None, :]
    col_scale = col_scale * jax.random.uniform(col_key, (1, D), jnp.float32, 0.8, 1.25)
    base = jnp.clip(jax.random.normal(base_key, (TOKENS, D), jnp.float32), -6.0, 6.0)
    return (base * row_scale * col_scale).astype(jnp.bfloat16)


def draw_shape_pick(key, part):
    key = jax.random.fold_in(key, 23)
    pick_key, first_key, second_key = jax.random.split(key, 3)
    picks = jax.random.randint(pick_key, (SEQUENCES,), 0, 2)
    first_seq = jax.random.randint(first_key, (), 0, SEQUENCES)
    second_seq = (first_seq + 1 + jax.random.randint(second_key, (), 0, SEQUENCES - 1)) % SEQUENCES
    return picks.at[first_seq].set(1).at[second_seq].set(0).astype(jnp.int32)


def shard_levels(stream_key, extent, cuts, low, high):
    gain, own = 1.0, jax.random.fold_in(stream_key, 6)
    for dim, parts in cuts:
        heights = jnp.exp(jax.random.uniform(jax.random.fold_in(own, dim), (parts,), jnp.float32, low / len(cuts), high / len(cuts)))
        gain = gain * jnp.repeat(heights, extent[dim] // parts).reshape([-1 if axis == dim else 1 for axis in range(len(extent))])
    return gain


def noise(rng, extent, width, reach, shards=(), dtype=jnp.bfloat16):
    level = shard_levels(rng, extent, shards, -0.22, 0.18) if shards else 1.0
    values = jax.random.normal(rng, extent, jnp.float32) * width * level
    return jnp.minimum(jnp.maximum(values, -reach), reach).astype(dtype)


def setup_inputs(seed: int = 0) -> dict:
    seeds = jax.random.split(jax.random.key(seed), 18)
    return {
        "inputs": draw_inputs(jax.random.fold_in(seeds[17], 71), 0),
        "out_grad": noise(seeds[1], (TOKENS, D), 1.0, 6.0, ((0, 8), (1, 16))),
        "shape_pick": draw_shape_pick(jax.random.fold_in(seeds[17], 71), 0),
        "filters": noise(seeds[3], (K, LONG), LONG ** -0.5, 0.125),
        "stu_gain": jnp.clip(1.0 + 0.15 * jax.random.normal(seeds[4], (D,), jnp.float32), 0.25, 1.75).astype(jnp.bfloat16),
        "stu_weight": noise(seeds[5], (K + LAGS, D, D), ((K + LAGS) * D) ** -0.5, 0.0546875, ((1, 16),)),
        "mlp_gain_a": jnp.clip(1.0 + 0.15 * jax.random.normal(seeds[6], (D,), jnp.float32), 0.25, 1.75).astype(jnp.bfloat16),
        "gate_a": noise(seeds[7], (D, FF), D ** -0.5, 0.25, ((1, 16),)),
        "up_a": noise(seeds[8], (D, FF), D ** -0.5, 0.25, ((1, 16),)),
        "down_a": noise(seeds[9], (FF, D), FF ** -0.5, 0.125, ((0, 16),)),
        "attn_gain": jnp.clip(1.0 + 0.15 * jax.random.normal(seeds[10], (D,), jnp.float32), 0.25, 1.75).astype(jnp.bfloat16),
        "qkv_weight": noise(seeds[11], (D, 3 * H * HD), D ** -0.5, 0.25, ((1, 16),)),
        "out_weight": noise(seeds[12], (H * HD, D), 4 ** -0.5, 3.0, ((0, 16),)),
        "mlp_gain_b": jnp.clip(1.0 + 0.15 * jax.random.normal(seeds[13], (D,), jnp.float32), 0.25, 1.75).astype(jnp.bfloat16),
        "gate_b": noise(seeds[14], (D, FF), D ** -0.5, 0.25, ((1, 16),)),
        "up_b": noise(seeds[15], (D, FF), D ** -0.5, 0.25, ((1, 16),)),
        "down_b": noise(seeds[16], (FF, D), FF ** -0.5, 0.125, ((0, 16),)),
    }


EPSILON = 1e-05
HIGHEST = lax.Precision.HIGHEST

@jax.custom_vjp
def low(v):
    return lax.optimization_barrier(v.astype(jnp.bfloat16)).astype(jnp.float32)

@jax.custom_vjp
def low_back(v):
    return v

def low_keep(v):
    return (low(v), None)

def low_pass(kept, grad):
    return (grad,)

def back_keep(v):
    return (v, None)

def back_low(kept, grad):
    return (low(grad),)
low.defvjp(low_keep, low_pass)
low_back.defvjp(back_keep, back_low)

def matmul(left, right):
    return jnp.dot(left, right, precision=HIGHEST)

def rms_norm(stream, norm_gain):
    scaling = lax.rsqrt(lax.optimization_barrier(jnp.mean(stream * stream, axis=-1, keepdims=True)) + EPSILON)
    return stream * scaling * norm_gain

def lagged(signal, pick, shift_by):
    position = jnp.arange(LONG)
    visible = (position >= shift_by) & ((pick == 1) | (position % (LONG // 2) >= shift_by))
    moved = jnp.concatenate([jnp.zeros((shift_by, D), jnp.float32), signal[:LONG - shift_by]], axis=0)
    return jnp.where(visible[:, None], moved, jnp.zeros_like(moved))

def causal_conv(signal, taps, length):
    size = 2 * length
    spectrum = jnp.fft.rfft(signal, n=size, axis=1)

    def one_filter(filter_taps):
        response = jnp.fft.rfft(filter_taps[:length], n=size)
        return jnp.fft.irfft(spectrum * response[None, :, None], n=size, axis=1)[:, :length]
    return lax.map(jax.checkpoint(one_filter), taps)

def stu_branch(signal, pick, taps, weight):
    long_part = causal_conv(signal[None], taps, LONG)[:, 0]
    short_part = causal_conv(signal.reshape(2, LONG // 2, D), taps, LONG // 2).reshape(K, LONG, D)
    convolved = jnp.where(pick == 1, long_part, short_part)
    convolved = low_back(low(jnp.transpose(convolved, (1, 0, 2))))
    lag_stack = jnp.stack([lagged(signal, pick, shift_by) for shift_by in range(LAGS)], axis=1)
    features = jnp.concatenate([convolved, lag_stack], axis=1)
    return low_back(jnp.einsum('tkc,kcd->td', features, weight, precision=HIGHEST))

def mlp_branch(stream, norm_gain, w_gate, w_up, w_down):
    normed = low(rms_norm(stream, norm_gain))
    gate_values = low_back(matmul(normed, w_gate))
    up_values = low_back(matmul(normed, w_up))
    hidden = low(jax.nn.silu(gate_values) * up_values)
    return low_back(matmul(hidden, w_down))

def attention_branch(stream, norm_gain, w_qkv, w_out, pick):
    normed = low(rms_norm(stream, norm_gain))
    columns = low_back(low(matmul(normed, w_qkv)))
    columns = columns.reshape(LONG, H, 3, HD).transpose(1, 2, 0, 3)
    position = jnp.arange(LONG)
    half_row = LONG // 2
    visible = (position[None, :] <= position[:, None]) & ((pick == 1) | (position[None, :] // half_row == position[:, None] // half_row))

    def one_head(head_parts):
        scores = low_back(matmul(head_parts[0], head_parts[1].T) * HD ** (-0.5))
        probs = jax.nn.softmax(jnp.where(visible, scores, -1e+30), axis=-1)
        return low_back(low(matmul(low(probs), head_parts[2])))
    heads = lax.map(jax.checkpoint(one_head), columns)
    return low_back(matmul(heads.transpose(1, 0, 2).reshape(LONG, H * HD), w_out))

def layer_pair(sequence, pick, weights, taps):
    stu_gain, stu_weight, mlp_gain_a, gate_a, up_a, down_a, attn_gain, qkv_weight, out_weight, mlp_gain_b, gate_b, up_b, down_b = weights
    stream = sequence + stu_branch(low(rms_norm(sequence, stu_gain)), pick, taps, stu_weight)
    stream = stream + mlp_branch(stream, mlp_gain_a, gate_a, up_a, down_a)
    stream = stream + attention_branch(stream, attn_gain, qkv_weight, out_weight, pick)
    return stream + mlp_branch(stream, mlp_gain_b, gate_b, up_b, down_b)

def reference(inputs, out_grad, shape_pick, filters, stu_gain, stu_weight, mlp_gain_a, gate_a, up_a, down_a, attn_gain, qkv_weight, out_weight, mlp_gain_b, gate_b, up_b, down_b):
    weights = tuple((array.astype(jnp.float32) for array in (stu_gain, stu_weight, mlp_gain_a, gate_a, up_a, down_a, attn_gain, qkv_weight, out_weight, mlp_gain_b, gate_b, up_b, down_b)))
    taps = filters.astype(jnp.float32)

    def whole_batch(signal, params):
        sequences = signal.reshape(SEQUENCES, LONG, D)

        def one_sequence(pair):
            return layer_pair(pair[0], pair[1], params, taps)
        outputs = lax.map(jax.checkpoint(one_sequence), (sequences, shape_pick))
        return outputs.reshape(TOKENS, D)
    result, pullback = jax.vjp(whole_batch, inputs.astype(jnp.float32), weights)
    input_grad, grads = pullback(out_grad.astype(jnp.float32))
    return (result.astype(jnp.bfloat16), input_grad, grads[0], grads[1], grads[2], grads[3], grads[4], grads[5], grads[6], grads[7], grads[8], grads[9], grads[10], grads[11], grads[12])
```

```python
import jax
import jax.numpy as jnp
from jax import lax
from jax.experimental import pallas as pl
from jax.experimental.pallas import tpu as pltpu
from jax.sharding import PartitionSpec as P

D = 512
T = 2048
OWN = 128
CH = 32
K = 24
LAGS = 3
FEAT = (K + LAGS) * CH
HD = 64
MP = 16
CHIPS = 8
EPSILON = 1e-05
NEG = -1e30
F32 = jnp.float32
BF16 = jnp.bfloat16
MESH = pl.DeviceIdType.MESH
VMEM = pl.BlockSpec(memory_space=pltpu.VMEM)
SMEM = pl.BlockSpec(memory_space=pltpu.SMEM)
LIMIT = 56 * 2**20


def nn(left, right):
    return jnp.dot(left, right, preferred_element_type=F32)


def tn(left, right):
    return lax.dot_general(left, right, (((0,), (0,)), ((), ())), preferred_element_type=F32)


def nt(left, right):
    return lax.dot_general(left, right, (((1,), (1,)), ((), ())), preferred_element_type=F32)


class Place:
    def __init__(self):
        self.me = lax.axis_index("mp")
        self.z = self.me // 4
        self.chip = self.me // 2
        self.y = self.chip % 2
        self.core = self.me % 2
        self.partner = self.me + 1 - 2 * self.core
        self.across = self.me + 2 - 4 * self.y
        self.query_core = ((self.z + 1) // 2) % 2
        self.quarters = (self.core, 3 - self.core)

    def around(self, step):
        return (self.me + step) % MP

    def chip_at(self, step):
        return (self.chip + step) % CHIPS


def half(index):
    return pl.ds(pl.multiple_of(index * OWN, OWN), OWN)


def rows(index, count):
    return pl.ds(pl.multiple_of(index * count, count), count)


def remote(src, dst, sems, slot, target):
    return pltpu.make_async_remote_copy(
        src_ref=src,
        dst_ref=dst,
        send_sem=sems.at[0, slot],
        recv_sem=sems.at[1, slot],
        device_id={"mp": target},
        device_id_type=MESH,
    )


def greet(targets):
    barrier = pltpu.get_barrier_semaphore()
    for target in targets:
        pl.semaphore_signal(barrier, inc=1, device_id={"mp": target}, device_id_type=MESH)
    pl.semaphore_wait(barrier, len(targets))


def sems(count):
    return pltpu.SemaphoreType.DMA((2, count))


def norm_forward(stream, gain):
    scaling = lax.rsqrt(jnp.sum(stream * stream, axis=0, keepdims=True) / D + EPSILON)
    return stream * scaling * gain, scaling


def norm_backward(upstream, stream, gain):
    scaling = lax.rsqrt(jnp.sum(stream * stream, axis=0, keepdims=True) / D + EPSILON)
    gain_grad = jnp.sum(upstream * stream * scaling, axis=1, keepdims=True)
    scaled = upstream * gain
    inner = jnp.sum(scaled * stream, axis=0, keepdims=True)
    return scaled * scaling - stream * (scaling * scaling * scaling * inner / D), gain_grad


def gather_four(place, buf, sem):
    own = buf.at[place.y, :, half(place.core)]
    there = buf.at[1 - place.y, :, half(place.core)]
    to_across = remote(own, own, sem, 0, place.across)
    to_across.start()
    to_partner = remote(own, own, sem, 1, place.partner)
    to_partner.start()

    def near():
        to_partner.wait_recv()

    def far():
        to_across.wait_recv()
        forward = remote(there, there, sem, 2, place.partner)
        forward.start()
        forward.wait()

    def close():
        to_across.wait_send()
        to_partner.wait_send()

    return near, far, close


def scatter_four(place, parts, got, sem):
    keep = half(place.core)
    away = half(1 - place.core)
    far_part = remote(parts.at[1 - place.y, :, away], got.at[0], sem, 0, place.partner)
    near_part = remote(parts.at[place.y, :, away], got.at[1], sem, 1, place.partner)
    across_part = remote(parts.at[1 - place.y, :, keep], got.at[2], sem, 2, place.across)

    def send_far():
        far_part.start()

    def send_near():
        near_part.start()

    def relay():
        far_part.wait_recv()
        total = parts[1 - place.y, :, keep].astype(F32) + got[0].astype(F32)
        parts[1 - place.y, :, keep] = total.astype(BF16)
        across_part.start()

    def total():
        near_part.wait_recv()
        across_part.wait_recv()
        return parts[place.y, :, keep].astype(F32) + got[1].astype(F32) + got[2].astype(F32)

    def close():
        far_part.wait_send()
        near_part.wait_send()
        across_part.wait_send()

    return send_far, send_near, relay, total, close


def first_norm_kernel(x_ref, go_ref, gain_ref, h_ref, scale_ref, x_own, go_own, squares, sem):
    place = Place()
    me = place.me
    stream = x_ref[...].astype(F32)
    squares[pl.ds(me, 1)] = jnp.sum(stream * stream, axis=0, keepdims=True)[None]
    greet([place.around(step) for step in range(1, MP)])
    sums, moves = [], []
    for step in range(1, MP):
        there = place.around(step)
        copy = remote(squares.at[me], squares.at[me], sem, step - 1, there)
        copy.start()
        sums.append(copy)
    for step in range(1, MP):
        there = place.around(step)
        copy = remote(x_ref.at[:, half(there)], x_own.at[rows(me, CH)], sem, 14 + step, there)
        copy.start()
        moves.append(copy)
        copy = remote(go_ref.at[:, half(there)], go_own.at[rows(me, CH)], sem, 29 + step, there)
        copy.start()
        moves.append(copy)
    x_own[rows(me, CH), :] = x_ref[:, half(me)]
    go_own[rows(me, CH), :] = go_ref[:, half(me)]
    for copy in sums:
        copy.wait()
    total = squares[0]
    for index in range(1, MP):
        total = total + squares[index]
    scaling = lax.rsqrt(total / D + EPSILON)
    scale_ref[...] = scaling
    h_ref[...] = (stream * scaling * gain_ref[...]).astype(BF16)
    for copy in moves:
        copy.wait()


def first_norm(x, go, gain):
    return pl.pallas_call(
        first_norm_kernel,
        out_shape=(
            jax.ShapeDtypeStruct((CH, T), BF16),
            jax.ShapeDtypeStruct((1, T), F32),
            jax.ShapeDtypeStruct((D, OWN), BF16),
            jax.ShapeDtypeStruct((D, OWN), BF16),
        ),
        in_specs=[VMEM] * 3,
        out_specs=(VMEM,) * 4,
        scratch_shapes=[pltpu.VMEM((MP, 1, T), F32), sems(45)],
        compiler_params=pltpu.CompilerParams(
            collective_id=0, has_side_effects=True, vmem_limit_bytes=LIMIT
        ),
        name="first_norm",
    )(x, go, gain)


def toeplitz(taps):
    wide = pltpu.roll(jnp.broadcast_to(taps, (OWN, T)), 0, 1, stride=1, stride_axis=0)
    lane = lax.broadcasted_iota(jnp.int32, (OWN, T), 1)
    row = lax.broadcasted_iota(jnp.int32, (OWN, T), 0)
    return jnp.where(lane >= row, wide, 0.0).astype(BF16)


def lag_mask(shift, pick):
    lane = lax.broadcasted_iota(jnp.int32, (CH, T), 1)
    inner = lane % (T // 2)
    return (lane >= shift) & ((inner >= shift) | (pick == 1))


def conv_forward_kernel(pick_ref, h_ref, taps_ref, weight_ref, x_ref, y_ref, blocks, table):
    step = pl.program_id(0)
    count = T // OWN

    @pl.when(step == 0)
    def _():
        pick = pick_ref[0]
        joined = jnp.full((CH, OWN), (pick == 1).astype(F32)).astype(BF16)
        for target in range(count):
            for offset in range(count):
                here = (slice(target * CH, (target + 1) * CH), slice(offset * OWN, (offset + 1) * OWN))
                if offset > target:
                    blocks[here] = jnp.zeros((CH, OWN), BF16)
                    continue
                source = target - offset
                value = h_ref[:, source * OWN : (source + 1) * OWN]
                if target >= count // 2 and source < count // 2:
                    value = value * joined
                blocks[here] = value

    for index in range(2):
        filter_table = toeplitz(taps_ref[0, index : index + 1, :])
        for offset in range(count):
            table[offset * OWN : (offset + 1) * OWN, index * OWN : (index + 1) * OWN] = filter_table[
                :, offset * OWN : (offset + 1) * OWN
            ]
    early = nn(blocks[: CH * count // 2, : T // 2], table[: T // 2, :]).astype(BF16)
    late = nn(blocks[CH * count // 2 :, :], table[...]).astype(BF16)
    for index in range(2):
        base = pl.multiple_of((step * 2 + index) * CH, CH)
        for target in range(count):
            part, place = (early, target) if target < count // 2 else (late, target - count // 2)
            x_ref[pl.ds(base, CH), target * OWN : (target + 1) * OWN] = part[
                place * CH : (place + 1) * CH, index * OWN : (index + 1) * OWN
            ]

    @pl.when(step == K // 2 - 1)
    def _():
        pick = pick_ref[0]
        own = h_ref[...].astype(F32)
        for shift in range(LAGS):
            moved = own if shift == 0 else pltpu.roll(own, shift, 1)
            moved = jnp.where(lag_mask(shift, pick), moved, 0.0).astype(BF16)
            x_ref[(K + shift) * CH : (K + shift + 1) * CH, :] = moved
        for group in range(4):
            y = tn(weight_ref[...], x_ref[:, group * 512 : (group + 1) * 512]).astype(BF16)
            for index in range(4):
                y_ref[group * 4 + index] = y[:, index * OWN : (index + 1) * OWN]


def conv_forward(pick, h, taps, weight):
    return pl.pallas_call(
        conv_forward_kernel,
        grid=(K // 2,),
        out_shape=(
            jax.ShapeDtypeStruct((FEAT, T), BF16),
            jax.ShapeDtypeStruct((MP, D, OWN), BF16),
        ),
        in_specs=[
            SMEM,
            pl.BlockSpec((CH, T), lambda i: (0, 0)),
            pl.BlockSpec((1, 2, T), lambda i: (i, 0, 0)),
            pl.BlockSpec((FEAT, D), lambda i: (0, 0)),
        ],
        out_specs=(
            pl.BlockSpec((FEAT, T), lambda i: (0, 0)),
            pl.BlockSpec((MP, D, OWN), lambda i: (0, 0, 0)),
        ),
        scratch_shapes=[pltpu.VMEM((CH * T // OWN, T), BF16), pltpu.VMEM((T, 2 * OWN), BF16)],
        compiler_params=pltpu.CompilerParams(vmem_limit_bytes=LIMIT),
        name="conv_forward",
    )(pick, h, taps, weight)


def layer_a_kernel(
    y_ref, x_ref, go_ref, gain_a, gain_n, wa_ref, wat_ref,
    x1_ref, x2_ref, na_ref, go4_ref, n3_ref, qkv_ref,
    core_got, chip_sum, chip_got, parts, got, heads, sem_y, sem_n, sem_g, sem_z, sem_q,
):
    place = Place()
    me, chip, core = place.me, place.chip, place.core
    greet([place.around(step) for step in range(1, MP)])
    order = list(range(1, CHIPS)) + [0]
    first = []
    for step in order:
        there = place.chip_at(step)
        copy = remote(y_ref.at[there, 1 - core], core_got.at[there], sem_y, step, place.partner)
        copy.start()
        first.append(copy)
    second = []
    for copy, step in zip(first, order):
        there = place.chip_at(step)
        copy.wait_recv()
        total = y_ref[there, core].astype(F32) + core_got[there].astype(F32)
        if step == 0:
            x1_ref[...] = total + x_ref[...].astype(F32)
        else:
            chip_sum[step - 1] = total.astype(BF16)
            move = remote(chip_sum.at[step - 1], chip_got.at[step - 1], sem_y, 7 + step, there * 2 + core)
            move.start()
            second.append(move)
    go4_ref[place.y, :, half(core)] = go_ref[...]
    for move in second:
        move.wait_recv()
    x1 = x1_ref[...]
    for index in range(CHIPS - 1):
        x1 = x1 + chip_got[index].astype(F32)
    x1_ref[...] = x1
    normed, _ = norm_forward(x1, gain_a[...])
    na_ref[place.y, :, half(core)] = normed.astype(BF16)
    near, far, close_n = gather_four(place, na_ref, sem_n)
    near_g, far_g, close_g = gather_four(place, go4_ref, sem_g)
    w_gate = wa_ref[:, 0].reshape(D, D)
    w_up = wa_ref[:, 1].reshape(D, D)
    w_down = wa_ref[:, 2].reshape(D, D)
    send_far, send_near, relay, total, close_z = scatter_four(place, parts, got, sem_z)

    def block(where):
        rows_here = na_ref[where]
        gate = nn(w_gate, rows_here)
        hidden = (gate * jax.nn.sigmoid(gate) * nn(w_up, rows_here)).astype(BF16)
        parts[where] = tn(w_down, hidden).astype(BF16)

    near()
    block(place.y)
    send_near()
    far()
    block(1 - place.y)
    send_far()
    relay()
    x2 = x1 + total()
    x2_ref[...] = x2
    n3 = norm_forward(x2, gain_n[...])[0].astype(BF16)
    n3_ref[...] = n3
    w_qkv = wat_ref[:, : 3 * CH].reshape(3 * D, D)
    heads[...] = nn(w_qkv, n3).astype(BF16).reshape(CHIPS, 3 * HD, OWN)
    sends = []
    for step in range(1, CHIPS):
        there = place.chip_at(step)
        copy = remote(heads.at[there], qkv_ref.at[me], sem_q, step - 1, there * 2 + core)
        copy.start()
        sends.append(copy)
    qkv_ref[me] = heads[chip]
    forwards = [remote(qkv_ref.at[me], qkv_ref.at[me], sem_q, 7, place.partner)]
    forwards[0].start()
    for step in range(1, CHIPS):
        source = place.chip_at(CHIPS - step) * 2 + core
        sends[step - 1].wait_recv()
        copy = remote(qkv_ref.at[source], qkv_ref.at[source], sem_q, 7 + step, place.partner)
        copy.start()
        forwards.append(copy)
    near_g()
    far_g()
    for copy in forwards:
        copy.wait()
    for copy in first + second + sends:
        copy.wait_send()
    close_n()
    close_g()
    close_z()


def layer_a(y, x_own, go_own, gain_a, gain_n, wa, wat):
    return pl.pallas_call(
        layer_a_kernel,
        out_shape=(
            jax.ShapeDtypeStruct((D, OWN), F32),
            jax.ShapeDtypeStruct((D, OWN), F32),
            jax.ShapeDtypeStruct((2, D, 2 * OWN), BF16),
            jax.ShapeDtypeStruct((2, D, 2 * OWN), BF16),
            jax.ShapeDtypeStruct((D, OWN), BF16),
            jax.ShapeDtypeStruct((MP, 3 * HD, OWN), BF16),
        ),
        in_specs=[VMEM] * 7,
        out_specs=(VMEM,) * 6,
        scratch_shapes=[
            pltpu.VMEM((CHIPS, D, OWN), BF16),
            pltpu.VMEM((CHIPS - 1, D, OWN), BF16),
            pltpu.VMEM((CHIPS - 1, D, OWN), BF16),
            pltpu.VMEM((2, D, 2 * OWN), BF16),
            pltpu.VMEM((3, D, OWN), BF16),
            pltpu.VMEM((CHIPS, 3 * HD, OWN), BF16),
            sems(15), sems(3), sems(3), sems(3), sems(15),
        ],
        compiler_params=pltpu.CompilerParams(
            collective_id=1, has_side_effects=True, vmem_limit_bytes=LIMIT
        ),
        name="layer_a",
    )(y, x_own, go_own, gain_a, gain_n, wa, wat)


def spread(qkv_ref, keys, values):
    for index in range(MP):
        keys[:, index * OWN : (index + 1) * OWN] = qkv_ref[index, HD : 2 * HD]
        values[:, index * OWN : (index + 1) * OWN] = qkv_ref[index, 2 * HD :]


def query_block(qkv_ref, quarter):
    parts = [qkv_ref[quarter * 4 + index, :HD] for index in range(4)]
    return jnp.concatenate(parts, axis=1) * jnp.asarray(HD**-0.5, BF16)


def score_mask(quarter, chunk, pick):
    query = quarter * 512 + lax.broadcasted_iota(jnp.int32, (512, 512), 1)
    key = chunk * 512 + lax.broadcasted_iota(jnp.int32, (512, 512), 0)
    same_half = (quarter // 2) == (chunk // 2)
    return (key <= query) & (same_half | (pick == 1))


def layer_b_kernel(
    pick_ref, qkv_ref, x2_ref, go4_ref, go_ref, gain_b, wat_ref, wb_ref,
    lse_ref, of_ref, go_heads, gx3_ref, out_ref, gwo_ref, gmlp_ref, ggain_ref,
    keys, values, own_heads, all_heads, x3_ref, nb, hidden_ref, ggate_ref, gup_ref,
    parts_n, got_n, parts_z, got_z, grad_heads, out_own, sem_o, sem_n, sem_gn, sem_z, sem_h, sem_out,
):
    place = Place()
    me, chip, core = place.me, place.chip, place.core
    greet([place.around(step) for step in range(1, MP)])
    pick = pick_ref[0]
    spread(qkv_ref, keys, values)
    for part in range(2):
        quarter = place.quarters[part]
        queries = query_block(qkv_ref, quarter)
        top = jnp.full((1, 512), NEG, F32)
        norm = jnp.zeros((1, 512), F32)
        total = jnp.zeros((HD, 512), F32)
        for chunk in range(2 + 2 * part):
            here = slice(chunk * 512, (chunk + 1) * 512)
            scores = jnp.where(score_mask(quarter, chunk, pick), tn(keys[:, here], queries), NEG)
            new_top = jnp.maximum(top, jnp.max(scores, axis=0, keepdims=True))
            weights = jnp.exp(scores - new_top)
            rescale = jnp.exp(top - new_top)
            norm = norm * rescale + jnp.sum(weights, axis=0, keepdims=True)
            total = total * rescale + nn(values[:, here], weights.astype(BF16))
            top = new_top
        total = total / norm
        lse_ref[part] = top + jnp.log(norm)
        of_ref[part] = total
        for index in range(4):
            own_heads[part * 4 + index] = total[:, index * OWN : (index + 1) * OWN].astype(BF16)
    targets = [place.quarters[slot // 4] * 4 + slot % 4 for slot in range(8)]
    copies = [
        pltpu.make_async_remote_copy(
            src_ref=own_heads.at[slot], dst_ref=all_heads.at[chip],
            send_sem=sem_o.at[0, slot], recv_sem=sem_o.at[1, chip],
            device_id={"mp": targets[slot]}, device_id_type=MESH,
        )
        for slot in range(8)
    ]
    for slot in range(8):
        pl.when(targets[slot] != me)(copies[slot].start)

        @pl.when(targets[slot] == me)
        def _():
            all_heads[chip] = own_heads[slot]

    arrivals = [
        remote(own_heads.at[0], all_heads.at[head], sem_o, head, place.partner) for head in range(CHIPS)
    ]
    for head in range(CHIPS):
        pl.when(head * 2 + place.query_core != me)(arrivals[head].wait_recv)
    w_out = wat_ref[:, 3 * CH :].reshape(D, D)
    outputs = all_heads[...].reshape(D, OWN)
    x3 = x2_ref[...] + tn(w_out, outputs)
    x3_ref[...] = x3
    nb[place.y, :, half(core)] = norm_forward(x3, gain_b[...])[0].astype(BF16)
    near, far, close_n = gather_four(place, nb, sem_n)
    w_gate = wb_ref[:, 0].reshape(D, D)
    w_up = wb_ref[:, 1].reshape(D, D)
    w_down = wb_ref[:, 2].reshape(D, D)
    far_gn, near_gn, relay_gn, total_gn, close_gn = scatter_four(place, parts_n, got_n, sem_gn)
    far_z, near_z, relay_z, total_z, close_z = scatter_four(place, parts_z, got_z, sem_z)

    def block(where):
        rows_here = nb[where]
        gate = nn(w_gate, rows_here)
        up = nn(w_up, rows_here)
        sig = jax.nn.sigmoid(gate)
        hidden_grad = nn(w_down, go4_ref[where])
        gate_grad = (hidden_grad * up * sig * (1.0 + gate * (1.0 - sig))).astype(BF16)
        up_grad = (hidden_grad * gate * sig).astype(BF16)
        ggate_ref[where] = gate_grad
        gup_ref[where] = up_grad
        parts_n[where] = (tn(w_gate, gate_grad) + tn(w_up, up_grad)).astype(BF16)
        hidden_ref[where] = (gate * sig * up).astype(BF16)

    near()
    block(place.y)
    near_gn()
    far()
    block(1 - place.y)
    far_gn()
    parts_z[place.y] = tn(w_down, hidden_ref[place.y]).astype(BF16)
    near_z()
    relay_gn()
    parts_z[1 - place.y] = tn(w_down, hidden_ref[1 - place.y]).astype(BF16)
    far_z()
    relay_z()
    stream_grad, gain_grad = norm_backward(total_gn(), x3_ref[...], gain_b[...])
    ggain_ref[...] = gain_grad
    gx3 = go_ref[...].astype(F32) + stream_grad
    gx3_ref[...] = gx3
    gy = gx3.astype(BF16)
    grad_heads[...] = nn(w_out, gy).astype(BF16).reshape(CHIPS, HD, OWN)
    slot = (place.z // 2) * 4 + me % 4
    sends = [
        pltpu.make_async_remote_copy(
            src_ref=grad_heads.at[head], dst_ref=go_heads.at[slot],
            send_sem=sem_h.at[0, head], recv_sem=sem_h.at[1, slot],
            device_id={"mp": head * 2 + place.query_core}, device_id_type=MESH,
        )
        for head in range(CHIPS)
    ]
    for head in range(CHIPS):
        pl.when(head * 2 + place.query_core != me)(sends[head].start)

        @pl.when(head * 2 + place.query_core == me)
        def _():
            go_heads[slot] = grad_heads[head]

    out_own[...] = (x3_ref[...] + total_z()).astype(BF16)
    moves = []
    for step in range(1, MP):
        there = place.around(step)
        copy = remote(out_own.at[rows(there, CH)], out_ref.at[:, half(me)], sem_out, step - 1, there)
        copy.start()
        moves.append(copy)
    out_ref[:, half(me)] = out_own[rows(me, CH), :]
    gwo_ref[...] = nt(outputs, gy).astype(BF16)
    for group, (left, right) in enumerate(((ggate_ref, nb), (gup_ref, nb), (hidden_ref, go4_ref))):
        value = (nt(left[0], right[0]) + nt(left[1], right[1])).astype(BF16)
        for index in range(4):
            gmlp_ref[index, group] = value[index * OWN : (index + 1) * OWN]
    for slot_in in range(8):
        arrival = remote(grad_heads.at[0], go_heads.at[slot_in], sem_h, slot_in, place.partner)
        pl.when(targets[slot_in] != me)(arrival.wait_recv)
    for slot_out in range(8):
        pl.when(targets[slot_out] != me)(copies[slot_out].wait_send)
        pl.when(slot_out * 2 + place.query_core != me)(sends[slot_out].wait_send)
    for copy in moves:
        copy.wait()
    close_n()
    close_gn()
    close_z()


def layer_b(pick, qkv, x2, go4, go_own, gain_b, wat, wb):
    return pl.pallas_call(
        layer_b_kernel,
        out_shape=(
            jax.ShapeDtypeStruct((2, 1, 512), F32),
            jax.ShapeDtypeStruct((2, HD, 512), F32),
            jax.ShapeDtypeStruct((8, HD, OWN), BF16),
            jax.ShapeDtypeStruct((D, OWN), F32),
            jax.ShapeDtypeStruct((CH, T), BF16),
            jax.ShapeDtypeStruct((D, D), BF16),
            jax.ShapeDtypeStruct((4, 3, OWN, D), BF16),
            jax.ShapeDtypeStruct((D, 1), F32),
        ),
        in_specs=[SMEM] + [VMEM] * 7,
        out_specs=(VMEM,) * 8,
        scratch_shapes=[
            pltpu.VMEM((HD, T), BF16),
            pltpu.VMEM((HD, T), BF16),
            pltpu.VMEM((8, HD, OWN), BF16),
            pltpu.VMEM((8, HD, OWN), BF16),
            pltpu.VMEM((D, OWN), F32),
            pltpu.VMEM((2, D, 2 * OWN), BF16),
            pltpu.VMEM((2, D, 2 * OWN), BF16),
            pltpu.VMEM((2, D, 2 * OWN), BF16),
            pltpu.VMEM((2, D, 2 * OWN), BF16),
            pltpu.VMEM((2, D, 2 * OWN), BF16),
            pltpu.VMEM((3, D, OWN), BF16),
            pltpu.VMEM((2, D, 2 * OWN), BF16),
            pltpu.VMEM((3, D, OWN), BF16),
            pltpu.VMEM((CHIPS, HD, OWN), BF16),
            pltpu.VMEM((D, OWN), BF16),
            sems(8), sems(3), sems(3), sems(3), sems(8), sems(15),
        ],
        compiler_params=pltpu.CompilerParams(
            collective_id=2, has_side_effects=True, vmem_limit_bytes=LIMIT
        ),
        name="layer_b",
    )(pick, qkv, x2, go4, go_own, gain_b, wat, wb)


def layer_c_kernel(
    pick_ref, qkv_ref, go_heads, lse_ref, of_ref, x1_ref, x2_ref, gx3_ref, na_ref, n3_ref,
    gain_a, gain_n, wat_ref, wa_ref,
    gy1_ref, gqkv_ref, gmlp_ref, ggain_ref,
    keys, values, kv_grad, q_grad, mine, core_got, chip_sum, head_grads, gz, parts, got,
    hidden_ref, ggate_ref, gup_ref, sem_q, sem_n, sem_z, sem_y,
):
    place = Place()
    me, chip, core = place.me, place.chip, place.core
    greet([place.around(step) for step in range(1, MP)])
    pick = pick_ref[0]
    spread(qkv_ref, keys, values)
    for part in range(2):
        quarter = place.quarters[part]
        queries = query_block(qkv_ref, quarter)
        out_grad = jnp.concatenate([go_heads[part * 4 + index] for index in range(4)], axis=1)
        inner = jnp.sum(of_ref[part] * out_grad.astype(F32), axis=0, keepdims=True)
        queries_t = queries.T
        out_grad_t = out_grad.T
        query_grad = jnp.zeros((HD, 512), F32)
        for chunk in range(2 + 2 * part):
            here = slice(chunk * 512, (chunk + 1) * 512)
            scores = tn(keys[:, here], queries) - lse_ref[part]
            probs = jnp.where(score_mask(quarter, chunk, pick), jnp.exp(scores), 0.0)
            score_grad = (probs * (tn(values[:, here], out_grad) - inner)).astype(BF16)
            query_grad = query_grad + nn(keys[:, here], score_grad)
            key_part = nn(score_grad, queries_t)
            value_part = nn(probs.astype(BF16), out_grad_t)
            both = jnp.concatenate([key_part, value_part], axis=1)
            if part == 1 and chunk < 2:
                both = both + kv_grad[here]
            kv_grad[here] = both
        q_grad[part] = (query_grad * HD**-0.5).astype(BF16)
    for index in range(MP):
        mine[index // 2, index % 2, :HD] = jnp.zeros((HD, OWN), BF16)
        mine[index // 2, index % 2, HD:] = kv_grad[index * OWN : (index + 1) * OWN].T.astype(BF16)
    for part in range(2):
        quarter = place.quarters[part]
        for index in range(4):
            mine[quarter * 2 + index // 2, index % 2, :HD] = q_grad[part, :, index * OWN : (index + 1) * OWN]
    order = list(range(1, CHIPS)) + [0]
    first = []
    for step in order:
        there = place.chip_at(step)
        copy = remote(mine.at[there, 1 - core], core_got.at[there], sem_q, step, place.partner)
        copy.start()
        first.append(copy)
    second = []
    for copy, step in zip(first, order):
        there = place.chip_at(step)
        copy.wait_recv()
        total = (mine[there, core].astype(F32) + core_got[there].astype(F32)).astype(BF16)
        if step == 0:
            head_grads[chip] = total
        else:
            chip_sum[step - 1] = total
            move = remote(chip_sum.at[step - 1], head_grads.at[chip], sem_q, 7 + step, there * 2 + core)
            move.start()
            second.append(move)
    for move in second:
        move.wait_recv()
    w_qkv = wat_ref[:, : 3 * CH].reshape(3 * D, D)
    columns = head_grads[...].reshape(3 * D, OWN)
    stream_grad, gain_grad = norm_backward(tn(w_qkv, columns), x2_ref[...], gain_n[...])
    ggain_ref[1] = gain_grad
    gx2 = gx3_ref[...] + stream_grad
    gz[place.y, :, half(core)] = gx2.astype(BF16)
    near, far, close_n = gather_four(place, gz, sem_n)
    w_gate = wa_ref[:, 0].reshape(D, D)
    w_up = wa_ref[:, 1].reshape(D, D)
    w_down = wa_ref[:, 2].reshape(D, D)
    send_far, send_near, relay, total_gn, close_z = scatter_four(place, parts, got, sem_z)

    def block(where):
        rows_here = na_ref[where]
        gate = nn(w_gate, rows_here)
        up = nn(w_up, rows_here)
        sig = jax.nn.sigmoid(gate)
        hidden_grad = nn(w_down, gz[where])
        gate_grad = (hidden_grad * up * sig * (1.0 + gate * (1.0 - sig))).astype(BF16)
        up_grad = (hidden_grad * gate * sig).astype(BF16)
        ggate_ref[where] = gate_grad
        gup_ref[where] = up_grad
        parts[where] = (tn(w_gate, gate_grad) + tn(w_up, up_grad)).astype(BF16)
        hidden_ref[where] = (gate * sig * up).astype(BF16)

    near()
    block(place.y)
    send_near()
    far()
    block(1 - place.y)
    send_far()
    relay()
    stream_grad, gain_grad = norm_backward(total_gn(), x1_ref[...], gain_a[...])
    ggain_ref[0] = gain_grad
    gy1_ref[:, half(me)] = (gx2 + stream_grad).astype(BF16)
    sends = []
    for step in range(1, CHIPS):
        there = place.chip_at(step)
        block_here = gy1_ref.at[:, half(me)]
        copy = remote(block_here, block_here, sem_y, step - 1, there * 2 + core)
        copy.start()
        sends.append(copy)
    block_here = gy1_ref.at[:, half(me)]
    forwards = [remote(block_here, block_here, sem_y, 7, place.partner)]
    forwards[0].start()
    gqkv_ref[...] = nt(columns, n3_ref[...]).astype(BF16)
    for group, (left, right) in enumerate(((ggate_ref, na_ref), (gup_ref, na_ref), (hidden_ref, gz))):
        value = (nt(left[0], right[0]) + nt(left[1], right[1])).astype(BF16)
        for index in range(4):
            gmlp_ref[index, group] = value[index * OWN : (index + 1) * OWN]
    for step in range(1, CHIPS):
        source = place.chip_at(CHIPS - step) * 2 + core
        sends[step - 1].wait_recv()
        block_here = gy1_ref.at[:, half(source)]
        copy = remote(block_here, block_here, sem_y, 7 + step, place.partner)
        copy.start()
        forwards.append(copy)
    for copy in forwards:
        copy.wait()
    for copy in first + second + sends:
        copy.wait_send()
    close_n()
    close_z()


def layer_c(pick, qkv, go_heads, lse, of, x1, x2, gx3, na, n3, gain_a, gain_n, wat, wa):
    return pl.pallas_call(
        layer_c_kernel,
        out_shape=(
            jax.ShapeDtypeStruct((D, T), BF16),
            jax.ShapeDtypeStruct((3 * D, D), BF16),
            jax.ShapeDtypeStruct((4, 3, OWN, D), BF16),
            jax.ShapeDtypeStruct((2, D, 1), F32),
        ),
        in_specs=[SMEM] + [VMEM] * 13,
        out_specs=(VMEM,) * 4,
        scratch_shapes=[
            pltpu.VMEM((HD, T), BF16),
            pltpu.VMEM((HD, T), BF16),
            pltpu.VMEM((T, 2 * HD), F32),
            pltpu.VMEM((2, HD, 512), BF16),
            pltpu.VMEM((CHIPS, 2, 3 * HD, OWN), BF16),
            pltpu.VMEM((CHIPS, 3 * HD, OWN), BF16),
            pltpu.VMEM((CHIPS - 1, 3 * HD, OWN), BF16),
            pltpu.VMEM((CHIPS, 3 * HD, OWN), BF16),
            pltpu.VMEM((2, D, 2 * OWN), BF16),
            pltpu.VMEM((2, D, 2 * OWN), BF16),
            pltpu.VMEM((3, D, OWN), BF16),
            pltpu.VMEM((2, D, 2 * OWN), BF16),
            pltpu.VMEM((2, D, 2 * OWN), BF16),
            pltpu.VMEM((2, D, 2 * OWN), BF16),
            sems(15), sems(3), sems(3), sems(15),
        ],
        compiler_params=pltpu.CompilerParams(
            collective_id=3, has_side_effects=True, vmem_limit_bytes=LIMIT
        ),
        name="layer_c",
    )(pick, qkv, go_heads, lse, of, x1, x2, gx3, na, n3, gain_a, gain_n, wat, wa)


def conv_backward_kernel(
    pick_ref, gy_ref, x_ref, taps_ref, weight_ref, gh_ref, gw_ref, feature_grad, shifted, table, total
):
    step = pl.program_id(0)
    wide = 2 * OWN
    count = T // wide

    @pl.when(step == 0)
    def _():
        for group in range(4):
            here = slice(group * 512, (group + 1) * 512)
            value = nn(weight_ref[: K * CH], gy_ref[:, here])
            feature_grad[:, here] = value.astype(BF16)
        total[...] = jnp.zeros_like(total)
        shifted[...] = jnp.zeros_like(shifted)

    joined = jnp.full((CH, T // 2), (pick_ref[0] == 1).astype(F32)).astype(BF16)
    for index in range(2):
        base = pl.multiple_of((step * 2 + index) * CH, CH)
        mine = feature_grad[pl.ds(base, CH), :]
        for source in range(count):
            here = slice(source * CH, (source + 1) * CH)
            begin = source * wide
            if source < count // 2:
                near = T // 2 - begin
                shifted[index, here, :near] = mine[:, begin : T // 2]
                shifted[index, here, near : T - begin] = mine[:, T // 2 :] * joined
            else:
                shifted[index, here, : T - begin] = mine[:, begin:]
        filter_table = toeplitz(taps_ref[0, index : index + 1, :])
        table[index, :OWN, :] = filter_table
        table[index, OWN:, OWN:] = filter_table[:, : T - OWN]
        table[index, OWN:, :OWN] = jnp.zeros((OWN, OWN), BF16)
    middle = CH * count // 2
    for index in range(2):
        total[:middle] += nt(shifted[index, :middle, :], table[index])
        total[middle:] += nt(shifted[index, middle:, : T // 2], table[index, :, : T // 2])

    @pl.when(step == K // 2 - 1)
    def _():
        gw_ref[...] = nt(x_ref[...], gy_ref[...]).astype(BF16)
        pick = pick_ref[0]
        for source in range(count):
            gh_ref[:, source * wide : (source + 1) * wide] = total[source * CH : (source + 1) * CH]
        for shift in range(LAGS):
            first = (K + shift) * CH
            value = nn(weight_ref[first : first + CH], gy_ref[...])
            value = jnp.where(lag_mask(shift, pick), value, 0.0)
            if shift:
                value = pltpu.roll(value, T - shift, 1)
            gh_ref[...] += value


def conv_backward(pick, gy, x, taps, weight):
    whole = lambda *shape: pl.BlockSpec(shape, lambda i: (0,) * len(shape))
    return pl.pallas_call(
        conv_backward_kernel,
        grid=(K // 2,),
        out_shape=(
            jax.ShapeDtypeStruct((CH, T), F32),
            jax.ShapeDtypeStruct((FEAT, D), BF16),
        ),
        in_specs=[
            SMEM,
            whole(D, T),
            whole(FEAT, T),
            pl.BlockSpec((1, 2, T), lambda i: (i, 0, 0)),
            whole(FEAT, D),
        ],
        out_specs=(whole(CH, T), whole(FEAT, D)),
        scratch_shapes=[
            pltpu.VMEM((K * CH, T), BF16),
            pltpu.VMEM((2, CH * T // (2 * OWN), T), BF16),
            pltpu.VMEM((2, 2 * OWN, T), BF16),
            pltpu.VMEM((CH * T // (2 * OWN), 2 * OWN), F32),
        ],
        compiler_params=pltpu.CompilerParams(vmem_limit_bytes=LIMIT),
        name="conv_backward",
    )(pick, gy, x, taps, weight)


def last_norm_kernel(x_ref, gh_ref, gy_ref, scale_ref, gain_ref, gx_ref, ggain_ref, inner, sem):
    place = Place()
    me = place.me
    stream = x_ref[...].astype(F32)
    scaled = gh_ref[...] * gain_ref[...]
    inner[pl.ds(me, 1)] = jnp.sum(scaled * stream, axis=0, keepdims=True)[None]
    greet([place.around(step) for step in range(1, MP)])
    sums = []
    for step in range(1, MP):
        copy = remote(inner.at[me], inner.at[me], sem, step - 1, place.around(step))
        copy.start()
        sums.append(copy)
    scaling = scale_ref[...]
    ggain_ref[...] = jnp.sum(gh_ref[...] * stream * scaling, axis=1, keepdims=True)
    for copy in sums:
        copy.wait()
    total = inner[0]
    for index in range(1, MP):
        total = total + inner[index]
    stream_grad = scaled * scaling - stream * (scaling * scaling * scaling * total / D)
    gx_ref[...] = stream_grad + gy_ref[rows(me, CH), :].astype(F32)


def last_norm(x, gh, gy, scaling, gain):
    return pl.pallas_call(
        last_norm_kernel,
        out_shape=(jax.ShapeDtypeStruct((CH, T), F32), jax.ShapeDtypeStruct((CH, 1), F32)),
        in_specs=[VMEM] * 5,
        out_specs=(VMEM,) * 2,
        scratch_shapes=[pltpu.VMEM((MP, 1, T), F32), sems(15)],
        compiler_params=pltpu.CompilerParams(
            collective_id=4, has_side_effects=True, vmem_limit_bytes=LIMIT
        ),
        name="last_norm",
    )(x, gh, gy, scaling, gain)


Z_GROUPS = [[b + 4 * z for z in range(4)] for b in range(4)]


def on_device(
    inputs, out_grad, shape_pick, filters, stu_gain, stu_weight,
    mlp_gain_a, gate_a, up_a, down_a, attn_gain, qkv_weight, out_weight,
    mlp_gain_b, gate_b, up_b, down_b,
):
    def over_z(*weights):
        return lax.all_gather(jnp.stack(weights), "mp", axis_index_groups=Z_GROUPS)

    wa = over_z(gate_a.T, up_a.T, down_a)
    wat = lax.all_gather(jnp.concatenate([qkv_weight.T, out_weight]), "mp")
    wb = over_z(gate_b.T, up_b.T, down_b)
    all_gains = lax.all_gather(jnp.stack([mlp_gain_a, attn_gain, mlp_gain_b]), "mp", axis=1, tiled=True)
    all_gains = all_gains.astype(F32)[:, :, None]
    gain_a, gain_n, gain_b = all_gains[0], all_gains[1], all_gains[2]
    gain_s = stu_gain.astype(F32)[:, None]
    taps = filters.astype(F32).reshape(K // 2, 2, T)
    weight = stu_weight.reshape(FEAT, D)
    x = inputs.T
    go = out_grad.T

    h, scaling, x_own, go_own = first_norm(x, go, gain_s)
    features, y = conv_forward(shape_pick, h, taps, weight)
    x1, x2, na, go4, n3, qkv = layer_a(
        y.reshape(CHIPS, 2, D, OWN), x_own, go_own, gain_a, gain_n, wa, wat
    )
    lse, of, go_heads, gx3, out, gwo, gmlp_b, ggain_b = layer_b(
        shape_pick, qkv, x2, go4, go_own, gain_b, wat, wb
    )
    gy1, gwqkv, gmlp_a, ggain_an = layer_c(
        shape_pick, qkv, go_heads, lse, of, x1, x2, gx3, na, n3, gain_a, gain_n, wat, wa
    )
    gh, gws = conv_backward(shape_pick, gy1, features, taps, weight)
    gx, ggain_s = last_norm(x, gh, gy1, scaling, gain_s)

    def mlp_total(terms):
        mine = lax.psum_scatter(terms, "mp", scatter_dimension=0, axis_index_groups=Z_GROUPS)
        return lax.psum(mine, "dp").astype(F32)

    ga = mlp_total(gmlp_a)
    gb = mlp_total(gmlp_b)
    gat = jnp.concatenate([gwqkv.reshape(MP, 3 * CH, D), gwo.reshape(MP, CH, D)], axis=1)
    gat = lax.psum_scatter(gat, "mp", scatter_dimension=0)
    gat = lax.psum(gat, "dp").astype(F32)
    gws = lax.psum(gws, "dp").astype(F32)
    ggains = jnp.concatenate([ggain_an, ggain_b[None]], axis=0)[:, :, 0]
    ggains = lax.psum_scatter(ggains, "mp", scatter_dimension=1, tiled=True)
    ggains = lax.psum(jnp.concatenate([ggains, ggain_s[:, 0][None]], axis=0), "dp")
    return (
        out.T,
        gx.T,
        ggains[3],
        gws.reshape(K + LAGS, CH, D),
        ggains[0],
        ga[0].T,
        ga[1].T,
        ga[2],
        ggains[1],
        gat[: 3 * CH].T,
        gat[3 * CH :],
        ggains[2],
        gb[0].T,
        gb[1].T,
        gb[2],
    )


def solution(mesh):
    cols, mid, row = P(None, "mp"), P(None, "mp", None), P("mp", None)
    return jax.shard_map(
        on_device,
        mesh=mesh,
        in_specs=(
            P("dp", "mp"), P("dp", "mp"), P("dp"), P(), P("mp"), mid,
            P("mp"), cols, cols, row, P("mp"), cols, row, P("mp"), cols, cols, row,
        ),
        out_specs=(
            P("dp", "mp"), P("dp", "mp"), P("mp"), mid, P("mp"), cols, cols, row,
            P("mp"), cols, row, P("mp"), cols, cols, row,
        ),
        check_vma=False,
    )
```

```python
import jax
import jax.numpy as jnp
from jax import lax
from jax.experimental import pallas as pl
from jax.experimental.pallas import tpu as pltpu
from jax.sharding import PartitionSpec as P

D = 512
T = 2048
OWN = 128
CH = 32
K = 24
LAGS = 3
FEAT = (K + LAGS) * CH
HD = 64
MP = 16
DP = 8
CHIPS = 8
EPSILON = 1e-05
NEG = -1e30
F32 = jnp.float32
BF16 = jnp.bfloat16
MESH = pl.DeviceIdType.MESH
VMEM = pl.BlockSpec(memory_space=pltpu.VMEM)
SMEM = pl.BlockSpec(memory_space=pltpu.SMEM)
LIMIT = 56 * 2**20


def nn(left, right):
    return jnp.dot(left, right, preferred_element_type=F32)


def tn(left, right):
    return lax.dot_general(left, right, (((0,), (0,)), ((), ())), preferred_element_type=F32)


def nt(left, right):
    return lax.dot_general(left, right, (((1,), (1,)), ((), ())), preferred_element_type=F32)


class Place:
    def __init__(self):
        self.me = lax.axis_index("mp")
        self.z = self.me // 4
        self.chip = self.me // 2
        self.y = self.chip % 2
        self.core = self.me % 2
        self.dp = lax.axis_index("dp")
        self.x = self.dp % 4
        self.partner = self.me + 1 - 2 * self.core
        self.across = self.me + 2 - 4 * self.y
        self.query_core = ((self.z + 1) // 2) % 2
        self.quarters = (self.core, 3 - self.core)

    def around(self, step):
        return (self.me + step) % MP

    def chip_at(self, step):
        return (self.chip + step) % CHIPS

    def along_z(self, step):
        return ((self.z + step) % 4) * 4 + self.me % 4

    def along_x(self, step):
        return {"dp": self.dp - self.x + (self.x + step) % 4}

    def along_dp(self, step):
        return (self.dp + step) % DP


def half(index):
    return pl.ds(pl.multiple_of(index * OWN, OWN), OWN)


def rows(index, count):
    return pl.ds(pl.multiple_of(index * count, count), count)


def remote(src, dst, sems, slot, target):
    return pltpu.make_async_remote_copy(
        src_ref=src,
        dst_ref=dst,
        send_sem=sems.at[0, slot],
        recv_sem=sems.at[1, slot],
        device_id=target if isinstance(target, dict) else {"mp": target},
        device_id_type=MESH,
    )


def greet(targets):
    barrier = pltpu.get_barrier_semaphore()
    for target in targets:
        where = target if isinstance(target, dict) else {"mp": target}
        pl.semaphore_signal(barrier, inc=1, device_id=where, device_id_type=MESH)
    pl.semaphore_wait(barrier, len(targets))


def sems(count):
    return pltpu.SemaphoreType.DMA((2, count))


def norm_forward(stream, gain):
    scaling = lax.rsqrt(jnp.sum(stream * stream, axis=0, keepdims=True) / D + EPSILON)
    return stream * scaling * gain, scaling


def norm_backward(upstream, stream, gain):
    scaling = lax.rsqrt(jnp.sum(stream * stream, axis=0, keepdims=True) / D + EPSILON)
    gain_grad = jnp.sum(upstream * stream * scaling, axis=1, keepdims=True)
    scaled = upstream * gain
    inner = jnp.sum(scaled * stream, axis=0, keepdims=True)
    return scaled * scaling - stream * (scaling * scaling * scaling * inner / D), gain_grad


def gather_four(place, buf, sem):
    own = buf.at[place.y, :, half(place.core)]
    there = buf.at[1 - place.y, :, half(place.core)]
    to_across = remote(own, own, sem, 0, place.across)
    to_across.start()
    to_partner = remote(own, own, sem, 1, place.partner)
    to_partner.start()

    def near():
        to_partner.wait_recv()

    def far():
        to_across.wait_recv()
        forward = remote(there, there, sem, 2, place.partner)
        forward.start()
        forward.wait()

    def close():
        to_across.wait_send()
        to_partner.wait_send()

    return near, far, close


def gather_all(place, buf, sem):
    own = buf.at[:, half(place.me)]
    sends = [
        remote(own, own, sem, step - 1, place.chip_at(step) * 2 + place.core) for step in range(1, CHIPS)
    ]
    forwards = [remote(own, own, sem, 7, place.partner)]
    for step in range(1, CHIPS):
        here = buf.at[:, half(place.chip_at(CHIPS - step) * 2 + place.core)]
        forwards.append(remote(here, here, sem, 7 + step, place.partner))

    def spread_own():
        for copy in sends + forwards[:1]:
            copy.start()

    def forward():
        for step in range(1, CHIPS):
            sends[step - 1].wait_recv()
            forwards[step].start()

    def close():
        for copy in sends:
            copy.wait_send()
        for copy in forwards:
            copy.wait()

    return spread_own, forward, close


def scatter_four(place, parts, got, sem):
    keep = half(place.core)
    away = half(1 - place.core)
    far_part = remote(parts.at[1 - place.y, :, away], got.at[0], sem, 0, place.partner)
    near_part = remote(parts.at[place.y, :, away], got.at[1], sem, 1, place.partner)
    across_part = remote(parts.at[1 - place.y, :, keep], got.at[2], sem, 2, place.across)

    def send_far():
        far_part.start()

    def send_near():
        near_part.start()

    def relay():
        far_part.wait_recv()
        total = parts[1 - place.y, :, keep].astype(F32) + got[0].astype(F32)
        parts[1 - place.y, :, keep] = total.astype(BF16)
        across_part.start()

    def total():
        near_part.wait_recv()
        across_part.wait_recv()
        return parts[place.y, :, keep].astype(F32) + got[1].astype(F32) + got[2].astype(F32)

    def close():
        far_part.wait_send()
        near_part.wait_send()
        across_part.wait_send()

    return send_far, send_near, relay, total, close


def toeplitz(taps):
    wide = pltpu.roll(jnp.broadcast_to(taps, (OWN, T)), 0, 1, stride=1, stride_axis=0)
    lane = lax.broadcasted_iota(jnp.int32, (OWN, T), 1)
    row = lax.broadcasted_iota(jnp.int32, (OWN, T), 0)
    return jnp.where(lane >= row, wide, 0.0).astype(BF16)


def lag_mask(shift, pick):
    lane = lax.broadcasted_iota(jnp.int32, (CH, T), 1)
    inner = lane % (T // 2)
    return (lane >= shift) & ((inner >= shift) | (pick == 1))


def front_kernel(
    pick_ref, x_ref, go_ref, gains_ref, taps_ref, weight_ref,
    gate_a, up_a, down_a, qkv_w, out_w, gate_b, up_b, down_b,
    scale_ref, feat_ref, x1_ref, x2_ref, na_ref, go4_ref, n3_ref, qkv_ref,
    wa_ref, wat_ref, wb_ref, gains_all, go_own,
    x_own, squares, taps, table, weight_t, blocks, y_ref,
    core_got, chip_sum, chip_got, parts, got, heads,
    sem_s, sem_x, sem_go, sem_gain, sem_wa, sem_wb, sem_wat, sem_y, sem_n, sem_g, sem_z, sem_q,
):
    place = Place()
    me, chip, core, x = place.me, place.chip, place.core, place.x
    count = T // OWN
    pick = pick_ref[0]
    stream = x_ref[...].astype(F32)
    squares[pl.ds(me, 1)] = jnp.sum(stream * stream, axis=0, keepdims=True)[None]
    wa_ref[place.z, :OWN] = gate_a[...].T
    wa_ref[place.z, OWN : 2 * OWN] = up_a[...].T
    wa_ref[place.z, 2 * OWN :] = down_a[...]
    wb_ref[place.z, :OWN] = gate_b[...].T
    wb_ref[place.z, OWN : 2 * OWN] = up_b[...].T
    wb_ref[place.z, 2 * OWN :] = down_b[...]
    wat_ref[me, : 3 * CH] = qkv_w[...].T
    wat_ref[me, 3 * CH :] = out_w[...]
    greet([place.around(step) for step in range(1, MP)] + [place.along_x(step) for step in range(1, 4)])
    sums, late = [], []
    for step in range(1, MP):
        there = place.around(step)
        copy = remote(squares.at[me], squares.at[me], sem_s, step - 1, there)
        copy.start()
        sums.append(copy)
    wa_sends, wb_sends, wat_sends = [], [], []
    for step in range(1, 4):
        there = place.along_z(step)
        copy = remote(wa_ref.at[place.z], wa_ref.at[place.z], sem_wa, step - 1, there)
        copy.start()
        wa_sends.append(copy)
    for step in range(1, MP):
        there = place.around(step)
        for src, dst, sem in (
            (x_ref.at[:, half(there)], x_own.at[rows(me, CH)], sem_x),
            (go_ref.at[:, half(there)], go_own.at[rows(me, CH)], sem_go),
            (gains_ref.at[:3], gains_all.at[:, rows(me, CH)], sem_gain),
        ):
            copy = remote(src, dst, sem, step - 1, there)
            copy.start()
            late.append(copy)
    part_t = wat_ref.at[me, rows(x, CH)]
    for step in range(1, MP):
        copy = remote(part_t, part_t, sem_wat, step - 1, place.around(step))
        copy.start()
        wat_sends.append(copy)
    part_b = wb_ref.at[place.z, rows(x, 96)]
    for step in range(1, 4):
        copy = remote(part_b, part_b, sem_wb, step - 1, place.along_z(step))
        copy.start()
        wb_sends.append(copy)
    x_own[rows(me, CH), :] = x_ref[:, half(me)]
    go_own[rows(me, CH), :] = go_ref[:, half(me)]
    gains_all[:, rows(me, CH)] = gains_ref[:3]
    taps[...] = taps_ref[...].astype(F32)
    weight_t[...] = weight_ref[...].T

    @pl.loop(0, K // 2)
    def _(step):
        for index in range(2):
            filter_table = toeplitz(taps[pl.ds(step * 2 + index, 1), :])
            for offset in range(count):
                table[step, offset * OWN : (offset + 1) * OWN, index * OWN : (index + 1) * OWN] = filter_table[
                    :, offset * OWN : (offset + 1) * OWN
                ]

    for copy in sums:
        copy.wait()
    total = squares[0]
    for index in range(1, MP):
        total = total + squares[index]
    scaling = lax.rsqrt(total / D + EPSILON)
    scale_ref[...] = scaling
    own = stream * scaling * gains_ref[3].astype(F32)[:, :1]
    h = own.astype(BF16)
    own = h.astype(F32)
    joined = jnp.full((CH, OWN), (pick == 1).astype(F32)).astype(BF16)
    for target in range(count):
        for offset in range(count):
            here = (slice(target * CH, (target + 1) * CH), slice(offset * OWN, (offset + 1) * OWN))
            if offset > target:
                blocks[here] = jnp.zeros((CH, OWN), BF16)
                continue
            source = target - offset
            value = h[:, source * OWN : (source + 1) * OWN]
            if target >= count // 2 and source < count // 2:
                value = value * joined
            blocks[here] = value
    for shift in range(LAGS):
        moved = own if shift == 0 else pltpu.roll(own, shift, 1)
        moved = jnp.where(lag_mask(shift, pick), moved, 0.0).astype(BF16)
        feat_ref[(K + shift) * CH : (K + shift + 1) * CH, :] = moved

    def convolve(step):
        early = nn(blocks[: CH * count // 2, : T // 2], table[step, : T // 2, :]).astype(BF16)
        late_half = nn(blocks[CH * count // 2 :, :], table[step]).astype(BF16)
        for index in range(2):
            base = pl.multiple_of((step * 2 + index) * CH, CH)
            for target in range(count):
                part, at = (early, target) if target < count // 2 else (late_half, target - count // 2)
                feat_ref[pl.ds(base, CH), target * OWN : (target + 1) * OWN] = part[
                    at * CH : (at + 1) * CH, index * OWN : (index + 1) * OWN
                ]

    pl.loop(0, K // 4)(convolve)
    more = []
    for copy in wat_sends:
        copy.wait_recv()
    for copy in wb_sends:
        copy.wait_recv()
    mine_t = wat_ref.at[:, rows(x, CH)]
    mine_b = wb_ref.at[:, rows(x, 96)]
    for step in range(1, 4):
        copy = remote(mine_t, mine_t, sem_wat, 14 + step, place.along_x(step))
        copy.start()
        more.append(copy)
    for step in range(1, 4):
        copy = remote(mine_b, mine_b, sem_wb, 2 + step, place.along_x(step))
        copy.start()
        more.append(copy)
    pl.loop(K // 4, K // 2)(convolve)
    for group in range(4):
        y = nn(weight_t[...], feat_ref[:, group * 512 : (group + 1) * 512]).astype(BF16)
        for index in range(4):
            y_ref[group * 2 + index // 2, index % 2] = y[:, index * OWN : (index + 1) * OWN]
    order = list(range(1, CHIPS)) + [0]
    first = []
    for step in order:
        there = place.chip_at(step)
        copy = remote(y_ref.at[there, 1 - core], core_got.at[there], sem_y, step, place.partner)
        copy.start()
        first.append(copy)
    second = []
    for copy, step in zip(first, order):
        there = place.chip_at(step)
        copy.wait_recv()
        total = y_ref[there, core].astype(F32) + core_got[there].astype(F32)
        if step == 0:
            x1_ref[...] = total
        else:
            chip_sum[step - 1] = total.astype(BF16)
            move = remote(chip_sum.at[step - 1], chip_got.at[step - 1], sem_y, 7 + step, there * 2 + core)
            move.start()
            second.append(move)
    for copy in late:
        copy.wait()
    go4_ref[place.y, :, half(core)] = go_own[...]
    for move in second:
        move.wait_recv()
    x1 = x1_ref[...] + x_own[...].astype(F32)
    for index in range(CHIPS - 1):
        x1 = x1 + chip_got[index].astype(F32)
    x1_ref[...] = x1
    normed, _ = norm_forward(x1, gains_all[0].astype(F32))
    na_ref[place.y, :, half(core)] = normed.astype(BF16)
    near, far, close_n = gather_four(place, na_ref, sem_n)
    near_g, far_g, close_g = gather_four(place, go4_ref, sem_g)
    for copy in wa_sends:
        copy.wait_recv()
    w_gate = wa_ref[:, :OWN].reshape(D, D)
    w_up = wa_ref[:, OWN : 2 * OWN].reshape(D, D)
    w_down = wa_ref[:, 2 * OWN :].reshape(D, D)
    send_far, send_near, relay, total_z, close_z = scatter_four(place, parts, got, sem_z)

    def block(where):
        rows_here = na_ref[where]
        gate = nn(w_gate, rows_here)
        hidden = (gate * jax.nn.sigmoid(gate) * nn(w_up, rows_here)).astype(BF16)
        parts[where] = tn(w_down, hidden).astype(BF16)

    near()
    block(place.y)
    send_near()
    far()
    block(1 - place.y)
    send_far()
    relay()
    x2 = x1 + total_z()
    x2_ref[...] = x2
    n3 = norm_forward(x2, gains_all[1].astype(F32))[0].astype(BF16)
    n3_ref[...] = n3
    for copy in more:
        copy.wait_recv()
    w_qkv = wat_ref[:, : 3 * CH].reshape(3 * D, D)
    heads[...] = nn(w_qkv, n3).astype(BF16).reshape(CHIPS, 3 * HD, OWN)
    sends = []
    for step in range(1, CHIPS):
        there = place.chip_at(step)
        copy = remote(heads.at[there], qkv_ref.at[me], sem_q, step - 1, there * 2 + core)
        copy.start()
        sends.append(copy)
    qkv_ref[me] = heads[chip]
    forwards = [remote(qkv_ref.at[me], qkv_ref.at[me], sem_q, 7, place.partner)]
    forwards[0].start()
    for step in range(1, CHIPS):
        source = place.chip_at(CHIPS - step) * 2 + core
        sends[step - 1].wait_recv()
        copy = remote(qkv_ref.at[source], qkv_ref.at[source], sem_q, 7 + step, place.partner)
        copy.start()
        forwards.append(copy)
    near_g()
    far_g()
    for copy in forwards:
        copy.wait()
    for copy in wa_sends + wb_sends + wat_sends + more + first + second + sends:
        copy.wait_send()
    close_n()
    close_g()
    close_z()


def front(pick, x, go, gains, taps, weight, *weights):
    return pl.pallas_call(
        front_kernel,
        out_shape=(
            jax.ShapeDtypeStruct((1, T), F32),
            jax.ShapeDtypeStruct((FEAT, T), BF16),
            jax.ShapeDtypeStruct((D, OWN), F32),
            jax.ShapeDtypeStruct((D, OWN), F32),
            jax.ShapeDtypeStruct((2, D, 2 * OWN), BF16),
            jax.ShapeDtypeStruct((2, D, 2 * OWN), BF16),
            jax.ShapeDtypeStruct((D, OWN), BF16),
            jax.ShapeDtypeStruct((MP, 3 * HD, OWN), BF16),
            jax.ShapeDtypeStruct((4, 3 * OWN, D), BF16),
            jax.ShapeDtypeStruct((MP, OWN, D), BF16),
            jax.ShapeDtypeStruct((4, 3 * OWN, D), BF16),
            jax.ShapeDtypeStruct((3, D, OWN), BF16),
            jax.ShapeDtypeStruct((D, OWN), BF16),
        ),
        in_specs=[SMEM] + [VMEM] * 13,
        out_specs=(VMEM,) * 13,
        scratch_shapes=[
            pltpu.VMEM((D, OWN), BF16),
            pltpu.VMEM((MP, 1, T), F32),
            pltpu.VMEM((K, T), F32),
            pltpu.VMEM((K // 2, T, 2 * OWN), BF16),
            pltpu.VMEM((D, FEAT), BF16),
            pltpu.VMEM((CH * T // OWN, T), BF16),
            pltpu.VMEM((CHIPS, 2, D, OWN), BF16),
            pltpu.VMEM((CHIPS, D, OWN), BF16),
            pltpu.VMEM((CHIPS - 1, D, OWN), BF16),
            pltpu.VMEM((CHIPS - 1, D, OWN), BF16),
            pltpu.VMEM((2, D, 2 * OWN), BF16),
            pltpu.VMEM((3, D, OWN), BF16),
            pltpu.VMEM((CHIPS, 3 * HD, OWN), BF16),
            sems(15), sems(15), sems(15), sems(15), sems(3), sems(6), sems(18),
            sems(15), sems(3), sems(3), sems(3), sems(15),
        ],
        compiler_params=pltpu.CompilerParams(
            collective_id=0, has_side_effects=True, vmem_limit_bytes=LIMIT
        ),
        name="front",
    )(pick, x, go, gains, taps, weight, *weights)


def spread(qkv_ref, keys, values):
    for index in range(MP):
        keys[:, index * OWN : (index + 1) * OWN] = qkv_ref[index, HD : 2 * HD]
        values[:, index * OWN : (index + 1) * OWN] = qkv_ref[index, 2 * HD :]


def query_block(qkv_ref, quarter):
    parts = [qkv_ref[quarter * 4 + index, :HD] for index in range(4)]
    return jnp.concatenate(parts, axis=1) * jnp.asarray(HD**-0.5, BF16)


def score_mask(quarter, chunk, pick):
    query = quarter * 512 + lax.broadcasted_iota(jnp.int32, (512, 512), 1)
    key = chunk * 512 + lax.broadcasted_iota(jnp.int32, (512, 512), 0)
    same_half = (quarter // 2) == (chunk // 2)
    return (key <= query) & (same_half | (pick == 1))


def layer_b_kernel(
    pick_ref, qkv_ref, x2_ref, go4_ref, go_ref, n3_ref, gains_all, wat_ref, wb_ref,
    lse_ref, of_ref, go_heads, gx3_ref, out_ref, n3_all, o_rows, gmlp_ref, ggain_ref,
    keys, values, own_heads, all_heads, x3_ref, nb, hidden_ref, ggate_ref, gup_ref,
    parts_n, got_n, parts_z, got_z, grad_heads, out_own,
    sem_o, sem_n, sem_gn, sem_z, sem_h, sem_out, sem_all, sem_rows,
):
    place = Place()
    me, chip, core = place.me, place.chip, place.core
    greet([place.around(step) for step in range(1, MP)])
    gain_b = gains_all[2].astype(F32)
    n3_all[:, half(me)] = n3_ref[...]
    spread_n3, forward_n3, close_n3 = gather_all(place, n3_all, sem_all)
    spread_n3()
    pick = pick_ref[0]
    spread(qkv_ref, keys, values)
    for part in range(2):
        quarter = place.quarters[part]
        queries = query_block(qkv_ref, quarter)
        top = jnp.full((1, 512), NEG, F32)
        norm = jnp.zeros((1, 512), F32)
        total = jnp.zeros((HD, 512), F32)
        for chunk in range(2 + 2 * part):
            here = slice(chunk * 512, (chunk + 1) * 512)
            scores = jnp.where(score_mask(quarter, chunk, pick), tn(keys[:, here], queries), NEG)
            new_top = jnp.maximum(top, jnp.max(scores, axis=0, keepdims=True))
            weights = jnp.exp(scores - new_top)
            rescale = jnp.exp(top - new_top)
            norm = norm * rescale + jnp.sum(weights, axis=0, keepdims=True)
            total = total * rescale + nn(values[:, here], weights.astype(BF16))
            top = new_top
        total = total / norm
        lse_ref[part] = top + jnp.log(norm)
        of_ref[part] = total
        for index in range(4):
            own_heads[part * 4 + index] = total[:, index * OWN : (index + 1) * OWN].astype(BF16)
    o_rows[0] = own_heads[:, rows(core, CH)]
    share = remote(own_heads.at[:, rows(1 - core, CH)], o_rows.at[1], sem_rows, 0, place.partner)
    share.start()
    targets = [place.quarters[slot // 4] * 4 + slot % 4 for slot in range(8)]
    copies = [
        pltpu.make_async_remote_copy(
            src_ref=own_heads.at[slot], dst_ref=all_heads.at[chip],
            send_sem=sem_o.at[0, slot], recv_sem=sem_o.at[1, chip],
            device_id={"mp": targets[slot]}, device_id_type=MESH,
        )
        for slot in range(8)
    ]
    for slot in range(8):
        pl.when(targets[slot] != me)(copies[slot].start)

        @pl.when(targets[slot] == me)
        def _():
            all_heads[chip] = own_heads[slot]

    arrivals = [
        remote(own_heads.at[0], all_heads.at[head], sem_o, head, place.partner) for head in range(CHIPS)
    ]
    for head in range(CHIPS):
        pl.when(head * 2 + place.query_core != me)(arrivals[head].wait_recv)
    w_out = wat_ref[:, 3 * CH :].reshape(D, D)
    outputs = all_heads[...].reshape(D, OWN)
    x3 = x2_ref[...] + tn(w_out, outputs)
    x3_ref[...] = x3
    nb[place.y, :, half(core)] = norm_forward(x3, gain_b)[0].astype(BF16)
    near, far, close_n = gather_four(place, nb, sem_n)
    w_gate = wb_ref[:, :OWN].reshape(D, D)
    w_up = wb_ref[:, OWN : 2 * OWN].reshape(D, D)
    w_down = wb_ref[:, 2 * OWN :].reshape(D, D)
    far_gn, near_gn, relay_gn, total_gn, close_gn = scatter_four(place, parts_n, got_n, sem_gn)
    far_z, near_z, relay_z, total_z, close_z = scatter_four(place, parts_z, got_z, sem_z)

    def block(where):
        rows_here = nb[where]
        gate = nn(w_gate, rows_here)
        up = nn(w_up, rows_here)
        sig = jax.nn.sigmoid(gate)
        hidden_grad = nn(w_down, go4_ref[where])
        gate_grad = (hidden_grad * up * sig * (1.0 + gate * (1.0 - sig))).astype(BF16)
        up_grad = (hidden_grad * gate * sig).astype(BF16)
        ggate_ref[where] = gate_grad
        gup_ref[where] = up_grad
        parts_n[where] = (tn(w_gate, gate_grad) + tn(w_up, up_grad)).astype(BF16)
        hidden_ref[where] = (gate * sig * up).astype(BF16)

    near()
    block(place.y)
    near_gn()
    far()
    block(1 - place.y)
    far_gn()
    forward_n3()
    parts_z[place.y] = tn(w_down, hidden_ref[place.y]).astype(BF16)
    near_z()
    relay_gn()
    parts_z[1 - place.y] = tn(w_down, hidden_ref[1 - place.y]).astype(BF16)
    far_z()
    relay_z()
    stream_grad, gain_grad = norm_backward(total_gn(), x3_ref[...], gain_b)
    ggain_ref[...] = gain_grad
    gx3 = go_ref[...].astype(F32) + stream_grad
    gx3_ref[...] = gx3
    gy = gx3.astype(BF16)
    grad_heads[...] = nn(w_out, gy).astype(BF16).reshape(CHIPS, HD, OWN)
    slot = (place.z // 2) * 4 + me % 4
    sends = [
        pltpu.make_async_remote_copy(
            src_ref=grad_heads.at[head], dst_ref=go_heads.at[slot],
            send_sem=sem_h.at[0, head], recv_sem=sem_h.at[1, slot],
            device_id={"mp": head * 2 + place.query_core}, device_id_type=MESH,
        )
        for head in range(CHIPS)
    ]
    for head in range(CHIPS):
        pl.when(head * 2 + place.query_core != me)(sends[head].start)

        @pl.when(head * 2 + place.query_core == me)
        def _():
            go_heads[slot] = grad_heads[head]

    out_own[...] = (x3_ref[...] + total_z()).astype(BF16)
    moves = []
    for step in range(1, MP):
        there = place.around(step)
        copy = remote(out_own.at[rows(there, CH)], out_ref.at[:, half(me)], sem_out, step - 1, there)
        copy.start()
        moves.append(copy)
    out_ref[:, half(me)] = out_own[rows(me, CH), :]
    for group, (left, right) in enumerate(((ggate_ref, nb), (gup_ref, nb), (hidden_ref, go4_ref))):
        value = (nt(left[0], right[0]) + nt(left[1], right[1])).astype(BF16)
        for index in range(4):
            gmlp_ref[index, group * OWN : (group + 1) * OWN] = value[index * OWN : (index + 1) * OWN]
    for slot_in in range(8):
        arrival = remote(grad_heads.at[0], go_heads.at[slot_in], sem_h, slot_in, place.partner)
        pl.when(targets[slot_in] != me)(arrival.wait_recv)
    for slot_out in range(8):
        pl.when(targets[slot_out] != me)(copies[slot_out].wait_send)
        pl.when(slot_out * 2 + place.query_core != me)(sends[slot_out].wait_send)
    for copy in moves:
        copy.wait()
    share.wait()
    close_n3()
    close_n()
    close_gn()
    close_z()


def layer_b(pick, qkv, x2, go4, go_own, n3, gains, wat, wb):
    return pl.pallas_call(
        layer_b_kernel,
        out_shape=(
            jax.ShapeDtypeStruct((2, 1, 512), F32),
            jax.ShapeDtypeStruct((2, HD, 512), F32),
            jax.ShapeDtypeStruct((8, HD, OWN), BF16),
            jax.ShapeDtypeStruct((D, OWN), F32),
            jax.ShapeDtypeStruct((CH, T), BF16),
            jax.ShapeDtypeStruct((D, T), BF16),
            jax.ShapeDtypeStruct((2, 8, CH, OWN), BF16),
            jax.ShapeDtypeStruct((4, 3 * OWN, D), BF16),
            jax.ShapeDtypeStruct((D, 1), F32),
        ),
        in_specs=[SMEM] + [VMEM] * 8,
        out_specs=(VMEM,) * 9,
        scratch_shapes=[
            pltpu.VMEM((HD, T), BF16),
            pltpu.VMEM((HD, T), BF16),
            pltpu.VMEM((8, HD, OWN), BF16),
            pltpu.VMEM((8, HD, OWN), BF16),
            pltpu.VMEM((D, OWN), F32),
            pltpu.VMEM((2, D, 2 * OWN), BF16),
            pltpu.VMEM((2, D, 2 * OWN), BF16),
            pltpu.VMEM((2, D, 2 * OWN), BF16),
            pltpu.VMEM((2, D, 2 * OWN), BF16),
            pltpu.VMEM((2, D, 2 * OWN), BF16),
            pltpu.VMEM((3, D, OWN), BF16),
            pltpu.VMEM((2, D, 2 * OWN), BF16),
            pltpu.VMEM((3, D, OWN), BF16),
            pltpu.VMEM((CHIPS, HD, OWN), BF16),
            pltpu.VMEM((D, OWN), BF16),
            sems(8), sems(3), sems(3), sems(3), sems(8), sems(15), sems(15), sems(1),
        ],
        compiler_params=pltpu.CompilerParams(
            collective_id=1, has_side_effects=True, vmem_limit_bytes=LIMIT
        ),
        name="layer_b",
    )(pick, qkv, x2, go4, go_own, n3, gains, wat, wb)


def layer_c_kernel(
    pick_ref, qkv_ref, go_heads, lse_ref, of_ref, x1_ref, x2_ref, gx3_ref, na_ref, n3_all, o_rows,
    gmlp_b, ggain_b, gains_all, wat_ref, wa_ref,
    gy1_ref, gat_ref, gmlp_ref, ggain_ref, sum_b,
    keys, values, kv_grad, q_grad, mine, core_got, chip_sum, head_grads, gz, parts, got,
    hidden_ref, ggate_ref, gup_ref, gy_all, row_got, q_rows, o_all, dp_got, dp_sum, z_got,
    sem_q, sem_n, sem_z, sem_y, sem_gy, sem_rows, sem_dp, sem_dz, sem_dg,
):
    place = Place()
    me, chip, core = place.me, place.chip, place.core
    greet(
        [place.around(step) for step in range(1, MP)]
        + [{"dp": place.along_dp(step)} for step in range(1, DP)]
    )
    gain_a = gains_all[0].astype(F32)
    gain_n = gains_all[1].astype(F32)
    gy_all[:, half(me)] = gx3_ref[...].astype(BF16)
    spread_gy, forward_gy, close_gy = gather_all(place, gy_all, sem_gy)
    spread_gy()
    b_first = []
    for step in range(1, DP):
        there = place.along_dp(step)
        copy = remote(gmlp_b.at[:, rows(there, 48)], dp_got.at[step - 1], sem_dp, step - 1, {"dp": there})
        copy.start()
        b_first.append(copy)
    pick = pick_ref[0]
    spread(qkv_ref, keys, values)
    for part in range(2):
        quarter = place.quarters[part]
        queries = query_block(qkv_ref, quarter)
        out_grad = jnp.concatenate([go_heads[part * 4 + index] for index in range(4)], axis=1)
        inner = jnp.sum(of_ref[part] * out_grad.astype(F32), axis=0, keepdims=True)
        queries_t = queries.T
        out_grad_t = out_grad.T
        query_grad = jnp.zeros((HD, 512), F32)
        for chunk in range(2 + 2 * part):
            here = slice(chunk * 512, (chunk + 1) * 512)
            scores = tn(keys[:, here], queries) - lse_ref[part]
            probs = jnp.where(score_mask(quarter, chunk, pick), jnp.exp(scores), 0.0)
            score_grad = (probs * (tn(values[:, here], out_grad) - inner)).astype(BF16)
            query_grad = query_grad + nn(keys[:, here], score_grad)
            key_part = nn(score_grad, queries_t)
            value_part = nn(probs.astype(BF16), out_grad_t)
            both = jnp.concatenate([key_part, value_part], axis=1)
            if part == 1 and chunk < 2:
                both = both + kv_grad[here]
            kv_grad[here] = both
        q_grad[part] = (query_grad * HD**-0.5).astype(BF16)
    for index in range(MP):
        mine[index // 2, index % 2, :HD] = jnp.zeros((HD, OWN), BF16)
        mine[index // 2, index % 2, HD:] = kv_grad[index * OWN : (index + 1) * OWN].T.astype(BF16)
    for part in range(2):
        quarter = place.quarters[part]
        for index in range(4):
            mine[quarter * 2 + index // 2, index % 2, :HD] = q_grad[part, :, index * OWN : (index + 1) * OWN]
    order = list(range(1, CHIPS)) + [0]
    first = []
    for step in order:
        there = place.chip_at(step)
        copy = remote(mine.at[there, 1 - core], core_got.at[there], sem_q, step, place.partner)
        copy.start()
        first.append(copy)
    second = []
    for copy, step in zip(first, order):
        there = place.chip_at(step)
        copy.wait_recv()
        total = (mine[there, core].astype(F32) + core_got[there].astype(F32)).astype(BF16)
        chip_sum[there] = total
        if step == 0:
            head_grads[chip] = total
        else:
            move = remote(chip_sum.at[there], head_grads.at[chip], sem_q, 7 + step, there * 2 + core)
            move.start()
            second.append(move)
    share = remote(chip_sum.at[:, rows(1 - core, 96)], row_got, sem_rows, 0, place.partner)
    share.start()
    forward_gy()
    for move in second:
        move.wait_recv()
    w_qkv = wat_ref[:, : 3 * CH].reshape(3 * D, D)
    columns = head_grads[...].reshape(3 * D, OWN)
    stream_grad, gain_grad = norm_backward(tn(w_qkv, columns), x2_ref[...], gain_n)
    lane = lax.broadcasted_iota(jnp.int32, (D, OWN), 1)
    gain_grads = jnp.where(lane == 1, gain_grad, 0.0) + jnp.where(lane == 2, ggain_b[...], 0.0)
    gx2 = gx3_ref[...] + stream_grad
    gz[place.y, :, half(core)] = gx2.astype(BF16)
    near, far, close_n = gather_four(place, gz, sem_n)
    w_gate = wa_ref[:, :OWN].reshape(D, D)
    w_up = wa_ref[:, OWN : 2 * OWN].reshape(D, D)
    w_down = wa_ref[:, 2 * OWN :].reshape(D, D)
    send_far, send_near, relay, total_gn, close_z = scatter_four(place, parts, got, sem_z)

    def block(where):
        rows_here = na_ref[where]
        gate = nn(w_gate, rows_here)
        up = nn(w_up, rows_here)
        sig = jax.nn.sigmoid(gate)
        hidden_grad = nn(w_down, gz[where])
        gate_grad = (hidden_grad * up * sig * (1.0 + gate * (1.0 - sig))).astype(BF16)
        up_grad = (hidden_grad * gate * sig).astype(BF16)
        ggate_ref[where] = gate_grad
        gup_ref[where] = up_grad
        parts[where] = (tn(w_gate, gate_grad) + tn(w_up, up_grad)).astype(BF16)
        hidden_ref[where] = (gate * sig * up).astype(BF16)

    near()
    block(place.y)
    send_near()
    for copy in b_first:
        copy.wait_recv()
    total = gmlp_b[:, rows(place.dp, 48)].astype(F32)
    for index in range(DP - 1):
        total = total + dp_got[index].astype(F32)
    dp_sum[...] = total.astype(BF16)
    b_second = []
    for step in range(1, 4):
        there = (place.z + step) % 4
        copy = remote(dp_sum.at[there], z_got.at[step - 1], sem_dz, step - 1, place.along_z(step))
        copy.start()
        b_second.append(copy)
    far()
    block(1 - place.y)
    send_far()
    for copy in b_second:
        copy.wait_recv()
    total = dp_sum[place.z].astype(F32)
    for index in range(3):
        total = total + z_got[index].astype(F32)
    sum_b[rows(place.dp, 48), :] = total.astype(BF16)
    b_third = []
    done_b = sum_b.at[rows(place.dp, 48)]
    for step in range(1, DP):
        copy = remote(done_b, done_b, sem_dg, step - 1, {"dp": place.along_dp(step)})
        copy.start()
        b_third.append(copy)
    relay()
    stream_grad, gain_grad = norm_backward(total_gn(), x1_ref[...], gain_a)
    ggain_ref[...] = gain_grads + jnp.where(lane == 0, gain_grad, 0.0)
    gy1_ref[:, half(me)] = (gx2 + stream_grad).astype(BF16)
    spread_gy1, forward_gy1, close_gy1 = gather_all(place, gy1_ref, sem_y)
    spread_gy1()
    share.wait_recv()
    for index in range(CHIPS):
        q_rows[:, half(index * 2 + core)] = chip_sum[index, rows(core, 96), :]
        q_rows[:, half(index * 2 + 1 - core)] = row_got[index]
    for source in range(2):
        holder = core if source == 0 else 1 - core
        for slot in range(8):
            quarter = holder if slot < 4 else 3 - holder
            o_all[:, half(quarter * 4 + slot % 4)] = o_rows[source, slot]
    close_gy()
    gat_ref[: 3 * CH] = nt(q_rows[...], n3_all[...]).astype(BF16)
    gat_ref[3 * CH :] = nt(o_all[...], gy_all[...]).astype(BF16)
    for group, (left, right) in enumerate(((ggate_ref, na_ref), (gup_ref, na_ref), (hidden_ref, gz))):
        value = (nt(left[0], right[0]) + nt(left[1], right[1])).astype(BF16)
        for index in range(4):
            gmlp_ref[index, group * OWN : (group + 1) * OWN] = value[index * OWN : (index + 1) * OWN]
    forward_gy1()
    close_gy1()
    for copy in first + second + [share] + b_first + b_second:
        copy.wait_send()
    for copy in b_third:
        copy.wait()
    close_n()
    close_z()


def layer_c(*operands):
    return pl.pallas_call(
        layer_c_kernel,
        out_shape=(
            jax.ShapeDtypeStruct((D, T), BF16),
            jax.ShapeDtypeStruct((OWN, D), BF16),
            jax.ShapeDtypeStruct((4, 3 * OWN, D), BF16),
            jax.ShapeDtypeStruct((D, OWN), F32),
            jax.ShapeDtypeStruct((3 * OWN, D), BF16),
        ),
        in_specs=[SMEM] + [VMEM] * 15,
        out_specs=(VMEM,) * 5,
        scratch_shapes=[
            pltpu.VMEM((HD, T), BF16),
            pltpu.VMEM((HD, T), BF16),
            pltpu.VMEM((T, 2 * HD), F32),
            pltpu.VMEM((2, HD, 512), BF16),
            pltpu.VMEM((CHIPS, 2, 3 * HD, OWN), BF16),
            pltpu.VMEM((CHIPS, 3 * HD, OWN), BF16),
            pltpu.VMEM((CHIPS, 3 * HD, OWN), BF16),
            pltpu.VMEM((CHIPS, 3 * HD, OWN), BF16),
            pltpu.VMEM((2, D, 2 * OWN), BF16),
            pltpu.VMEM((2, D, 2 * OWN), BF16),
            pltpu.VMEM((3, D, OWN), BF16),
            pltpu.VMEM((2, D, 2 * OWN), BF16),
            pltpu.VMEM((2, D, 2 * OWN), BF16),
            pltpu.VMEM((2, D, 2 * OWN), BF16),
            pltpu.VMEM((D, T), BF16),
            pltpu.VMEM((CHIPS, 96, OWN), BF16),
            pltpu.VMEM((96, T), BF16),
            pltpu.VMEM((CH, T), BF16),
            pltpu.VMEM((DP - 1, 4, 48, D), BF16),
            pltpu.VMEM((4, 48, D), BF16),
            pltpu.VMEM((3, 48, D), BF16),
            sems(15), sems(3), sems(3), sems(15), sems(15), sems(1), sems(7), sems(3), sems(7),
        ],
        compiler_params=pltpu.CompilerParams(
            collective_id=2, has_side_effects=True, vmem_limit_bytes=LIMIT
        ),
        name="layer_c",
    )(*operands)


def tail_kernel(
    pick_ref, x_ref, scale_ref, gy_ref, feat_ref, taps_ref, weight_ref, gains_ref, gmlp_a, gat_ref, ggain_ref,
    gx_ref, joint_ref, sum_a, gain_sum,
    feature_grad, shifted, table, total, taps, gh_ref, joint, joint_got, z_sum, z_got, a_got, gain_got,
    gain_own, gain_dp, inner,
    sem_p, sem_z, sem_j, sem_jg, sem_a, sem_ag, sem_g, sem_gd,
):
    place = Place()
    me, dp = place.me, place.dp
    wide = 2 * OWN
    count = T // wide
    greet(
        [place.around(step) for step in range(1, MP)]
        + [{"dp": place.along_dp(step)} for step in range(1, DP)]
    )
    a_first = []
    for step in range(1, 4):
        there = (place.z + step) % 4
        copy = remote(gmlp_a.at[there], z_got.at[step - 1], sem_z, step - 1, place.along_z(step))
        copy.start()
        a_first.append(copy)
    gain_first = []
    for step in range(1, MP):
        there = place.around(step)
        copy = remote(ggain_ref.at[rows(there, CH)], gain_got.at[step - 1], sem_g, step - 1, there)
        copy.start()
        gain_first.append(copy)
    pick = pick_ref[0]
    joint[:FEAT] = nt(feat_ref[...], gy_ref[...]).astype(BF16)
    joint[FEAT : FEAT + OWN] = gat_ref[...]
    joint[FEAT + OWN :] = jnp.zeros((CH, D), BF16)
    j_first = []
    for step in range(1, DP):
        there = place.along_dp(step)
        copy = remote(joint.at[rows(there, OWN)], joint_got.at[step - 1], sem_j, step - 1, {"dp": there})
        copy.start()
        j_first.append(copy)
    taps[...] = taps_ref[...].astype(F32)
    for group in range(4):
        here = slice(group * 512, (group + 1) * 512)
        feature_grad[:, here] = nn(weight_ref[: K * CH], gy_ref[:, here]).astype(BF16)
    total[...] = jnp.zeros_like(total)
    shifted[...] = jnp.zeros_like(shifted)
    joined = jnp.full((CH, T // 2), (pick == 1).astype(F32)).astype(BF16)
    middle = CH * count // 2

    def convolve(step):
        for index in range(2):
            base = pl.multiple_of((step * 2 + index) * CH, CH)
            mine = feature_grad[pl.ds(base, CH), :]
            for source in range(count):
                here = slice(source * CH, (source + 1) * CH)
                begin = source * wide
                if source < count // 2:
                    near = T // 2 - begin
                    shifted[index, here, :near] = mine[:, begin : T // 2]
                    shifted[index, here, near : T - begin] = mine[:, T // 2 :] * joined
                else:
                    shifted[index, here, : T - begin] = mine[:, begin:]
            filter_table = toeplitz(taps[pl.ds(step * 2 + index, 1), :])
            table[index, :OWN, :] = filter_table
            table[index, OWN:, OWN:] = filter_table[:, : T - OWN]
            table[index, OWN:, :OWN] = jnp.zeros((OWN, OWN), BF16)
        for index in range(2):
            total[:middle] += nt(shifted[index, :middle, :], table[index])
            total[middle:] += nt(shifted[index, middle:, : T // 2], table[index, :, : T // 2])

    pl.loop(0, 4)(convolve)
    for copy in a_first:
        copy.wait_recv()
    value = gmlp_a[place.z].astype(F32)
    for index in range(3):
        value = value + z_got[index].astype(F32)
    z_sum[...] = value.astype(BF16)
    a_second = []
    for step in range(1, DP):
        there = place.along_dp(step)
        copy = remote(z_sum.at[rows(there, 48)], a_got.at[step - 1], sem_a, step - 1, {"dp": there})
        copy.start()
        a_second.append(copy)
    pl.loop(4, 8)(convolve)
    for copy in j_first:
        copy.wait_recv()
    value = joint[rows(dp, OWN), :].astype(F32)
    for index in range(DP - 1):
        value = value + joint_got[index].astype(F32)
    joint_ref[rows(dp, OWN), :] = value.astype(BF16)
    last = []
    done_j = joint_ref.at[rows(dp, OWN)]
    for step in range(1, DP):
        copy = remote(done_j, done_j, sem_jg, step - 1, {"dp": place.along_dp(step)})
        copy.start()
        last.append(copy)
    for copy in a_second:
        copy.wait_recv()
    value = z_sum[rows(dp, 48), :].astype(F32)
    for index in range(DP - 1):
        value = value + a_got[index].astype(F32)
    sum_a[rows(dp, 48), :] = value.astype(BF16)
    done_a = sum_a.at[rows(dp, 48)]
    for step in range(1, DP):
        copy = remote(done_a, done_a, sem_ag, step - 1, {"dp": place.along_dp(step)})
        copy.start()
        last.append(copy)
    pl.loop(8, K // 2)(convolve)
    for source in range(count):
        gh_ref[:, source * wide : (source + 1) * wide] = total[source * CH : (source + 1) * CH]
    for shift in range(LAGS):
        begin = (K + shift) * CH
        value = nn(weight_ref[begin : begin + CH], gy_ref[...])
        value = jnp.where(lag_mask(shift, pick), value, 0.0)
        if shift:
            value = pltpu.roll(value, T - shift, 1)
        gh_ref[...] += value
    stream = x_ref[...].astype(F32)
    scaled = gh_ref[...] * gains_ref[3].astype(F32)[:, :1]
    inner[pl.ds(me, 1)] = jnp.sum(scaled * stream, axis=0, keepdims=True)[None]
    sums = []
    for step in range(1, MP):
        copy = remote(inner.at[me], inner.at[me], sem_p, step - 1, place.around(step))
        copy.start()
        sums.append(copy)
    scaling = scale_ref[...]
    gain_grad = jnp.sum(gh_ref[...] * stream * scaling, axis=1, keepdims=True)
    for copy in gain_first:
        copy.wait_recv()
    value = ggain_ref[rows(me, CH), :]
    for index in range(MP - 1):
        value = value + gain_got[index]
    lane = lax.broadcasted_iota(jnp.int32, (CH, OWN), 1)
    gain_own[...] = value + jnp.where(lane == 3, gain_grad, 0.0)
    for step in range(1, DP):
        copy = remote(gain_own, gain_dp.at[step - 1], sem_gd, step - 1, {"dp": place.along_dp(step)})
        copy.start()
        last.append(copy)
    for copy in sums:
        copy.wait()
    value = inner[0]
    for index in range(1, MP):
        value = value + inner[index]
    stream_grad = scaled * scaling - stream * (scaling * scaling * scaling * value / D)
    gx_ref[...] = stream_grad + gy_ref[rows(me, CH), :].astype(F32)
    for copy in last:
        copy.wait()
    value = gain_own[...]
    for index in range(DP - 1):
        value = value + gain_dp[index]
    gain_sum[...] = value
    for copy in a_first + a_second + j_first + gain_first:
        copy.wait_send()


def tail(*operands):
    return pl.pallas_call(
        tail_kernel,
        out_shape=(
            jax.ShapeDtypeStruct((CH, T), F32),
            jax.ShapeDtypeStruct((DP * OWN, D), BF16),
            jax.ShapeDtypeStruct((3 * OWN, D), BF16),
            jax.ShapeDtypeStruct((CH, OWN), F32),
        ),
        in_specs=[SMEM] + [VMEM] * 10,
        out_specs=(VMEM,) * 4,
        scratch_shapes=[
            pltpu.VMEM((K * CH, T), BF16),
            pltpu.VMEM((2, CH * T // (2 * OWN), T), BF16),
            pltpu.VMEM((2, 2 * OWN, T), BF16),
            pltpu.VMEM((CH * T // (2 * OWN), 2 * OWN), F32),
            pltpu.VMEM((K, T), F32),
            pltpu.VMEM((CH, T), F32),
            pltpu.VMEM((DP * OWN, D), BF16),
            pltpu.VMEM((DP - 1, OWN, D), BF16),
            pltpu.VMEM((3 * OWN, D), BF16),
            pltpu.VMEM((3, 3 * OWN, D), BF16),
            pltpu.VMEM((DP - 1, 48, D), BF16),
            pltpu.VMEM((MP - 1, CH, OWN), F32),
            pltpu.VMEM((CH, OWN), F32),
            pltpu.VMEM((DP - 1, CH, OWN), F32),
            pltpu.VMEM((MP, 1, T), F32),
            sems(15), sems(3), sems(7), sems(7), sems(7), sems(7), sems(15), sems(7),
        ],
        compiler_params=pltpu.CompilerParams(
            collective_id=3, has_side_effects=True, vmem_limit_bytes=LIMIT
        ),
        name="tail",
    )(*operands)


def on_device(
    inputs, out_grad, shape_pick, filters, stu_gain, stu_weight,
    mlp_gain_a, gate_a, up_a, down_a, attn_gain, qkv_weight, out_weight,
    mlp_gain_b, gate_b, up_b, down_b,
):
    gains = jnp.stack([mlp_gain_a, attn_gain, mlp_gain_b, stu_gain])
    gains = jnp.broadcast_to(gains[:, :, None], (4, CH, OWN))
    weight = stu_weight.reshape(FEAT, D)
    x = inputs.T
    go = out_grad.T
    (
        scaling, features, x1, x2, na, go4, n3, qkv, wa, wat, wb, gains_all, go_own
    ) = front(
        shape_pick, x, go, gains, filters, weight,
        gate_a, up_a, down_a, qkv_weight, out_weight, gate_b, up_b, down_b,
    )
    lse, of, go_heads, gx3, out, n3_all, o_rows, gmlp_b, ggain_b = layer_b(
        shape_pick, qkv, x2, go4, go_own, n3, gains_all, wat, wb
    )
    gy1, gat, gmlp_a, ggain, gb = layer_c(
        shape_pick, qkv, go_heads, lse, of, x1, x2, gx3, na, n3_all, o_rows,
        gmlp_b, ggain_b, gains_all, wat, wa,
    )
    gx, joint, ga, gain_sum = tail(
        shape_pick, x, scaling, gy1, features, filters, weight, gains, gmlp_a, gat, ggain
    )
    joint, ga, gb = joint.astype(F32), ga.astype(F32), gb.astype(F32)
    return (
        out.T,
        gx.T,
        gain_sum[:, 3],
        joint[:FEAT].reshape(K + LAGS, CH, D),
        gain_sum[:, 0],
        ga[:OWN].T,
        ga[OWN : 2 * OWN].T,
        ga[2 * OWN :],
        gain_sum[:, 1],
        joint[FEAT : FEAT + 3 * CH].T,
        joint[FEAT + 3 * CH : FEAT + OWN],
        gain_sum[:, 2],
        gb[:OWN].T,
        gb[OWN : 2 * OWN].T,
        gb[2 * OWN :],
    )


def solution(mesh):
    cols, mid, row = P(None, "mp"), P(None, "mp", None), P("mp", None)
    return jax.shard_map(
        on_device,
        mesh=mesh,
        in_specs=(
            P("dp", "mp"), P("dp", "mp"), P("dp"), P(), P("mp"), mid,
            P("mp"), cols, cols, row, P("mp"), cols, row, P("mp"), cols, cols, row,
        ),
        out_specs=(
            P("dp", "mp"), P("dp", "mp"), P("mp"), mid, P("mp"), cols, cols, row,
            P("mp"), cols, row, P("mp"), cols, cols, row,
        ),
        check_vma=False,
    )
```

```python
import jax
import jax.numpy as jnp
from jax import lax
from jax.experimental import pallas as pl
from jax.experimental.pallas import tpu as pltpu
from jax.sharding import PartitionSpec as P

D = 512
T = 2048
OWN = 128
CH = 32
K = 24
LAGS = 3
FEAT = (K + LAGS) * CH
HD = 64
MP = 16
DP = 8
CHIPS = 8
EPSILON = 1e-05
NEG = -1e30
F32 = jnp.float32
BF16 = jnp.bfloat16
MESH = pl.DeviceIdType.MESH
VMEM = pl.BlockSpec(memory_space=pltpu.VMEM)
SMEM = pl.BlockSpec(memory_space=pltpu.SMEM)
LIMIT = 56 * 2**20


def nn(left, right):
    return jnp.dot(left, right, preferred_element_type=F32)


def tn(left, right):
    return lax.dot_general(left, right, (((0,), (0,)), ((), ())), preferred_element_type=F32)


def nt(left, right):
    return lax.dot_general(left, right, (((1,), (1,)), ((), ())), preferred_element_type=F32)


class Place:
    def __init__(self):
        self.me = lax.axis_index("mp")
        self.z = self.me // 4
        self.chip = self.me // 2
        self.y = self.chip % 2
        self.core = self.me % 2
        self.dp = lax.axis_index("dp")
        self.x = self.dp % 4
        self.partner = self.me + 1 - 2 * self.core
        self.across = self.me + 2 - 4 * self.y
        self.query_core = ((self.z + 1) // 2) % 2
        self.quarters = (self.core, 3 - self.core)

    def around(self, step):
        return (self.me + step) % MP

    def chip_at(self, step):
        return (self.chip + step) % CHIPS

    def along_z(self, step):
        return ((self.z + step) % 4) * 4 + self.me % 4

    def along_x(self, step):
        return {"dp": self.dp - self.x + (self.x + step) % 4}

    def along_dp(self, step):
        return (self.dp + step) % DP


def half(index):
    return pl.ds(pl.multiple_of(index * OWN, OWN), OWN)


def rows(index, count):
    return pl.ds(pl.multiple_of(index * count, count), count)


def remote(src, dst, sems, slot, target):
    return pltpu.make_async_remote_copy(
        src_ref=src,
        dst_ref=dst,
        send_sem=sems.at[0, slot],
        recv_sem=sems.at[1, slot],
        device_id=target if isinstance(target, dict) else {"mp": target},
        device_id_type=MESH,
    )


def greet(targets):
    barrier = pltpu.get_barrier_semaphore()
    for target in targets:
        where = target if isinstance(target, dict) else {"mp": target}
        pl.semaphore_signal(barrier, inc=1, device_id=where, device_id_type=MESH)
    pl.semaphore_wait(barrier, len(targets))


def sems(count):
    return pltpu.SemaphoreType.DMA((2, count))


def norm_forward(stream, gain):
    scaling = lax.rsqrt(jnp.sum(stream * stream, axis=0, keepdims=True) / D + EPSILON)
    return stream * scaling * gain, scaling


def norm_backward(upstream, stream, gain):
    scaling = lax.rsqrt(jnp.sum(stream * stream, axis=0, keepdims=True) / D + EPSILON)
    gain_grad = jnp.sum(upstream * stream * scaling, axis=1, keepdims=True)
    scaled = upstream * gain
    inner = jnp.sum(scaled * stream, axis=0, keepdims=True)
    return scaled * scaling - stream * (scaling * scaling * scaling * inner / D), gain_grad


def gather_four(place, buf, sem):
    own = buf.at[place.y, :, half(place.core)]
    there = buf.at[1 - place.y, :, half(place.core)]
    to_across = remote(own, own, sem, 0, place.across)
    to_across.start()
    to_partner = remote(own, own, sem, 1, place.partner)
    to_partner.start()

    def near():
        to_partner.wait_recv()

    forward = remote(there, there, sem, 2, place.partner)

    def relay():
        to_across.wait_recv()
        forward.start()

    def far():
        forward.wait()

    def close():
        to_across.wait_send()
        to_partner.wait_send()

    return near, relay, far, close


def gather_all(place, buf, sem):
    own = buf.at[:, half(place.me)]
    sends = [
        remote(own, own, sem, step - 1, place.chip_at(step) * 2 + place.core) for step in range(1, CHIPS)
    ]
    forwards = [remote(own, own, sem, 7, place.partner)]
    for step in range(1, CHIPS):
        here = buf.at[:, half(place.chip_at(CHIPS - step) * 2 + place.core)]
        forwards.append(remote(here, here, sem, 7 + step, place.partner))

    def spread_own():
        for copy in sends + forwards[:1]:
            copy.start()

    def forward():
        for step in range(1, CHIPS):
            sends[step - 1].wait_recv()
            forwards[step].start()

    def close():
        for copy in sends:
            copy.wait_send()
        for copy in forwards:
            copy.wait()

    return spread_own, forward, close


def scatter_four(place, parts, got, sem):
    keep = half(place.core)
    away = half(1 - place.core)
    far_part = remote(parts.at[1 - place.y, :, away], got.at[0], sem, 0, place.partner)
    near_part = remote(parts.at[place.y, :, away], got.at[1], sem, 1, place.partner)
    across_part = remote(parts.at[1 - place.y, :, keep], got.at[2], sem, 2, place.across)

    def send_far():
        far_part.start()

    def send_near():
        near_part.start()

    def relay():
        far_part.wait_recv()
        total = parts[1 - place.y, :, keep].astype(F32) + got[0].astype(F32)
        parts[1 - place.y, :, keep] = total.astype(BF16)
        across_part.start()

    def total():
        near_part.wait_recv()
        across_part.wait_recv()
        return parts[place.y, :, keep].astype(F32) + got[1].astype(F32) + got[2].astype(F32)

    def close():
        far_part.wait_send()
        near_part.wait_send()
        across_part.wait_send()

    return send_far, send_near, relay, total, close


def toeplitz(taps):
    wide = pltpu.roll(jnp.broadcast_to(taps, (OWN, T)), 0, 1, stride=1, stride_axis=0)
    lane = lax.broadcasted_iota(jnp.int32, (OWN, T), 1)
    row = lax.broadcasted_iota(jnp.int32, (OWN, T), 0)
    return jnp.where(lane >= row, wide, 0.0).astype(BF16)


def reverse_taps(taps_ref, reverse):
    row = lax.broadcasted_iota(jnp.int32, (2 * OWN, OWN), 0)
    lane = lax.broadcasted_iota(jnp.int32, (2 * OWN, OWN), 1)
    inside = (lane >= 1) & (row == OWN - lane)
    edge = (lane == 0) & (row == OWN)
    flip = jnp.where(inside | edge, 1.0, 0.0).astype(BF16)
    for index in range(T // OWN):
        begin = T - (index + 1) * OWN
        piece = taps_ref[:, begin : begin + min(2 * OWN, T - begin)]
        reverse[:, index * OWN : (index + 1) * OWN] = nn(piece, flip[: piece.shape[1]])
    reverse[:, T : T + OWN] = nn(taps_ref[:, :OWN], flip[OWN:])
    reverse[:, T + OWN :] = jnp.zeros((K, OWN), F32)


def toeplitz_down(reverse, store):
    wide = pltpu.roll(jnp.broadcast_to(reverse, (OWN, T + 2 * OWN)), 0, 1, stride=1, stride_axis=0).astype(BF16)
    for block in range(T // OWN):
        begin = T - block * OWN
        store(block, wide[:, begin : begin + 2 * OWN])


def lag_mask(shift, pick):
    lane = lax.broadcasted_iota(jnp.int32, (CH, T), 1)
    inner = lane % (T // 2)
    return (lane >= shift) & ((inner >= shift) | (pick == 1))


def spread(qkv_ref, keys, values):
    for index in range(MP):
        keys[:, index * OWN : (index + 1) * OWN] = qkv_ref[index, HD : 2 * HD]
        values[:, index * OWN : (index + 1) * OWN] = qkv_ref[index, 2 * HD :]


def query_block(qkv_ref, quarter):
    parts = [qkv_ref[quarter * 4 + index, :HD] for index in range(4)]
    return jnp.concatenate(parts, axis=1) * jnp.asarray(HD**-0.5, BF16)


def score_mask(quarter, chunk, pick):
    query = quarter * 512 + lax.broadcasted_iota(jnp.int32, (512, 512), 1)
    key = chunk * 512 + lax.broadcasted_iota(jnp.int32, (512, 512), 0)
    same_half = (quarter // 2) == (chunk // 2)
    return (key <= query) & (same_half | (pick == 1))


def first_kernel(
    pick_ref, x_ref, go_ref, gains_ref, taps_ref, weight_ref,
    gate_a, up_a, down_a, qkv_w, out_w, gate_b, up_b, down_b,
    scale_ref, feat_ref, x1_ref, x2_ref, na_ref, qkv_ref, wa_ref, wat_ref, gains_all,
    lse_ref, of_ref, go_heads, gx3_ref, out_ref, n3_all, gwo_ref, gmlp_ref, ggain_ref,
    x_own, go_own, squares, taps, table, weight_t, blocks, y_ref, core_got, chip_got, parts, got, heads,
    go4_ref, wb_ref, keys, values, own_heads, all_heads, x3_ref, nb, hidden_ref, ggate_ref, gup_ref,
    got_n, parts_z, got_z, grad_heads, out_own,
    sem_s, sem_x, sem_go, sem_gain, sem_wa, sem_wb, sem_wat, sem_y, sem_n, sem_g, sem_z, sem_q,
    sem_o, sem_nb, sem_gn, sem_zb, sem_h, sem_out, sem_all,
):
    place = Place()
    me, chip, core, x = place.me, place.chip, place.core, place.x
    count = T // OWN
    pick = pick_ref[0]
    stream = x_ref[...].astype(F32)
    squares[pl.ds(me, 1)] = jnp.sum(stream * stream, axis=0, keepdims=True)[None]
    for ref, (gate, up, down) in ((wa_ref, (gate_a, up_a, down_a)), (wb_ref, (gate_b, up_b, down_b))):
        ref[0, :OWN] = gate[...].T
        ref[0, OWN : 2 * OWN] = up[...].T
        ref[0, 2 * OWN :] = down[...]
    wat_ref[chip, core, : 3 * CH] = qkv_w[...]
    wat_ref[chip, core, 3 * CH :] = out_w[...]
    greet([place.around(step) for step in range(1, MP)] + [place.along_x(step) for step in range(1, 4)])
    sums, late, fetch_a, fetch_b, fetch_t, rest_a, rest_b, rest_t = [], [], [], [], [], [], [], []
    for step in range(1, MP):
        there = place.around(step)
        copy = remote(squares.at[me], squares.at[me], sem_s, step - 1, there)
        copy.start()
        sums.append(copy)
    for step in range(1, 4):
        copy = remote(
            wa_ref.at[0, rows(x, 96)], wa_ref.at[4 - step, rows(x, 96)], sem_wa, step - 1, place.along_z(step)
        )
        copy.start()
        fetch_a.append(copy)
    mine_t = wat_ref.at[chip, core, rows(x, CH)]
    for step in range(1, CHIPS):
        copy = remote(mine_t, mine_t, sem_wat, step - 1, place.chip_at(step) * 2 + core)
        copy.start()
        fetch_t.append(copy)
    for step in range(1, MP):
        there = place.around(step)
        for src, dst, sem in (
            (x_ref.at[:, half(there)], x_own.at[rows(me, CH)], sem_x),
            (go_ref.at[:, half(there)], go_own.at[rows(me, CH)], sem_go),
            (gains_ref, gains_all.at[rows(me, CH)], sem_gain),
        ):
            copy = remote(src, dst, sem, step - 1, there)
            copy.start()
            late.append(copy)
    for step in range(1, 4):
        copy = remote(
            wb_ref.at[0, rows(x, 96)], wb_ref.at[4 - step, rows(x, 96)], sem_wb, step - 1, place.along_z(step)
        )
        copy.start()
        fetch_b.append(copy)
    x_own[rows(me, CH), :] = x_ref[:, half(me)]
    go_own[rows(me, CH), :] = go_ref[:, half(me)]
    gains_all[rows(me, CH)] = gains_ref[...]
    taps[...] = taps_ref[...].astype(F32)
    weight_t[...] = weight_ref[...].T

    @pl.loop(0, K // 2)
    def _(step):
        for index in range(2):
            filter_table = toeplitz(taps[pl.ds(step * 2 + index, 1), :])
            for offset in range(count):
                table[step, offset * OWN : (offset + 1) * OWN, index * OWN : (index + 1) * OWN] = filter_table[
                    :, offset * OWN : (offset + 1) * OWN
                ]

    for copy in sums:
        copy.wait()
    total = squares[0]
    for index in range(1, MP):
        total = total + squares[index]
    scaling = lax.rsqrt(total / D + EPSILON)
    scale_ref[...] = scaling
    own = stream * scaling * gains_ref[:, 3:4].astype(F32)
    h = own.astype(BF16)
    own = h.astype(F32)
    joined = jnp.full((CH, OWN), (pick == 1).astype(F32)).astype(BF16)
    for target in range(count):
        for offset in range(count):
            here = (slice(target * CH, (target + 1) * CH), slice(offset * OWN, (offset + 1) * OWN))
            if offset > target:
                blocks[here] = jnp.zeros((CH, OWN), BF16)
                continue
            source = target - offset
            value = h[:, source * OWN : (source + 1) * OWN]
            if target >= count // 2 and source < count // 2:
                value = value * joined
            blocks[here] = value
    for shift in range(LAGS):
        moved = own if shift == 0 else pltpu.roll(own, shift, 1)
        moved = jnp.where(lag_mask(shift, pick), moved, 0.0).astype(BF16)
        feat_ref[(K + shift) * CH : (K + shift + 1) * CH, :] = moved

    def convolve(step):
        early = nn(blocks[: CH * count // 2, : T // 2], table[step, : T // 2, :]).astype(BF16)
        late_half = nn(blocks[CH * count // 2 :, :], table[step]).astype(BF16)
        for index in range(2):
            base = pl.multiple_of((step * 2 + index) * CH, CH)
            for target in range(count):
                part, at = (early, target) if target < count // 2 else (late_half, target - count // 2)
                feat_ref[pl.ds(base, CH), target * OWN : (target + 1) * OWN] = part[
                    at * CH : (at + 1) * CH, index * OWN : (index + 1) * OWN
                ]

    pl.loop(0, K // 4)(convolve)
    for fetched, source, sem, done, rest in (
        (fetch_a, wa_ref.at[1:4, rows(x, 96)], sem_wa, 3, rest_a),
        (fetch_t, wat_ref.at[:, core, rows(x, CH)], sem_wat, 7, rest_t),
        (fetch_b, wb_ref.at[1:4, rows(x, 96)], sem_wb, 3, rest_b),
    ):
        for copy in fetched:
            copy.wait_recv()
        for step in range(1, 4):
            copy = remote(source, source, sem, done + step - 1, place.along_x(step))
            copy.start()
            rest.append(copy)
    for copy in late:
        copy.wait()
    go4_ref[place.y, :, half(core)] = go_own[...]
    near_g, relay_g, far_g, close_g = gather_four(place, go4_ref, sem_g)
    pl.loop(K // 4, K // 2)(convolve)
    for group in range(4):
        y = nn(weight_t[...], feat_ref[:, group * 512 : (group + 1) * 512]).astype(BF16)
        for index in range(4):
            y_ref[group * 2 + index // 2, index % 2] = y[:, index * OWN : (index + 1) * OWN]
    order = list(range(1, CHIPS)) + [0]
    first, second = [], []
    for step in order:
        there = place.chip_at(step)
        copy = remote(y_ref.at[there, 1 - core], core_got.at[there], sem_y, step, place.partner)
        copy.start()
        first.append(copy)
    for copy, step in zip(first, order):
        there = place.chip_at(step)
        copy.wait_recv()
        total = y_ref[there, core].astype(F32) + core_got[there].astype(F32)
        if step == 0:
            x1_ref[...] = total
        else:
            y_ref[there, core] = total.astype(BF16)
            move = remote(y_ref.at[there, core], chip_got.at[step - 1], sem_y, 7 + step, there * 2 + core)
            move.start()
            second.append(move)
    near_g()
    relay_g()
    for move in second:
        move.wait_recv()
    x1 = x1_ref[...] + x_own[...].astype(F32)
    for index in range(CHIPS - 1):
        x1 = x1 + chip_got[index].astype(F32)
    x1_ref[...] = x1
    normed, _ = norm_forward(x1, gains_all[:, 0:1].astype(F32))
    na_ref[place.y, :, half(core)] = normed.astype(BF16)
    near, relay_n, far, close_n = gather_four(place, na_ref, sem_n)
    for copy in rest_a:
        copy.wait_recv()
    w_gate = wa_ref[:, :OWN].reshape(D, D)
    w_up = wa_ref[:, OWN : 2 * OWN].reshape(D, D)
    w_down = wa_ref[:, 2 * OWN :].reshape(D, D)
    send_far, send_near, relay, total_z, close_z = scatter_four(place, parts, got, sem_z)

    def block(where):
        rows_here = na_ref[where]
        gate = nn(w_gate, rows_here)
        hidden = (gate * jax.nn.sigmoid(gate) * nn(w_up, rows_here)).astype(BF16)
        parts[where] = tn(w_down, hidden).astype(BF16)

    near()
    block(place.y)
    send_near()
    relay_n()
    for copy in rest_t:
        copy.wait_recv()
    half_t = wat_ref.at[:, core]
    share_t = remote(half_t, half_t, sem_wat, 10, place.partner)
    share_t.start()
    far()
    block(1 - place.y)
    send_far()
    relay()
    x2 = x1 + total_z()
    x2_ref[...] = x2
    n3 = norm_forward(x2, gains_all[:, 1:2].astype(F32))[0].astype(BF16)
    n3_all[:, half(me)] = n3
    share_t.wait_recv()
    w_qkv = wat_ref[:, :, : 3 * CH].reshape(3 * D, D)
    heads[...] = nn(w_qkv, n3).astype(BF16).reshape(CHIPS, 3 * HD, OWN)
    sends = []
    for step in range(1, CHIPS):
        there = place.chip_at(step)
        copy = remote(heads.at[there], qkv_ref.at[me], sem_q, step - 1, there * 2 + core)
        copy.start()
        sends.append(copy)
    qkv_ref[me] = heads[chip]
    forwards = [remote(qkv_ref.at[me], qkv_ref.at[me], sem_q, 7, place.partner)]
    forwards[0].start()
    for step in range(1, CHIPS):
        source = place.chip_at(CHIPS - step) * 2 + core
        sends[step - 1].wait_recv()
        copy = remote(qkv_ref.at[source], qkv_ref.at[source], sem_q, 7 + step, place.partner)
        copy.start()
        forwards.append(copy)
    far_g()
    for copy in forwards:
        copy.wait()
    for copy in fetch_a + fetch_b + fetch_t + rest_a + rest_t + [share_t] + first + second + sends:
        copy.wait_send()
    close_n()
    close_g()
    close_z()
    spread_n3, forward_n3, close_n3 = gather_all(place, n3_all, sem_all)
    spread_n3()
    spread(qkv_ref, keys, values)
    for part in range(2):
        quarter = place.quarters[part]
        queries = query_block(qkv_ref, quarter)
        top = jnp.full((1, 512), NEG, F32)
        norm = jnp.zeros((1, 512), F32)
        total = jnp.zeros((HD, 512), F32)
        for chunk in range(2 + 2 * part):
            here = slice(chunk * 512, (chunk + 1) * 512)
            scores = jnp.where(score_mask(quarter, chunk, pick), tn(keys[:, here], queries), NEG)
            new_top = jnp.maximum(top, jnp.max(scores, axis=0, keepdims=True))
            weights = jnp.exp(scores - new_top)
            rescale = jnp.exp(top - new_top)
            norm = norm * rescale + jnp.sum(weights, axis=0, keepdims=True)
            total = total * rescale + nn(values[:, here], weights.astype(BF16))
            top = new_top
        total = total / norm
        lse_ref[part] = top + jnp.log(norm)
        of_ref[part] = total
        for index in range(4):
            own_heads[part * 4 + index] = total[:, index * OWN : (index + 1) * OWN].astype(BF16)
    targets = [place.quarters[slot // 4] * 4 + slot % 4 for slot in range(8)]
    copies = [
        pltpu.make_async_remote_copy(
            src_ref=own_heads.at[slot], dst_ref=all_heads.at[chip],
            send_sem=sem_o.at[0, slot], recv_sem=sem_o.at[1, chip],
            device_id={"mp": targets[slot]}, device_id_type=MESH,
        )
        for slot in range(8)
    ]
    for slot in range(8):
        pl.when(targets[slot] != me)(copies[slot].start)

        @pl.when(targets[slot] == me)
        def _():
            all_heads[chip] = own_heads[slot]

    arrivals = [
        remote(own_heads.at[0], all_heads.at[head], sem_o, head, place.partner) for head in range(CHIPS)
    ]
    for head in range(CHIPS):
        pl.when(head * 2 + place.query_core != me)(arrivals[head].wait_recv)
    w_out = wat_ref[:, :, 3 * CH :].reshape(D, D)
    outputs = all_heads[...].reshape(D, OWN)
    x3 = x2 + tn(w_out, outputs)
    x3_ref[...] = x3
    gain_b = gains_all[:, 2:3].astype(F32)
    nb[place.y, :, half(core)] = norm_forward(x3, gain_b)[0].astype(BF16)
    near, relay_n, far, close_n = gather_four(place, nb, sem_nb)
    for copy in rest_b:
        copy.wait()
    w_gate = wb_ref[:, :OWN].reshape(D, D)
    w_up = wb_ref[:, OWN : 2 * OWN].reshape(D, D)
    w_down = wb_ref[:, 2 * OWN :].reshape(D, D)
    far_gn, near_gn, relay_gn, total_gn, close_gn = scatter_four(place, parts, got_n, sem_gn)
    far_z, near_z, relay_z, total_z, close_z = scatter_four(place, parts_z, got_z, sem_zb)

    def block(where):
        rows_here = nb[where]
        gate = nn(w_gate, rows_here)
        up = nn(w_up, rows_here)
        sig = jax.nn.sigmoid(gate)
        hidden_grad = nn(w_down, go4_ref[where])
        gate_grad = (hidden_grad * up * sig * (1.0 + gate * (1.0 - sig))).astype(BF16)
        up_grad = (hidden_grad * gate * sig).astype(BF16)
        ggate_ref[where] = gate_grad
        gup_ref[where] = up_grad
        parts[where] = (tn(w_gate, gate_grad) + tn(w_up, up_grad)).astype(BF16)
        hidden_ref[where] = (gate * sig * up).astype(BF16)

    near()
    block(place.y)
    near_gn()
    relay_n()
    far()
    block(1 - place.y)
    far_gn()
    forward_n3()
    parts_z[place.y] = tn(w_down, hidden_ref[place.y]).astype(BF16)
    near_z()
    relay_gn()
    parts_z[1 - place.y] = tn(w_down, hidden_ref[1 - place.y]).astype(BF16)
    far_z()
    relay_z()
    stream_grad, gain_grad = norm_backward(total_gn(), x3_ref[...], gain_b)
    ggain_ref[...] = gain_grad
    gx3 = go_own[...].astype(F32) + stream_grad
    gx3_ref[...] = gx3
    gy = gx3.astype(BF16)
    grad_heads[...] = nn(w_out, gy).astype(BF16).reshape(CHIPS, HD, OWN)
    slot = (place.z // 2) * 4 + me % 4
    sends = [
        pltpu.make_async_remote_copy(
            src_ref=grad_heads.at[head], dst_ref=go_heads.at[slot],
            send_sem=sem_h.at[0, head], recv_sem=sem_h.at[1, slot],
            device_id={"mp": head * 2 + place.query_core}, device_id_type=MESH,
        )
        for head in range(CHIPS)
    ]
    for head in range(CHIPS):
        pl.when(head * 2 + place.query_core != me)(sends[head].start)

        @pl.when(head * 2 + place.query_core == me)
        def _():
            go_heads[slot] = grad_heads[head]

    out_own[...] = (x3_ref[...] + total_z()).astype(BF16)
    moves = []
    for step in range(1, MP):
        there = place.around(step)
        copy = remote(out_own.at[rows(there, CH)], out_ref.at[:, half(me)], sem_out, step - 1, there)
        copy.start()
        moves.append(copy)
    out_ref[:, half(me)] = out_own[rows(me, CH), :]
    gwo_ref[...] = nt(outputs, gy).astype(BF16).reshape(MP, CH, D)
    for group, (left, right) in enumerate(((ggate_ref, nb), (gup_ref, nb), (hidden_ref, go4_ref))):
        value = (nt(left[0], right[0]) + nt(left[1], right[1])).astype(BF16)
        for index in range(4):
            gmlp_ref[index, group * OWN : (group + 1) * OWN] = value[index * OWN : (index + 1) * OWN]
    for slot_in in range(8):
        arrival = remote(grad_heads.at[0], go_heads.at[slot_in], sem_h, slot_in, place.partner)
        pl.when(targets[slot_in] != me)(arrival.wait_recv)
    for slot_out in range(8):
        pl.when(targets[slot_out] != me)(copies[slot_out].wait_send)
        pl.when(slot_out * 2 + place.query_core != me)(sends[slot_out].wait_send)
    for copy in moves:
        copy.wait()
    close_n3()
    close_n()
    close_gn()
    close_z()


def first(*operands):
    return pl.pallas_call(
        first_kernel,
        out_shape=(
            jax.ShapeDtypeStruct((1, T), F32),
            jax.ShapeDtypeStruct((FEAT, T), BF16),
            jax.ShapeDtypeStruct((D, OWN), F32),
            jax.ShapeDtypeStruct((D, OWN), F32),
            jax.ShapeDtypeStruct((2, D, 2 * OWN), BF16),
            jax.ShapeDtypeStruct((MP, 3 * HD, OWN), BF16),
            jax.ShapeDtypeStruct((4, 3 * OWN, D), BF16),
            jax.ShapeDtypeStruct((CHIPS, 2, OWN, D), BF16),
            jax.ShapeDtypeStruct((D, OWN), BF16),
            jax.ShapeDtypeStruct((2, 1, 512), F32),
            jax.ShapeDtypeStruct((2, HD, 512), F32),
            jax.ShapeDtypeStruct((8, HD, OWN), BF16),
            jax.ShapeDtypeStruct((D, OWN), F32),
            jax.ShapeDtypeStruct((CH, T), BF16),
            jax.ShapeDtypeStruct((D, T), BF16),
            jax.ShapeDtypeStruct((MP, CH, D), BF16),
            jax.ShapeDtypeStruct((4, 3 * OWN, D), BF16),
            jax.ShapeDtypeStruct((D, 1), F32),
        ),
        in_specs=[SMEM] + [VMEM] * 13,
        out_specs=(VMEM,) * 18,
        scratch_shapes=[
            pltpu.VMEM((D, OWN), BF16),
            pltpu.VMEM((D, OWN), BF16),
            pltpu.VMEM((MP, 1, T), F32),
            pltpu.VMEM((K, T), F32),
            pltpu.VMEM((K // 2, T, 2 * OWN), BF16),
            pltpu.VMEM((D, FEAT), BF16),
            pltpu.VMEM((CH * T // OWN, T), BF16),
            pltpu.VMEM((CHIPS, 2, D, OWN), BF16),
            pltpu.VMEM((CHIPS, D, OWN), BF16),
            pltpu.VMEM((CHIPS - 1, D, OWN), BF16),
            pltpu.VMEM((2, D, 2 * OWN), BF16),
            pltpu.VMEM((3, D, OWN), BF16),
            pltpu.VMEM((CHIPS, 3 * HD, OWN), BF16),
            pltpu.VMEM((2, D, 2 * OWN), BF16),
            pltpu.VMEM((4, 3 * OWN, D), BF16),
            pltpu.VMEM((HD, T), BF16),
            pltpu.VMEM((HD, T), BF16),
            pltpu.VMEM((8, HD, OWN), BF16),
            pltpu.VMEM((8, HD, OWN), BF16),
            pltpu.VMEM((D, OWN), F32),
            pltpu.VMEM((2, D, 2 * OWN), BF16),
            pltpu.VMEM((2, D, 2 * OWN), BF16),
            pltpu.VMEM((2, D, 2 * OWN), BF16),
            pltpu.VMEM((2, D, 2 * OWN), BF16),
            pltpu.VMEM((3, D, OWN), BF16),
            pltpu.VMEM((2, D, 2 * OWN), BF16),
            pltpu.VMEM((3, D, OWN), BF16),
            pltpu.VMEM((CHIPS, HD, OWN), BF16),
            pltpu.VMEM((D, OWN), BF16),
            sems(15), sems(15), sems(15), sems(15), sems(6), sems(6), sems(11),
            sems(15), sems(3), sems(3), sems(3), sems(15),
            sems(8), sems(3), sems(3), sems(3), sems(8), sems(15), sems(15),
        ],
        compiler_params=pltpu.CompilerParams(
            collective_id=0, has_side_effects=True, vmem_limit_bytes=LIMIT
        ),
        name="first",
    )(*operands)


def second_kernel(
    pick_ref, x_ref, scale_ref, feat_ref, x1_ref, x2_ref, na_ref, qkv_ref, wa_ref, wat_ref, gains_all,
    lse_ref, of_ref, go_heads, gx3_ref, n3_all, gwo_ref, gmlp_b, ggain_b, gains_ref, taps_ref, weight_ref,
    gx_ref, joint_ref, sum_a, sum_b, gain_sum,
    keys, values, kv_grad, q_grad, mine, core_got, chip_sum, head_grads, gz, parts, got,
    hidden_ref, ggate_ref, gup_ref, gy1_ref, row_got, q_rows, gwo_got, dp_got, dp_sum, z_got,
    gmlp_a, a_got, a_sum, a_z_got, ggain_ref, gain_got, gain_own, gain_dp,
    reverse, table, feature_grad, shifted, total, gh_ref, joint, joint_got, inner,
    sem_q, sem_n, sem_z, sem_y, sem_gwo, sem_rows, sem_dp, sem_dz, sem_dg,
    sem_a, sem_az, sem_ag, sem_g, sem_gd, sem_j, sem_jg, sem_p,
):
    place = Place()
    me, dp, chip, core = place.me, place.dp, place.chip, place.core
    wide = 2 * OWN
    count = T // wide
    greet(
        [place.around(step) for step in range(1, MP)]
        + [{"dp": place.along_dp(step)} for step in range(1, DP)]
    )
    gain_a = gains_all[:, 0:1].astype(F32)
    gain_n = gains_all[:, 1:2].astype(F32)
    b_first = []
    for step in range(1, DP):
        there = place.along_dp(step)
        copy = remote(gmlp_b.at[:, rows(there, 48)], dp_got.at[step - 1], sem_dp, step - 1, {"dp": there})
        copy.start()
        b_first.append(copy)
    o_first = []
    for step in range(1, MP):
        there = place.around(step)
        copy = remote(gwo_ref.at[there], gwo_got.at[step - 1], sem_gwo, step - 1, there)
        copy.start()
        o_first.append(copy)
    pick = pick_ref[0]
    spread(qkv_ref, keys, values)
    for part in range(2):
        quarter = place.quarters[part]
        queries = query_block(qkv_ref, quarter)
        out_grad = jnp.concatenate([go_heads[part * 4 + index] for index in range(4)], axis=1)
        weighted = jnp.sum(of_ref[part] * out_grad.astype(F32), axis=0, keepdims=True)
        queries_t = queries.T
        out_grad_t = out_grad.T
        query_grad = jnp.zeros((HD, 512), F32)
        for chunk in range(2 + 2 * part):
            here = slice(chunk * 512, (chunk + 1) * 512)
            scores = tn(keys[:, here], queries) - lse_ref[part]
            probs = jnp.where(score_mask(quarter, chunk, pick), jnp.exp(scores), 0.0)
            score_grad = (probs * (tn(values[:, here], out_grad) - weighted)).astype(BF16)
            query_grad = query_grad + nn(keys[:, here], score_grad)
            key_part = nn(score_grad, queries_t)
            value_part = nn(probs.astype(BF16), out_grad_t)
            both = jnp.concatenate([key_part, value_part], axis=1)
            if part == 1 and chunk < 2:
                both = both + kv_grad[here]
            kv_grad[here] = both
        q_grad[part] = (query_grad * HD**-0.5).astype(BF16)
    for index in range(MP):
        mine[index // 2, index % 2, :HD] = jnp.zeros((HD, OWN), BF16)
        mine[index // 2, index % 2, HD:] = kv_grad[index * OWN : (index + 1) * OWN].T.astype(BF16)
    for part in range(2):
        quarter = place.quarters[part]
        for index in range(4):
            mine[quarter * 2 + index // 2, index % 2, :HD] = q_grad[part, :, index * OWN : (index + 1) * OWN]
    order = list(range(1, CHIPS)) + [0]
    first = []
    for step in order:
        there = place.chip_at(step)
        copy = remote(mine.at[there, 1 - core], core_got.at[there], sem_q, step, place.partner)
        copy.start()
        first.append(copy)
    second = []
    for copy, step in zip(first, order):
        there = place.chip_at(step)
        copy.wait_recv()
        amount = (mine[there, core].astype(F32) + core_got[there].astype(F32)).astype(BF16)
        chip_sum[there] = amount
        if step == 0:
            head_grads[chip] = amount
        else:
            move = remote(chip_sum.at[there], head_grads.at[chip], sem_q, 7 + step, there * 2 + core)
            move.start()
            second.append(move)
    share = remote(chip_sum.at[:, rows(1 - core, 96)], row_got, sem_rows, 0, place.partner)
    share.start()
    for move in second:
        move.wait_recv()
    w_qkv = wat_ref[:, :, : 3 * CH].reshape(3 * D, D)
    columns = head_grads[...].reshape(3 * D, OWN)
    stream_grad, gain_grad = norm_backward(tn(w_qkv, columns), x2_ref[...], gain_n)
    lane = lax.broadcasted_iota(jnp.int32, (D, OWN), 1)
    gain_grads = jnp.where(lane == 1, gain_grad, 0.0) + jnp.where(lane == 2, ggain_b[...], 0.0)
    gx2 = gx3_ref[...] + stream_grad
    gz[place.y, :, half(core)] = gx2.astype(BF16)
    near, relay_n, far, close_n = gather_four(place, gz, sem_n)
    w_gate = wa_ref[:, :OWN].reshape(D, D)
    w_up = wa_ref[:, OWN : 2 * OWN].reshape(D, D)
    w_down = wa_ref[:, 2 * OWN :].reshape(D, D)
    send_far, send_near, relay, total_gn, close_z = scatter_four(place, parts, got, sem_z)

    def block(where):
        rows_here = na_ref[where]
        gate = nn(w_gate, rows_here)
        up = nn(w_up, rows_here)
        sig = jax.nn.sigmoid(gate)
        hidden_grad = nn(w_down, gz[where])
        gate_grad = (hidden_grad * up * sig * (1.0 + gate * (1.0 - sig))).astype(BF16)
        up_grad = (hidden_grad * gate * sig).astype(BF16)
        ggate_ref[where] = gate_grad
        gup_ref[where] = up_grad
        parts[where] = (tn(w_gate, gate_grad) + tn(w_up, up_grad)).astype(BF16)
        hidden_ref[where] = (gate * sig * up).astype(BF16)

    near()
    block(place.y)
    send_near()
    for copy in b_first:
        copy.wait_recv()
    amount = gmlp_b[:, rows(place.dp, 48)].astype(F32)
    for index in range(DP - 1):
        amount = amount + dp_got[index].astype(F32)
    dp_sum[...] = amount.astype(BF16)
    b_second = []
    for step in range(1, 4):
        copy = remote(dp_sum.at[step], z_got.at[step - 1], sem_dz, step - 1, place.along_z(step))
        copy.start()
        b_second.append(copy)
    relay_n()
    far()
    block(1 - place.y)
    send_far()
    relay()
    for group, (left, right) in enumerate(((ggate_ref, na_ref), (gup_ref, na_ref), (hidden_ref, gz))):
        value = (nt(left[0], right[0]) + nt(left[1], right[1])).astype(BF16)
        for index in range(4):
            gmlp_a[index, group * OWN : (group + 1) * OWN] = value[index * OWN : (index + 1) * OWN]
    a_first = []
    for step in range(1, DP):
        there = place.along_dp(step)
        copy = remote(gmlp_a.at[:, rows(there, 48)], a_got.at[step - 1], sem_a, step - 1, {"dp": there})
        copy.start()
        a_first.append(copy)
    stream_grad, gain_grad = norm_backward(total_gn(), x1_ref[...], gain_a)
    ggain_ref[...] = gain_grads + jnp.where(lane == 0, gain_grad, 0.0)
    gy1_ref[:, half(me)] = (gx2 + stream_grad).astype(BF16)
    spread_gy1, forward_gy1, close_gy1 = gather_all(place, gy1_ref, sem_y)
    spread_gy1()
    for copy in b_second:
        copy.wait_recv()
    amount = dp_sum[0].astype(F32)
    for index in range(3):
        amount = amount + z_got[index].astype(F32)
    sum_b[rows(place.dp, 48), :] = amount.astype(BF16)
    b_third = []
    done_b = sum_b.at[rows(place.dp, 48)]
    for step in range(1, DP):
        copy = remote(done_b, done_b, sem_dg, step - 1, {"dp": place.along_dp(step)})
        copy.start()
        b_third.append(copy)
    share.wait_recv()
    for index in range(CHIPS):
        q_rows[:, half(index * 2 + core)] = chip_sum[index, rows(core, 96), :]
        q_rows[:, half(index * 2 + 1 - core)] = row_got[index]
    joint[FEAT : FEAT + 3 * CH] = nt(q_rows[...], n3_all[...]).astype(BF16)
    for copy in o_first:
        copy.wait_recv()
    value = gwo_ref[me].astype(F32)
    for index in range(MP - 1):
        value = value + gwo_got[index].astype(F32)
    joint[FEAT + 3 * CH : FEAT + OWN] = value.astype(BF16)
    joint[FEAT + OWN :] = jnp.zeros((CH, D), BF16)
    reverse_taps(taps_ref, reverse)

    def build(filter_index, slot):
        def store(block, value):
            table[slot, block * OWN : (block + 1) * OWN, :] = value

        toeplitz_down(reverse[pl.ds(filter_index, 1), :], store)

    @pl.loop(0, K // 2)
    def _(index):
        build(index, index)

    forward_gy1()
    close_gy1()
    gain_first = []
    for step in range(1, MP):
        there = place.around(step)
        copy = remote(ggain_ref.at[rows(there, CH)], gain_got.at[step - 1], sem_g, step - 1, there)
        copy.start()
        gain_first.append(copy)
    joint[:FEAT] = nt(feat_ref[...], gy1_ref[...]).astype(BF16)
    j_first = []
    for step in range(1, DP):
        there = place.along_dp(step)
        copy = remote(joint.at[rows(there, OWN)], joint_got.at[step - 1], sem_j, step - 1, {"dp": there})
        copy.start()
        j_first.append(copy)
    for group in range(4):
        here = slice(group * 512, (group + 1) * 512)
        feature_grad[:, here] = nn(weight_ref[: K * CH], gy1_ref[:, here]).astype(BF16)
    total[...] = jnp.zeros_like(total)
    shifted[...] = jnp.zeros_like(shifted)
    joined = jnp.full((CH, T // 2), (pick == 1).astype(F32)).astype(BF16)
    middle = CH * count // 2

    def convolve(filter_index, slot):
        mine = feature_grad[pl.ds(pl.multiple_of(filter_index * CH, CH), CH), :]
        for source in range(count):
            here = slice(source * CH, (source + 1) * CH)
            begin = source * wide
            if source < count // 2:
                near_end = T // 2 - begin
                shifted[here, :near_end] = mine[:, begin : T // 2]
                shifted[here, near_end : T - begin] = mine[:, T // 2 :] * joined
            else:
                shifted[here, : T - begin] = mine[:, begin:]
        total[:middle] += nn(shifted[:middle, :], table[slot])
        total[middle:] += nn(shifted[middle:, : T // 2], table[slot, : T // 2, :])

    @pl.loop(0, K // 2)
    def _(index):
        convolve(index, index)

    for copy in a_first:
        copy.wait_recv()
    value = gmlp_a[:, rows(dp, 48)].astype(F32)
    for index in range(DP - 1):
        value = value + a_got[index].astype(F32)
    a_sum[...] = value.astype(BF16)
    a_second = []
    for step in range(1, 4):
        copy = remote(a_sum.at[step], a_z_got.at[step - 1], sem_az, step - 1, place.along_z(step))
        copy.start()
        a_second.append(copy)

    @pl.loop(K // 2, K * 3 // 4)
    def _(index):
        build(index, index - K // 2)
        convolve(index, index - K // 2)

    for copy in j_first:
        copy.wait_recv()
    value = joint[rows(dp, OWN), :].astype(F32)
    for index in range(DP - 1):
        value = value + joint_got[index].astype(F32)
    joint_ref[rows(dp, OWN), :] = value.astype(BF16)
    last = []
    done_j = joint_ref.at[rows(dp, OWN)]
    for step in range(1, DP):
        copy = remote(done_j, done_j, sem_jg, step - 1, {"dp": place.along_dp(step)})
        copy.start()
        last.append(copy)
    for copy in a_second:
        copy.wait_recv()
    value = a_sum[0].astype(F32)
    for index in range(3):
        value = value + a_z_got[index].astype(F32)
    sum_a[rows(dp, 48), :] = value.astype(BF16)
    done_a = sum_a.at[rows(dp, 48)]
    for step in range(1, DP):
        copy = remote(done_a, done_a, sem_ag, step - 1, {"dp": place.along_dp(step)})
        copy.start()
        last.append(copy)
    @pl.loop(K * 3 // 4, K)
    def _(index):
        build(index, index - K // 2)
        convolve(index, index - K // 2)

    for source in range(count):
        gh_ref[:, source * wide : (source + 1) * wide] = total[source * CH : (source + 1) * CH]
    for shift in range(LAGS):
        begin = (K + shift) * CH
        value = nn(weight_ref[begin : begin + CH], gy1_ref[...])
        value = jnp.where(lag_mask(shift, pick), value, 0.0)
        if shift:
            value = pltpu.roll(value, T - shift, 1)
        gh_ref[...] += value
    stream = x_ref[...].astype(F32)
    scaled = gh_ref[...] * gains_ref[:, 3:4].astype(F32)
    inner[pl.ds(me, 1)] = jnp.sum(scaled * stream, axis=0, keepdims=True)[None]
    sums = []
    for step in range(1, MP):
        copy = remote(inner.at[me], inner.at[me], sem_p, step - 1, place.around(step))
        copy.start()
        sums.append(copy)
    scaling = scale_ref[...]
    gain_grad = jnp.sum(gh_ref[...] * stream * scaling, axis=1, keepdims=True)
    for copy in gain_first:
        copy.wait_recv()
    value = ggain_ref[rows(me, CH), :]
    for index in range(MP - 1):
        value = value + gain_got[index]
    lane = lax.broadcasted_iota(jnp.int32, (CH, OWN), 1)
    gain_own[...] = value + jnp.where(lane == 3, gain_grad, 0.0)
    for step in range(1, DP):
        copy = remote(gain_own, gain_dp.at[step - 1], sem_gd, step - 1, {"dp": place.along_dp(step)})
        copy.start()
        last.append(copy)
    for copy in sums:
        copy.wait()
    value = inner[0]
    for index in range(1, MP):
        value = value + inner[index]
    stream_grad = scaled * scaling - stream * (scaling * scaling * scaling * value / D)
    gx_ref[...] = stream_grad + gy1_ref[rows(me, CH), :].astype(F32)
    for copy in last:
        copy.wait()
    value = gain_own[...]
    for index in range(DP - 1):
        value = value + gain_dp[index]
    gain_sum[...] = value
    for copy in first + second + [share] + b_first + b_second + o_first + a_first + a_second + j_first + gain_first:
        copy.wait_send()
    for copy in b_third:
        copy.wait()
    close_n()
    close_z()


def second(*operands):
    return pl.pallas_call(
        second_kernel,
        out_shape=(
            jax.ShapeDtypeStruct((CH, T), F32),
            jax.ShapeDtypeStruct((DP * OWN, D), BF16),
            jax.ShapeDtypeStruct((3 * OWN, D), BF16),
            jax.ShapeDtypeStruct((3 * OWN, D), BF16),
            jax.ShapeDtypeStruct((CH, OWN), F32),
        ),
        in_specs=[SMEM] + [VMEM] * 21,
        out_specs=(VMEM,) * 5,
        scratch_shapes=[
            pltpu.VMEM((HD, T), BF16),
            pltpu.VMEM((HD, T), BF16),
            pltpu.VMEM((T, 2 * HD), F32),
            pltpu.VMEM((2, HD, 512), BF16),
            pltpu.VMEM((CHIPS, 2, 3 * HD, OWN), BF16),
            pltpu.VMEM((CHIPS, 3 * HD, OWN), BF16),
            pltpu.VMEM((CHIPS, 3 * HD, OWN), BF16),
            pltpu.VMEM((CHIPS, 3 * HD, OWN), BF16),
            pltpu.VMEM((2, D, 2 * OWN), BF16),
            pltpu.VMEM((2, D, 2 * OWN), BF16),
            pltpu.VMEM((3, D, OWN), BF16),
            pltpu.VMEM((2, D, 2 * OWN), BF16),
            pltpu.VMEM((2, D, 2 * OWN), BF16),
            pltpu.VMEM((2, D, 2 * OWN), BF16),
            pltpu.VMEM((D, T), BF16),
            pltpu.VMEM((CHIPS, 96, OWN), BF16),
            pltpu.VMEM((96, T), BF16),
            pltpu.VMEM((MP - 1, CH, D), BF16),
            pltpu.VMEM((DP - 1, 4, 48, D), BF16),
            pltpu.VMEM((4, 48, D), BF16),
            pltpu.VMEM((3, 48, D), BF16),
            pltpu.VMEM((4, 3 * OWN, D), BF16),
            pltpu.VMEM((DP - 1, 4, 48, D), BF16),
            pltpu.VMEM((4, 48, D), BF16),
            pltpu.VMEM((3, 48, D), BF16),
            pltpu.VMEM((D, OWN), F32),
            pltpu.VMEM((MP - 1, CH, OWN), F32),
            pltpu.VMEM((CH, OWN), F32),
            pltpu.VMEM((DP - 1, CH, OWN), F32),
            pltpu.VMEM((K, T + 2 * OWN), F32),
            pltpu.VMEM((K // 2, T, 2 * OWN), BF16),
            pltpu.VMEM((K * CH, T), BF16),
            pltpu.VMEM((CH * T // (2 * OWN), T), BF16),
            pltpu.VMEM((CH * T // (2 * OWN), 2 * OWN), F32),
            pltpu.VMEM((CH, T), F32),
            pltpu.VMEM((DP * OWN, D), BF16),
            pltpu.VMEM((DP - 1, OWN, D), BF16),
            pltpu.VMEM((MP, 1, T), F32),
            sems(15), sems(3), sems(3), sems(15), sems(15), sems(1), sems(7), sems(3), sems(7),
            sems(7), sems(3), sems(7), sems(15), sems(7), sems(7), sems(7), sems(15),
        ],
        compiler_params=pltpu.CompilerParams(
            collective_id=1, has_side_effects=True, vmem_limit_bytes=LIMIT
        ),
        name="second",
    )(*operands)


def on_device(
    inputs, out_grad, shape_pick, filters, stu_gain, stu_weight,
    mlp_gain_a, gate_a, up_a, down_a, attn_gain, qkv_weight, out_weight,
    mlp_gain_b, gate_b, up_b, down_b,
):
    gains = jnp.stack([mlp_gain_a, attn_gain, mlp_gain_b, stu_gain], axis=1)
    gains = jnp.pad(gains, ((0, 0), (0, OWN - 4)))
    weight = stu_weight.reshape(FEAT, D)
    x = inputs.T
    (
        scaling, features, x1, x2, na, qkv, wa, wat, gains_all,
        lse, of, go_heads, gx3, out, n3_all, gwo, gmlp_b, ggain_b,
    ) = first(
        shape_pick, x, out_grad.T, gains, filters, weight,
        gate_a, up_a, down_a, qkv_weight.T, out_weight, gate_b, up_b, down_b,
    )
    gx, joint, ga, gb, gain_sum = second(
        shape_pick, x, scaling, features, x1, x2, na, qkv, wa, wat, gains_all,
        lse, of, go_heads, gx3, n3_all, gwo, gmlp_b, ggain_b, gains, filters, weight,
    )
    joint, ga, gb = joint.astype(F32), ga.astype(F32), gb.astype(F32)
    return (
        out.T,
        gx.T,
        gain_sum[:, 3],
        joint[:FEAT].reshape(K + LAGS, CH, D),
        gain_sum[:, 0],
        ga[:OWN].T,
        ga[OWN : 2 * OWN].T,
        ga[2 * OWN :],
        gain_sum[:, 1],
        joint[FEAT : FEAT + 3 * CH].T,
        joint[FEAT + 3 * CH : FEAT + OWN],
        gain_sum[:, 2],
        gb[:OWN].T,
        gb[OWN : 2 * OWN].T,
        gb[2 * OWN :],
    )


def solution(mesh):
    cols, mid, row = P(None, "mp"), P(None, "mp", None), P("mp", None)
    return jax.shard_map(
        on_device,
        mesh=mesh,
        in_specs=(
            P("dp", "mp"), P("dp", "mp"), P("dp"), P(), P("mp"), mid,
            P("mp"), cols, cols, row, P("mp"), cols, row, P("mp"), cols, cols, row,
        ),
        out_specs=(
            P("dp", "mp"), P("dp", "mp"), P("mp"), mid, P("mp"), cols, cols, row,
            P("mp"), cols, row, P("mp"), cols, cols, row,
        ),
        check_vma=False,
    )
```

```python
import jax
import jax.numpy as jnp
from jax import lax
from jax.experimental import pallas as pl
from jax.experimental.pallas import tpu as pltpu
from jax.sharding import PartitionSpec as P

D = 512
T = 2048
OWN = 128
CH = 32
K = 24
LAGS = 3
FEAT = (K + LAGS) * CH
HD = 64
MP = 16
DP = 8
CHIPS = 8
EPSILON = 1e-05
NEG = -1e30
F32 = jnp.float32
BF16 = jnp.bfloat16
MESH = pl.DeviceIdType.MESH
VMEM = pl.BlockSpec(memory_space=pltpu.VMEM)
SMEM = pl.BlockSpec(memory_space=pltpu.SMEM)
ANY = pl.BlockSpec(memory_space=pl.ANY)
LIMIT = 62 * 2**20


def nn(left, right):
    return jnp.dot(left, right, preferred_element_type=F32)


def tn(left, right):
    return lax.dot_general(left, right, (((0,), (0,)), ((), ())), preferred_element_type=F32)


def nt(left, right):
    return lax.dot_general(left, right, (((1,), (1,)), ((), ())), preferred_element_type=F32)


class Place:
    def __init__(self):
        self.me = lax.axis_index("mp")
        self.z = self.me // 4
        self.chip = self.me // 2
        self.y = self.chip % 2
        self.core = self.me % 2
        self.dp = lax.axis_index("dp")
        self.x = self.dp % 4
        self.ylo = self.dp // 4
        self.partner = self.me + 1 - 2 * self.core
        self.across = self.me + 2 - 4 * self.y
        self.query_core = ((self.z + 1) // 2) % 2
        self.quarters = (self.core, 3 - self.core)

    def around(self, step):
        return (self.me + step) % MP

    def chip_at(self, step):
        return (self.chip + step) % CHIPS

    def along_z(self, step):
        return ((self.z + step) % 4) * 4 + self.me % 4

    def along_x(self, step):
        return {"dp": self.dp - self.x + (self.x + step) % 4}

    def along_dp(self, step):
        return (self.dp + step) % DP


def half(index):
    return pl.ds(pl.multiple_of(index * OWN, OWN), OWN)


def rows(index, count):
    return pl.ds(pl.multiple_of(index * count, count), count)


def remote(src, dst, sems, slot, target):
    return pltpu.make_async_remote_copy(
        src_ref=src,
        dst_ref=dst,
        send_sem=sems.at[0, slot],
        recv_sem=sems.at[1, slot],
        device_id=target if isinstance(target, dict) else {"mp": target},
        device_id_type=MESH,
    )


def greet(targets):
    barrier = pltpu.get_barrier_semaphore()
    for target in targets:
        where = target if isinstance(target, dict) else {"mp": target}
        pl.semaphore_signal(barrier, inc=1, device_id=where, device_id_type=MESH)
    pl.semaphore_wait(barrier, len(targets))


def sems(count):
    return pltpu.SemaphoreType.DMA((2, count))


def norm_forward(stream, gain):
    scaling = lax.rsqrt(jnp.sum(stream * stream, axis=0, keepdims=True) / D + EPSILON)
    return stream * scaling * gain, scaling


def norm_backward(upstream, stream, gain):
    scaling = lax.rsqrt(jnp.sum(stream * stream, axis=0, keepdims=True) / D + EPSILON)
    gain_grad = jnp.sum(upstream * stream * scaling, axis=1, keepdims=True)
    scaled = upstream * gain
    inner = jnp.sum(scaled * stream, axis=0, keepdims=True)
    return scaled * scaling - stream * (scaling * scaling * scaling * inner / D), gain_grad


def swap(place, src, dst, sem, slot=0):
    copy = remote(src, dst, sem, slot, place.across)
    copy.start()
    return copy


def share(place, src, dst, sem, slot):
    copy = remote(src, dst, sem, slot, place.partner)
    copy.start()
    return copy


def hidden_weights(ref):
    return [ref[:, :, group * OWN : (group + 1) * OWN].reshape(2 * D, D) for group in range(3)]


def hidden_backward(weights, normed, grad, acts, where):
    w_gate, w_up, w_down = weights
    gate = nn(w_gate, normed)
    up = nn(w_up, normed)
    sig = jax.nn.sigmoid(gate)
    hidden_grad = nn(w_down, grad)
    gate_grad = (hidden_grad * up * sig * (1.0 + gate * (1.0 - sig))).astype(BF16)
    up_grad = (hidden_grad * gate * sig).astype(BF16)
    acts[0, :, where] = gate_grad
    acts[1, :, where] = up_grad
    acts[2, :, where] = (gate * sig * up).astype(BF16)
    return tn(w_gate, gate_grad) + tn(w_up, up_grad)


def hidden_weight_grads(acts, acts_got, inputs, out):
    for group, (right, right_got) in enumerate(inputs):
        value = (nt(acts[group, :D], right[...]) + nt(acts_got[group], right_got[...])).astype(BF16)
        for index in range(4):
            out[index, group * OWN : (group + 1) * OWN] = value[index * OWN : (index + 1) * OWN]


def gather_all(place, buf, sem):
    own = buf.at[:, half(place.me)]
    sends = [
        remote(own, own, sem, step - 1, place.chip_at(step) * 2 + place.core) for step in range(1, CHIPS)
    ]
    forwards = [remote(own, own, sem, 7, place.partner)]
    for step in range(1, CHIPS):
        here = buf.at[:, half(place.chip_at(CHIPS - step) * 2 + place.core)]
        forwards.append(remote(here, here, sem, 7 + step, place.partner))

    def spread_own():
        for copy in sends + forwards[:1]:
            copy.start()

    def forward():
        for step in range(1, CHIPS):
            sends[step - 1].wait_recv()
            forwards[step].start()

    def close():
        for copy in sends:
            copy.wait_send()
        for copy in forwards:
            copy.wait()

    return spread_own, forward, close


def toeplitz(taps):
    wide = pltpu.roll(jnp.broadcast_to(taps, (OWN, T)), 0, 1, stride=1, stride_axis=0)
    lane = lax.broadcasted_iota(jnp.int32, (OWN, OWN), 1)
    row = lax.broadcasted_iota(jnp.int32, (OWN, OWN), 0)
    first = jnp.where(lane >= row, wide[:, :OWN], 0.0)
    return jnp.concatenate([first.astype(BF16), wide[:, OWN:].astype(BF16)], axis=1)


def reverse_taps(taps_ref, reverse):
    row = lax.broadcasted_iota(jnp.int32, (2 * OWN, OWN), 0)
    lane = lax.broadcasted_iota(jnp.int32, (2 * OWN, OWN), 1)
    inside = (lane >= 1) & (row == OWN - lane)
    edge = (lane == 0) & (row == OWN)
    flip = jnp.where(inside | edge, 1.0, 0.0).astype(BF16)
    for index in range(T // OWN):
        begin = T - (index + 1) * OWN
        piece = taps_ref[:, begin : begin + min(2 * OWN, T - begin)]
        reverse[:, index * OWN : (index + 1) * OWN] = nn(piece, flip[: piece.shape[1]])
    reverse[:, T : T + OWN] = nn(taps_ref[:, :OWN], flip[OWN:])
    reverse[:, T + OWN :] = jnp.zeros((K, OWN), F32)


def toeplitz_down(reverse, store):
    wide = pltpu.roll(jnp.broadcast_to(reverse, (OWN, T + 2 * OWN)), 0, 1, stride=1, stride_axis=0).astype(BF16)
    for block in range(T // OWN):
        begin = T - block * OWN
        store(block, wide[:, begin : begin + 2 * OWN])


def lag_mask(shift, pick):
    lane = lax.broadcasted_iota(jnp.int32, (CH, T), 1)
    inner = lane % (T // 2)
    return (lane >= shift) & ((inner >= shift) | (pick == 1))


def spread(qkv_ref, keys, values):
    for index in range(MP):
        keys[:, index * OWN : (index + 1) * OWN] = qkv_ref[index, HD : 2 * HD]
        values[:, index * OWN : (index + 1) * OWN] = qkv_ref[index, 2 * HD :]


def query_block(qkv_ref, quarter):
    parts = [qkv_ref[quarter * 4 + index, :HD] for index in range(4)]
    return jnp.concatenate(parts, axis=1) * jnp.asarray(HD**-0.5, BF16)


def score_mask(quarter, chunk, pick):
    query = quarter * 512 + lax.broadcasted_iota(jnp.int32, (512, 512), 1)
    key = chunk * 512 + lax.broadcasted_iota(jnp.int32, (512, 512), 0)
    same_half = (quarter // 2) == (chunk // 2)
    return (key <= query) & (same_half | (pick == 1))


class GradientSum:
    def __init__(self, place, parts, done, bufs, sem):
        self.place, self.parts, self.done, self.sem = place, parts, done, sem
        self.x_got, self.x_sum, self.y_got, self.y_sum, self.z_got = bufs
        self.copies = []

    def over_x(self):
        place = self.place
        for step in range(1, 4):
            there = (place.x + step) % 4
            copy = remote(
                self.parts.at[:, rows(there, 96)], self.x_got.at[step - 1], self.sem, step - 1, place.along_x(step)
            )
            copy.start()
            self.copies.append(copy)

    def over_y(self):
        place = self.place
        for copy in self.copies[:3]:
            copy.wait_recv()
        value = self.parts[:, rows(place.x, 96)].astype(F32)
        for index in range(3):
            value = value + self.x_got[index].astype(F32)
        self.x_sum[...] = value.astype(BF16)
        there = {"dp": place.dp + 4 - 8 * place.ylo}
        copy = remote(self.x_sum.at[:, rows(1 - place.ylo, 48)], self.y_got, self.sem, 3, there)
        copy.start()
        self.copies.append(copy)

    def over_z(self):
        place = self.place
        self.copies[3].wait_recv()
        value = self.x_sum[:, rows(place.ylo, 48)].astype(F32) + self.y_got[...].astype(F32)
        self.y_sum[...] = value.astype(BF16)
        for step in range(1, 4):
            copy = remote(self.y_sum.at[step], self.z_got.at[step - 1], self.sem, 3 + step, place.along_z(step))
            copy.start()
            self.copies.append(copy)

    def back(self):
        place = self.place
        for copy in self.copies[4:7]:
            copy.wait_recv()
        value = self.y_sum[0].astype(F32)
        for index in range(3):
            value = value + self.z_got[index].astype(F32)
        part = place.x * 2 + place.ylo
        self.done[rows(part, 48), :] = value.astype(BF16)
        mine = self.done.at[rows(part, 48)]
        for step in range(1, DP):
            copy = remote(mine, mine, self.sem, 6 + step, {"dp": place.along_dp(step)})
            copy.start()
            self.copies.append(copy)

    def close(self):
        for copy in self.copies[:7]:
            copy.wait_send()
        for copy in self.copies[7:]:
            copy.wait()


def first_kernel(
    pick_ref, x_ref, go_ref, gains_ref, taps_ref, weight_ref,
    gate_a, up_a, down_a, qkv_w, out_w, gate_b, up_b, down_b,
    scale_ref, feat_out, x1_ref, x2_ref, na_out, qkv_out, wa_out, wat_out, gains_all,
    lse_ref, of_ref, go_heads, gx3_ref, out_ref, n3_all, gwo_ref, gmlp_ref, ggain_ref,
    feat_ref, na_ref, qkv_ref, wa_ref, wat_ref, x_own, go2, squares, taps, table, weight_t, blocks, y_ref,
    core_got, chip_got, parts, got, heads, wb_ref, keys, values, own_heads, all_heads, x3_ref, nb, nb_got, go_got,
    acts, acts_got, parts_n, got_n, parts_z, got_z, grad_heads, out_own,
    sem_s, sem_x, sem_go, sem_gain, sem_wa, sem_wb, sem_wat, sem_y, sem_n, sem_g, sem_z, sem_q,
    sem_o, sem_nb, sem_gn, sem_zb, sem_h, sem_out, sem_all, sem_act, sem_save,
):
    place = Place()
    me, chip, core, x = place.me, place.chip, place.core, place.x
    count = T // OWN
    pick = pick_ref[0]
    stream = x_ref[...].astype(F32)
    squares[pl.ds(me, 1)] = jnp.sum(stream * stream, axis=0, keepdims=True)[None]
    for ref, (gate, up, down) in ((wa_ref, (gate_a, up_a, down_a)), (wb_ref, (gate_b, up_b, down_b))):
        ref[0, 0, :OWN] = gate[...].T
        ref[0, 0, OWN : 2 * OWN] = up[...].T
        ref[0, 0, 2 * OWN :] = down[...]
    wat_ref[chip, core, : 3 * CH] = qkv_w[...]
    wat_ref[chip, core, 3 * CH :] = out_w[...]
    greet([place.around(step) for step in range(1, MP)] + [place.along_x(step) for step in range(1, 4)])
    sums, late, fetch_a, fetch_b, fetch_t, rest_a, rest_b, rest_t = [], [], [], [], [], [], [], []
    for step in range(1, MP):
        there = place.around(step)
        copy = remote(squares.at[me], squares.at[me], sem_s, step - 1, there)
        copy.start()
        sums.append(copy)
    for step in range(1, 4):
        copy = remote(
            wa_ref.at[0, 0, rows(x, 96)], wa_ref.at[0, 4 - step, rows(x, 96)], sem_wa, step - 1, place.along_z(step)
        )
        copy.start()
        fetch_a.append(copy)
    mine_t = wat_ref.at[chip, core, rows(x, CH)]
    for step in range(1, CHIPS):
        copy = remote(mine_t, mine_t, sem_wat, step - 1, place.chip_at(step) * 2 + core)
        copy.start()
        fetch_t.append(copy)
    for step in range(1, MP):
        there = place.around(step)
        for src, dst, sem in (
            (x_ref.at[:, half(there)], x_own.at[rows(me, CH)], sem_x),
            (go_ref.at[:, half(there)], go2.at[rows(me, CH), :OWN], sem_go),
            (gains_ref, gains_all.at[rows(me, CH)], sem_gain),
        ):
            copy = remote(src, dst, sem, step - 1, there)
            copy.start()
            late.append(copy)
    for step in range(1, 4):
        copy = remote(
            wb_ref.at[0, 0, rows(x, 96)], wb_ref.at[0, 4 - step, rows(x, 96)], sem_wb, step - 1, place.along_z(step)
        )
        copy.start()
        fetch_b.append(copy)
    share_a = [share(place, wa_ref.at[0, 0], wa_ref.at[1, 0], sem_wa, 6)]
    share_b = [share(place, wb_ref.at[0, 0], wb_ref.at[1, 0], sem_wb, 6)]
    x_own[rows(me, CH), :] = x_ref[:, half(me)]
    go2[rows(me, CH), :OWN] = go_ref[:, half(me)]
    gains_all[rows(me, CH)] = gains_ref[...]
    taps[...] = taps_ref[...].astype(F32)
    weight_t[...] = weight_ref[...].T

    @pl.loop(0, K // 2)
    def _(step):
        for index in range(2):
            filter_table = toeplitz(taps[pl.ds(step * 2 + index, 1), :])
            for offset in range(count):
                table[step, offset * OWN : (offset + 1) * OWN, index * OWN : (index + 1) * OWN] = filter_table[
                    :, offset * OWN : (offset + 1) * OWN
                ]

    for copy in sums:
        copy.wait()
    total = squares[0]
    for index in range(1, MP):
        total = total + squares[index]
    scaling = lax.rsqrt(total / D + EPSILON)
    scale_ref[...] = scaling
    own = stream * scaling * gains_ref[:, 3:4].astype(F32)
    h = own.astype(BF16)
    own = h.astype(F32)
    joined = jnp.full((CH, OWN), (pick == 1).astype(F32)).astype(BF16)
    for target in range(count):
        for offset in range(count):
            here = (slice(target * CH, (target + 1) * CH), slice(offset * OWN, (offset + 1) * OWN))
            if offset > target:
                blocks[here] = jnp.zeros((CH, OWN), BF16)
                continue
            source = target - offset
            value = h[:, source * OWN : (source + 1) * OWN]
            if target >= count // 2 and source < count // 2:
                value = value * joined
            blocks[here] = value
    for shift in range(LAGS):
        moved = own if shift == 0 else pltpu.roll(own, shift, 1)
        moved = jnp.where(lag_mask(shift, pick), moved, 0.0).astype(BF16)
        feat_ref[(K + shift) * CH : (K + shift + 1) * CH, :] = moved

    def convolve(step):
        early = nn(blocks[: CH * count // 2, : T // 2], table[step, : T // 2, :]).astype(BF16)
        late_half = nn(blocks[CH * count // 2 :, :], table[step]).astype(BF16)
        for index in range(2):
            base = pl.multiple_of((step * 2 + index) * CH, CH)
            for target in range(count):
                part, at = (early, target) if target < count // 2 else (late_half, target - count // 2)
                feat_ref[pl.ds(base, CH), target * OWN : (target + 1) * OWN] = part[
                    at * CH : (at + 1) * CH, index * OWN : (index + 1) * OWN
                ]


    def pass_on(fetched, source, sem, done, rest):
        for copy in fetched:
            copy.wait_recv()
        for step in range(1, 4):
            copy = remote(source, source, sem, done + step - 1, place.along_x(step))
            copy.start()
            rest.append(copy)

    pl.loop(0, K // 4)(convolve)
    pass_on(fetch_a, wa_ref.at[0, 1:4, rows(x, 96)], sem_wa, 3, rest_a)
    pl.loop(K // 4, K // 2)(convolve)
    saves = []

    def save(src, dst):
        copy = pltpu.make_async_copy(src, dst, sem_save.at[len(saves)])
        copy.start()
        saves.append(copy)

    save(feat_ref, feat_out)
    for group in range(4):
        y = nn(weight_t[...], feat_ref[:, group * 512 : (group + 1) * 512]).astype(BF16)
        for index in range(4):
            y_ref[group * 2 + index // 2, index % 2] = y[:, index * OWN : (index + 1) * OWN]
    order = list(range(1, CHIPS)) + [0]
    first, second = [], []
    for step in order:
        there = place.chip_at(step)
        copy = remote(y_ref.at[there, 1 - core], core_got.at[there], sem_y, step, place.partner)
        copy.start()
        first.append(copy)
    for copy, step in zip(first, order):
        there = place.chip_at(step)
        copy.wait_recv()
        total = y_ref[there, core].astype(F32) + core_got[there].astype(F32)
        if step == 0:
            x1_ref[...] = total
        else:
            y_ref[there, core] = total.astype(BF16)
            move = remote(y_ref.at[there, core], chip_got.at[step - 1], sem_y, 7 + step, there * 2 + core)
            move.start()
            second.append(move)
    pass_on(fetch_t, wat_ref.at[:, core, rows(x, CH)], sem_wat, 7, rest_t)
    for copy in late:
        copy.wait()
    move_go = swap(place, go2.at[:, :OWN], go2.at[:, OWN:], sem_g)
    for copy in rest_a:
        copy.wait_recv()
    share_a.append(share(place, wa_ref.at[0, 1:], wa_ref.at[1, 1:], sem_wa, 7))
    for move in second:
        move.wait_recv()
    x1 = x1_ref[...] + x_own[...].astype(F32)
    for index in range(CHIPS - 1):
        x1 = x1 + chip_got[index].astype(F32)
    x1_ref[...] = x1
    normed, _ = norm_forward(x1, gains_all[:, 0:1].astype(F32))
    na_ref[:, :OWN] = normed.astype(BF16)
    move_n = swap(place, na_ref.at[:, :OWN], na_ref.at[:, OWN:], sem_n)
    for copy in share_a:
        copy.wait_recv()
    save(wa_ref, wa_out)
    w_gate, w_up, w_down = hidden_weights(wa_ref)

    def forward(normed):
        gate = nn(w_gate, normed)
        hidden = (gate * jax.nn.sigmoid(gate) * nn(w_up, normed)).astype(BF16)
        return tn(w_down, hidden)

    z = forward(na_ref[:, :OWN])
    pass_on(fetch_b, wb_ref.at[0, 1:4, rows(x, 96)], sem_wb, 3, rest_b)
    move_n.wait_recv()
    parts[...] = forward(na_ref[:, OWN:]).astype(BF16)
    move_z = swap(place, parts, got, sem_z)
    save(na_ref, na_out)
    for copy in rest_t:
        copy.wait_recv()
    half_t = wat_ref.at[:, core]
    share_t = share(place, half_t, half_t, sem_wat, 10)
    move_z.wait_recv()
    x2 = x1 + z + got[...].astype(F32)
    x2_ref[...] = x2
    n3 = norm_forward(x2, gains_all[:, 1:2].astype(F32))[0].astype(BF16)
    n3_all[:, half(me)] = n3
    share_t.wait_recv()
    save(wat_ref, wat_out)
    w_qkv = wat_ref[:, :, : 3 * CH].reshape(3 * D, D)
    heads[...] = nn(w_qkv, n3).astype(BF16).reshape(CHIPS, 3 * HD, OWN)
    sends = []
    for step in range(1, CHIPS):
        there = place.chip_at(step)
        copy = remote(heads.at[there], qkv_ref.at[me], sem_q, step - 1, there * 2 + core)
        copy.start()
        sends.append(copy)
    qkv_ref[me] = heads[chip]
    forwards = [remote(qkv_ref.at[me], qkv_ref.at[me], sem_q, 7, place.partner)]
    forwards[0].start()
    for step in range(1, CHIPS):
        source = place.chip_at(CHIPS - step) * 2 + core
        sends[step - 1].wait_recv()
        copy = remote(qkv_ref.at[source], qkv_ref.at[source], sem_q, 7 + step, place.partner)
        copy.start()
        forwards.append(copy)
    for copy in forwards:
        copy.wait()
    save(qkv_ref, qkv_out)
    for copy in rest_b:
        copy.wait_recv()
    share_b.append(share(place, wb_ref.at[0, 1:], wb_ref.at[1, 1:], sem_wb, 7))
    for copy in fetch_a + fetch_b + fetch_t + rest_a + rest_t + share_a + [share_t] + first + second + sends:
        copy.wait_send()
    move_go.wait()
    move_n.wait_send()
    move_z.wait_send()
    spread_n3, forward_n3, close_n3 = gather_all(place, n3_all, sem_all)
    spread_n3()
    spread(qkv_ref, keys, values)
    for part in range(2):
        quarter = place.quarters[part]
        queries = query_block(qkv_ref, quarter)
        top = jnp.full((1, 512), NEG, F32)
        norm = jnp.zeros((1, 512), F32)
        total = jnp.zeros((HD, 512), F32)
        for chunk in range(2 + 2 * part):
            here = slice(chunk * 512, (chunk + 1) * 512)
            scores = jnp.where(score_mask(quarter, chunk, pick), tn(keys[:, here], queries), NEG)
            new_top = jnp.maximum(top, jnp.max(scores, axis=0, keepdims=True))
            weights = jnp.exp(scores - new_top)
            rescale = jnp.exp(top - new_top)
            norm = norm * rescale + jnp.sum(weights, axis=0, keepdims=True)
            total = total * rescale + nn(values[:, here], weights.astype(BF16))
            top = new_top
        total = total / norm
        lse_ref[part] = top + jnp.log(norm)
        of_ref[part] = total
        for index in range(4):
            own_heads[part * 4 + index] = total[:, index * OWN : (index + 1) * OWN].astype(BF16)
    targets = [place.quarters[slot // 4] * 4 + slot % 4 for slot in range(8)]
    copies = [
        pltpu.make_async_remote_copy(
            src_ref=own_heads.at[slot], dst_ref=all_heads.at[chip],
            send_sem=sem_o.at[0, slot], recv_sem=sem_o.at[1, chip],
            device_id={"mp": targets[slot]}, device_id_type=MESH,
        )
        for slot in range(8)
    ]
    for slot in range(8):
        pl.when(targets[slot] != me)(copies[slot].start)

        @pl.when(targets[slot] == me)
        def _():
            all_heads[chip] = own_heads[slot]

    arrivals = [
        remote(own_heads.at[0], all_heads.at[head], sem_o, head, place.partner) for head in range(CHIPS)
    ]
    for head in range(CHIPS):
        pl.when(head * 2 + place.query_core != me)(arrivals[head].wait_recv)
    w_out = wat_ref[:, :, 3 * CH :].reshape(D, D)
    outputs = all_heads[...].reshape(D, OWN)
    x3 = x2 + tn(w_out, outputs)
    x3_ref[...] = x3
    gain_b = gains_all[:, 2:3].astype(F32)
    nb[:, :OWN] = norm_forward(x3, gain_b)[0].astype(BF16)
    move_n = swap(place, nb.at[:, :OWN], nb.at[:, OWN:], sem_nb)
    for copy in share_b:
        copy.wait_recv()
    weights = hidden_weights(wb_ref)
    normed_grad = hidden_backward(weights, nb[:, :OWN], go2[:, :OWN], acts, slice(0, OWN))
    move_n.wait_recv()
    parts_n[...] = hidden_backward(
        weights, nb[:, OWN:], go2[:, OWN:], acts, slice(OWN, 2 * OWN)
    ).astype(BF16)
    move_gn = swap(place, parts_n, got_n, sem_gn)
    shares = [
        share(place, acts.at[:, D:], acts_got, sem_act, 0),
        share(place, nb, nb_got, sem_act, 1),
        share(place, go2, go_got, sem_act, 2),
    ]
    parts_z[...] = tn(weights[2], acts[2, :, OWN:]).astype(BF16)
    move_z = swap(place, parts_z, got_z, sem_zb)
    z = tn(weights[2], acts[2, :, :OWN])
    move_gn.wait_recv()
    normed_grad = normed_grad + got_n[...].astype(F32)
    stream_grad, gain_grad = norm_backward(normed_grad, x3_ref[...], gain_b)
    ggain_ref[...] = gain_grad
    gx3 = go2[:, :OWN].astype(F32) + stream_grad
    gx3_ref[...] = gx3
    gy = gx3.astype(BF16)
    grad_heads[...] = nn(w_out, gy).astype(BF16).reshape(CHIPS, HD, OWN)
    slot = (place.z // 2) * 4 + me % 4
    sends = [
        pltpu.make_async_remote_copy(
            src_ref=grad_heads.at[head], dst_ref=go_heads.at[slot],
            send_sem=sem_h.at[0, head], recv_sem=sem_h.at[1, slot],
            device_id={"mp": head * 2 + place.query_core}, device_id_type=MESH,
        )
        for head in range(CHIPS)
    ]
    for head in range(CHIPS):
        pl.when(head * 2 + place.query_core != me)(sends[head].start)

        @pl.when(head * 2 + place.query_core == me)
        def _():
            go_heads[slot] = grad_heads[head]

    move_z.wait_recv()
    out_own[...] = (x3_ref[...] + z + got_z[...].astype(F32)).astype(BF16)
    moves = []
    for step in range(1, MP):
        there = place.around(step)
        copy = remote(out_own.at[rows(there, CH)], out_ref.at[:, half(me)], sem_out, step - 1, there)
        copy.start()
        moves.append(copy)
    out_ref[:, half(me)] = out_own[rows(me, CH), :]
    forward_n3()
    gwo_ref[...] = nt(outputs, gy).astype(BF16).reshape(MP, CH, D)
    for copy in shares:
        copy.wait_recv()
    hidden_weight_grads(acts, acts_got, ((nb, nb_got), (nb, nb_got), (go2, go_got)), gmlp_ref)
    for slot_in in range(8):
        arrival = remote(grad_heads.at[0], go_heads.at[slot_in], sem_h, slot_in, place.partner)
        pl.when(targets[slot_in] != me)(arrival.wait_recv)
    for slot_out in range(8):
        pl.when(targets[slot_out] != me)(copies[slot_out].wait_send)
        pl.when(slot_out * 2 + place.query_core != me)(sends[slot_out].wait_send)
    for copy in moves:
        copy.wait()
    close_n3()
    for copy in rest_b + share_b + shares + [move_n, move_gn, move_z]:
        copy.wait_send()
    for copy in saves:
        copy.wait()


def first(*operands):
    return pl.pallas_call(
        first_kernel,
        out_shape=(
            jax.ShapeDtypeStruct((1, T), F32),
            jax.ShapeDtypeStruct((FEAT, T), BF16),
            jax.ShapeDtypeStruct((D, OWN), F32),
            jax.ShapeDtypeStruct((D, OWN), F32),
            jax.ShapeDtypeStruct((D, 2 * OWN), BF16),
            jax.ShapeDtypeStruct((MP, 3 * HD, OWN), BF16),
            jax.ShapeDtypeStruct((2, 4, 3 * OWN, D), BF16),
            jax.ShapeDtypeStruct((CHIPS, 2, OWN, D), BF16),
            jax.ShapeDtypeStruct((D, OWN), BF16),
            jax.ShapeDtypeStruct((2, 1, 512), F32),
            jax.ShapeDtypeStruct((2, HD, 512), F32),
            jax.ShapeDtypeStruct((8, HD, OWN), BF16),
            jax.ShapeDtypeStruct((D, OWN), F32),
            jax.ShapeDtypeStruct((CH, T), BF16),
            jax.ShapeDtypeStruct((D, T), BF16),
            jax.ShapeDtypeStruct((MP, CH, D), BF16),
            jax.ShapeDtypeStruct((4, 3 * OWN, D), BF16),
            jax.ShapeDtypeStruct((D, 1), F32),
        ),
        in_specs=[SMEM] + [VMEM] * 13,
        out_specs=(VMEM, ANY, VMEM, VMEM, ANY, ANY, ANY, ANY) + (VMEM,) * 10,
        scratch_shapes=[
            pltpu.VMEM((FEAT, T), BF16),
            pltpu.VMEM((D, 2 * OWN), BF16),
            pltpu.VMEM((MP, 3 * HD, OWN), BF16),
            pltpu.VMEM((2, 4, 3 * OWN, D), BF16),
            pltpu.VMEM((CHIPS, 2, OWN, D), BF16),
            pltpu.VMEM((D, OWN), BF16),
            pltpu.VMEM((D, 2 * OWN), BF16),
            pltpu.VMEM((MP, 1, T), F32),
            pltpu.VMEM((K, T), F32),
            pltpu.VMEM((K // 2, T, 2 * OWN), BF16),
            pltpu.VMEM((D, FEAT), BF16),
            pltpu.VMEM((CH * T // OWN, T), BF16),
            pltpu.VMEM((CHIPS, 2, D, OWN), BF16),
            pltpu.VMEM((CHIPS, D, OWN), BF16),
            pltpu.VMEM((CHIPS - 1, D, OWN), BF16),
            pltpu.VMEM((D, OWN), BF16),
            pltpu.VMEM((D, OWN), BF16),
            pltpu.VMEM((CHIPS, 3 * HD, OWN), BF16),
            pltpu.VMEM((2, 4, 3 * OWN, D), BF16),
            pltpu.VMEM((HD, T), BF16),
            pltpu.VMEM((HD, T), BF16),
            pltpu.VMEM((8, HD, OWN), BF16),
            pltpu.VMEM((8, HD, OWN), BF16),
            pltpu.VMEM((D, OWN), F32),
            pltpu.VMEM((D, 2 * OWN), BF16),
            pltpu.VMEM((D, 2 * OWN), BF16),
            pltpu.VMEM((D, 2 * OWN), BF16),
            pltpu.VMEM((3, 2 * D, 2 * OWN), BF16),
            pltpu.VMEM((3, D, 2 * OWN), BF16),
            pltpu.VMEM((D, OWN), BF16),
            pltpu.VMEM((D, OWN), BF16),
            pltpu.VMEM((D, OWN), BF16),
            pltpu.VMEM((D, OWN), BF16),
            pltpu.VMEM((CHIPS, HD, OWN), BF16),
            pltpu.VMEM((D, OWN), BF16),
            sems(15), sems(15), sems(15), sems(15), sems(8), sems(8), sems(11),
            sems(15), sems(1), sems(1), sems(1), sems(15),
            sems(8), sems(1), sems(1), sems(1), sems(8), sems(15), sems(15), sems(3),
            pltpu.SemaphoreType.DMA((5,)),
        ],
        compiler_params=pltpu.CompilerParams(
            collective_id=0, has_side_effects=True, vmem_limit_bytes=LIMIT
        ),
        name="first",
    )(*operands)


def second_kernel(
    pick_ref, x_ref, scale_ref, feat_in, x1_ref, x2_ref, na_ref, qkv_ref, wa_in, wat_in, gains_all,
    lse_ref, of_ref, go_heads, gx3_ref, n3_in, gwo_ref, gmlp_b, ggain_b, gains_ref, taps_ref, weight_in,
    gx_ref, joint_ref, sum_a, sum_b, gain_sum,
    feat_ref, wa_ref, wat_ref, n3_all, weight_ref,
    keys, values, kv_grad, q_grad, mine, core_got, chip_sum, head_grads, gz, gz_got, na_got, parts, got,
    acts, acts_got, gy1_ref, row_got, q_rows, gwo_got,
    bx_got, bx_sum, by_got, by_sum, bz_got, gmlp_a, ax_got, ax_sum, ay_got, ay_sum, az_got, ggain_ref, gain_got, gain_own, gain_dp,
    reverse, table, feature_grad, shifted, total, gh_ref, joint, joint_got, inner,
    sem_q, sem_n, sem_z, sem_y, sem_gwo, sem_rows, sem_b, sem_a, sem_g, sem_gd, sem_j, sem_jg, sem_p, sem_act, sem_load,
):
    place = Place()
    me, dp, chip, core = place.me, place.dp, place.chip, place.core
    wide = 2 * OWN
    count = T // wide
    loads = []
    for src, dst in (
        (wat_in, wat_ref), (wa_in, wa_ref), (n3_in, n3_all), (feat_in, feat_ref), (weight_in, weight_ref)
    ):
        copy = pltpu.make_async_copy(src, dst, sem_load.at[len(loads)])
        copy.start()
        loads.append(copy)
    greet(
        [place.around(step) for step in range(1, MP)]
        + [{"dp": place.along_dp(step)} for step in range(1, DP)]
    )
    gain_a = gains_all[:, 0:1].astype(F32)
    gain_n = gains_all[:, 1:2].astype(F32)
    sum_of_b = GradientSum(place, gmlp_b, sum_b, (bx_got, bx_sum, by_got, by_sum, bz_got), sem_b)
    sum_of_a = GradientSum(place, gmlp_a, sum_a, (ax_got, ax_sum, ay_got, ay_sum, az_got), sem_a)
    share_n = share(place, na_ref, na_got, sem_act, 0)
    sum_of_b.over_x()
    o_first = []
    for step in range(1, MP):
        there = place.around(step)
        copy = remote(gwo_ref.at[there], gwo_got.at[step - 1], sem_gwo, step - 1, there)
        copy.start()
        o_first.append(copy)
    pick = pick_ref[0]
    spread(qkv_ref, keys, values)
    for part in range(2):
        quarter = place.quarters[part]
        queries = query_block(qkv_ref, quarter)
        out_grad = jnp.concatenate([go_heads[part * 4 + index] for index in range(4)], axis=1)
        weighted = jnp.sum(of_ref[part] * out_grad.astype(F32), axis=0, keepdims=True)
        queries_t = queries.T
        out_grad_t = out_grad.T
        query_grad = jnp.zeros((HD, 512), F32)
        for chunk in range(2 + 2 * part):
            here = slice(chunk * 512, (chunk + 1) * 512)
            scores = tn(keys[:, here], queries) - lse_ref[part]
            probs = jnp.where(score_mask(quarter, chunk, pick), jnp.exp(scores), 0.0)
            score_grad = (probs * (tn(values[:, here], out_grad) - weighted)).astype(BF16)
            query_grad = query_grad + nn(keys[:, here], score_grad)
            key_part = nn(score_grad, queries_t)
            value_part = nn(probs.astype(BF16), out_grad_t)
            both = jnp.concatenate([key_part, value_part], axis=1)
            if part == 1 and chunk < 2:
                both = both + kv_grad[here]
            kv_grad[here] = both
        q_grad[part] = (query_grad * HD**-0.5).astype(BF16)
    for index in range(MP):
        mine[index // 2, index % 2, :HD] = jnp.zeros((HD, OWN), BF16)
        mine[index // 2, index % 2, HD:] = kv_grad[index * OWN : (index + 1) * OWN].T.astype(BF16)
    for part in range(2):
        quarter = place.quarters[part]
        for index in range(4):
            mine[quarter * 2 + index // 2, index % 2, :HD] = q_grad[part, :, index * OWN : (index + 1) * OWN]
    order = list(range(1, CHIPS)) + [0]
    first = []
    for step in order:
        there = place.chip_at(step)
        copy = remote(mine.at[there, 1 - core], core_got.at[there], sem_q, step, place.partner)
        copy.start()
        first.append(copy)
    second = []
    for copy, step in zip(first, order):
        there = place.chip_at(step)
        copy.wait_recv()
        amount = (mine[there, core].astype(F32) + core_got[there].astype(F32)).astype(BF16)
        chip_sum[there] = amount
        if step == 0:
            head_grads[chip] = amount
        else:
            move = remote(chip_sum.at[there], head_grads.at[chip], sem_q, 7 + step, there * 2 + core)
            move.start()
            second.append(move)
    share_q = share(place, chip_sum.at[:, rows(1 - core, 96)], row_got, sem_rows, 0)
    for move in second:
        move.wait_recv()
    loads[0].wait()
    w_qkv = wat_ref[:, :, : 3 * CH].reshape(3 * D, D)
    columns = head_grads[...].reshape(3 * D, OWN)
    stream_grad, gain_grad = norm_backward(tn(w_qkv, columns), x2_ref[...], gain_n)
    lane = lax.broadcasted_iota(jnp.int32, (D, OWN), 1)
    gain_grads = jnp.where(lane == 1, gain_grad, 0.0) + jnp.where(lane == 2, ggain_b[...], 0.0)
    gx2 = gx3_ref[...] + stream_grad
    gz[:, :OWN] = gx2.astype(BF16)
    move_gz = swap(place, gz.at[:, :OWN], gz.at[:, OWN:], sem_n)
    sum_of_b.over_y()
    loads[1].wait()
    weights = hidden_weights(wa_ref)
    normed_grad = hidden_backward(weights, na_ref[:, :OWN], gz[:, :OWN], acts, slice(0, OWN))
    move_gz.wait_recv()
    parts[...] = hidden_backward(
        weights, na_ref[:, OWN:], gz[:, OWN:], acts, slice(OWN, 2 * OWN)
    ).astype(BF16)
    move_gn = swap(place, parts, got, sem_z)
    shares = [
        share_n,
        share(place, acts.at[:, D:], acts_got, sem_act, 1),
        share(place, gz, gz_got, sem_act, 2),
    ]
    sum_of_b.over_z()
    for copy in shares:
        copy.wait_recv()
    hidden_weight_grads(acts, acts_got, ((na_ref, na_got), (na_ref, na_got), (gz, gz_got)), gmlp_a)
    sum_of_a.over_x()
    move_gn.wait_recv()
    normed_grad = normed_grad + got[...].astype(F32)
    stream_grad, gain_grad = norm_backward(normed_grad, x1_ref[...], gain_a)
    ggain_ref[...] = gain_grads + jnp.where(lane == 0, gain_grad, 0.0)
    gy1_ref[:, half(me)] = (gx2 + stream_grad).astype(BF16)
    spread_gy1, forward_gy1, close_gy1 = gather_all(place, gy1_ref, sem_y)
    spread_gy1()
    sum_of_b.back()
    share_q.wait_recv()
    loads[2].wait()
    for index in range(CHIPS):
        q_rows[:, half(index * 2 + core)] = chip_sum[index, rows(core, 96), :]
        q_rows[:, half(index * 2 + 1 - core)] = row_got[index]
    joint[FEAT : FEAT + 3 * CH] = nt(q_rows[...], n3_all[...]).astype(BF16)
    for copy in o_first:
        copy.wait_recv()
    value = gwo_ref[me].astype(F32)
    for index in range(MP - 1):
        value = value + gwo_got[index].astype(F32)
    joint[FEAT + 3 * CH : FEAT + OWN] = value.astype(BF16)
    joint[FEAT + OWN :] = jnp.zeros((CH, D), BF16)
    reverse_taps(taps_ref, reverse)

    def build(filter_index, slot):
        def store(block, value):
            table[slot, block * OWN : (block + 1) * OWN, :] = value

        toeplitz_down(reverse[pl.ds(filter_index, 1), :], store)

    @pl.loop(0, K // 2)
    def _(index):
        build(index, index)

    forward_gy1()
    close_gy1()
    gain_first = []
    for step in range(1, MP):
        there = place.around(step)
        copy = remote(ggain_ref.at[rows(there, CH)], gain_got.at[step - 1], sem_g, step - 1, there)
        copy.start()
        gain_first.append(copy)
    loads[3].wait()
    loads[4].wait()
    joint[:FEAT] = nt(feat_ref[...], gy1_ref[...]).astype(BF16)
    j_first = []
    for step in range(1, DP):
        there = place.along_dp(step)
        copy = remote(joint.at[rows(there, OWN)], joint_got.at[step - 1], sem_j, step - 1, {"dp": there})
        copy.start()
        j_first.append(copy)
    for group in range(4):
        here = slice(group * 512, (group + 1) * 512)
        feature_grad[:, here] = nn(weight_ref[: K * CH], gy1_ref[:, here]).astype(BF16)
    total[...] = jnp.zeros_like(total)
    shifted[...] = jnp.zeros_like(shifted)
    joined = jnp.full((CH, T // 2), (pick == 1).astype(F32)).astype(BF16)
    middle = CH * count // 2

    def convolve(filter_index, slot):
        mine = feature_grad[pl.ds(pl.multiple_of(filter_index * CH, CH), CH), :]
        for source in range(count):
            here = slice(source * CH, (source + 1) * CH)
            begin = source * wide
            if source < count // 2:
                near_end = T // 2 - begin
                shifted[here, :near_end] = mine[:, begin : T // 2]
                shifted[here, near_end : T - begin] = mine[:, T // 2 :] * joined
            else:
                shifted[here, : T - begin] = mine[:, begin:]
        total[:middle] += nn(shifted[:middle, :], table[slot])
        total[middle:] += nn(shifted[middle:, : T // 2], table[slot, : T // 2, :])

    sum_of_a.over_y()

    @pl.loop(0, K // 2)
    def _(index):
        convolve(index, index)

    sum_of_a.over_z()

    @pl.loop(K // 2, K)
    def _(index):
        build(index, index - K // 2)
        convolve(index, index - K // 2)

    for source in range(count):
        gh_ref[:, source * wide : (source + 1) * wide] = total[source * CH : (source + 1) * CH]
    for shift in range(LAGS):
        begin = (K + shift) * CH
        value = nn(weight_ref[begin : begin + CH], gy1_ref[...])
        value = jnp.where(lag_mask(shift, pick), value, 0.0)
        if shift:
            value = pltpu.roll(value, T - shift, 1)
        gh_ref[...] += value
    stream = x_ref[...].astype(F32)
    scaled = gh_ref[...] * gains_ref[:, 3:4].astype(F32)
    inner[pl.ds(me, 1)] = jnp.sum(scaled * stream, axis=0, keepdims=True)[None]
    sums = []
    for step in range(1, MP):
        copy = remote(inner.at[me], inner.at[me], sem_p, step - 1, place.around(step))
        copy.start()
        sums.append(copy)
    last = []
    scaling = scale_ref[...]
    gain_grad = jnp.sum(gh_ref[...] * stream * scaling, axis=1, keepdims=True)
    for copy in gain_first:
        copy.wait_recv()
    value = ggain_ref[rows(me, CH), :]
    for index in range(MP - 1):
        value = value + gain_got[index]
    lane = lax.broadcasted_iota(jnp.int32, (CH, OWN), 1)
    gain_own[...] = value + jnp.where(lane == 3, gain_grad, 0.0)
    for step in range(1, DP):
        copy = remote(gain_own, gain_dp.at[step - 1], sem_gd, step - 1, {"dp": place.along_dp(step)})
        copy.start()
        last.append(copy)
    for copy in j_first:
        copy.wait_recv()
    value = joint[rows(dp, OWN), :].astype(F32)
    for index in range(DP - 1):
        value = value + joint_got[index].astype(F32)
    joint_ref[rows(dp, OWN), :] = value.astype(BF16)
    done_j = joint_ref.at[rows(dp, OWN)]
    for step in range(1, DP):
        copy = remote(done_j, done_j, sem_jg, step - 1, {"dp": place.along_dp(step)})
        copy.start()
        last.append(copy)
    sum_of_a.back()
    for copy in sums:
        copy.wait()
    value = inner[0]
    for index in range(1, MP):
        value = value + inner[index]
    stream_grad = scaled * scaling - stream * (scaling * scaling * scaling * value / D)
    gx_ref[...] = stream_grad + gy1_ref[rows(me, CH), :].astype(F32)
    for copy in last:
        copy.wait()
    value = gain_own[...]
    for index in range(DP - 1):
        value = value + gain_dp[index]
    gain_sum[...] = value
    for copy in first + second + [share_q] + shares + [move_gz, move_gn] + o_first + j_first + gain_first:
        copy.wait_send()
    sum_of_a.close()
    sum_of_b.close()


def second(*operands):
    return pl.pallas_call(
        second_kernel,
        out_shape=(
            jax.ShapeDtypeStruct((CH, T), F32),
            jax.ShapeDtypeStruct((DP * OWN, D), BF16),
            jax.ShapeDtypeStruct((3 * OWN, D), BF16),
            jax.ShapeDtypeStruct((3 * OWN, D), BF16),
            jax.ShapeDtypeStruct((CH, OWN), F32),
        ),
        in_specs=[SMEM, VMEM, VMEM, ANY, VMEM, VMEM, VMEM, VMEM, ANY, ANY]
        + [VMEM] * 5
        + [ANY]
        + [VMEM] * 5
        + [ANY],
        out_specs=(VMEM,) * 5,
        scratch_shapes=[
            pltpu.VMEM((FEAT, T), BF16),
            pltpu.VMEM((2, 4, 3 * OWN, D), BF16),
            pltpu.VMEM((CHIPS, 2, OWN, D), BF16),
            pltpu.VMEM((D, T), BF16),
            pltpu.VMEM((FEAT, D), BF16),
            pltpu.VMEM((HD, T), BF16),
            pltpu.VMEM((HD, T), BF16),
            pltpu.VMEM((T, 2 * HD), F32),
            pltpu.VMEM((2, HD, 512), BF16),
            pltpu.VMEM((CHIPS, 2, 3 * HD, OWN), BF16),
            pltpu.VMEM((CHIPS, 3 * HD, OWN), BF16),
            pltpu.VMEM((CHIPS, 3 * HD, OWN), BF16),
            pltpu.VMEM((CHIPS, 3 * HD, OWN), BF16),
            pltpu.VMEM((D, 2 * OWN), BF16),
            pltpu.VMEM((D, 2 * OWN), BF16),
            pltpu.VMEM((D, 2 * OWN), BF16),
            pltpu.VMEM((D, OWN), BF16),
            pltpu.VMEM((D, OWN), BF16),
            pltpu.VMEM((3, 2 * D, 2 * OWN), BF16),
            pltpu.VMEM((3, D, 2 * OWN), BF16),
            pltpu.VMEM((D, T), BF16),
            pltpu.VMEM((CHIPS, 96, OWN), BF16),
            pltpu.VMEM((96, T), BF16),
            pltpu.VMEM((MP - 1, CH, D), BF16),
            pltpu.VMEM((3, 4, 96, D), BF16),
            pltpu.VMEM((4, 96, D), BF16),
            pltpu.VMEM((4, 48, D), BF16),
            pltpu.VMEM((4, 48, D), BF16),
            pltpu.VMEM((3, 48, D), BF16),
            pltpu.VMEM((4, 3 * OWN, D), BF16),
            pltpu.VMEM((3, 4, 96, D), BF16),
            pltpu.VMEM((4, 96, D), BF16),
            pltpu.VMEM((4, 48, D), BF16),
            pltpu.VMEM((4, 48, D), BF16),
            pltpu.VMEM((3, 48, D), BF16),
            pltpu.VMEM((D, OWN), F32),
            pltpu.VMEM((MP - 1, CH, OWN), F32),
            pltpu.VMEM((CH, OWN), F32),
            pltpu.VMEM((DP - 1, CH, OWN), F32),
            pltpu.VMEM((K, T + 2 * OWN), F32),
            pltpu.VMEM((K // 2, T, 2 * OWN), BF16),
            pltpu.VMEM((K * CH, T), BF16),
            pltpu.VMEM((CH * T // (2 * OWN), T), BF16),
            pltpu.VMEM((CH * T // (2 * OWN), 2 * OWN), F32),
            pltpu.VMEM((CH, T), F32),
            pltpu.VMEM((DP * OWN, D), BF16),
            pltpu.VMEM((DP - 1, OWN, D), BF16),
            pltpu.VMEM((MP, 1, T), F32),
            sems(15), sems(1), sems(1), sems(15), sems(15), sems(1), sems(14), sems(14), sems(15),
            sems(7), sems(7), sems(7), sems(15), sems(3),
            pltpu.SemaphoreType.DMA((5,)),
        ],
        compiler_params=pltpu.CompilerParams(
            collective_id=1, has_side_effects=True, vmem_limit_bytes=LIMIT
        ),
        name="second",
    )(*operands)


def final_kernel(
    joint_ref, a_ref, b_ref, gain_ref,
    gws, gate_ga, up_ga, down_ga, gqkv, gout, gate_gb, up_gb, down_gb, *gain_grads,
):
    gws[...] = joint_ref[:FEAT].astype(F32)
    gqkv[...] = joint_ref[FEAT : FEAT + 3 * CH].astype(F32)
    gout[...] = joint_ref[FEAT + 3 * CH : FEAT + OWN].astype(F32)
    for ref, (gate, up, down) in ((a_ref, (gate_ga, up_ga, down_ga)), (b_ref, (gate_gb, up_gb, down_gb))):
        gate[...] = ref[:OWN].astype(F32).T
        up[...] = ref[OWN : 2 * OWN].astype(F32).T
        down[...] = ref[2 * OWN :].astype(F32)
    columns = gain_ref[...].T
    for index, grad in enumerate(gain_grads):
        grad[...] = columns[index : index + 1]


def final(*operands):
    mlp = [jax.ShapeDtypeStruct(shape, F32) for shape in ((D, OWN), (D, OWN), (OWN, D))]
    return pl.pallas_call(
        final_kernel,
        out_shape=(
            jax.ShapeDtypeStruct((FEAT, D), F32),
            *mlp,
            jax.ShapeDtypeStruct((3 * CH, D), F32),
            jax.ShapeDtypeStruct((CH, D), F32),
            *mlp,
            *[jax.ShapeDtypeStruct((1, CH), F32)] * 4,
        ),
        in_specs=[VMEM] * 4,
        out_specs=(VMEM,) * 13,
        compiler_params=pltpu.CompilerParams(vmem_limit_bytes=LIMIT),
        name="final",
    )(*operands)


def on_device(
    inputs, out_grad, shape_pick, filters, stu_gain, stu_weight,
    mlp_gain_a, gate_a, up_a, down_a, attn_gain, qkv_weight, out_weight,
    mlp_gain_b, gate_b, up_b, down_b,
):
    gains = jnp.stack([mlp_gain_a, attn_gain, mlp_gain_b, stu_gain], axis=1)
    gains = jnp.pad(gains, ((0, 0), (0, OWN - 4)))
    weight = stu_weight.reshape(FEAT, D)
    x = inputs.T
    (
        scaling, features, x1, x2, na, qkv, wa, wat, gains_all,
        lse, of, go_heads, gx3, out, n3_all, gwo, gmlp_b, ggain_b,
    ) = first(
        shape_pick, x, out_grad.T, gains, filters, weight,
        gate_a, up_a, down_a, qkv_weight.T, out_weight, gate_b, up_b, down_b,
    )
    gx, joint, ga, gb, gain_sum = second(
        shape_pick, x, scaling, features, x1, x2, na, qkv, wa, wat, gains_all,
        lse, of, go_heads, gx3, n3_all, gwo, gmlp_b, ggain_b, gains, filters, weight,
    )
    gws, gate_ga, up_ga, down_ga, gqkv, gout, gate_gb, up_gb, down_gb, *gain_grads = final(joint, ga, gb, gain_sum)
    gain_a, gain_n, gain_b, gain_s = (grad.reshape(CH) for grad in gain_grads)
    return (
        out.T, gx.T, gain_s, gws.reshape(K + LAGS, CH, D), gain_a, gate_ga, up_ga, down_ga,
        gain_n, gqkv.T, gout, gain_b, gate_gb, up_gb, down_gb,
    )


def solution(mesh):
    cols, mid, row = P(None, "mp"), P(None, "mp", None), P("mp", None)
    return jax.shard_map(
        on_device,
        mesh=mesh,
        in_specs=(
            P("dp", "mp"), P("dp", "mp"), P("dp"), P(), P("mp"), mid,
            P("mp"), cols, cols, row, P("mp"), cols, row, P("mp"), cols, cols, row,
        ),
        out_specs=(
            P("dp", "mp"), P("dp", "mp"), P("mp"), mid, P("mp"), cols, cols, row,
            P("mp"), cols, row, P("mp"), cols, cols, row,
        ),
        check_vma=False,
    )
```

```python
import jax
import jax.numpy as jnp
from jax import lax
from jax.experimental import pallas as pl
from jax.experimental.pallas import tpu as pltpu
from jax.sharding import PartitionSpec as P

D = 512
T = 2048
OWN = 128
CH = 32
K = 24
LAGS = 3
FEAT = (K + LAGS) * CH
HD = 64
MP = 16
DP = 8
CHIPS = 8
EPSILON = 1e-05
NEG = -1e30
F32 = jnp.float32
BF16 = jnp.bfloat16
MESH = pl.DeviceIdType.MESH
VMEM = pl.BlockSpec(memory_space=pltpu.VMEM)
SMEM = pl.BlockSpec(memory_space=pltpu.SMEM)
ANY = pl.BlockSpec(memory_space=pl.ANY)
LIMIT = 62 * 2**20
EARLY_TABLES = 4


def nn(left, right):
    return jnp.dot(left, right, preferred_element_type=F32)


def tn(left, right):
    return lax.dot_general(left, right, (((0,), (0,)), ((), ())), preferred_element_type=F32)


def tn_narrow(weights, right):
    return tn(right, weights).T


def nt(left, right):
    return lax.dot_general(left, right, (((1,), (1,)), ((), ())), preferred_element_type=F32)


class Place:
    def __init__(self):
        self.me = lax.axis_index("mp")
        self.z = self.me // 4
        self.chip = self.me // 2
        self.y = self.chip % 2
        self.core = self.me % 2
        self.dp = lax.axis_index("dp")
        self.x = self.dp % 4
        self.ylo = self.dp // 4
        self.partner = self.me + 1 - 2 * self.core
        self.beside = self.me + 2 - 4 * self.y
        self.across = self.me + 4 - 8 * (self.z % 2)
        self.query_core = ((self.z + 1) // 2) % 2
        self.quarters = (self.core, 3 - self.core)

    def around(self, step):
        return (self.me + step) % MP

    def chip_at(self, step):
        return (self.chip + step) % CHIPS

    def same_units(self, slot):
        return ((self.z + 2 * (slot // 2)) % 4) * 4 + ((self.y + slot % 2) % 2) * 2 + self.core

    def along_z(self, step):
        return ((self.z + step) % 4) * 4 + self.me % 4

    def along_x(self, step):
        return {"dp": self.dp - self.x + (self.x + step) % 4}

    def along_dp(self, step):
        return (self.dp + step) % DP


def half(index):
    return pl.ds(pl.multiple_of(index * OWN, OWN), OWN)


def rows(index, count):
    return pl.ds(pl.multiple_of(index * count, count), count)


def remote(src, dst, sems, slot, target):
    return pltpu.make_async_remote_copy(
        src_ref=src,
        dst_ref=dst,
        send_sem=sems.at[0, slot],
        recv_sem=sems.at[1, slot],
        device_id=target if isinstance(target, dict) else {"mp": target},
        device_id_type=MESH,
    )


def greet(targets):
    barrier = pltpu.get_barrier_semaphore()
    for target in targets:
        where = target if isinstance(target, dict) else {"mp": target}
        pl.semaphore_signal(barrier, inc=1, device_id=where, device_id_type=MESH)
    return lambda: pl.semaphore_wait(barrier, len(targets))


def sems(count):
    return pltpu.SemaphoreType.DMA((2, count))


def norm_forward(stream, gain):
    scaling = lax.rsqrt(jnp.sum(stream * stream, axis=0, keepdims=True) / D + EPSILON)
    return stream * scaling * gain, scaling


def norm_backward(upstream, stream, gain):
    scaling = lax.rsqrt(jnp.sum(stream * stream, axis=0, keepdims=True) / D + EPSILON)
    gain_grad = jnp.sum(upstream * stream * scaling, axis=1, keepdims=True)
    scaled = upstream * gain
    inner = jnp.sum(scaled * stream, axis=0, keepdims=True)
    return scaled * scaling - stream * (scaling * scaling * scaling * inner / D), gain_grad


def swap(place, src, dst, sem, slot=0):
    copy = remote(src, dst, sem, slot, place.across)
    copy.start()
    return copy


def share(place, src, dst, sem, slot):
    copy = remote(src, dst, sem, slot, place.partner)
    copy.start()
    return copy


def hidden_weights(ref):
    return [ref[:, :, group * OWN : (group + 1) * OWN].reshape(2 * D, D) for group in range(3)]


def hidden_backward(weights, normed, grad, acts, where):
    w_gate, w_up, w_down = weights
    gate = nn(w_gate, normed)
    up = nn(w_up, normed)
    sig = jax.nn.sigmoid(gate)
    hidden_grad = nn(w_down, grad)
    gate_grad = (hidden_grad * up * sig * (1.0 + gate * (1.0 - sig))).astype(BF16)
    up_grad = (hidden_grad * gate * sig).astype(BF16)
    acts[0, :, where] = gate_grad
    acts[1, :, where] = up_grad
    acts[2, :, where] = (gate * sig * up).astype(BF16)
    return (tn(gate_grad, w_gate) + tn(up_grad, w_up)).T


def hidden_weight_grads(acts, acts_got, inputs, out):
    for group, (right, right_got) in enumerate(inputs):
        value = (nt(acts[group, :D], right[...]) + nt(acts_got[group], right_got[...])).astype(BF16)
        for index in range(4):
            out[index, group * OWN : (group + 1) * OWN] = value[index * OWN : (index + 1) * OWN]


class Gather:
    steps = (1, 3, 2)

    def __init__(self, place, buf, sem):
        me = place.me
        own = buf.at[:, half(me)]
        beside = buf.at[:, half(place.beside)]
        self.to_beside = remote(own, own, sem, 0, place.beside)
        self.to_z = [remote(own, own, sem, step, place.along_z(step)) for step in self.steps]
        self.relays = [remote(beside, beside, sem, 3 + step, place.along_z(step)) for step in self.steps]
        self.forwards = [remote(own, own, sem, 7, place.partner), remote(beside, beside, sem, 8, place.partner)]
        for step in self.steps:
            for shift, other in ((8, me), (11, place.beside)):
                index = ((place.z + 4 - step) % 4) * 4 + other % 4
                here = buf.at[:, half(index)]
                self.forwards.append(remote(here, here, sem, shift + step, place.partner))

    def begin(self):
        for copy in [self.to_beside, *self.to_z, self.forwards[0]]:
            copy.start()

    def relay(self):
        self.to_beside.wait_recv()
        for copy in [*self.relays, self.forwards[1]]:
            copy.start()

    def arrive(self, index):
        self.to_z[index].wait_recv()
        self.forwards[2 + 2 * index].start()
        self.relays[index].wait_recv()
        self.forwards[3 + 2 * index].start()

    def joined(self, index):
        for copy in self.forwards[2 + 2 * index : 4 + 2 * index]:
            copy.wait_recv()

    def close(self):
        for copy in [self.to_beside, *self.to_z, *self.relays, *self.forwards]:
            copy.wait_send()


def toeplitz(taps):
    wide = pltpu.roll(jnp.broadcast_to(taps, (OWN, T)), 0, 1, stride=1, stride_axis=0)
    lane = lax.broadcasted_iota(jnp.int32, (OWN, OWN), 1)
    row = lax.broadcasted_iota(jnp.int32, (OWN, OWN), 0)
    first = jnp.where(lane >= row, wide[:, :OWN], 0.0)
    return jnp.concatenate([first.astype(BF16), wide[:, OWN:].astype(BF16)], axis=1)


def reverse_taps(taps_ref, reverse):
    row = lax.broadcasted_iota(jnp.int32, (2 * OWN, OWN), 0)
    lane = lax.broadcasted_iota(jnp.int32, (2 * OWN, OWN), 1)
    inside = (lane >= 1) & (row == OWN - lane)
    edge = (lane == 0) & (row == OWN)
    flip = jnp.where(inside | edge, 1.0, 0.0).astype(BF16)
    for index in range(T // OWN):
        begin = T - (index + 1) * OWN
        piece = taps_ref[:, begin : begin + min(2 * OWN, T - begin)]
        reverse[:, index * OWN : (index + 1) * OWN] = nn(piece, flip[: piece.shape[1]])
    reverse[:, T : T + OWN] = nn(taps_ref[:, :OWN], flip[OWN:])
    reverse[:, T + OWN :] = jnp.zeros((K, OWN), F32)


def toeplitz_down(reverse, store):
    wide = pltpu.roll(jnp.broadcast_to(reverse, (OWN, T + 2 * OWN)), 0, 1, stride=1, stride_axis=0).astype(BF16)
    for block in range(T // OWN):
        begin = T - block * OWN
        store(block, wide[:, begin : begin + 2 * OWN])


def lag_mask(shift, pick):
    lane = lax.broadcasted_iota(jnp.int32, (CH, T), 1)
    inner = lane % (T // 2)
    return (lane >= shift) & ((inner >= shift) | (pick == 1))


def spread(qkv_ref, keys, values):
    for index in range(MP):
        keys[:, index * OWN : (index + 1) * OWN] = qkv_ref[index, HD : 2 * HD]
        values[:, index * OWN : (index + 1) * OWN] = qkv_ref[index, 2 * HD :]


def query_block(qkv_ref, quarter):
    parts = [qkv_ref[quarter * 4 + index, :HD] for index in range(4)]
    return jnp.concatenate(parts, axis=1) * jnp.asarray(HD**-0.5, BF16)


def score_mask(quarter, chunk, pick):
    query = quarter * 512 + lax.broadcasted_iota(jnp.int32, (512, 512), 1)
    key = chunk * 512 + lax.broadcasted_iota(jnp.int32, (512, 512), 0)
    same_half = (quarter // 2) == (chunk // 2)
    return (key <= query) & (same_half | (pick == 1))


class GradientSum:
    def __init__(self, place, parts, done, bufs, sem, begin, each, y_first):
        self.place, self.parts, self.done, self.sem = place, parts, done, sem
        self.got, self.sum_1, self.got_2, self.sum_2, self.z_got = bufs
        self.begin, self.each, self.y_first = begin, each, y_first
        self.copies = []
        self.to_y = [(1 - place.ylo, {"dp": place.dp + 4 - 8 * place.ylo})]
        self.to_x = [((place.x + step) % 4, place.along_x(step)) for step in range(1, 4)]

    def at(self, index, count, begin=0):
        return pl.ds(pl.multiple_of(begin + index * count, 16), count)

    def send(self, src, dst, target):
        copy = remote(src, dst, self.sem, len(self.copies), target)
        copy.start()
        self.copies.append(copy)

    def arrived(self, count):
        for copy in self.copies[-count:]:
            copy.wait_recv()

    def first(self):
        count = self.each * (4 if self.y_first else 2)
        for slot, (there, target) in enumerate(self.to_y if self.y_first else self.to_x):
            self.send(self.parts.at[:, self.at(there, count, self.begin)], self.got.at[slot], target)

    def second(self):
        place, each = self.place, self.each
        here, peers, count = (place.ylo, 1, each * 4) if self.y_first else (place.x, 3, each * 2)
        self.arrived(peers)
        value = self.parts[:, self.at(here, count, self.begin)].astype(F32)
        for slot in range(peers):
            value = value + self.got[slot].astype(F32)
        self.sum_1[...] = value.astype(BF16)
        for slot, (there, target) in enumerate(self.to_x if self.y_first else self.to_y):
            self.send(self.sum_1.at[:, self.at(there, each)], self.got_2.at[slot], target)

    def third(self):
        place, each = self.place, self.each
        here, peers = (place.x, 3) if self.y_first else (place.ylo, 1)
        self.arrived(peers)
        value = self.sum_1[:, self.at(here, each)].astype(F32)
        for slot in range(peers):
            value = value + self.got_2[slot].astype(F32)
        self.sum_2[...] = value.astype(BF16)
        for step in range(1, 4):
            self.send(self.sum_2.at[step], self.z_got.at[step - 1], place.same_units(step))

    def back(self):
        place, each = self.place, self.each
        self.arrived(3)
        value = self.sum_2[0].astype(F32)
        for slot in range(3):
            value = value + self.z_got[slot].astype(F32)
        index = place.ylo * 4 + place.x if self.y_first else place.x * 2 + place.ylo
        mine = self.at(index, each, self.begin)
        self.done[mine, :] = value.astype(BF16)
        for step in range(1, DP):
            self.send(self.done.at[mine], self.done.at[mine], {"dp": place.along_dp(step)})

    def close(self):
        for copy in self.copies[:7]:
            copy.wait_send()
        for copy in self.copies[7:]:
            copy.wait()


def sum_buffers(each, y_first):
    first, second = (1, 3) if y_first else (3, 1)
    wide = each * (4 if y_first else 2)
    return [
        pltpu.VMEM((first, 4, wide, D), BF16),
        pltpu.VMEM((4, wide, D), BF16),
        pltpu.VMEM((second, 4, each, D), BF16),
        pltpu.VMEM((4, each, D), BF16),
        pltpu.VMEM((3, each, D), BF16),
    ]


def first_kernel(
    pick_ref, x_ref, go_ref, gains_ref, taps_ref, weight_ref,
    gate_a, up_a, down_a, qkv_w, out_w, gate_b, up_b, down_b,
    scale_ref, feat_out, x1_ref, x2_ref, na_out, qkv_out, wa_out, wat_out, gains_all,
    lse_ref, of_ref, go_heads, gx3_ref, out_ref, n3_all, gwo_ref, gmlp_ref, ggain_ref,
    feat_ref, na_ref, qkv_ref, wa_ref, wat_ref, x_own, go2, squares, taps, table, weight_t, blocks, y_ref,
    core_got, chip_got, parts, got, heads, wb_ref, keys, values, own_heads, all_heads, x3_ref, nb, nb_got, go_got,
    acts, acts_got, parts_n, got_n, parts_z, got_z, grad_heads, out_own,
    sem_s, sem_x, sem_go, sem_gain, sem_wa, sem_wb, sem_wat, sem_y, sem_n, sem_g, sem_z, sem_q,
    sem_o, sem_nb, sem_gn, sem_zb, sem_h, sem_out, sem_all, sem_act, sem_save,
):
    place = Place()
    me, chip, core, x = place.me, place.chip, place.core, place.x
    count = T // OWN
    pick = pick_ref[0]
    wat_ref[chip, core, : 3 * CH] = qkv_w[...]
    wat_ref[chip, core, 3 * CH :] = out_w[...]
    arrived = greet(
        [place.around(step) for step in range(1, MP)] + [place.along_x(step) for step in range(1, 4)]
    )
    stream = x_ref[...].astype(F32)
    squares[pl.ds(me, 1)] = jnp.sum(stream * stream, axis=0, keepdims=True)[None]
    for ref, (gate, up, down) in ((wa_ref, (gate_a, up_a, down_a)), (wb_ref, (gate_b, up_b, down_b))):
        ref[0, 0, :OWN] = gate[...].T
        ref[0, 0, OWN : 2 * OWN] = up[...].T
        ref[0, 0, 2 * OWN :] = down[...]
    taps[...] = taps_ref[...].astype(F32)

    def build(step):
        for index in range(2):
            filter_table = toeplitz(taps[pl.ds(step * 2 + index, 1), :])
            for offset in range(count):
                table[step, offset * OWN : (offset + 1) * OWN, index * OWN : (index + 1) * OWN] = filter_table[
                    :, offset * OWN : (offset + 1) * OWN
                ]

    pl.loop(0, EARLY_TABLES)(build)
    arrived()
    sums, late, fetch_a, fetch_b, fetch_t, rest_a, rest_b, rest_t = [], [], [], [], [], [], [], []
    for step in range(1, MP):
        there = place.around(step)
        copy = remote(squares.at[me], squares.at[me], sem_s, step - 1, there)
        copy.start()
        sums.append(copy)
    for step in range(1, 4):
        copy = remote(
            wa_ref.at[0, 0, rows(x, 96)], wa_ref.at[0, step, rows(x, 96)], sem_wa, step - 1, place.same_units(step)
        )
        copy.start()
        fetch_a.append(copy)
    mine_t = wat_ref.at[chip, core, rows(x, CH)]
    for step in range(1, CHIPS):
        copy = remote(mine_t, mine_t, sem_wat, step - 1, place.chip_at(step) * 2 + core)
        copy.start()
        fetch_t.append(copy)
    for step in range(1, MP):
        there = place.around(step)
        for src, dst, sem in (
            (x_ref.at[:, half(there)], x_own.at[rows(me, CH)], sem_x),
            (go_ref.at[:, half(there)], go2.at[rows(me, CH), :OWN], sem_go),
            (gains_ref, gains_all.at[rows(me, CH)], sem_gain),
        ):
            copy = remote(src, dst, sem, step - 1, there)
            copy.start()
            late.append(copy)
    for step in range(1, 4):
        copy = remote(
            wb_ref.at[0, 0, rows(x, 96)], wb_ref.at[0, step, rows(x, 96)], sem_wb, step - 1, place.same_units(step)
        )
        copy.start()
        fetch_b.append(copy)
    share_a = [share(place, wa_ref.at[0, 0], wa_ref.at[1, 0], sem_wa, 6)]
    share_b = [share(place, wb_ref.at[0, 0], wb_ref.at[1, 0], sem_wb, 6)]
    x_own[rows(me, CH), :] = x_ref[:, half(me)]
    go2[rows(me, CH), :OWN] = go_ref[:, half(me)]
    gains_all[rows(me, CH)] = gains_ref[...]
    weight_t[...] = weight_ref[...].T
    pl.loop(EARLY_TABLES, K // 2)(build)
    for copy in sums:
        copy.wait()
    total = squares[0]
    for index in range(1, MP):
        total = total + squares[index]
    scaling = lax.rsqrt(total / D + EPSILON)
    scale_ref[...] = scaling
    own = stream * scaling * gains_ref[:, 3:4].astype(F32)
    h = own.astype(BF16)
    own = h.astype(F32)
    joined = jnp.full((CH, OWN), (pick == 1).astype(F32)).astype(BF16)
    for target in range(count):
        for offset in range(count):
            here = (slice(target * CH, (target + 1) * CH), slice(offset * OWN, (offset + 1) * OWN))
            if offset > target:
                blocks[here] = jnp.zeros((CH, OWN), BF16)
                continue
            source = target - offset
            value = h[:, source * OWN : (source + 1) * OWN]
            if target >= count // 2 and source < count // 2:
                value = value * joined
            blocks[here] = value
    for shift in range(LAGS):
        moved = own if shift == 0 else pltpu.roll(own, shift, 1)
        moved = jnp.where(lag_mask(shift, pick), moved, 0.0).astype(BF16)
        feat_ref[(K + shift) * CH : (K + shift + 1) * CH, :] = moved

    def convolve(step):
        early = nn(blocks[: CH * count // 2, : T // 2], table[step, : T // 2, :]).astype(BF16)
        late_half = nn(blocks[CH * count // 2 :, :], table[step]).astype(BF16)
        for index in range(2):
            base = pl.multiple_of((step * 2 + index) * CH, CH)
            for target in range(count):
                part, at = (early, target) if target < count // 2 else (late_half, target - count // 2)
                feat_ref[pl.ds(base, CH), target * OWN : (target + 1) * OWN] = part[
                    at * CH : (at + 1) * CH, index * OWN : (index + 1) * OWN
                ]


    def pass_on(fetched, source, sem, done, rest):
        for copy in fetched:
            copy.wait_recv()
        for step in range(1, 4):
            copy = remote(source, source, sem, done + step - 1, place.along_x(step))
            copy.start()
            rest.append(copy)

    pl.loop(0, K // 4)(convolve)
    pass_on(fetch_a, wa_ref.at[0, 1:4, rows(x, 96)], sem_wa, 3, rest_a)
    pl.loop(K // 4, K // 2)(convolve)
    saves = []

    def save(src, dst):
        copy = pltpu.make_async_copy(src, dst, sem_save.at[len(saves)])
        copy.start()
        saves.append(copy)

    save(feat_ref, feat_out)
    for group in range(4):
        y = nn(weight_t[...], feat_ref[:, group * 512 : (group + 1) * 512]).astype(BF16)
        for index in range(4):
            y_ref[group * 2 + index // 2, index % 2] = y[:, index * OWN : (index + 1) * OWN]
    order = list(range(1, CHIPS)) + [0]
    first, second = [], []
    for step in order:
        there = place.chip_at(step)
        copy = remote(y_ref.at[there, 1 - core], core_got.at[there], sem_y, step, place.partner)
        copy.start()
        first.append(copy)
    for copy, step in zip(first, order):
        there = place.chip_at(step)
        copy.wait_recv()
        total = y_ref[there, core].astype(F32) + core_got[there].astype(F32)
        if step == 0:
            x1_ref[...] = total
        else:
            y_ref[there, core] = total.astype(BF16)
            move = remote(y_ref.at[there, core], chip_got.at[step - 1], sem_y, 7 + step, there * 2 + core)
            move.start()
            second.append(move)
    pass_on(fetch_t, wat_ref.at[:, core, rows(x, CH)], sem_wat, 7, rest_t)
    for copy in late:
        copy.wait()
    for copy in rest_a:
        copy.wait_recv()
    share_a.append(share(place, wa_ref.at[0, 1:], wa_ref.at[1, 1:], sem_wa, 7))
    for move in second:
        move.wait_recv()
    x1 = x1_ref[...] + x_own[...].astype(F32)
    for index in range(CHIPS - 1):
        x1 = x1 + chip_got[index].astype(F32)
    x1_ref[...] = x1
    normed, _ = norm_forward(x1, gains_all[:, 0:1].astype(F32))
    na_ref[:, :OWN] = normed.astype(BF16)
    move_n = swap(place, na_ref.at[:, :OWN], na_ref.at[:, OWN:], sem_n)
    for copy in share_a:
        copy.wait_recv()
    save(wa_ref, wa_out)
    w_gate, w_up, w_down = hidden_weights(wa_ref)

    def forward(normed):
        gate = nn(w_gate, normed)
        hidden = (gate * jax.nn.sigmoid(gate) * nn(w_up, normed)).astype(BF16)
        return tn_narrow(w_down, hidden)

    z = forward(na_ref[:, :OWN])
    pass_on(fetch_b, wb_ref.at[0, 1:4, rows(x, 96)], sem_wb, 3, rest_b)
    move_n.wait_recv()
    parts[...] = forward(na_ref[:, OWN:]).astype(BF16)
    move_z = swap(place, parts, got, sem_z)
    save(na_ref, na_out)
    for copy in rest_t:
        copy.wait_recv()
    half_t = wat_ref.at[:, core]
    share_t = share(place, half_t, half_t, sem_wat, 10)
    move_z.wait_recv()
    x2 = x1 + z + got[...].astype(F32)
    x2_ref[...] = x2
    n3 = norm_forward(x2, gains_all[:, 1:2].astype(F32))[0].astype(BF16)
    n3_all[:, half(me)] = n3
    share_t.wait_recv()
    save(wat_ref, wat_out)
    w_qkv = wat_ref[:, :, : 3 * CH].reshape(3 * D, D)
    heads[...] = nn(w_qkv, n3).astype(BF16).reshape(CHIPS, 3 * HD, OWN)
    sends = []
    for step in range(1, CHIPS):
        there = place.chip_at(step)
        copy = remote(heads.at[there], qkv_ref.at[me], sem_q, step - 1, there * 2 + core)
        copy.start()
        sends.append(copy)
    qkv_ref[me] = heads[chip]
    forwards = [remote(qkv_ref.at[me], qkv_ref.at[me], sem_q, 7, place.partner)]
    forwards[0].start()
    for step in range(1, CHIPS):
        source = place.chip_at(CHIPS - step) * 2 + core
        sends[step - 1].wait_recv()
        copy = remote(qkv_ref.at[source], qkv_ref.at[source], sem_q, 7 + step, place.partner)
        copy.start()
        forwards.append(copy)
    for copy in forwards:
        copy.wait()
    save(qkv_ref, qkv_out)
    for copy in rest_b:
        copy.wait_recv()
    share_b.append(share(place, wb_ref.at[0, 1:], wb_ref.at[1, 1:], sem_wb, 7))
    for copy in fetch_a + fetch_b + fetch_t + rest_a + rest_t + share_a + [share_t] + first + second + sends:
        copy.wait_send()
    move_n.wait_send()
    move_z.wait_send()
    gather_n3 = Gather(place, n3_all, sem_all)
    gather_n3.begin()
    move_go = swap(place, go2.at[:, :OWN], go2.at[:, OWN:], sem_g)
    spread(qkv_ref, keys, values)
    for part in range(2):
        quarter = place.quarters[part]
        queries = query_block(qkv_ref, quarter)
        top = jnp.full((1, 512), NEG, F32)
        norm = jnp.zeros((1, 512), F32)
        total = jnp.zeros((HD, 512), F32)
        for chunk in range(2 + 2 * part):
            here = slice(chunk * 512, (chunk + 1) * 512)
            scores = jnp.where(score_mask(quarter, chunk, pick), tn(keys[:, here], queries), NEG)
            new_top = jnp.maximum(top, jnp.max(scores, axis=0, keepdims=True))
            weights = jnp.exp(scores - new_top)
            rescale = jnp.exp(top - new_top)
            norm = norm * rescale + jnp.sum(weights, axis=0, keepdims=True)
            total = total * rescale + nn(values[:, here], weights.astype(BF16))
            top = new_top
        total = total / norm
        lse_ref[part] = top + jnp.log(norm)
        of_ref[part] = total
        for index in range(4):
            own_heads[part * 4 + index] = total[:, index * OWN : (index + 1) * OWN].astype(BF16)
    targets = [place.quarters[slot // 4] * 4 + slot % 4 for slot in range(8)]
    copies = [
        pltpu.make_async_remote_copy(
            src_ref=own_heads.at[slot], dst_ref=all_heads.at[chip],
            send_sem=sem_o.at[0, slot], recv_sem=sem_o.at[1, chip],
            device_id={"mp": targets[slot]}, device_id_type=MESH,
        )
        for slot in range(8)
    ]
    for slot in range(8):
        pl.when(targets[slot] != me)(copies[slot].start)

        @pl.when(targets[slot] == me)
        def _():
            all_heads[chip] = own_heads[slot]

    gather_n3.relay()
    arrivals = [
        remote(own_heads.at[0], all_heads.at[head], sem_o, head, place.partner) for head in range(CHIPS)
    ]
    for head in range(CHIPS):
        pl.when(head * 2 + place.query_core != me)(arrivals[head].wait_recv)
    w_out = wat_ref[:, :, 3 * CH :].reshape(D, D)
    outputs = all_heads[...].reshape(D, OWN)
    x3 = x2 + tn_narrow(w_out, outputs)
    x3_ref[...] = x3
    gain_b = gains_all[:, 2:3].astype(F32)
    nb[:, :OWN] = norm_forward(x3, gain_b)[0].astype(BF16)
    move_n = swap(place, nb.at[:, :OWN], nb.at[:, OWN:], sem_nb)
    for copy in share_b + [move_go]:
        copy.wait_recv()
    weights = hidden_weights(wb_ref)
    normed_grad = hidden_backward(weights, nb[:, :OWN], go2[:, :OWN], acts, slice(0, OWN))
    move_n.wait_recv()
    parts_n[...] = hidden_backward(
        weights, nb[:, OWN:], go2[:, OWN:], acts, slice(OWN, 2 * OWN)
    ).astype(BF16)
    move_gn = swap(place, parts_n, got_n, sem_gn)
    shares = [
        share(place, acts.at[:, D:], acts_got, sem_act, 0),
        share(place, nb, nb_got, sem_act, 1),
        share(place, go2, go_got, sem_act, 2),
    ]
    parts_z[...] = tn_narrow(weights[2], acts[2, :, OWN:]).astype(BF16)
    move_z = swap(place, parts_z, got_z, sem_zb)
    z = tn_narrow(weights[2], acts[2, :, :OWN])
    move_gn.wait_recv()
    normed_grad = normed_grad + got_n[...].astype(F32)
    stream_grad, gain_grad = norm_backward(normed_grad, x3_ref[...], gain_b)
    ggain_ref[...] = gain_grad
    gx3 = go2[:, :OWN].astype(F32) + stream_grad
    gx3_ref[...] = gx3
    gy = gx3.astype(BF16)
    grad_heads[...] = nn(w_out, gy).astype(BF16).reshape(CHIPS, HD, OWN)
    slot = (place.z // 2) * 4 + me % 4
    sends = [
        pltpu.make_async_remote_copy(
            src_ref=grad_heads.at[head], dst_ref=go_heads.at[slot],
            send_sem=sem_h.at[0, head], recv_sem=sem_h.at[1, slot],
            device_id={"mp": head * 2 + place.query_core}, device_id_type=MESH,
        )
        for head in range(CHIPS)
    ]
    for head in range(CHIPS):
        pl.when(head * 2 + place.query_core != me)(sends[head].start)

        @pl.when(head * 2 + place.query_core == me)
        def _():
            go_heads[slot] = grad_heads[head]

    move_z.wait_recv()
    out_own[...] = (x3_ref[...] + z + got_z[...].astype(F32)).astype(BF16)
    moves = []
    for step in range(1, MP):
        there = place.around(step)
        copy = remote(out_own.at[rows(there, CH)], out_ref.at[:, half(me)], sem_out, step - 1, there)
        copy.start()
        moves.append(copy)
    out_ref[:, half(me)] = out_own[rows(me, CH), :]
    for index in range(3):
        gather_n3.arrive(index)
    gwo_ref[...] = nt(outputs, gy).astype(BF16).reshape(MP, CH, D)
    for copy in shares:
        copy.wait_recv()
    hidden_weight_grads(acts, acts_got, ((nb, nb_got), (nb, nb_got), (go2, go_got)), gmlp_ref)
    for slot_in in range(8):
        arrival = remote(grad_heads.at[0], go_heads.at[slot_in], sem_h, slot_in, place.partner)
        pl.when(targets[slot_in] != me)(arrival.wait_recv)
    for slot_out in range(8):
        pl.when(targets[slot_out] != me)(copies[slot_out].wait_send)
        pl.when(slot_out * 2 + place.query_core != me)(sends[slot_out].wait_send)
    for copy in moves:
        copy.wait()
    for index in range(-1, 3):
        gather_n3.joined(index)
    gather_n3.close()
    for copy in rest_b + share_b + shares + [move_go, move_n, move_gn, move_z]:
        copy.wait_send()
    for copy in saves:
        copy.wait()


def first(*operands):
    return pl.pallas_call(
        first_kernel,
        out_shape=(
            jax.ShapeDtypeStruct((1, T), F32),
            jax.ShapeDtypeStruct((FEAT, T), BF16),
            jax.ShapeDtypeStruct((D, OWN), F32),
            jax.ShapeDtypeStruct((D, OWN), F32),
            jax.ShapeDtypeStruct((D, 2 * OWN), BF16),
            jax.ShapeDtypeStruct((MP, 3 * HD, OWN), BF16),
            jax.ShapeDtypeStruct((2, 4, 3 * OWN, D), BF16),
            jax.ShapeDtypeStruct((CHIPS, 2, OWN, D), BF16),
            jax.ShapeDtypeStruct((D, OWN), BF16),
            jax.ShapeDtypeStruct((2, 1, 512), F32),
            jax.ShapeDtypeStruct((2, HD, 512), F32),
            jax.ShapeDtypeStruct((8, HD, OWN), BF16),
            jax.ShapeDtypeStruct((D, OWN), F32),
            jax.ShapeDtypeStruct((CH, T), BF16),
            jax.ShapeDtypeStruct((D, T), BF16),
            jax.ShapeDtypeStruct((MP, CH, D), BF16),
            jax.ShapeDtypeStruct((4, 3 * OWN, D), BF16),
            jax.ShapeDtypeStruct((D, 1), F32),
        ),
        in_specs=[SMEM] + [VMEM] * 13,
        out_specs=(VMEM, ANY, VMEM, VMEM, ANY, ANY, ANY, ANY) + (VMEM,) * 10,
        scratch_shapes=[
            pltpu.VMEM((FEAT, T), BF16),
            pltpu.VMEM((D, 2 * OWN), BF16),
            pltpu.VMEM((MP, 3 * HD, OWN), BF16),
            pltpu.VMEM((2, 4, 3 * OWN, D), BF16),
            pltpu.VMEM((CHIPS, 2, OWN, D), BF16),
            pltpu.VMEM((D, OWN), BF16),
            pltpu.VMEM((D, 2 * OWN), BF16),
            pltpu.VMEM((MP, 1, T), F32),
            pltpu.VMEM((K, T), F32),
            pltpu.VMEM((K // 2, T, 2 * OWN), BF16),
            pltpu.VMEM((D, FEAT), BF16),
            pltpu.VMEM((CH * T // OWN, T), BF16),
            pltpu.VMEM((CHIPS, 2, D, OWN), BF16),
            pltpu.VMEM((CHIPS, D, OWN), BF16),
            pltpu.VMEM((CHIPS - 1, D, OWN), BF16),
            pltpu.VMEM((D, OWN), BF16),
            pltpu.VMEM((D, OWN), BF16),
            pltpu.VMEM((CHIPS, 3 * HD, OWN), BF16),
            pltpu.VMEM((2, 4, 3 * OWN, D), BF16),
            pltpu.VMEM((HD, T), BF16),
            pltpu.VMEM((HD, T), BF16),
            pltpu.VMEM((8, HD, OWN), BF16),
            pltpu.VMEM((8, HD, OWN), BF16),
            pltpu.VMEM((D, OWN), F32),
            pltpu.VMEM((D, 2 * OWN), BF16),
            pltpu.VMEM((D, 2 * OWN), BF16),
            pltpu.VMEM((D, 2 * OWN), BF16),
            pltpu.VMEM((3, 2 * D, 2 * OWN), BF16),
            pltpu.VMEM((3, D, 2 * OWN), BF16),
            pltpu.VMEM((D, OWN), BF16),
            pltpu.VMEM((D, OWN), BF16),
            pltpu.VMEM((D, OWN), BF16),
            pltpu.VMEM((D, OWN), BF16),
            pltpu.VMEM((CHIPS, HD, OWN), BF16),
            pltpu.VMEM((D, OWN), BF16),
            sems(15), sems(15), sems(15), sems(15), sems(8), sems(8), sems(11),
            sems(15), sems(1), sems(1), sems(1), sems(15),
            sems(8), sems(1), sems(1), sems(1), sems(8), sems(15), sems(15), sems(3),
            pltpu.SemaphoreType.DMA((5,)),
        ],
        compiler_params=pltpu.CompilerParams(
            collective_id=0, has_side_effects=True, vmem_limit_bytes=LIMIT
        ),
        name="first",
    )(*operands)


def second_kernel(
    pick_ref, x_ref, scale_ref, feat_in, x1_ref, x2_ref, na_ref, qkv_ref, wa_in, wat_in, gains_all,
    lse_ref, of_ref, go_heads, gx3_ref, n3_in, gwo_ref, gmlp_b, ggain_b, gains_ref, taps_ref, weight_in,
    gx_ref, joint_ref, sum_t, sum_a, sum_b, gain_sum,
    feat_ref, wa_ref, wat_ref, n3_all, weight_ref,
    keys, values, kv_grad, q_grad, mine, core_got, chip_sum, head_grads, gz, gz_got, na_got, parts, got,
    acts, acts_got, gy1_ref, row_got, q_rows, gwo_got,
    b_1, b_2, b_3, b_4, b_5, gmlp_a, a_1, a_2, a_3, a_4, a_5, a_6, a_7, a_8, a_9, a_10, gat, gat_got, ggain_ref, gain_got, gain_own, gain_dp,
    reverse, table, feature_grad, shifted, total, gh_ref, joint_sum, joint, joint_got, inner,
    sem_q, sem_n, sem_z, sem_y, sem_gwo, sem_rows, sem_b, sem_a, sem_a2, sem_t, sem_tg, sem_g, sem_gd, sem_j, sem_jg, sem_p, sem_act, sem_load,
):
    place = Place()
    me, dp, chip, core = place.me, place.dp, place.chip, place.core
    wide = 2 * OWN
    count = T // wide
    loads = []
    for src, dst in (
        (wat_in, wat_ref), (wa_in, wa_ref), (n3_in, n3_all), (feat_in, feat_ref), (weight_in, weight_ref)
    ):
        copy = pltpu.make_async_copy(src, dst, sem_load.at[len(loads)])
        copy.start()
        loads.append(copy)
    arrived = greet(
        [place.around(step) for step in range(1, MP)]
        + [{"dp": place.along_dp(step)} for step in range(1, DP)]
    )
    gain_a = gains_all[:, 0:1].astype(F32)
    gain_n = gains_all[:, 1:2].astype(F32)
    sum_of_b = GradientSum(place, gmlp_b, sum_b, (b_1, b_2, b_3, b_4, b_5), sem_b, 0, 48, False)
    sums_of_a = (
        GradientSum(place, gmlp_a, sum_a, (a_1, a_2, a_3, a_4, a_5), sem_a, 0, 32, False),
        GradientSum(place, gmlp_a, sum_a, (a_6, a_7, a_8, a_9, a_10), sem_a2, 256, 16, True),
    )
    pick = pick_ref[0]
    spread(qkv_ref, keys, values)
    for part in range(2):
        quarter = place.quarters[part]
        queries = query_block(qkv_ref, quarter)
        out_grad = jnp.concatenate([go_heads[part * 4 + index] for index in range(4)], axis=1)
        weighted = jnp.sum(of_ref[part] * out_grad.astype(F32), axis=0, keepdims=True)
        queries_t = queries.T
        out_grad_t = out_grad.T
        query_grad = jnp.zeros((HD, 512), F32)
        for chunk in range(2 + 2 * part):
            here = slice(chunk * 512, (chunk + 1) * 512)
            scores = tn(keys[:, here], queries) - lse_ref[part]
            probs = jnp.where(score_mask(quarter, chunk, pick), jnp.exp(scores), 0.0)
            score_grad = (probs * (tn(values[:, here], out_grad) - weighted)).astype(BF16)
            query_grad = query_grad + nn(keys[:, here], score_grad)
            key_part = nn(score_grad, queries_t)
            value_part = nn(probs.astype(BF16), out_grad_t)
            both = jnp.concatenate([key_part, value_part], axis=1)
            if part == 1 and chunk < 2:
                both = both + kv_grad[here]
            kv_grad[here] = both
        q_grad[part] = (query_grad * HD**-0.5).astype(BF16)
        if part == 0:
            arrived()
            share_n = share(place, na_ref, na_got, sem_act, 0)
            sum_of_b.first()
            o_first = []
            for step in range(1, MP):
                there = place.around(step)
                copy = remote(gwo_ref.at[there], gwo_got.at[step - 1], sem_gwo, step - 1, there)
                copy.start()
                o_first.append(copy)
    for index in range(MP):
        mine[index // 2, index % 2, :HD] = jnp.zeros((HD, OWN), BF16)
        mine[index // 2, index % 2, HD:] = kv_grad[index * OWN : (index + 1) * OWN].T.astype(BF16)
    for part in range(2):
        quarter = place.quarters[part]
        for index in range(4):
            mine[quarter * 2 + index // 2, index % 2, :HD] = q_grad[part, :, index * OWN : (index + 1) * OWN]
    order = list(range(1, CHIPS)) + [0]
    first = []
    for step in order:
        there = place.chip_at(step)
        copy = remote(mine.at[there, 1 - core], core_got.at[there], sem_q, step, place.partner)
        copy.start()
        first.append(copy)
    second = []
    for copy, step in zip(first, order):
        there = place.chip_at(step)
        copy.wait_recv()
        amount = (mine[there, core].astype(F32) + core_got[there].astype(F32)).astype(BF16)
        chip_sum[there] = amount
        if step == 0:
            head_grads[chip] = amount
        else:
            move = remote(chip_sum.at[there], head_grads.at[chip], sem_q, 7 + step, there * 2 + core)
            move.start()
            second.append(move)
    share_q = share(place, chip_sum.at[:, rows(1 - core, 96)], row_got, sem_rows, 0)
    for move in second:
        move.wait_recv()
    loads[0].wait()
    w_qkv = wat_ref[:, :, : 3 * CH].reshape(3 * D, D)
    columns = head_grads[...].reshape(3 * D, OWN)
    stream_grad, gain_grad = norm_backward(tn_narrow(w_qkv, columns), x2_ref[...], gain_n)
    lane = lax.broadcasted_iota(jnp.int32, (D, OWN), 1)
    gain_grads = jnp.where(lane == 1, gain_grad, 0.0) + jnp.where(lane == 2, ggain_b[...], 0.0)
    gx2 = gx3_ref[...] + stream_grad
    gz[:, :OWN] = gx2.astype(BF16)
    move_gz = swap(place, gz.at[:, :OWN], gz.at[:, OWN:], sem_n)
    sum_of_b.second()
    loads[1].wait()
    weights = hidden_weights(wa_ref)
    normed_grad = hidden_backward(weights, na_ref[:, :OWN], gz[:, :OWN], acts, slice(0, OWN))
    move_gz.wait_recv()
    parts[...] = hidden_backward(
        weights, na_ref[:, OWN:], gz[:, OWN:], acts, slice(OWN, 2 * OWN)
    ).astype(BF16)
    move_gn = swap(place, parts, got, sem_z)
    shares = [
        share_n,
        share(place, acts.at[:, D:], acts_got, sem_act, 1),
        share(place, gz, gz_got, sem_act, 2),
    ]
    sum_of_b.third()
    for copy in shares:
        copy.wait_recv()
    hidden_weight_grads(acts, acts_got, ((na_ref, na_got), (na_ref, na_got), (gz, gz_got)), gmlp_a)
    for part in sums_of_a:
        part.first()
    move_gn.wait_recv()
    normed_grad = normed_grad + got[...].astype(F32)
    stream_grad, gain_grad = norm_backward(normed_grad, x1_ref[...], gain_a)
    ggain_ref[...] = gain_grads + jnp.where(lane == 0, gain_grad, 0.0)
    gy1_ref[:, half(me)] = (gx2 + stream_grad).astype(BF16)
    gather_gy1 = Gather(place, gy1_ref, sem_y)
    gather_gy1.begin()
    sum_of_b.back()
    share_q.wait_recv()
    loads[2].wait()
    for index in range(CHIPS):
        q_rows[:, half(index * 2 + core)] = chip_sum[index, rows(core, 96), :]
        q_rows[:, half(index * 2 + 1 - core)] = row_got[index]
    gat[: 3 * CH] = nt(q_rows[...], n3_all[...]).astype(BF16)
    for copy in o_first:
        copy.wait_recv()
    value = gwo_ref[me].astype(F32)
    for index in range(MP - 1):
        value = value + gwo_got[index].astype(F32)
    gat[3 * CH :] = value.astype(BF16)
    t_first = []
    for step in range(1, DP):
        there = place.along_dp(step)
        copy = remote(gat.at[rows(there, 16)], gat_got.at[step - 1], sem_t, step - 1, {"dp": there})
        copy.start()
        t_first.append(copy)
    gather_gy1.relay()
    reverse_taps(taps_ref, reverse)

    def build(filter_index, slot):
        def store(block, value):
            table[slot, block * OWN : (block + 1) * OWN, :] = value

        toeplitz_down(reverse[pl.ds(filter_index, 1), :], store)

    def build_some(begin, end):
        @pl.loop(begin, end)
        def _(index):
            build(index, index)

    joint_sum[...] = jnp.zeros_like(joint_sum)

    def absorb(quarter):
        here = pl.ds(pl.multiple_of(quarter * 512, 512), 512)
        grads = gy1_ref[:, here]
        joint_sum[...] += nt(feat_ref[:, here], grads)
        feature_grad[:, here] = nn(weight_ref[: K * CH], grads).astype(BF16)

    loads[3].wait()
    loads[4].wait()
    build_some(0, 4)
    gather_gy1.joined(-1)
    absorb(place.z)
    gather_gy1.arrive(0)
    build_some(4, 8)
    gather_gy1.joined(0)
    absorb((place.z + 3) % 4)
    gather_gy1.arrive(1)
    build_some(8, K // 2)
    gather_gy1.joined(1)
    absorb((place.z + 1) % 4)
    gather_gy1.arrive(2)
    for part in sums_of_a:
        part.second()
    gather_gy1.joined(2)
    absorb((place.z + 2) % 4)
    gain_first = []
    for step in range(1, MP):
        there = place.around(step)
        copy = remote(ggain_ref.at[rows(there, CH)], gain_got.at[step - 1], sem_g, step - 1, there)
        copy.start()
        gain_first.append(copy)
    joint[:FEAT] = joint_sum[...].astype(BF16)
    joint[FEAT:] = jnp.zeros((CH, D), BF16)
    j_first = []
    for step in range(1, DP):
        there = place.along_dp(step)
        copy = remote(joint.at[rows(there, 112)], joint_got.at[step - 1], sem_j, step - 1, {"dp": there})
        copy.start()
        j_first.append(copy)
    total[...] = jnp.zeros_like(total)
    shifted[...] = jnp.zeros_like(shifted)
    joined = jnp.full((CH, T // 2), (pick == 1).astype(F32)).astype(BF16)
    middle = CH * count // 2

    def convolve(filter_index, slot):
        mine = feature_grad[pl.ds(pl.multiple_of(filter_index * CH, CH), CH), :]
        for source in range(count):
            here = slice(source * CH, (source + 1) * CH)
            begin = source * wide
            if source < count // 2:
                near_end = T // 2 - begin
                shifted[here, :near_end] = mine[:, begin : T // 2]
                shifted[here, near_end : T - begin] = mine[:, T // 2 :] * joined
            else:
                shifted[here, : T - begin] = mine[:, begin:]
        total[:middle] += nn(shifted[:middle, :], table[slot])
        total[middle:] += nn(shifted[middle:, : T // 2], table[slot, : T // 2, :])


    @pl.loop(0, K // 2)
    def _(index):
        convolve(index, index)

    for part in sums_of_a:
        part.third()
    last = []
    for copy in t_first:
        copy.wait_recv()
    value = gat[rows(dp, 16), :].astype(F32)
    for index in range(DP - 1):
        value = value + gat_got[index].astype(F32)
    sum_t[rows(dp, 16), :] = value.astype(BF16)
    done_t = sum_t.at[rows(dp, 16)]
    for step in range(1, DP):
        copy = remote(done_t, done_t, sem_tg, step - 1, {"dp": place.along_dp(step)})
        copy.start()
        last.append(copy)

    @pl.loop(K // 2, K)
    def _(index):
        build(index, index - K // 2)
        convolve(index, index - K // 2)

    for source in range(count):
        gh_ref[:, source * wide : (source + 1) * wide] = total[source * CH : (source + 1) * CH]
    for shift in range(LAGS):
        begin = (K + shift) * CH
        value = nn(weight_ref[begin : begin + CH], gy1_ref[...])
        value = jnp.where(lag_mask(shift, pick), value, 0.0)
        if shift:
            value = pltpu.roll(value, T - shift, 1)
        gh_ref[...] += value
    stream = x_ref[...].astype(F32)
    scaled = gh_ref[...] * gains_ref[:, 3:4].astype(F32)
    inner[pl.ds(me, 1)] = jnp.sum(scaled * stream, axis=0, keepdims=True)[None]
    sums = []
    for step in range(1, MP):
        copy = remote(inner.at[me], inner.at[me], sem_p, step - 1, place.around(step))
        copy.start()
        sums.append(copy)
    scaling = scale_ref[...]
    gain_grad = jnp.sum(gh_ref[...] * stream * scaling, axis=1, keepdims=True)
    for copy in gain_first:
        copy.wait_recv()
    value = ggain_ref[rows(me, CH), :]
    for index in range(MP - 1):
        value = value + gain_got[index]
    lane = lax.broadcasted_iota(jnp.int32, (CH, OWN), 1)
    gain_own[...] = value + jnp.where(lane == 3, gain_grad, 0.0)
    for step in range(1, DP):
        copy = remote(gain_own, gain_dp.at[step - 1], sem_gd, step - 1, {"dp": place.along_dp(step)})
        copy.start()
        last.append(copy)
    for copy in j_first:
        copy.wait_recv()
    value = joint[rows(dp, 112), :].astype(F32)
    for index in range(DP - 1):
        value = value + joint_got[index].astype(F32)
    joint_ref[rows(dp, 112), :] = value.astype(BF16)
    done_j = joint_ref.at[rows(dp, 112)]
    for step in range(1, DP):
        copy = remote(done_j, done_j, sem_jg, step - 1, {"dp": place.along_dp(step)})
        copy.start()
        last.append(copy)
    for part in sums_of_a:
        part.back()
    for copy in sums:
        copy.wait()
    value = inner[0]
    for index in range(1, MP):
        value = value + inner[index]
    stream_grad = scaled * scaling - stream * (scaling * scaling * scaling * value / D)
    gx_ref[...] = stream_grad + gy1_ref[rows(me, CH), :].astype(F32)
    for copy in last:
        copy.wait()
    value = gain_own[...]
    for index in range(DP - 1):
        value = value + gain_dp[index]
    gain_sum[...] = value
    for copy in first + second + [share_q] + shares + [move_gz, move_gn] + o_first + t_first + j_first + gain_first:
        copy.wait_send()
    gather_gy1.close()
    for part in sums_of_a:
        part.close()
    sum_of_b.close()


def second(*operands):
    return pl.pallas_call(
        second_kernel,
        out_shape=(
            jax.ShapeDtypeStruct((CH, T), F32),
            jax.ShapeDtypeStruct((DP * 112, D), BF16),
            jax.ShapeDtypeStruct((OWN, D), BF16),
            jax.ShapeDtypeStruct((3 * OWN, D), BF16),
            jax.ShapeDtypeStruct((3 * OWN, D), BF16),
            jax.ShapeDtypeStruct((CH, OWN), F32),
        ),
        in_specs=[SMEM, VMEM, VMEM, ANY, VMEM, VMEM, VMEM, VMEM, ANY, ANY]
        + [VMEM] * 5
        + [ANY]
        + [VMEM] * 5
        + [ANY],
        out_specs=(VMEM,) * 6,
        scratch_shapes=[
            pltpu.VMEM((FEAT, T), BF16),
            pltpu.VMEM((2, 4, 3 * OWN, D), BF16),
            pltpu.VMEM((CHIPS, 2, OWN, D), BF16),
            pltpu.VMEM((D, T), BF16),
            pltpu.VMEM((FEAT, D), BF16),
            pltpu.VMEM((HD, T), BF16),
            pltpu.VMEM((HD, T), BF16),
            pltpu.VMEM((T, 2 * HD), F32),
            pltpu.VMEM((2, HD, 512), BF16),
            pltpu.VMEM((CHIPS, 2, 3 * HD, OWN), BF16),
            pltpu.VMEM((CHIPS, 3 * HD, OWN), BF16),
            pltpu.VMEM((CHIPS, 3 * HD, OWN), BF16),
            pltpu.VMEM((CHIPS, 3 * HD, OWN), BF16),
            pltpu.VMEM((D, 2 * OWN), BF16),
            pltpu.VMEM((D, 2 * OWN), BF16),
            pltpu.VMEM((D, 2 * OWN), BF16),
            pltpu.VMEM((D, OWN), BF16),
            pltpu.VMEM((D, OWN), BF16),
            pltpu.VMEM((3, 2 * D, 2 * OWN), BF16),
            pltpu.VMEM((3, D, 2 * OWN), BF16),
            pltpu.VMEM((D, T), BF16),
            pltpu.VMEM((CHIPS, 96, OWN), BF16),
            pltpu.VMEM((96, T), BF16),
            pltpu.VMEM((MP - 1, CH, D), BF16),
            *sum_buffers(48, False),
            pltpu.VMEM((4, 3 * OWN, D), BF16),
            *sum_buffers(32, False),
            *sum_buffers(16, True),
            pltpu.VMEM((OWN, D), BF16),
            pltpu.VMEM((DP - 1, 16, D), BF16),
            pltpu.VMEM((D, OWN), F32),
            pltpu.VMEM((MP - 1, CH, OWN), F32),
            pltpu.VMEM((CH, OWN), F32),
            pltpu.VMEM((DP - 1, CH, OWN), F32),
            pltpu.VMEM((K, T + 2 * OWN), F32),
            pltpu.VMEM((K // 2, T, 2 * OWN), BF16),
            pltpu.VMEM((K * CH, T), BF16),
            pltpu.VMEM((CH * T // (2 * OWN), T), BF16),
            pltpu.VMEM((CH * T // (2 * OWN), 2 * OWN), F32),
            pltpu.VMEM((CH, T), F32),
            pltpu.VMEM((FEAT, D), F32),
            pltpu.VMEM((DP * 112, D), BF16),
            pltpu.VMEM((DP - 1, 112, D), BF16),
            pltpu.VMEM((MP, 1, T), F32),
            sems(15), sems(1), sems(1), sems(15), sems(15), sems(1), sems(14), sems(14), sems(14), sems(7), sems(7), sems(15),
            sems(7), sems(7), sems(7), sems(15), sems(3),
            pltpu.SemaphoreType.DMA((5,)),
        ],
        compiler_params=pltpu.CompilerParams(
            collective_id=1, has_side_effects=True, vmem_limit_bytes=LIMIT
        ),
        name="second",
    )(*operands)


def final_kernel(
    joint_ref, t_ref, a_ref, b_ref, gain_ref,
    gws, gate_ga, up_ga, down_ga, gqkv, gout, gate_gb, up_gb, down_gb, *gain_grads,
):
    gws[...] = joint_ref[:FEAT].astype(F32)
    gqkv[...] = t_ref[: 3 * CH].astype(F32)
    gout[...] = t_ref[3 * CH :].astype(F32)
    for ref, (gate, up, down) in ((a_ref, (gate_ga, up_ga, down_ga)), (b_ref, (gate_gb, up_gb, down_gb))):
        gate[...] = ref[:OWN].astype(F32).T
        up[...] = ref[OWN : 2 * OWN].astype(F32).T
        down[...] = ref[2 * OWN :].astype(F32)
    columns = gain_ref[...].T
    for index, grad in enumerate(gain_grads):
        grad[...] = columns[index : index + 1]


def final(*operands):
    mlp = [jax.ShapeDtypeStruct(shape, F32) for shape in ((D, OWN), (D, OWN), (OWN, D))]
    return pl.pallas_call(
        final_kernel,
        out_shape=(
            jax.ShapeDtypeStruct((FEAT, D), F32),
            *mlp,
            jax.ShapeDtypeStruct((3 * CH, D), F32),
            jax.ShapeDtypeStruct((CH, D), F32),
            *mlp,
            *[jax.ShapeDtypeStruct((1, CH), F32)] * 4,
        ),
        in_specs=[VMEM] * 5,
        out_specs=(VMEM,) * 13,
        compiler_params=pltpu.CompilerParams(vmem_limit_bytes=LIMIT),
        name="final",
    )(*operands)


def on_device(
    inputs, out_grad, shape_pick, filters, stu_gain, stu_weight,
    mlp_gain_a, gate_a, up_a, down_a, attn_gain, qkv_weight, out_weight,
    mlp_gain_b, gate_b, up_b, down_b,
):
    gains = jnp.stack([mlp_gain_a, attn_gain, mlp_gain_b, stu_gain], axis=1)
    gains = jnp.pad(gains, ((0, 0), (0, OWN - 4)))
    weight = stu_weight.reshape(FEAT, D)
    x = inputs.T
    (
        scaling, features, x1, x2, na, qkv, wa, wat, gains_all,
        lse, of, go_heads, gx3, out, n3_all, gwo, gmlp_b, ggain_b,
    ) = first(
        shape_pick, x, out_grad.T, gains, filters, weight,
        gate_a, up_a, down_a, qkv_weight.T, out_weight, gate_b, up_b, down_b,
    )
    gx, joint, gat, ga, gb, gain_sum = second(
        shape_pick, x, scaling, features, x1, x2, na, qkv, wa, wat, gains_all,
        lse, of, go_heads, gx3, n3_all, gwo, gmlp_b, ggain_b, gains, filters, weight,
    )
    gws, gate_ga, up_ga, down_ga, gqkv, gout, gate_gb, up_gb, down_gb, *gain_grads = final(joint, gat, ga, gb, gain_sum)
    gain_a, gain_n, gain_b, gain_s = (grad.reshape(CH) for grad in gain_grads)
    return (
        out.T, gx.T, gain_s, gws.reshape(K + LAGS, CH, D), gain_a, gate_ga, up_ga, down_ga,
        gain_n, gqkv.T, gout, gain_b, gate_gb, up_gb, down_gb,
    )


def solution(mesh):
    cols, mid, row = P(None, "mp"), P(None, "mp", None), P("mp", None)
    return jax.shard_map(
        on_device,
        mesh=mesh,
        in_specs=(
            P("dp", "mp"), P("dp", "mp"), P("dp"), P(), P("mp"), mid,
            P("mp"), cols, cols, row, P("mp"), cols, row, P("mp"), cols, cols, row,
        ),
        out_specs=(
            P("dp", "mp"), P("dp", "mp"), P("mp"), mid, P("mp"), cols, cols, row,
            P("mp"), cols, row, P("mp"), cols, cols, row,
        ),
        check_vma=False,
    )
```

```python
import jax
import jax.numpy as jnp
from jax import lax
from jax.experimental import pallas as pl
from jax.experimental.pallas import tpu as pltpu
from jax.sharding import PartitionSpec as P

D = 512
T = 2048
OWN = 128
CH = 32
K = 24
LAGS = 3
FEAT = (K + LAGS) * CH
HD = 64
MP = 16
DP = 8
CHIPS = 8
EPSILON = 1e-05
NEG = -1e30
F32 = jnp.float32
BF16 = jnp.bfloat16
MESH = pl.DeviceIdType.MESH
VMEM = pl.BlockSpec(memory_space=pltpu.VMEM)
SMEM = pl.BlockSpec(memory_space=pltpu.SMEM)
ANY = pl.BlockSpec(memory_space=pl.ANY)
LIMIT = 62 * 2**20
EARLY_TABLES = 4


def nn(left, right):
    return jnp.dot(left, right, preferred_element_type=F32)


def tn(left, right):
    return lax.dot_general(left, right, (((0,), (0,)), ((), ())), preferred_element_type=F32)


def tn_narrow(weights, right):
    return tn(right, weights).T


def nt(left, right):
    return lax.dot_general(left, right, (((1,), (1,)), ((), ())), preferred_element_type=F32)


class Place:
    def __init__(self):
        self.me = lax.axis_index("mp")
        self.z = self.me // 4
        self.chip = self.me // 2
        self.y = self.chip % 2
        self.core = self.me % 2
        self.dp = lax.axis_index("dp")
        self.x = self.dp % 4
        self.ylo = self.dp // 4
        self.partner = self.me + 1 - 2 * self.core
        self.beside = self.me + 2 - 4 * self.y
        self.across = self.me + 4 - 8 * (self.z % 2)
        self.query_core = ((self.z + 1) // 2) % 2
        self.quarters = (self.core, 3 - self.core)

    def around(self, step):
        return (self.me + step) % MP

    def chip_at(self, step):
        return (self.chip + step) % CHIPS

    def same_units(self, slot):
        return ((self.z + 2 * (slot // 2)) % 4) * 4 + ((self.y + slot % 2) % 2) * 2 + self.core

    def along_z(self, step):
        return ((self.z + step) % 4) * 4 + self.me % 4

    def along_x(self, step):
        return {"dp": self.dp - self.x + (self.x + step) % 4}

    def along_dp(self, step):
        return (self.dp + step) % DP


def half(index):
    return pl.ds(pl.multiple_of(index * OWN, OWN), OWN)


def rows(index, count):
    return pl.ds(pl.multiple_of(index * count, count), count)


def remote(src, dst, sems, slot, target):
    return pltpu.make_async_remote_copy(
        src_ref=src,
        dst_ref=dst,
        send_sem=sems.at[0, slot],
        recv_sem=sems.at[1, slot],
        device_id=target if isinstance(target, dict) else {"mp": target},
        device_id_type=MESH,
    )


def greet(targets):
    barrier = pltpu.get_barrier_semaphore()
    for target in targets:
        where = target if isinstance(target, dict) else {"mp": target}
        pl.semaphore_signal(barrier, inc=1, device_id=where, device_id_type=MESH)
    return lambda: pl.semaphore_wait(barrier, len(targets))


def sems(count):
    return pltpu.SemaphoreType.DMA((2, count))


def norm_forward(stream, gain):
    scaling = lax.rsqrt(jnp.sum(stream * stream, axis=0, keepdims=True) / D + EPSILON)
    return stream * scaling * gain, scaling


def norm_backward(upstream, stream, gain):
    scaling = lax.rsqrt(jnp.sum(stream * stream, axis=0, keepdims=True) / D + EPSILON)
    gain_grad = jnp.sum(upstream * stream * scaling, axis=1, keepdims=True)
    scaled = upstream * gain
    inner = jnp.sum(scaled * stream, axis=0, keepdims=True)
    return scaled * scaling - stream * (scaling * scaling * scaling * inner / D), gain_grad


def swap(place, src, dst, sem, slot=0):
    copy = remote(src, dst, sem, slot, place.across)
    copy.start()
    return copy


def share(place, src, dst, sem, slot):
    copy = remote(src, dst, sem, slot, place.partner)
    copy.start()
    return copy


def hidden_weights(ref):
    return [ref[:, :, group * OWN : (group + 1) * OWN].reshape(2 * D, D) for group in range(3)]


def hidden_backward(weights, normed, grad, acts, where):
    w_gate, w_up, w_down = weights
    gate = nn(w_gate, normed)
    up = nn(w_up, normed)
    sig = jax.nn.sigmoid(gate)
    hidden_grad = nn(w_down, grad)
    gate_grad = (hidden_grad * up * sig * (1.0 + gate * (1.0 - sig))).astype(BF16)
    up_grad = (hidden_grad * gate * sig).astype(BF16)
    acts[0, :, where] = gate_grad
    acts[1, :, where] = up_grad
    acts[2, :, where] = (gate * sig * up).astype(BF16)
    return (tn(gate_grad, w_gate) + tn(up_grad, w_up)).T


def hidden_weight_grads(acts, acts_got, inputs, out):
    for group, (right, right_got) in enumerate(inputs):
        value = (nt(acts[group, :D], right[...]) + nt(acts_got[group], right_got[...])).astype(BF16)
        for index in range(4):
            out[index, group * OWN : (group + 1) * OWN] = value[index * OWN : (index + 1) * OWN]


class Gather:
    steps = (1, 3, 2)

    def __init__(self, place, buf, sem):
        me = place.me
        own = buf.at[:, half(me)]
        beside = buf.at[:, half(place.beside)]
        self.to_beside = remote(own, own, sem, 0, place.beside)
        self.to_z = [remote(own, own, sem, step, place.along_z(step)) for step in self.steps]
        self.relays = [remote(beside, beside, sem, 3 + step, place.along_z(step)) for step in self.steps]
        self.forwards = [remote(own, own, sem, 7, place.partner), remote(beside, beside, sem, 8, place.partner)]
        for step in self.steps:
            for shift, other in ((8, me), (11, place.beside)):
                index = ((place.z + 4 - step) % 4) * 4 + other % 4
                here = buf.at[:, half(index)]
                self.forwards.append(remote(here, here, sem, shift + step, place.partner))

    def begin(self):
        for copy in [self.to_beside, *self.to_z, self.forwards[0]]:
            copy.start()

    def relay(self):
        self.to_beside.wait_recv()
        for copy in [*self.relays, self.forwards[1]]:
            copy.start()

    def arrive(self, index):
        self.to_z[index].wait_recv()
        self.forwards[2 + 2 * index].start()
        self.relays[index].wait_recv()
        self.forwards[3 + 2 * index].start()

    def joined(self, index):
        for copy in self.forwards[2 + 2 * index : 4 + 2 * index]:
            copy.wait_recv()

    def close(self):
        for copy in [self.to_beside, *self.to_z, *self.relays, *self.forwards]:
            copy.wait_send()


def toeplitz(taps):
    wide = pltpu.roll(jnp.broadcast_to(taps, (OWN, T)), 0, 1, stride=1, stride_axis=0)
    lane = lax.broadcasted_iota(jnp.int32, (OWN, OWN), 1)
    row = lax.broadcasted_iota(jnp.int32, (OWN, OWN), 0)
    first = jnp.where(lane >= row, wide[:, :OWN], 0.0)
    return jnp.concatenate([first.astype(BF16), wide[:, OWN:].astype(BF16)], axis=1)


def reverse_taps(taps_ref, reverse):
    row = lax.broadcasted_iota(jnp.int32, (2 * OWN, OWN), 0)
    lane = lax.broadcasted_iota(jnp.int32, (2 * OWN, OWN), 1)
    inside = (lane >= 1) & (row == OWN - lane)
    edge = (lane == 0) & (row == OWN)
    flip = jnp.where(inside | edge, 1.0, 0.0).astype(BF16)
    for index in range(T // OWN):
        begin = T - (index + 1) * OWN
        piece = taps_ref[:, begin : begin + min(2 * OWN, T - begin)]
        reverse[:, index * OWN : (index + 1) * OWN] = nn(piece, flip[: piece.shape[1]])
    reverse[:, T : T + OWN] = nn(taps_ref[:, :OWN], flip[OWN:])
    reverse[:, T + OWN :] = jnp.zeros((K, OWN), F32)


def toeplitz_down(reverse, store):
    wide = pltpu.roll(jnp.broadcast_to(reverse, (OWN, T + 2 * OWN)), 0, 1, stride=1, stride_axis=0).astype(BF16)
    for block in range(T // OWN):
        begin = T - block * OWN
        store(block, wide[:, begin : begin + 2 * OWN])


def lag_mask(shift, pick):
    lane = lax.broadcasted_iota(jnp.int32, (CH, T), 1)
    inner = lane % (T // 2)
    return (lane >= shift) & ((inner >= shift) | (pick == 1))


def spread(qkv_ref, keys, values):
    for index in range(MP):
        keys[:, index * OWN : (index + 1) * OWN] = qkv_ref[index, HD : 2 * HD]
        values[:, index * OWN : (index + 1) * OWN] = qkv_ref[index, 2 * HD :]


def query_block(qkv_ref, quarter):
    parts = [qkv_ref[quarter * 4 + index, :HD] for index in range(4)]
    return jnp.concatenate(parts, axis=1) * jnp.asarray(HD**-0.5, BF16)


def score_mask(quarter, chunk, pick):
    query = quarter * 512 + lax.broadcasted_iota(jnp.int32, (512, 512), 1)
    key = chunk * 512 + lax.broadcasted_iota(jnp.int32, (512, 512), 0)
    same_half = (quarter // 2) == (chunk // 2)
    return (key <= query) & (same_half | (pick == 1))


class GradientSum:
    def __init__(self, place, parts, done, bufs, sem, begin, each, y_first):
        self.place, self.parts, self.done, self.sem = place, parts, done, sem
        self.got, self.sum_1, self.got_2, self.sum_2, self.z_got = bufs
        self.begin, self.each, self.y_first = begin, each, y_first
        self.copies = []
        self.to_y = [(1 - place.ylo, {"dp": place.dp + 4 - 8 * place.ylo})]
        self.to_x = [((place.x + step) % 4, place.along_x(step)) for step in range(1, 4)]

    def at(self, index, count, begin=0):
        return pl.ds(pl.multiple_of(begin + index * count, 16), count)

    def send(self, src, dst, target):
        copy = remote(src, dst, self.sem, len(self.copies), target)
        copy.start()
        self.copies.append(copy)

    def arrived(self, count):
        for copy in self.copies[-count:]:
            copy.wait_recv()

    def first(self):
        count = self.each * (4 if self.y_first else 2)
        for slot, (there, target) in enumerate(self.to_y if self.y_first else self.to_x):
            self.send(self.parts.at[:, self.at(there, count, self.begin)], self.got.at[slot], target)

    def second(self):
        place, each = self.place, self.each
        here, peers, count = (place.ylo, 1, each * 4) if self.y_first else (place.x, 3, each * 2)
        self.arrived(peers)
        value = self.parts[:, self.at(here, count, self.begin)].astype(F32)
        for slot in range(peers):
            value = value + self.got[slot].astype(F32)
        self.sum_1[...] = value.astype(BF16)
        for slot, (there, target) in enumerate(self.to_x if self.y_first else self.to_y):
            self.send(self.sum_1.at[:, self.at(there, each)], self.got_2.at[slot], target)

    def third(self):
        place, each = self.place, self.each
        here, peers = (place.x, 3) if self.y_first else (place.ylo, 1)
        self.arrived(peers)
        value = self.sum_1[:, self.at(here, each)].astype(F32)
        for slot in range(peers):
            value = value + self.got_2[slot].astype(F32)
        self.sum_2[...] = value.astype(BF16)
        for step in range(1, 4):
            self.send(self.sum_2.at[step], self.z_got.at[step - 1], place.same_units(step))

    def back(self):
        place, each = self.place, self.each
        self.arrived(3)
        value = self.sum_2[0].astype(F32)
        for slot in range(3):
            value = value + self.z_got[slot].astype(F32)
        index = place.ylo * 4 + place.x if self.y_first else place.x * 2 + place.ylo
        mine = self.at(index, each, self.begin)
        self.done[mine, :] = value.astype(BF16)
        for step in range(1, DP):
            self.send(self.done.at[mine], self.done.at[mine], {"dp": place.along_dp(step)})

    def close(self):
        for copy in self.copies[:7]:
            copy.wait_send()
        for copy in self.copies[7:]:
            copy.wait()


def sum_buffers(each, y_first):
    first, second = (1, 3) if y_first else (3, 1)
    wide = each * (4 if y_first else 2)
    return [
        pltpu.VMEM((first, 4, wide, D), BF16),
        pltpu.VMEM((4, wide, D), BF16),
        pltpu.VMEM((second, 4, each, D), BF16),
        pltpu.VMEM((4, each, D), BF16),
        pltpu.VMEM((3, each, D), BF16),
    ]


def first_kernel(
    pick_ref, x_ref, go_ref, gains_ref, taps_ref, weight_ref,
    gate_a, up_a, down_a, qkv_w, out_w, gate_b, up_b, down_b,
    scale_ref, feat_out, x1_ref, x2_ref, na_out, qkv_out, wa_out, wat_out, gains_all,
    lse_ref, of_ref, go_heads, gx3_ref, out_ref, n3_ref, gwo_ref, gmlp_ref, ggain_ref,
    feat_ref, na_ref, qkv_ref, wa_ref, wat_ref, streams, streams_own, go2, squares, taps, table, table_late, weight_t, blocks, y_ref,
    core_got, chip_got, parts, got, heads, wb_ref, keys, values, own_heads, all_heads, x3_ref, nb, nb_got, go_got,
    acts, acts_got, parts_n, got_n, parts_z, got_z, grad_heads, out_own,
    sem_s, sem_x, sem_wa, sem_wb, sem_wat, sem_y, sem_n, sem_g, sem_z, sem_q,
    sem_o, sem_nb, sem_gn, sem_zb, sem_h, sem_out, sem_act, sem_save,
):
    place = Place()
    me, chip, core, x = place.me, place.chip, place.core, place.x
    count = T // OWN
    pick = pick_ref[0]
    wat_ref[chip, core, : 3 * CH] = qkv_w[...]
    wat_ref[chip, core, 3 * CH :] = out_w[...]
    arrived = greet(
        [place.around(step) for step in range(1, MP)] + [place.along_x(step) for step in range(1, 4)]
    )
    stream = x_ref[...].astype(F32)
    squares[pl.ds(me, 1)] = jnp.sum(stream * stream, axis=0, keepdims=True)[None]
    for ref, (gate, up, down) in ((wa_ref, (gate_a, up_a, down_a)), (wb_ref, (gate_b, up_b, down_b))):
        ref[0, 0, :OWN] = gate[...].T
        ref[0, 0, OWN : 2 * OWN] = up[...].T
        ref[0, 0, 2 * OWN :] = down[...]
    streams[0] = x_ref[...]
    streams[1] = go_ref[...]
    for index in range(MP):
        streams[2, :, index * OWN : (index + 1) * OWN] = gains_ref[...]
    streams_own[:, rows(me, CH)] = streams[:, :, half(me)]
    taps[...] = taps_ref[...].astype(F32)

    def build(step, table, shift=0):
        for index in range(2):
            filter_table = toeplitz(taps[pl.ds((step + shift) * 2 + index, 1), :])
            for offset in range(count):
                table[step, offset * OWN : (offset + 1) * OWN, index * OWN : (index + 1) * OWN] = filter_table[
                    :, offset * OWN : (offset + 1) * OWN
                ]

    build_early = lambda step: build(step, table)
    pl.loop(0, EARLY_TABLES)(build_early)
    arrived()
    sums, late, fetch_a, fetch_b, fetch_t, rest_a, rest_b, rest_t = [], [], [], [], [], [], [], []
    for step in range(1, MP):
        there = place.around(step)
        copy = remote(squares.at[me], squares.at[me], sem_s, step - 1, there)
        copy.start()
        sums.append(copy)
    for step in range(1, 4):
        copy = remote(
            wa_ref.at[0, 0, rows(x, 96)], wa_ref.at[0, step, rows(x, 96)], sem_wa, step - 1, place.same_units(step)
        )
        copy.start()
        fetch_a.append(copy)
    mine_t = wat_ref.at[chip, core, rows(x, CH)]
    for step in range(1, CHIPS):
        copy = remote(mine_t, mine_t, sem_wat, step - 1, place.chip_at(step) * 2 + core)
        copy.start()
        fetch_t.append(copy)
    for step in range(1, MP):
        there = place.around(step)
        copy = remote(
            streams.at[:, :, half(there)], streams_own.at[:, rows(me, CH)], sem_x, step - 1, there
        )
        copy.start()
        late.append(copy)
    for step in range(1, 4):
        copy = remote(
            wb_ref.at[0, 0, rows(x, 96)], wb_ref.at[0, step, rows(x, 96)], sem_wb, step - 1, place.same_units(step)
        )
        copy.start()
        fetch_b.append(copy)
    share_a = [share(place, wa_ref.at[0, 0], wa_ref.at[1, 0], sem_wa, 6)]
    share_b = [share(place, wb_ref.at[0, 0], wb_ref.at[1, 0], sem_wb, 6)]
    weight_t[...] = weight_ref[...].T
    pl.loop(EARLY_TABLES, K // 4)(build_early)
    for copy in sums:
        copy.wait()
    total = squares[0]
    for index in range(1, MP):
        total = total + squares[index]
    scaling = lax.rsqrt(total / D + EPSILON)
    scale_ref[...] = scaling
    own = stream * scaling * gains_ref[:, 3:4].astype(F32)
    h = own.astype(BF16)
    own = h.astype(F32)
    joined = jnp.full((CH, OWN), (pick == 1).astype(F32)).astype(BF16)
    for target in range(count):
        for offset in range(count):
            here = (slice(target * CH, (target + 1) * CH), slice(offset * OWN, (offset + 1) * OWN))
            if offset > target:
                blocks[here] = jnp.zeros((CH, OWN), BF16)
                continue
            source = target - offset
            value = h[:, source * OWN : (source + 1) * OWN]
            if target >= count // 2 and source < count // 2:
                value = value * joined
            blocks[here] = value
    for shift in range(LAGS):
        moved = own if shift == 0 else pltpu.roll(own, shift, 1)
        moved = jnp.where(lag_mask(shift, pick), moved, 0.0).astype(BF16)
        feat_ref[(K + shift) * CH : (K + shift + 1) * CH, :] = moved

    def convolve(step, table, shift=0):
        early = nn(blocks[: CH * count // 2, : T // 2], table[step, : T // 2, :]).astype(BF16)
        late_half = nn(blocks[CH * count // 2 :, :], table[step]).astype(BF16)
        for index in range(2):
            base = pl.multiple_of(((step + shift) * 2 + index) * CH, CH)
            for target in range(count):
                part, at = (early, target) if target < count // 2 else (late_half, target - count // 2)
                feat_ref[pl.ds(base, CH), target * OWN : (target + 1) * OWN] = part[
                    at * CH : (at + 1) * CH, index * OWN : (index + 1) * OWN
                ]


    def pass_on(fetched, source, sem, done, rest):
        for copy in fetched:
            copy.wait_recv()
        for step in range(1, 4):
            copy = remote(source, source, sem, done + step - 1, place.along_x(step))
            copy.start()
            rest.append(copy)

    @pl.loop(0, K // 4)
    def _(step):
        build(step, table_late, K // 4)
        convolve(step, table)

    pass_on(fetch_a, wa_ref.at[0, 1:4, rows(x, 96)], sem_wa, 3, rest_a)

    @pl.loop(0, K // 4)
    def _(step):
        convolve(step, table_late, K // 4)

    saves = []

    def save(src, dst):
        copy = pltpu.make_async_copy(src, dst, sem_save.at[len(saves)])
        copy.start()
        saves.append(copy)

    save(feat_ref, feat_out)
    for group in range(4):
        y = nn(weight_t[...], feat_ref[:, group * 512 : (group + 1) * 512]).astype(BF16)
        for index in range(4):
            y_ref[group * 2 + index // 2, index % 2] = y[:, index * OWN : (index + 1) * OWN]
    order = list(range(1, CHIPS)) + [0]
    first, second = [], []
    for step in order:
        there = place.chip_at(step)
        copy = remote(y_ref.at[there, 1 - core], core_got.at[there], sem_y, step, place.partner)
        copy.start()
        first.append(copy)
    for copy, step in zip(first, order):
        there = place.chip_at(step)
        copy.wait_recv()
        total = y_ref[there, core].astype(F32) + core_got[there].astype(F32)
        if step == 0:
            x1_ref[...] = total
        else:
            y_ref[there, core] = total.astype(BF16)
            move = remote(y_ref.at[there, core], chip_got.at[step - 1], sem_y, 7 + step, there * 2 + core)
            move.start()
            second.append(move)
    pass_on(fetch_t, wat_ref.at[:, core, rows(x, CH)], sem_wat, 7, rest_t)
    for copy in late:
        copy.wait()
    go2[:, :OWN] = streams_own[1]
    move_go = swap(place, go2.at[:, :OWN], go2.at[:, OWN:], sem_g)
    gains_all[...] = streams_own[2]
    for copy in rest_a:
        copy.wait_recv()
    share_a.append(share(place, wa_ref.at[0, 1:], wa_ref.at[1, 1:], sem_wa, 7))
    for move in second:
        move.wait_recv()
    x1 = x1_ref[...] + streams_own[0].astype(F32)
    for index in range(CHIPS - 1):
        x1 = x1 + chip_got[index].astype(F32)
    x1_ref[...] = x1
    normed, _ = norm_forward(x1, gains_all[:, 0:1].astype(F32))
    na_ref[:, :OWN] = normed.astype(BF16)
    move_n = swap(place, na_ref.at[:, :OWN], na_ref.at[:, OWN:], sem_n)
    for copy in share_a:
        copy.wait_recv()
    save(wa_ref, wa_out)
    w_gate, w_up, w_down = hidden_weights(wa_ref)

    def forward(normed):
        gate = nn(w_gate, normed)
        hidden = (gate * jax.nn.sigmoid(gate) * nn(w_up, normed)).astype(BF16)
        return tn_narrow(w_down, hidden)

    z = forward(na_ref[:, :OWN])
    pass_on(fetch_b, wb_ref.at[0, 1:4, rows(x, 96)], sem_wb, 3, rest_b)
    move_n.wait_recv()
    parts[...] = forward(na_ref[:, OWN:]).astype(BF16)
    move_z = swap(place, parts, got, sem_z)
    save(na_ref, na_out)
    for copy in rest_t:
        copy.wait_recv()
    half_t = wat_ref.at[:, core]
    share_t = share(place, half_t, half_t, sem_wat, 10)
    move_z.wait_recv()
    x2 = x1 + z + got[...].astype(F32)
    x2_ref[...] = x2
    n3 = norm_forward(x2, gains_all[:, 1:2].astype(F32))[0].astype(BF16)
    n3_ref[...] = n3
    share_t.wait_recv()
    save(wat_ref, wat_out)
    w_qkv = wat_ref[:, :, : 3 * CH].reshape(3 * D, D)
    heads[...] = nn(w_qkv, n3).astype(BF16).reshape(CHIPS, 3 * HD, OWN)
    sends = []
    for step in range(1, CHIPS):
        there = place.chip_at(step)
        copy = remote(heads.at[there], qkv_ref.at[me], sem_q, step - 1, there * 2 + core)
        copy.start()
        sends.append(copy)
    qkv_ref[me] = heads[chip]
    forwards = [remote(qkv_ref.at[me], qkv_ref.at[me], sem_q, 7, place.partner)]
    forwards[0].start()
    for step in range(1, CHIPS):
        source = place.chip_at(CHIPS - step) * 2 + core
        sends[step - 1].wait_recv()
        copy = remote(qkv_ref.at[source], qkv_ref.at[source], sem_q, 7 + step, place.partner)
        copy.start()
        forwards.append(copy)
    for copy in forwards:
        copy.wait()
    save(qkv_ref, qkv_out)
    for copy in rest_b:
        copy.wait_recv()
    share_b.append(share(place, wb_ref.at[0, 1:], wb_ref.at[1, 1:], sem_wb, 7))
    for copy in fetch_a + fetch_b + fetch_t + rest_a + rest_t + share_a + [share_t] + first + second + sends:
        copy.wait_send()
    move_n.wait_send()
    move_z.wait_send()
    spread(qkv_ref, keys, values)
    for part in range(2):
        quarter = place.quarters[part]
        queries = query_block(qkv_ref, quarter)
        top = jnp.full((1, 512), NEG, F32)
        norm = jnp.zeros((1, 512), F32)
        total = jnp.zeros((HD, 512), F32)
        for chunk in range(2 + 2 * part):
            here = slice(chunk * 512, (chunk + 1) * 512)
            scores = jnp.where(score_mask(quarter, chunk, pick), tn(keys[:, here], queries), NEG)
            new_top = jnp.maximum(top, jnp.max(scores, axis=0, keepdims=True))
            weights = jnp.exp(scores - new_top)
            rescale = jnp.exp(top - new_top)
            norm = norm * rescale + jnp.sum(weights, axis=0, keepdims=True)
            total = total * rescale + nn(values[:, here], weights.astype(BF16))
            top = new_top
        total = total / norm
        lse_ref[part] = top + jnp.log(norm)
        of_ref[part] = total
        for index in range(4):
            own_heads[part * 4 + index] = total[:, index * OWN : (index + 1) * OWN].astype(BF16)
    targets = [place.quarters[slot // 4] * 4 + slot % 4 for slot in range(8)]
    copies = [
        pltpu.make_async_remote_copy(
            src_ref=own_heads.at[slot], dst_ref=all_heads.at[chip],
            send_sem=sem_o.at[0, slot], recv_sem=sem_o.at[1, chip],
            device_id={"mp": targets[slot]}, device_id_type=MESH,
        )
        for slot in range(8)
    ]
    for slot in range(8):
        pl.when(targets[slot] != me)(copies[slot].start)

        @pl.when(targets[slot] == me)
        def _():
            all_heads[chip] = own_heads[slot]

    arrivals = [
        remote(own_heads.at[0], all_heads.at[head], sem_o, head, place.partner) for head in range(CHIPS)
    ]
    for head in range(CHIPS):
        pl.when(head * 2 + place.query_core != me)(arrivals[head].wait_recv)
    w_out = wat_ref[:, :, 3 * CH :].reshape(D, D)
    outputs = all_heads[...].reshape(D, OWN)
    x3 = x2 + tn_narrow(w_out, outputs)
    x3_ref[...] = x3
    gain_b = gains_all[:, 2:3].astype(F32)
    nb[:, :OWN] = norm_forward(x3, gain_b)[0].astype(BF16)
    move_n = swap(place, nb.at[:, :OWN], nb.at[:, OWN:], sem_nb)
    for copy in share_b + [move_go]:
        copy.wait_recv()
    weights = hidden_weights(wb_ref)
    normed_grad = hidden_backward(weights, nb[:, :OWN], go2[:, :OWN], acts, slice(0, OWN))
    move_n.wait_recv()
    parts_n[...] = hidden_backward(
        weights, nb[:, OWN:], go2[:, OWN:], acts, slice(OWN, 2 * OWN)
    ).astype(BF16)
    move_gn = swap(place, parts_n, got_n, sem_gn)
    shares = [
        share(place, acts.at[:, D:], acts_got, sem_act, 0),
        share(place, nb, nb_got, sem_act, 1),
        share(place, go2, go_got, sem_act, 2),
    ]
    parts_z[...] = tn_narrow(weights[2], acts[2, :, OWN:]).astype(BF16)
    move_z = swap(place, parts_z, got_z, sem_zb)
    z = tn_narrow(weights[2], acts[2, :, :OWN])
    move_gn.wait_recv()
    normed_grad = normed_grad + got_n[...].astype(F32)
    stream_grad, gain_grad = norm_backward(normed_grad, x3_ref[...], gain_b)
    ggain_ref[...] = gain_grad
    gx3 = go2[:, :OWN].astype(F32) + stream_grad
    gx3_ref[...] = gx3
    gy = gx3.astype(BF16)
    grad_heads[...] = nn(w_out, gy).astype(BF16).reshape(CHIPS, HD, OWN)
    slot = (place.z // 2) * 4 + me % 4
    sends = [
        pltpu.make_async_remote_copy(
            src_ref=grad_heads.at[head], dst_ref=go_heads.at[slot],
            send_sem=sem_h.at[0, head], recv_sem=sem_h.at[1, slot],
            device_id={"mp": head * 2 + place.query_core}, device_id_type=MESH,
        )
        for head in range(CHIPS)
    ]
    for head in range(CHIPS):
        pl.when(head * 2 + place.query_core != me)(sends[head].start)

        @pl.when(head * 2 + place.query_core == me)
        def _():
            go_heads[slot] = grad_heads[head]

    move_z.wait_recv()
    out_own[...] = (x3_ref[...] + z + got_z[...].astype(F32)).astype(BF16)
    moves = []
    for step in range(1, MP):
        there = place.around(step)
        copy = remote(out_own.at[rows(there, CH)], out_ref.at[:, half(me)], sem_out, step - 1, there)
        copy.start()
        moves.append(copy)
    out_ref[:, half(me)] = out_own[rows(me, CH), :]
    gwo_ref[...] = nt(outputs, gy).astype(BF16).reshape(MP, CH, D)
    for copy in shares:
        copy.wait_recv()
    hidden_weight_grads(acts, acts_got, ((nb, nb_got), (nb, nb_got), (go2, go_got)), gmlp_ref)
    for slot_in in range(8):
        arrival = remote(grad_heads.at[0], go_heads.at[slot_in], sem_h, slot_in, place.partner)
        pl.when(targets[slot_in] != me)(arrival.wait_recv)
    for slot_out in range(8):
        pl.when(targets[slot_out] != me)(copies[slot_out].wait_send)
        pl.when(slot_out * 2 + place.query_core != me)(sends[slot_out].wait_send)
    for copy in moves:
        copy.wait()
    for copy in rest_b + share_b + shares + [move_go, move_n, move_gn, move_z]:
        copy.wait_send()
    for copy in saves:
        copy.wait()


def first(*operands):
    return pl.pallas_call(
        first_kernel,
        out_shape=(
            jax.ShapeDtypeStruct((1, T), F32),
            jax.ShapeDtypeStruct((FEAT, T), BF16),
            jax.ShapeDtypeStruct((D, OWN), F32),
            jax.ShapeDtypeStruct((D, OWN), F32),
            jax.ShapeDtypeStruct((D, 2 * OWN), BF16),
            jax.ShapeDtypeStruct((MP, 3 * HD, OWN), BF16),
            jax.ShapeDtypeStruct((2, 4, 3 * OWN, D), BF16),
            jax.ShapeDtypeStruct((CHIPS, 2, OWN, D), BF16),
            jax.ShapeDtypeStruct((D, OWN), BF16),
            jax.ShapeDtypeStruct((2, 1, 512), F32),
            jax.ShapeDtypeStruct((2, HD, 512), F32),
            jax.ShapeDtypeStruct((8, HD, OWN), BF16),
            jax.ShapeDtypeStruct((D, OWN), F32),
            jax.ShapeDtypeStruct((CH, T), BF16),
            jax.ShapeDtypeStruct((D, OWN), BF16),
            jax.ShapeDtypeStruct((MP, CH, D), BF16),
            jax.ShapeDtypeStruct((4, 3 * OWN, D), BF16),
            jax.ShapeDtypeStruct((D, 1), F32),
        ),
        in_specs=[SMEM] + [VMEM] * 13,
        out_specs=(VMEM, ANY, VMEM, VMEM, ANY, ANY, ANY, ANY) + (VMEM,) * 10,
        scratch_shapes=[
            pltpu.VMEM((FEAT, T), BF16),
            pltpu.VMEM((D, 2 * OWN), BF16),
            pltpu.VMEM((MP, 3 * HD, OWN), BF16),
            pltpu.VMEM((2, 4, 3 * OWN, D), BF16),
            pltpu.VMEM((CHIPS, 2, OWN, D), BF16),
            pltpu.VMEM((3, CH, T), BF16),
            pltpu.VMEM((3, D, OWN), BF16),
            pltpu.VMEM((D, 2 * OWN), BF16),
            pltpu.VMEM((MP, 1, T), F32),
            pltpu.VMEM((K, T), F32),
            pltpu.VMEM((K // 4, T, 2 * OWN), BF16),
            pltpu.VMEM((K // 4, T, 2 * OWN), BF16),
            pltpu.VMEM((D, FEAT), BF16),
            pltpu.VMEM((CH * T // OWN, T), BF16),
            pltpu.VMEM((CHIPS, 2, D, OWN), BF16),
            pltpu.VMEM((CHIPS, D, OWN), BF16),
            pltpu.VMEM((CHIPS - 1, D, OWN), BF16),
            pltpu.VMEM((D, OWN), BF16),
            pltpu.VMEM((D, OWN), BF16),
            pltpu.VMEM((CHIPS, 3 * HD, OWN), BF16),
            pltpu.VMEM((2, 4, 3 * OWN, D), BF16),
            pltpu.VMEM((HD, T), BF16),
            pltpu.VMEM((HD, T), BF16),
            pltpu.VMEM((8, HD, OWN), BF16),
            pltpu.VMEM((8, HD, OWN), BF16),
            pltpu.VMEM((D, OWN), F32),
            pltpu.VMEM((D, 2 * OWN), BF16),
            pltpu.VMEM((D, 2 * OWN), BF16),
            pltpu.VMEM((D, 2 * OWN), BF16),
            pltpu.VMEM((3, 2 * D, 2 * OWN), BF16),
            pltpu.VMEM((3, D, 2 * OWN), BF16),
            pltpu.VMEM((D, OWN), BF16),
            pltpu.VMEM((D, OWN), BF16),
            pltpu.VMEM((D, OWN), BF16),
            pltpu.VMEM((D, OWN), BF16),
            pltpu.VMEM((CHIPS, HD, OWN), BF16),
            pltpu.VMEM((D, OWN), BF16),
            sems(15), sems(15), sems(8), sems(8), sems(11),
            sems(15), sems(1), sems(1), sems(1), sems(15),
            sems(8), sems(1), sems(1), sems(1), sems(8), sems(15), sems(3),
            pltpu.SemaphoreType.DMA((5,)),
        ],
        compiler_params=pltpu.CompilerParams(
            collective_id=0, has_side_effects=True, vmem_limit_bytes=LIMIT
        ),
        name="first",
    )(*operands)


def second_kernel(
    pick_ref, x_ref, scale_ref, feat_in, x1_ref, x2_ref, na_ref, qkv_ref, wa_in, wat_in, gains_all,
    lse_ref, of_ref, go_heads, gx3_ref, n3_ref, gwo_ref, gmlp_b, ggain_b, gains_ref, taps_ref, weight_in,
    gx_ref, joint_ref, sum_t, sum_a, sum_b, gain_sum,
    feat_ref, wa_ref, wat_ref, n3_all, weight_ref,
    keys, values, kv_grad, q_grad, mine, core_got, chip_sum, head_grads, gz, gz_got, na_got, parts, got,
    acts, acts_got, gy1_ref, row_got, q_rows, gwo_got,
    b_1, b_2, b_3, b_4, b_5, gmlp_a, a_1, a_2, a_3, a_4, a_5, a_6, a_7, a_8, a_9, a_10, gat, gat_got, ggain_ref, gain_own, gain_dp,
    reverse, table, feature_grad, shifted, total, gh_ref, joint_sum, joint, joint_got, inner,
    sem_q, sem_n, sem_z, sem_y, sem_gwo, sem_rows, sem_b, sem_a, sem_a2, sem_t, sem_tg, sem_gd, sem_j, sem_jg, sem_p, sem_act, sem_all, sem_load,
):
    place = Place()
    me, dp, chip, core = place.me, place.dp, place.chip, place.core
    wide = 2 * OWN
    count = T // wide
    n3_all[:, half(me)] = n3_ref[...]
    loads = []
    for src, dst in (
        (wat_in, wat_ref), (wa_in, wa_ref), (feat_in, feat_ref), (weight_in, weight_ref)
    ):
        copy = pltpu.make_async_copy(src, dst, sem_load.at[len(loads)])
        copy.start()
        loads.append(copy)
    arrived = greet(
        [place.around(step) for step in range(1, MP)]
        + [{"dp": place.along_dp(step)} for step in range(1, DP)]
    )
    gain_a = gains_all[:, 0:1].astype(F32)
    gain_n = gains_all[:, 1:2].astype(F32)
    sum_of_b = GradientSum(place, gmlp_b, sum_b, (b_1, b_2, b_3, b_4, b_5), sem_b, 0, 48, False)
    sums_of_a = (
        GradientSum(place, gmlp_a, sum_a, (a_1, a_2, a_3, a_4, a_5), sem_a, 0, 32, False),
        GradientSum(place, gmlp_a, sum_a, (a_6, a_7, a_8, a_9, a_10), sem_a2, 256, 16, True),
    )
    pick = pick_ref[0]
    spread(qkv_ref, keys, values)
    for part in range(2):
        quarter = place.quarters[part]
        queries = query_block(qkv_ref, quarter)
        out_grad = jnp.concatenate([go_heads[part * 4 + index] for index in range(4)], axis=1)
        weighted = jnp.sum(of_ref[part] * out_grad.astype(F32), axis=0, keepdims=True)
        queries_t = queries.T
        out_grad_t = out_grad.T
        query_grad = jnp.zeros((HD, 512), F32)
        for chunk in range(2 + 2 * part):
            here = slice(chunk * 512, (chunk + 1) * 512)
            scores = tn(keys[:, here], queries) - lse_ref[part]
            probs = jnp.where(score_mask(quarter, chunk, pick), jnp.exp(scores), 0.0)
            score_grad = (probs * (tn(values[:, here], out_grad) - weighted)).astype(BF16)
            query_grad = query_grad + nn(keys[:, here], score_grad)
            key_part = nn(score_grad, queries_t)
            value_part = nn(probs.astype(BF16), out_grad_t)
            both = jnp.concatenate([key_part, value_part], axis=1)
            if part == 1 and chunk < 2:
                both = both + kv_grad[here]
            kv_grad[here] = both
        q_grad[part] = (query_grad * HD**-0.5).astype(BF16)
        if part == 0:
            arrived()
            gather_n3 = Gather(place, n3_all, sem_all)
            gather_n3.begin()
            share_n = share(place, na_ref, na_got, sem_act, 0)
            sum_of_b.first()
            o_first = []
            for step in range(1, MP):
                there = place.around(step)
                copy = remote(gwo_ref.at[there], gwo_got.at[step - 1], sem_gwo, step - 1, there)
                copy.start()
                o_first.append(copy)
    for index in range(MP):
        mine[index // 2, index % 2, :HD] = jnp.zeros((HD, OWN), BF16)
        mine[index // 2, index % 2, HD:] = kv_grad[index * OWN : (index + 1) * OWN].T.astype(BF16)
    for part in range(2):
        quarter = place.quarters[part]
        for index in range(4):
            mine[quarter * 2 + index // 2, index % 2, :HD] = q_grad[part, :, index * OWN : (index + 1) * OWN]
    order = list(range(1, CHIPS)) + [0]
    first = []
    for step in order:
        there = place.chip_at(step)
        copy = remote(mine.at[there, 1 - core], core_got.at[there], sem_q, step, place.partner)
        copy.start()
        first.append(copy)
    second = []
    for copy, step in zip(first, order):
        there = place.chip_at(step)
        copy.wait_recv()
        amount = (mine[there, core].astype(F32) + core_got[there].astype(F32)).astype(BF16)
        chip_sum[there] = amount
        if step == 0:
            head_grads[chip] = amount
        else:
            move = remote(chip_sum.at[there], head_grads.at[chip], sem_q, 7 + step, there * 2 + core)
            move.start()
            second.append(move)
    share_q = share(place, chip_sum.at[:, rows(1 - core, 96)], row_got, sem_rows, 0)
    for move in second:
        move.wait_recv()
    loads[0].wait()
    w_qkv = wat_ref[:, :, : 3 * CH].reshape(3 * D, D)
    columns = head_grads[...].reshape(3 * D, OWN)
    stream_grad, gain_grad = norm_backward(tn_narrow(w_qkv, columns), x2_ref[...], gain_n)
    lane = lax.broadcasted_iota(jnp.int32, (D, OWN), 1)
    gain_grads = jnp.where(lane == 1, gain_grad, 0.0) + jnp.where(lane == 2, ggain_b[...], 0.0)
    gx2 = gx3_ref[...] + stream_grad
    gz[:, :OWN] = gx2.astype(BF16)
    move_gz = swap(place, gz.at[:, :OWN], gz.at[:, OWN:], sem_n)
    sum_of_b.second()
    loads[1].wait()
    weights = hidden_weights(wa_ref)
    normed_grad = hidden_backward(weights, na_ref[:, :OWN], gz[:, :OWN], acts, slice(0, OWN))
    move_gz.wait_recv()
    parts[...] = hidden_backward(
        weights, na_ref[:, OWN:], gz[:, OWN:], acts, slice(OWN, 2 * OWN)
    ).astype(BF16)
    move_gn = swap(place, parts, got, sem_z)
    shares = [
        share_n,
        share(place, acts.at[:, D:], acts_got, sem_act, 1),
        share(place, gz, gz_got, sem_act, 2),
    ]
    sum_of_b.third()
    gather_n3.relay()
    for copy in shares:
        copy.wait_recv()
    hidden_weight_grads(acts, acts_got, ((na_ref, na_got), (na_ref, na_got), (gz, gz_got)), gmlp_a)
    for part in sums_of_a:
        part.first()
    move_gn.wait_recv()
    normed_grad = normed_grad + got[...].astype(F32)
    stream_grad, gain_grad = norm_backward(normed_grad, x1_ref[...], gain_a)
    ggain_ref[...] = gain_grads + jnp.where(lane == 0, gain_grad, 0.0)
    gy1_ref[:, half(me)] = (gx2 + stream_grad).astype(BF16)
    gather_gy1 = Gather(place, gy1_ref, sem_y)
    gather_gy1.begin()
    sum_of_b.back()
    for index in range(3):
        gather_n3.arrive(index)
    share_q.wait_recv()
    for index in range(-1, 3):
        gather_n3.joined(index)
    for index in range(CHIPS):
        q_rows[:, half(index * 2 + core)] = chip_sum[index, rows(core, 96), :]
        q_rows[:, half(index * 2 + 1 - core)] = row_got[index]
    gat[: 3 * CH] = nt(q_rows[...], n3_all[...]).astype(BF16)
    for copy in o_first:
        copy.wait_recv()
    value = gwo_ref[me].astype(F32)
    for index in range(MP - 1):
        value = value + gwo_got[index].astype(F32)
    gat[3 * CH :] = value.astype(BF16)
    t_first = []
    for step in range(1, DP):
        there = place.along_dp(step)
        copy = remote(gat.at[rows(there, 16)], gat_got.at[step - 1], sem_t, step - 1, {"dp": there})
        copy.start()
        t_first.append(copy)
    gather_gy1.relay()
    reverse_taps(taps_ref, reverse)

    def build(filter_index, slot):
        def store(block, value):
            table[slot, block * OWN : (block + 1) * OWN, :] = value

        toeplitz_down(reverse[pl.ds(filter_index, 1), :], store)

    def build_some(begin, end):
        @pl.loop(begin, end)
        def _(index):
            build(index, index)

    joint_sum[...] = jnp.zeros_like(joint_sum)

    def absorb(quarter):
        here = pl.ds(pl.multiple_of(quarter * 512, 512), 512)
        grads = gy1_ref[:, here]
        joint_sum[...] += nt(feat_ref[:, here], grads)
        feature_grad[:, here] = nn(weight_ref[: K * CH], grads).astype(BF16)

    loads[2].wait()
    loads[3].wait()
    build_some(0, 4)
    gather_gy1.joined(-1)
    absorb(place.z)
    gather_gy1.arrive(0)
    build_some(4, 8)
    gather_gy1.joined(0)
    absorb((place.z + 3) % 4)
    gather_gy1.arrive(1)
    build_some(8, K // 2)
    gather_gy1.joined(1)
    absorb((place.z + 1) % 4)
    gather_gy1.arrive(2)
    for part in sums_of_a:
        part.second()
    gather_gy1.joined(2)
    absorb((place.z + 2) % 4)
    joint[:FEAT] = joint_sum[...].astype(BF16)
    joint[FEAT:] = jnp.zeros((CH, D), BF16)
    j_first = []
    for step in range(1, DP):
        there = place.along_dp(step)
        copy = remote(joint.at[rows(there, 112)], joint_got.at[step - 1], sem_j, step - 1, {"dp": there})
        copy.start()
        j_first.append(copy)
    total[...] = jnp.zeros_like(total)
    shifted[...] = jnp.zeros_like(shifted)
    joined = jnp.full((CH, T // 2), (pick == 1).astype(F32)).astype(BF16)
    middle = CH * count // 2

    def convolve(filter_index, slot):
        mine = feature_grad[pl.ds(pl.multiple_of(filter_index * CH, CH), CH), :]
        for source in range(count):
            here = slice(source * CH, (source + 1) * CH)
            begin = source * wide
            if source < count // 2:
                near_end = T // 2 - begin
                shifted[here, :near_end] = mine[:, begin : T // 2]
                shifted[here, near_end : T - begin] = mine[:, T // 2 :] * joined
            else:
                shifted[here, : T - begin] = mine[:, begin:]
        total[:middle] += nn(shifted[:middle, :], table[slot])
        total[middle:] += nn(shifted[middle:, : T // 2], table[slot, : T // 2, :])


    @pl.loop(0, K // 2)
    def _(index):
        convolve(index, index)

    for part in sums_of_a:
        part.third()
    last = []
    for copy in t_first:
        copy.wait_recv()
    value = gat[rows(dp, 16), :].astype(F32)
    for index in range(DP - 1):
        value = value + gat_got[index].astype(F32)
    sum_t[rows(dp, 16), :] = value.astype(BF16)
    done_t = sum_t.at[rows(dp, 16)]
    for step in range(1, DP):
        copy = remote(done_t, done_t, sem_tg, step - 1, {"dp": place.along_dp(step)})
        copy.start()
        last.append(copy)

    @pl.loop(K // 2, K)
    def _(index):
        build(index, index - K // 2)
        convolve(index, index - K // 2)

    for source in range(count):
        gh_ref[:, source * wide : (source + 1) * wide] = total[source * CH : (source + 1) * CH]
    for shift in range(LAGS):
        begin = (K + shift) * CH
        value = nn(weight_ref[begin : begin + CH], gy1_ref[...])
        value = jnp.where(lag_mask(shift, pick), value, 0.0)
        if shift:
            value = pltpu.roll(value, T - shift, 1)
        gh_ref[...] += value
    stream = x_ref[...].astype(F32)
    scaled = gh_ref[...] * gains_ref[:, 3:4].astype(F32)
    partial = jnp.sum(scaled * stream, axis=0, keepdims=True)
    for index in range(4):
        inner[me, index : index + 1] = partial[:, index * 512 : (index + 1) * 512]
    inner[me, 4:] = ggain_ref[...].T[:4]
    sums = []
    for step in range(1, MP):
        copy = remote(inner.at[me], inner.at[me], sem_p, step - 1, place.around(step))
        copy.start()
        sums.append(copy)
    scaling = scale_ref[...]
    gain_grad = jnp.sum(gh_ref[...] * stream * scaling, axis=1, keepdims=True)
    gain_grad = jnp.concatenate(
        [jnp.broadcast_to(gain_grad, (CH, OWN)), jnp.zeros((OWN - CH, OWN), F32)], axis=0
    ).T
    for copy in j_first:
        copy.wait_recv()
    value = joint[rows(dp, 112), :].astype(F32)
    for index in range(DP - 1):
        value = value + joint_got[index].astype(F32)
    joint_ref[rows(dp, 112), :] = value.astype(BF16)
    done_j = joint_ref.at[rows(dp, 112)]
    for step in range(1, DP):
        copy = remote(done_j, done_j, sem_jg, step - 1, {"dp": place.along_dp(step)})
        copy.start()
        last.append(copy)
    for part in sums_of_a:
        part.back()
    for copy in sums:
        copy.wait()
    value = inner[0]
    for index in range(1, MP):
        value = value + inner[index]
    gain_own[...] = pltpu.roll(value, (D - CH * me) % D, 1)[:, :OWN]
    gain_own[7:] = gain_grad[:1]
    for step in range(1, DP):
        copy = remote(gain_own, gain_dp.at[step - 1], sem_gd, step - 1, {"dp": place.along_dp(step)})
        copy.start()
        last.append(copy)
    value = jnp.concatenate([value[index : index + 1] for index in range(4)], axis=1)
    stream_grad = scaled * scaling - stream * (scaling * scaling * scaling * value / D)
    gx_ref[...] = stream_grad + gy1_ref[rows(me, CH), :].astype(F32)
    for copy in last:
        copy.wait()
    value = gain_own[...]
    for index in range(DP - 1):
        value = value + gain_dp[index]
    gain_sum[...] = value
    for copy in first + second + [share_q] + shares + [move_gz, move_gn] + o_first + t_first + j_first:
        copy.wait_send()
    gather_n3.close()
    gather_gy1.close()
    for part in sums_of_a:
        part.close()
    sum_of_b.close()


def second(*operands):
    return pl.pallas_call(
        second_kernel,
        out_shape=(
            jax.ShapeDtypeStruct((CH, T), F32),
            jax.ShapeDtypeStruct((DP * 112, D), BF16),
            jax.ShapeDtypeStruct((OWN, D), BF16),
            jax.ShapeDtypeStruct((3 * OWN, D), BF16),
            jax.ShapeDtypeStruct((3 * OWN, D), BF16),
            jax.ShapeDtypeStruct((8, OWN), F32),
        ),
        in_specs=[SMEM, VMEM, VMEM, ANY, VMEM, VMEM, VMEM, VMEM, ANY, ANY] + [VMEM] * 11 + [ANY],
        out_specs=(VMEM,) * 6,
        scratch_shapes=[
            pltpu.VMEM((FEAT, T), BF16),
            pltpu.VMEM((2, 4, 3 * OWN, D), BF16),
            pltpu.VMEM((CHIPS, 2, OWN, D), BF16),
            pltpu.VMEM((D, T), BF16),
            pltpu.VMEM((FEAT, D), BF16),
            pltpu.VMEM((HD, T), BF16),
            pltpu.VMEM((HD, T), BF16),
            pltpu.VMEM((T, 2 * HD), F32),
            pltpu.VMEM((2, HD, 512), BF16),
            pltpu.VMEM((CHIPS, 2, 3 * HD, OWN), BF16),
            pltpu.VMEM((CHIPS, 3 * HD, OWN), BF16),
            pltpu.VMEM((CHIPS, 3 * HD, OWN), BF16),
            pltpu.VMEM((CHIPS, 3 * HD, OWN), BF16),
            pltpu.VMEM((D, 2 * OWN), BF16),
            pltpu.VMEM((D, 2 * OWN), BF16),
            pltpu.VMEM((D, 2 * OWN), BF16),
            pltpu.VMEM((D, OWN), BF16),
            pltpu.VMEM((D, OWN), BF16),
            pltpu.VMEM((3, 2 * D, 2 * OWN), BF16),
            pltpu.VMEM((3, D, 2 * OWN), BF16),
            pltpu.VMEM((D, T), BF16),
            pltpu.VMEM((CHIPS, 96, OWN), BF16),
            pltpu.VMEM((96, T), BF16),
            pltpu.VMEM((MP - 1, CH, D), BF16),
            *sum_buffers(48, False),
            pltpu.VMEM((4, 3 * OWN, D), BF16),
            *sum_buffers(32, False),
            *sum_buffers(16, True),
            pltpu.VMEM((OWN, D), BF16),
            pltpu.VMEM((DP - 1, 16, D), BF16),
            pltpu.VMEM((D, OWN), F32),
            pltpu.VMEM((8, OWN), F32),
            pltpu.VMEM((DP - 1, 8, OWN), F32),
            pltpu.VMEM((K, T + 2 * OWN), F32),
            pltpu.VMEM((K // 2, T, 2 * OWN), BF16),
            pltpu.VMEM((K * CH, T), BF16),
            pltpu.VMEM((CH * T // (2 * OWN), T), BF16),
            pltpu.VMEM((CH * T // (2 * OWN), 2 * OWN), F32),
            pltpu.VMEM((CH, T), F32),
            pltpu.VMEM((FEAT, D), F32),
            pltpu.VMEM((DP * 112, D), BF16),
            pltpu.VMEM((DP - 1, 112, D), BF16),
            pltpu.VMEM((MP, 8, D), F32),
            sems(15), sems(1), sems(1), sems(15), sems(15), sems(1), sems(14), sems(14), sems(14), sems(7), sems(7),
            sems(7), sems(7), sems(7), sems(15), sems(3), sems(15),
            pltpu.SemaphoreType.DMA((4,)),
        ],
        compiler_params=pltpu.CompilerParams(
            collective_id=1, has_side_effects=True, vmem_limit_bytes=LIMIT
        ),
        name="second",
    )(*operands)


def final_kernel(
    joint_ref, t_ref, a_ref, b_ref, gain_ref, out_in, gx_in,
    out_ref, gx_ref, gws, gate_ga, up_ga, down_ga, gqkv, gout, gate_gb, up_gb, down_gb, *gain_grads,
):
    out_ref[...] = out_in[...]
    gx_ref[...] = gx_in[...]
    gws[...] = joint_ref[:FEAT].astype(F32)
    gqkv[...] = t_ref[: 3 * CH].astype(F32)
    gout[...] = t_ref[3 * CH :].astype(F32)
    for ref, (gate, up, down) in ((a_ref, (gate_ga, up_ga, down_ga)), (b_ref, (gate_gb, up_gb, down_gb))):
        gate[...] = ref[:OWN].astype(F32).T
        up[...] = ref[OWN : 2 * OWN].astype(F32).T
        down[...] = ref[2 * OWN :].astype(F32)
    for index, grad in enumerate(gain_grads):
        grad[...] = gain_ref[4 + index : 5 + index, :CH]


def final(*operands):
    mlp = [jax.ShapeDtypeStruct(shape, F32) for shape in ((D, OWN), (D, OWN), (OWN, D))]
    return pl.pallas_call(
        final_kernel,
        out_shape=(
            jax.ShapeDtypeStruct((CH, T), BF16),
            jax.ShapeDtypeStruct((CH, T), F32),
            jax.ShapeDtypeStruct((FEAT, D), F32),
            *mlp,
            jax.ShapeDtypeStruct((3 * CH, D), F32),
            jax.ShapeDtypeStruct((CH, D), F32),
            *mlp,
            *[jax.ShapeDtypeStruct((1, CH), F32)] * 4,
        ),
        in_specs=[VMEM] * 7,
        out_specs=(VMEM,) * 15,
        compiler_params=pltpu.CompilerParams(vmem_limit_bytes=LIMIT),
        name="final",
    )(*operands)


def on_device(
    inputs, out_grad, shape_pick, filters, stu_gain, stu_weight,
    mlp_gain_a, gate_a, up_a, down_a, attn_gain, qkv_weight, out_weight,
    mlp_gain_b, gate_b, up_b, down_b,
):
    gains = jnp.stack([mlp_gain_a, attn_gain, mlp_gain_b, stu_gain], axis=1)
    gains = jnp.pad(gains, ((0, 0), (0, OWN - 4)))
    weight = stu_weight.reshape(FEAT, D)
    x = inputs.T
    (
        scaling, features, x1, x2, na, qkv, wa, wat, gains_all,
        lse, of, go_heads, gx3, out, n3, gwo, gmlp_b, ggain_b,
    ) = first(
        shape_pick, x, out_grad.T, gains, filters, weight,
        gate_a, up_a, down_a, qkv_weight.T, out_weight, gate_b, up_b, down_b,
    )
    gx, joint, gat, ga, gb, gain_sum = second(
        shape_pick, x, scaling, features, x1, x2, na, qkv, wa, wat, gains_all,
        lse, of, go_heads, gx3, n3, gwo, gmlp_b, ggain_b, gains, filters, weight,
    )
    out, gx, gws, gate_ga, up_ga, down_ga, gqkv, gout, gate_gb, up_gb, down_gb, *gain_grads = final(
        joint, gat, ga, gb, gain_sum, out, gx
    )
    gain_a, gain_n, gain_b, gain_s = (grad.reshape(CH) for grad in gain_grads)
    return (
        out.T, gx.T, gain_s, gws.reshape(K + LAGS, CH, D), gain_a, gate_ga, up_ga, down_ga,
        gain_n, gqkv.T, gout, gain_b, gate_gb, up_gb, down_gb,
    )


def solution(mesh):
    cols, mid, row = P(None, "mp"), P(None, "mp", None), P("mp", None)
    return jax.shard_map(
        on_device,
        mesh=mesh,
        in_specs=(
            P("dp", "mp"), P("dp", "mp"), P("dp"), P(), P("mp"), mid,
            P("mp"), cols, cols, row, P("mp"), cols, row, P("mp"), cols, cols, row,
        ),
        out_specs=(
            P("dp", "mp"), P("dp", "mp"), P("mp"), mid, P("mp"), cols, cols, row,
            P("mp"), cols, row, P("mp"), cols, cols, row,
        ),
        check_vma=False,
    )
```

```python
import jax
import jax.numpy as jnp
from jax import lax
from jax.experimental import pallas as pl
from jax.experimental.pallas import tpu as pltpu
from jax.sharding import PartitionSpec as P

D = 512
T = 2048
OWN = 128
CH = 32
K = 24
LAGS = 3
FEAT = (K + LAGS) * CH
HD = 64
MP = 16
DP = 8
CHIPS = 8
EPSILON = 1e-05
NEG = -1e30
F32 = jnp.float32
BF16 = jnp.bfloat16
MESH = pl.DeviceIdType.MESH
VMEM = pl.BlockSpec(memory_space=pltpu.VMEM)
SMEM = pl.BlockSpec(memory_space=pltpu.SMEM)
ANY = pl.BlockSpec(memory_space=pl.ANY)
LIMIT = 62 * 2**20
EARLY_TABLES = 4


def nn(left, right):
    return jnp.dot(left, right, preferred_element_type=F32)


def tn(left, right):
    return lax.dot_general(left, right, (((0,), (0,)), ((), ())), preferred_element_type=F32)


def tn_narrow(weights, right):
    return tn(right, weights).T


def nt(left, right):
    return lax.dot_general(left, right, (((1,), (1,)), ((), ())), preferred_element_type=F32)


class Place:
    def __init__(self):
        self.me = lax.axis_index("mp")
        self.z = self.me // 4
        self.chip = self.me // 2
        self.y = self.chip % 2
        self.core = self.me % 2
        self.dp = lax.axis_index("dp")
        self.x = self.dp % 4
        self.ylo = self.dp // 4
        self.partner = self.me + 1 - 2 * self.core
        self.beside = self.me + 2 - 4 * self.y
        self.across = self.me + 4 - 8 * (self.z % 2)
        self.query_core = ((self.z + 1) // 2) % 2
        self.quarters = (self.core, 3 - self.core)

    def around(self, step):
        return (self.me + step) % MP

    def chip_at(self, step):
        return (self.chip + step) % CHIPS

    def same_units(self, slot):
        return ((self.z + 2 * (slot // 2)) % 4) * 4 + ((self.y + slot % 2) % 2) * 2 + self.core

    def along_z(self, step):
        return ((self.z + step) % 4) * 4 + self.me % 4

    def along_x(self, step):
        return {"dp": self.dp - self.x + (self.x + step) % 4}

    def along_dp(self, step):
        return (self.dp + step) % DP


def half(index):
    return pl.ds(pl.multiple_of(index * OWN, OWN), OWN)


def rows(index, count):
    return pl.ds(pl.multiple_of(index * count, count), count)


def remote(src, dst, sems, slot, target):
    return pltpu.make_async_remote_copy(
        src_ref=src,
        dst_ref=dst,
        send_sem=sems.at[0, slot],
        recv_sem=sems.at[1, slot],
        device_id=target if isinstance(target, dict) else {"mp": target},
        device_id_type=MESH,
    )


def greet(targets):
    barrier = pltpu.get_barrier_semaphore()
    for target in targets:
        where = target if isinstance(target, dict) else {"mp": target}
        pl.semaphore_signal(barrier, inc=1, device_id=where, device_id_type=MESH)
    return lambda: pl.semaphore_wait(barrier, len(targets))


def sems(count):
    return pltpu.SemaphoreType.DMA((2, count))


def norm_forward(stream, gain):
    scaling = lax.rsqrt(jnp.sum(stream * stream, axis=0, keepdims=True) / D + EPSILON)
    return stream * scaling * gain, scaling


def norm_backward(upstream, stream, gain):
    scaling = lax.rsqrt(jnp.sum(stream * stream, axis=0, keepdims=True) / D + EPSILON)
    gain_grad = jnp.sum(upstream * stream * scaling, axis=1, keepdims=True)
    scaled = upstream * gain
    inner = jnp.sum(scaled * stream, axis=0, keepdims=True)
    return scaled * scaling - stream * (scaling * scaling * scaling * inner / D), gain_grad


def swap(place, src, dst, sem, slot=0):
    copy = remote(src, dst, sem, slot, place.across)
    copy.start()
    return copy


def share(place, src, dst, sem, slot):
    copy = remote(src, dst, sem, slot, place.partner)
    copy.start()
    return copy


def hidden_weights(ref):
    return [ref[:, :, group * OWN : (group + 1) * OWN].reshape(2 * D, D) for group in range(3)]


def hidden_backward(weights, normed, grad, acts, where):
    w_gate, w_up, w_down = weights
    gate = nn(w_gate, normed)
    up = nn(w_up, normed)
    sig = jax.nn.sigmoid(gate)
    hidden_grad = nn(w_down, grad)
    gate_grad = (hidden_grad * up * sig * (1.0 + gate * (1.0 - sig))).astype(BF16)
    up_grad = (hidden_grad * gate * sig).astype(BF16)
    acts[0, :, where] = gate_grad
    acts[1, :, where] = up_grad
    acts[2, :, where] = (gate * sig * up).astype(BF16)
    return (tn(gate_grad, w_gate) + tn(up_grad, w_up)).T


def hidden_weight_grads(acts, acts_got, inputs, out):
    for group, (right, right_got) in enumerate(inputs):
        value = (nt(acts[group, :D], right[...]) + nt(acts_got[group], right_got[...])).astype(BF16)
        for index in range(4):
            out[index, group * OWN : (group + 1) * OWN] = value[index * OWN : (index + 1) * OWN]


class Gather:
    steps = (1, 3, 2)

    def __init__(self, place, buf, sem):
        me = place.me
        own = buf.at[:, half(me)]
        beside = buf.at[:, half(place.beside)]
        self.to_beside = remote(own, own, sem, 0, place.beside)
        self.to_z = [remote(own, own, sem, step, place.along_z(step)) for step in self.steps]
        farthest = buf.at[:, half(((place.z + 2) % 4) * 4 + me % 4)]
        self.relays = [remote(beside, beside, sem, 3 + step, place.along_z(step)) for step in self.steps[:2]]
        self.relays.append(remote(farthest, farthest, sem, 5, place.beside))
        self.forwards = [remote(own, own, sem, 7, place.partner), remote(beside, beside, sem, 8, place.partner)]
        for step in self.steps:
            for shift, other in ((8, me), (11, place.beside)):
                index = ((place.z + 4 - step) % 4) * 4 + other % 4
                here = buf.at[:, half(index)]
                self.forwards.append(remote(here, here, sem, shift + step, place.partner))

    def begin(self):
        for copy in [self.to_beside, *self.to_z, self.forwards[0]]:
            copy.start()

    def relay(self):
        self.to_beside.wait_recv()
        for copy in [*self.relays[:2], self.forwards[1]]:
            copy.start()

    def cross(self):
        self.to_z[2].wait_recv()
        self.relays[2].start()
        self.forwards[6].start()

    def arrive(self, index):
        if index < 2:
            self.to_z[index].wait_recv()
            self.forwards[2 + 2 * index].start()
        self.relays[index].wait_recv()
        self.forwards[3 + 2 * index].start()

    def joined(self, index):
        for copy in self.forwards[2 + 2 * index : 4 + 2 * index]:
            copy.wait_recv()

    def close(self):
        for copy in [self.to_beside, *self.to_z, *self.relays, *self.forwards]:
            copy.wait_send()


def toeplitz(taps):
    wide = pltpu.roll(jnp.broadcast_to(taps, (OWN, T)), 0, 1, stride=1, stride_axis=0)
    lane = lax.broadcasted_iota(jnp.int32, (OWN, OWN), 1)
    row = lax.broadcasted_iota(jnp.int32, (OWN, OWN), 0)
    first = jnp.where(lane >= row, wide[:, :OWN], 0.0)
    return jnp.concatenate([first.astype(BF16), wide[:, OWN:].astype(BF16)], axis=1)


def reverse_taps(taps_ref, reverse):
    row = lax.broadcasted_iota(jnp.int32, (2 * OWN, OWN), 0)
    lane = lax.broadcasted_iota(jnp.int32, (2 * OWN, OWN), 1)
    inside = (lane >= 1) & (row == OWN - lane)
    edge = (lane == 0) & (row == OWN)
    flip = jnp.where(inside | edge, 1.0, 0.0).astype(BF16)
    for index in range(T // OWN):
        begin = T - (index + 1) * OWN
        piece = taps_ref[:, begin : begin + min(2 * OWN, T - begin)]
        reverse[:, index * OWN : (index + 1) * OWN] = nn(piece, flip[: piece.shape[1]])
    reverse[:, T : T + OWN] = nn(taps_ref[:, :OWN], flip[OWN:])
    reverse[:, T + OWN :] = jnp.zeros((K, OWN), F32)


def toeplitz_down(reverse, store):
    wide = pltpu.roll(jnp.broadcast_to(reverse, (OWN, T + 2 * OWN)), 0, 1, stride=1, stride_axis=0).astype(BF16)
    for block in range(T // OWN):
        begin = T - block * OWN
        store(block, wide[:, begin : begin + 2 * OWN])


def lag_mask(shift, pick):
    lane = lax.broadcasted_iota(jnp.int32, (CH, T), 1)
    inner = lane % (T // 2)
    return (lane >= shift) & ((inner >= shift) | (pick == 1))


def spread(qkv_ref, keys, values):
    for index in range(MP):
        keys[:, index * OWN : (index + 1) * OWN] = qkv_ref[index, HD : 2 * HD]
        values[:, index * OWN : (index + 1) * OWN] = qkv_ref[index, 2 * HD :]


def query_block(qkv_ref, quarter):
    parts = [qkv_ref[quarter * 4 + index, :HD] for index in range(4)]
    return jnp.concatenate(parts, axis=1) * jnp.asarray(HD**-0.5, BF16)


def score_mask(quarter, chunk, pick):
    query = quarter * 512 + lax.broadcasted_iota(jnp.int32, (512, 512), 1)
    key = chunk * 512 + lax.broadcasted_iota(jnp.int32, (512, 512), 0)
    same_half = (quarter // 2) == (chunk // 2)
    return (key <= query) & (same_half | (pick == 1))


class GradientSum:
    def __init__(self, place, parts, done, bufs, sem, begin, each, y_first, source=None):
        self.place, self.parts, self.done, self.sem = place, parts, done, sem
        self.source = parts if source is None else source
        self.got, self.sum_1, self.got_2, self.sum_2, self.z_got = bufs
        self.begin, self.each, self.y_first = begin, each, y_first
        self.copies = []
        self.to_y = [(1 - place.ylo, {"dp": place.dp + 4 - 8 * place.ylo})]
        self.to_x = [((place.x + step) % 4, place.along_x(step)) for step in range(1, 4)]

    def at(self, index, count, begin=0):
        return pl.ds(pl.multiple_of(begin + index * count, 16), count)

    def send(self, src, dst, target):
        copy = remote(src, dst, self.sem, len(self.copies), target)
        copy.start()
        self.copies.append(copy)

    def arrived(self, count):
        for copy in self.copies[-count:]:
            copy.wait_recv()

    def first(self):
        count = self.each * (4 if self.y_first else 2)
        for slot, (there, target) in enumerate(self.to_y if self.y_first else self.to_x):
            self.send(self.source.at[:, self.at(there, count, self.begin)], self.got.at[slot], target)

    def second(self):
        place, each = self.place, self.each
        here, peers, count = (place.ylo, 1, each * 4) if self.y_first else (place.x, 3, each * 2)
        self.arrived(peers)
        value = self.parts[:, self.at(here, count, self.begin)].astype(F32)
        for slot in range(peers):
            value = value + self.got[slot].astype(F32)
        self.sum_1[...] = value.astype(BF16)
        for slot, (there, target) in enumerate(self.to_x if self.y_first else self.to_y):
            self.send(self.sum_1.at[:, self.at(there, each)], self.got_2.at[slot], target)

    def third(self):
        place, each = self.place, self.each
        here, peers = (place.x, 3) if self.y_first else (place.ylo, 1)
        self.arrived(peers)
        value = self.sum_1[:, self.at(here, each)].astype(F32)
        for slot in range(peers):
            value = value + self.got_2[slot].astype(F32)
        self.sum_2[...] = value.astype(BF16)
        for step in range(1, 4):
            self.send(self.sum_2.at[step], self.z_got.at[step - 1], place.same_units(step))

    def back(self):
        place, each = self.place, self.each
        self.arrived(3)
        value = self.sum_2[0].astype(F32)
        for slot in range(3):
            value = value + self.z_got[slot].astype(F32)
        index = place.ylo * 4 + place.x if self.y_first else place.x * 2 + place.ylo
        mine = self.at(index, each, self.begin)
        self.done[mine, :] = value.astype(BF16)
        for _, target in self.to_x:
            self.send(self.done.at[mine], self.done.at[mine], target)

    def back_y(self):
        place, each = self.place, self.each
        self.arrived(3)
        for x in range(4):
            index = place.ylo * 4 + x if self.y_first else x * 2 + place.ylo
            part = self.done.at[self.at(index, each, self.begin)]
            self.send(part, part, self.to_y[0][1])

    def close(self):
        self.arrived(4)
        for copy in self.copies:
            copy.wait_send()


def sum_buffers(each, y_first):
    first, second = (1, 3) if y_first else (3, 1)
    wide = each * (4 if y_first else 2)
    return [
        pltpu.VMEM((first, 4, wide, D), BF16),
        pltpu.VMEM((4, wide, D), BF16),
        pltpu.VMEM((second, 4, each, D), BF16),
        pltpu.VMEM((4, each, D), BF16),
        pltpu.VMEM((3, each, D), BF16),
    ]


def first_kernel(
    pick_ref, x_ref, go_ref, gain_a, gain_n, gain_b_in, gain_s, taps_ref, weight_ref,
    gate_a, up_a, down_a, qkv_w, out_w, gate_b, up_b, down_b,
    gains_ref, scale_ref, feat_out, x1_ref, x2_ref, na_out, qkv_out, wa_out, wat_out, gains_all,
    lse_ref, of_ref, go_heads, gx3_ref, out_ref, n3_ref, gwo_ref, gmlp_ref, ggain_ref,
    feat_ref, na_ref, qkv_ref, wa_ref, wat_ref, streams, streams_own, go2, squares, taps, table, table_late, weight_t, blocks, y_ref,
    core_got, chip_got, parts, got, heads, wb_ref, keys, values, own_heads, all_heads, x3_ref, nb, nb_got, go_got,
    acts, acts_got, parts_n, got_n, parts_z, got_z, grad_heads, out_own,
    sem_s, sem_x, sem_wa, sem_wb, sem_wat, sem_y, sem_n, sem_g, sem_z, sem_q,
    sem_o, sem_nb, sem_gn, sem_zb, sem_h, sem_out, sem_act, sem_save,
):
    place = Place()
    me, chip, core, x = place.me, place.chip, place.core, place.x
    count = T // OWN
    pick = pick_ref[0]
    wat_ref[chip, core, : 3 * CH] = qkv_w[...]
    wat_ref[chip, core, 3 * CH :] = out_w[...]
    arrived = greet(
        [place.around(step) for step in range(1, MP)] + [place.along_x(step) for step in range(1, 4)]
    )
    stream = x_ref[...].astype(F32)
    squares[pl.ds(me, 1)] = jnp.sum(stream * stream, axis=0, keepdims=True)[None]
    for ref, (gate, up, down) in ((wa_ref, (gate_a, up_a, down_a)), (wb_ref, (gate_b, up_b, down_b))):
        ref[0, 0, :OWN] = gate[...].T
        ref[0, 0, OWN : 2 * OWN] = up[...].T
        ref[0, 0, 2 * OWN :] = down[...]
    lines = [ref[...].astype(F32) for ref in (gain_a, gain_n, gain_b_in, gain_s)]
    lines = jnp.concatenate(lines + [jnp.zeros((OWN - 4, CH), F32)], axis=0)
    lines = jnp.concatenate([lines, jnp.zeros((OWN, OWN - CH), F32)], axis=1)
    gains_ref[...] = lines.T[:CH].astype(BF16)
    streams[0] = x_ref[...]
    streams[1] = go_ref[...]
    for index in range(MP):
        streams[2, :, index * OWN : (index + 1) * OWN] = gains_ref[...]
    streams_own[:, rows(me, CH)] = streams[:, :, half(me)]
    taps[...] = taps_ref[...].astype(F32)

    def build(step, table, shift=0):
        for index in range(2):
            filter_table = toeplitz(taps[pl.ds((step + shift) * 2 + index, 1), :])
            for offset in range(count):
                table[step, offset * OWN : (offset + 1) * OWN, index * OWN : (index + 1) * OWN] = filter_table[
                    :, offset * OWN : (offset + 1) * OWN
                ]

    build_early = lambda step: build(step, table)
    pl.loop(0, EARLY_TABLES)(build_early)
    arrived()
    sums, late, fetch_a, fetch_b, fetch_t, rest_a, rest_b, rest_t = [], [], [], [], [], [], [], []
    for step in range(1, MP):
        there = place.around(step)
        copy = remote(squares.at[me], squares.at[me], sem_s, step - 1, there)
        copy.start()
        sums.append(copy)
    for step in range(1, 4):
        copy = remote(
            wa_ref.at[0, 0, rows(x, 96)], wa_ref.at[0, step, rows(x, 96)], sem_wa, step - 1, place.same_units(step)
        )
        copy.start()
        fetch_a.append(copy)
    mine_t = wat_ref.at[chip, core, rows(x, CH)]
    for step in range(1, CHIPS):
        copy = remote(mine_t, mine_t, sem_wat, step - 1, place.chip_at(step) * 2 + core)
        copy.start()
        fetch_t.append(copy)
    for step in range(1, MP):
        there = place.around(step)
        copy = remote(
            streams.at[:, :, half(there)], streams_own.at[:, rows(me, CH)], sem_x, step - 1, there
        )
        copy.start()
        late.append(copy)
    for step in range(1, 4):
        copy = remote(
            wb_ref.at[0, 0, rows(x, 96)], wb_ref.at[0, step, rows(x, 96)], sem_wb, step - 1, place.same_units(step)
        )
        copy.start()
        fetch_b.append(copy)
    share_a = [share(place, wa_ref.at[0, 0], wa_ref.at[1, 0], sem_wa, 6)]
    share_b = [share(place, wb_ref.at[0, 0], wb_ref.at[1, 0], sem_wb, 6)]
    weight_t[...] = weight_ref[...].T
    pl.loop(EARLY_TABLES, K // 4)(build_early)
    for copy in sums:
        copy.wait()
    total = squares[0]
    for index in range(1, MP):
        total = total + squares[index]
    scaling = lax.rsqrt(total / D + EPSILON)
    scale_ref[...] = scaling
    own = stream * scaling * gains_ref[:, 3:4].astype(F32)
    h = own.astype(BF16)
    own = h.astype(F32)
    joined = jnp.full((CH, OWN), (pick == 1).astype(F32)).astype(BF16)
    for target in range(count):
        for offset in range(count):
            here = (slice(target * CH, (target + 1) * CH), slice(offset * OWN, (offset + 1) * OWN))
            if offset > target:
                blocks[here] = jnp.zeros((CH, OWN), BF16)
                continue
            source = target - offset
            value = h[:, source * OWN : (source + 1) * OWN]
            if target >= count // 2 and source < count // 2:
                value = value * joined
            blocks[here] = value
    for shift in range(LAGS):
        moved = own if shift == 0 else pltpu.roll(own, shift, 1)
        moved = jnp.where(lag_mask(shift, pick), moved, 0.0).astype(BF16)
        feat_ref[(K + shift) * CH : (K + shift + 1) * CH, :] = moved

    def convolve(step, table, shift=0):
        early = nn(blocks[: CH * count // 2, : T // 2], table[step, : T // 2, :]).astype(BF16)
        late_half = nn(blocks[CH * count // 2 :, :], table[step]).astype(BF16)
        for index in range(2):
            base = pl.multiple_of(((step + shift) * 2 + index) * CH, CH)
            for target in range(count):
                part, at = (early, target) if target < count // 2 else (late_half, target - count // 2)
                feat_ref[pl.ds(base, CH), target * OWN : (target + 1) * OWN] = part[
                    at * CH : (at + 1) * CH, index * OWN : (index + 1) * OWN
                ]


    def pass_on(fetched, source, sem, done, rest):
        for copy in fetched:
            copy.wait_recv()
        for step in range(1, 4):
            copy = remote(source, source, sem, done + step - 1, place.along_x(step))
            copy.start()
            rest.append(copy)

    @pl.loop(0, K // 4)
    def _(step):
        build(step, table_late, K // 4)
        convolve(step, table)

    pass_on(fetch_a, wa_ref.at[0, 1:4, rows(x, 96)], sem_wa, 3, rest_a)

    @pl.loop(0, K // 4)
    def _(step):
        convolve(step, table_late, K // 4)

    saves = []

    def save(src, dst):
        copy = pltpu.make_async_copy(src, dst, sem_save.at[len(saves)])
        copy.start()
        saves.append(copy)

    save(feat_ref, feat_out)
    for group in range(4):
        y = nn(weight_t[...], feat_ref[:, group * 512 : (group + 1) * 512]).astype(BF16)
        for index in range(4):
            y_ref[group * 2 + index // 2, index % 2] = y[:, index * OWN : (index + 1) * OWN]
    order = list(range(1, CHIPS)) + [0]
    first, second = [], []
    for step in order:
        there = place.chip_at(step)
        copy = remote(y_ref.at[there, 1 - core], core_got.at[there], sem_y, step, place.partner)
        copy.start()
        first.append(copy)
    for copy, step in zip(first, order):
        there = place.chip_at(step)
        copy.wait_recv()
        total = y_ref[there, core].astype(F32) + core_got[there].astype(F32)
        if step == 0:
            x1_ref[...] = total
        else:
            y_ref[there, core] = total.astype(BF16)
            move = remote(y_ref.at[there, core], chip_got.at[step - 1], sem_y, 7 + step, there * 2 + core)
            move.start()
            second.append(move)
    pass_on(fetch_t, wat_ref.at[:, core, rows(x, CH)], sem_wat, 7, rest_t)
    for copy in late:
        copy.wait()
    go2[:, :OWN] = streams_own[1]
    move_go = swap(place, go2.at[:, :OWN], go2.at[:, OWN:], sem_g)
    gains_all[...] = streams_own[2]
    for copy in rest_a:
        copy.wait_recv()
    share_a.append(share(place, wa_ref.at[0, 1:], wa_ref.at[1, 1:], sem_wa, 7))
    for move in second:
        move.wait_recv()
    x1 = x1_ref[...] + streams_own[0].astype(F32)
    for index in range(CHIPS - 1):
        x1 = x1 + chip_got[index].astype(F32)
    x1_ref[...] = x1
    normed, _ = norm_forward(x1, gains_all[:, 0:1].astype(F32))
    na_ref[:, :OWN] = normed.astype(BF16)
    move_n = swap(place, na_ref.at[:, :OWN], na_ref.at[:, OWN:], sem_n)
    for copy in share_a:
        copy.wait_recv()
    save(wa_ref, wa_out)
    w_gate, w_up, w_down = hidden_weights(wa_ref)

    def forward(normed):
        gate = nn(w_gate, normed)
        hidden = (gate * jax.nn.sigmoid(gate) * nn(w_up, normed)).astype(BF16)
        return tn_narrow(w_down, hidden)

    z = forward(na_ref[:, :OWN])
    pass_on(fetch_b, wb_ref.at[0, 1:4, rows(x, 96)], sem_wb, 3, rest_b)
    move_n.wait_recv()
    parts[...] = forward(na_ref[:, OWN:]).astype(BF16)
    move_z = swap(place, parts, got, sem_z)
    save(na_ref, na_out)
    for copy in rest_t:
        copy.wait_recv()
    half_t = wat_ref.at[:, core]
    share_t = share(place, half_t, half_t, sem_wat, 10)
    move_z.wait_recv()
    x2 = x1 + z + got[...].astype(F32)
    x2_ref[...] = x2
    n3 = norm_forward(x2, gains_all[:, 1:2].astype(F32))[0].astype(BF16)
    n3_ref[...] = n3
    share_t.wait_recv()
    save(wat_ref, wat_out)
    w_qkv = wat_ref[:, :, : 3 * CH].reshape(3 * D, D)
    heads[...] = nn(w_qkv, n3).astype(BF16).reshape(CHIPS, 3 * HD, OWN)
    sends = []
    for step in range(1, CHIPS):
        there = place.chip_at(step)
        copy = remote(heads.at[there], qkv_ref.at[me], sem_q, step - 1, there * 2 + core)
        copy.start()
        sends.append(copy)
    qkv_ref[me] = heads[chip]
    forwards = [remote(qkv_ref.at[me], qkv_ref.at[me], sem_q, 7, place.partner)]
    forwards[0].start()
    for step in range(1, CHIPS):
        source = place.chip_at(CHIPS - step) * 2 + core
        sends[step - 1].wait_recv()
        copy = remote(qkv_ref.at[source], qkv_ref.at[source], sem_q, 7 + step, place.partner)
        copy.start()
        forwards.append(copy)
    for copy in forwards:
        copy.wait()
    save(qkv_ref, qkv_out)
    for copy in rest_b:
        copy.wait_recv()
    share_b.append(share(place, wb_ref.at[0, 1:], wb_ref.at[1, 1:], sem_wb, 7))
    for copy in fetch_a + fetch_b + fetch_t + rest_a + rest_t + share_a + [share_t] + first + second + sends:
        copy.wait_send()
    move_n.wait_send()
    move_z.wait_send()
    spread(qkv_ref, keys, values)
    targets = [place.quarters[slot // 4] * 4 + slot % 4 for slot in range(8)]
    copies = [
        pltpu.make_async_remote_copy(
            src_ref=own_heads.at[slot], dst_ref=all_heads.at[chip],
            send_sem=sem_o.at[0, slot], recv_sem=sem_o.at[1, chip],
            device_id={"mp": targets[slot]}, device_id_type=MESH,
        )
        for slot in range(8)
    ]
    for part in range(2):
        quarter = place.quarters[part]
        queries = query_block(qkv_ref, quarter)
        top = jnp.full((1, 512), NEG, F32)
        norm = jnp.zeros((1, 512), F32)
        total = jnp.zeros((HD, 512), F32)
        for chunk in range(2 + 2 * part):
            here = slice(chunk * 512, (chunk + 1) * 512)
            scores = jnp.where(score_mask(quarter, chunk, pick), tn(keys[:, here], queries), NEG)
            new_top = jnp.maximum(top, jnp.max(scores, axis=0, keepdims=True))
            weights = jnp.exp(scores - new_top)
            rescale = jnp.exp(top - new_top)
            norm = norm * rescale + jnp.sum(weights, axis=0, keepdims=True)
            total = total * rescale + nn(values[:, here], weights.astype(BF16))
            top = new_top
        total = total / norm
        lse_ref[part] = top + jnp.log(norm)
        of_ref[part] = total
        for index in range(4):
            own_heads[part * 4 + index] = total[:, index * OWN : (index + 1) * OWN].astype(BF16)
        for slot in range(part * 4, part * 4 + 4):
            pl.when(targets[slot] != me)(copies[slot].start)

            @pl.when(targets[slot] == me)
            def _():
                all_heads[chip] = own_heads[slot]
    arrivals = [
        remote(own_heads.at[0], all_heads.at[head], sem_o, head, place.partner) for head in range(CHIPS)
    ]
    for head in range(CHIPS):
        pl.when(head * 2 + place.query_core != me)(arrivals[head].wait_recv)
    w_out = wat_ref[:, :, 3 * CH :].reshape(D, D)
    outputs = all_heads[...].reshape(D, OWN)
    x3 = x2 + tn_narrow(w_out, outputs)
    x3_ref[...] = x3
    gain_b = gains_all[:, 2:3].astype(F32)
    nb[:, :OWN] = norm_forward(x3, gain_b)[0].astype(BF16)
    move_n = swap(place, nb.at[:, :OWN], nb.at[:, OWN:], sem_nb)
    for copy in share_b + [move_go]:
        copy.wait_recv()
    weights = hidden_weights(wb_ref)
    normed_grad = hidden_backward(weights, nb[:, :OWN], go2[:, :OWN], acts, slice(0, OWN))
    move_n.wait_recv()
    parts_n[...] = hidden_backward(
        weights, nb[:, OWN:], go2[:, OWN:], acts, slice(OWN, 2 * OWN)
    ).astype(BF16)
    move_gn = swap(place, parts_n, got_n, sem_gn)
    shares = [
        share(place, acts.at[:, D:], acts_got, sem_act, 0),
        share(place, nb, nb_got, sem_act, 1),
        share(place, go2, go_got, sem_act, 2),
    ]
    parts_z[...] = tn_narrow(weights[2], acts[2, :, OWN:]).astype(BF16)
    move_z = swap(place, parts_z, got_z, sem_zb)
    z = tn_narrow(weights[2], acts[2, :, :OWN])
    move_gn.wait_recv()
    normed_grad = normed_grad + got_n[...].astype(F32)
    stream_grad, gain_grad = norm_backward(normed_grad, x3_ref[...], gain_b)
    ggain_ref[...] = gain_grad
    gx3 = go2[:, :OWN].astype(F32) + stream_grad
    gx3_ref[...] = gx3
    gy = gx3.astype(BF16)
    grad_heads[...] = nn(w_out, gy).astype(BF16).reshape(CHIPS, HD, OWN)
    slot = (place.z // 2) * 4 + me % 4
    sends = [
        pltpu.make_async_remote_copy(
            src_ref=grad_heads.at[head], dst_ref=go_heads.at[slot],
            send_sem=sem_h.at[0, head], recv_sem=sem_h.at[1, slot],
            device_id={"mp": head * 2 + place.query_core}, device_id_type=MESH,
        )
        for head in range(CHIPS)
    ]
    for head in range(CHIPS):
        pl.when(head * 2 + place.query_core != me)(sends[head].start)

        @pl.when(head * 2 + place.query_core == me)
        def _():
            go_heads[slot] = grad_heads[head]

    move_z.wait_recv()
    out_own[...] = (x3_ref[...] + z + got_z[...].astype(F32)).astype(BF16)
    moves = []
    for step in range(1, MP):
        there = place.around(step)
        copy = remote(out_own.at[rows(there, CH)], out_ref.at[:, half(me)], sem_out, step - 1, there)
        copy.start()
        moves.append(copy)
    out_ref[:, half(me)] = out_own[rows(me, CH), :]
    gwo_ref[...] = nt(outputs, gy).astype(BF16).reshape(MP, CH, D)
    for copy in shares:
        copy.wait_recv()
    hidden_weight_grads(acts, acts_got, ((nb, nb_got), (nb, nb_got), (go2, go_got)), gmlp_ref)
    for slot_in in range(8):
        arrival = remote(grad_heads.at[0], go_heads.at[slot_in], sem_h, slot_in, place.partner)
        pl.when(targets[slot_in] != me)(arrival.wait_recv)
    for slot_out in range(8):
        pl.when(targets[slot_out] != me)(copies[slot_out].wait_send)
        pl.when(slot_out * 2 + place.query_core != me)(sends[slot_out].wait_send)
    for copy in moves:
        copy.wait()
    for copy in rest_b + share_b + shares + [move_go, move_n, move_gn, move_z]:
        copy.wait_send()
    for copy in saves:
        copy.wait()


def first(*operands):
    return pl.pallas_call(
        first_kernel,
        out_shape=(
            jax.ShapeDtypeStruct((CH, OWN), BF16),
            jax.ShapeDtypeStruct((1, T), F32),
            jax.ShapeDtypeStruct((FEAT, T), BF16),
            jax.ShapeDtypeStruct((D, OWN), F32),
            jax.ShapeDtypeStruct((D, OWN), F32),
            jax.ShapeDtypeStruct((D, 2 * OWN), BF16),
            jax.ShapeDtypeStruct((MP, 3 * HD, OWN), BF16),
            jax.ShapeDtypeStruct((2, 4, 3 * OWN, D), BF16),
            jax.ShapeDtypeStruct((CHIPS, 2, OWN, D), BF16),
            jax.ShapeDtypeStruct((D, OWN), BF16),
            jax.ShapeDtypeStruct((2, 1, 512), F32),
            jax.ShapeDtypeStruct((2, HD, 512), F32),
            jax.ShapeDtypeStruct((8, HD, OWN), BF16),
            jax.ShapeDtypeStruct((D, OWN), F32),
            jax.ShapeDtypeStruct((CH, T), BF16),
            jax.ShapeDtypeStruct((D, OWN), BF16),
            jax.ShapeDtypeStruct((MP, CH, D), BF16),
            jax.ShapeDtypeStruct((4, 3 * OWN, D), BF16),
            jax.ShapeDtypeStruct((D, 1), F32),
        ),
        in_specs=[SMEM] + [VMEM] * 16,
        out_specs=(VMEM, VMEM, ANY, VMEM, VMEM, ANY, ANY, ANY, ANY) + (VMEM,) * 10,
        scratch_shapes=[
            pltpu.VMEM((FEAT, T), BF16),
            pltpu.VMEM((D, 2 * OWN), BF16),
            pltpu.VMEM((MP, 3 * HD, OWN), BF16),
            pltpu.VMEM((2, 4, 3 * OWN, D), BF16),
            pltpu.VMEM((CHIPS, 2, OWN, D), BF16),
            pltpu.VMEM((3, CH, T), BF16),
            pltpu.VMEM((3, D, OWN), BF16),
            pltpu.VMEM((D, 2 * OWN), BF16),
            pltpu.VMEM((MP, 1, T), F32),
            pltpu.VMEM((K, T), F32),
            pltpu.VMEM((K // 4, T, 2 * OWN), BF16),
            pltpu.VMEM((K // 4, T, 2 * OWN), BF16),
            pltpu.VMEM((D, FEAT), BF16),
            pltpu.VMEM((CH * T // OWN, T), BF16),
            pltpu.VMEM((CHIPS, 2, D, OWN), BF16),
            pltpu.VMEM((CHIPS, D, OWN), BF16),
            pltpu.VMEM((CHIPS - 1, D, OWN), BF16),
            pltpu.VMEM((D, OWN), BF16),
            pltpu.VMEM((D, OWN), BF16),
            pltpu.VMEM((CHIPS, 3 * HD, OWN), BF16),
            pltpu.VMEM((2, 4, 3 * OWN, D), BF16),
            pltpu.VMEM((HD, T), BF16),
            pltpu.VMEM((HD, T), BF16),
            pltpu.VMEM((8, HD, OWN), BF16),
            pltpu.VMEM((8, HD, OWN), BF16),
            pltpu.VMEM((D, OWN), F32),
            pltpu.VMEM((D, 2 * OWN), BF16),
            pltpu.VMEM((D, 2 * OWN), BF16),
            pltpu.VMEM((D, 2 * OWN), BF16),
            pltpu.VMEM((3, 2 * D, 2 * OWN), BF16),
            pltpu.VMEM((3, D, 2 * OWN), BF16),
            pltpu.VMEM((D, OWN), BF16),
            pltpu.VMEM((D, OWN), BF16),
            pltpu.VMEM((D, OWN), BF16),
            pltpu.VMEM((D, OWN), BF16),
            pltpu.VMEM((CHIPS, HD, OWN), BF16),
            pltpu.VMEM((D, OWN), BF16),
            sems(15), sems(15), sems(8), sems(8), sems(11),
            sems(15), sems(1), sems(1), sems(1), sems(15),
            sems(8), sems(1), sems(1), sems(1), sems(8), sems(15), sems(3),
            pltpu.SemaphoreType.DMA((5,)),
        ],
        compiler_params=pltpu.CompilerParams(
            collective_id=0, has_side_effects=True, vmem_limit_bytes=LIMIT
        ),
        name="first",
    )(*operands)


def second_kernel(
    pick_ref, x_ref, scale_ref, feat_in, x1_ref, x2_ref, na_ref, qkv_ref, wa_in, wat_in, gains_all,
    lse_ref, of_ref, go_heads, gx3_ref, n3_ref, gwo_in, gmlp_in, ggain_b, gains_ref, taps_ref, weight_in,
    gx_ref, joint_ref, sum_t, sum_a, sum_b, gain_sum,
    feat_ref, wa_ref, wat_ref, n3_all, weight_ref, gmlp_b, gwo_own,
    keys, values, kv_grad, q_grad, mine, core_got, chip_sum, head_grads, gz, gz_got, na_got, parts, got,
    acts, acts_got, gy1_ref, row_got, q_rows, gwo_got,
    b_1, b_2, b_3, b_4, b_5, gmlp_a, a_1, a_2, a_3, a_4, a_5, a_6, a_7, a_8, a_9, a_10, gat, gat_got, ggain_ref, gain_own, gain_dp,
    reverse, table, feature_grad, shifted, total, gh_ref, joint_sum, joint, joint_got, inner,
    sem_q, sem_n, sem_z, sem_y, sem_gwo, sem_rows, sem_b, sem_a, sem_a2, sem_t, sem_tg, sem_gd, sem_j, sem_jg, sem_p, sem_act, sem_all, sem_load,
):
    place = Place()
    me, dp, chip, core = place.me, place.dp, place.chip, place.core
    wide = 2 * OWN
    count = T // wide
    n3_all[:, half(me)] = n3_ref[...]
    loads = []
    for src, dst in (
        (wat_in, wat_ref), (wa_in, wa_ref), (feat_in, feat_ref), (weight_in, weight_ref),
        (gmlp_in, gmlp_b), (gwo_in.at[me], gwo_own),
    ):
        copy = pltpu.make_async_copy(src, dst, sem_load.at[len(loads)])
        copy.start()
        loads.append(copy)
    arrived = greet(
        [place.around(step) for step in range(1, MP)]
        + [{"dp": place.along_dp(step)} for step in range(1, DP)]
    )
    gain_a = gains_all[:, 0:1].astype(F32)
    gain_n = gains_all[:, 1:2].astype(F32)
    sum_of_b = GradientSum(place, gmlp_b, sum_b, (b_1, b_2, b_3, b_4, b_5), sem_b, 0, 48, False, gmlp_in)
    sums_of_a = (
        GradientSum(place, gmlp_a, sum_a, (a_1, a_2, a_3, a_4, a_5), sem_a, 0, 32, False),
        GradientSum(place, gmlp_a, sum_a, (a_6, a_7, a_8, a_9, a_10), sem_a2, 256, 16, True),
    )
    pick = pick_ref[0]
    spread(qkv_ref, keys, values)
    for part in range(2):
        quarter = place.quarters[part]
        queries = query_block(qkv_ref, quarter)
        out_grad = jnp.concatenate([go_heads[part * 4 + index] for index in range(4)], axis=1)
        weighted = jnp.sum(of_ref[part] * out_grad.astype(F32), axis=0, keepdims=True)
        queries_t = queries.T
        out_grad_t = out_grad.T
        query_grad = jnp.zeros((HD, 512), F32)
        for chunk in range(2 + 2 * part):
            here = slice(chunk * 512, (chunk + 1) * 512)
            scores = tn(keys[:, here], queries) - lse_ref[part]
            probs = jnp.where(score_mask(quarter, chunk, pick), jnp.exp(scores), 0.0)
            score_grad = (probs * (tn(values[:, here], out_grad) - weighted)).astype(BF16)
            query_grad = query_grad + nn(keys[:, here], score_grad)
            key_part = nn(score_grad, queries_t)
            value_part = nn(probs.astype(BF16), out_grad_t)
            both = jnp.concatenate([key_part, value_part], axis=1)
            if part == 1 and chunk < 2:
                both = both + kv_grad[here]
            kv_grad[here] = both
        q_grad[part] = (query_grad * HD**-0.5).astype(BF16)
        if part == 0:
            arrived()
            gather_n3 = Gather(place, n3_all, sem_all)
            gather_n3.begin()
            share_n = share(place, na_ref, na_got, sem_act, 0)
            sum_of_b.first()
            o_first = []
            for step in range(1, MP):
                there = place.around(step)
                copy = remote(gwo_in.at[there], gwo_got.at[step - 1], sem_gwo, step - 1, there)
                copy.start()
                o_first.append(copy)
    for index in range(MP):
        mine[index // 2, index % 2, :HD] = jnp.zeros((HD, OWN), BF16)
        mine[index // 2, index % 2, HD:] = kv_grad[index * OWN : (index + 1) * OWN].T.astype(BF16)
    for part in range(2):
        quarter = place.quarters[part]
        for index in range(4):
            mine[quarter * 2 + index // 2, index % 2, :HD] = q_grad[part, :, index * OWN : (index + 1) * OWN]
    order = list(range(1, CHIPS)) + [0]
    first = []
    for step in order:
        there = place.chip_at(step)
        copy = remote(mine.at[there, 1 - core], core_got.at[there], sem_q, step, place.partner)
        copy.start()
        first.append(copy)
    second = []
    for copy, step in zip(first, order):
        there = place.chip_at(step)
        copy.wait_recv()
        amount = (mine[there, core].astype(F32) + core_got[there].astype(F32)).astype(BF16)
        chip_sum[there] = amount
        if step == 0:
            head_grads[chip] = amount
        else:
            move = remote(chip_sum.at[there], head_grads.at[chip], sem_q, 7 + step, there * 2 + core)
            move.start()
            second.append(move)
    share_q = share(place, chip_sum.at[:, rows(1 - core, 96)], row_got, sem_rows, 0)
    for move in second:
        move.wait_recv()
    loads[0].wait()
    w_qkv = wat_ref[:, :, : 3 * CH].reshape(3 * D, D)
    columns = head_grads[...].reshape(3 * D, OWN)
    stream_grad, gain_grad = norm_backward(tn_narrow(w_qkv, columns), x2_ref[...], gain_n)
    lane = lax.broadcasted_iota(jnp.int32, (D, OWN), 1)
    gain_grads = jnp.where(lane == 1, gain_grad, 0.0) + jnp.where(lane == 2, ggain_b[...], 0.0)
    gx2 = gx3_ref[...] + stream_grad
    gz[:, :OWN] = gx2.astype(BF16)
    move_gz = swap(place, gz.at[:, :OWN], gz.at[:, OWN:], sem_n)
    loads[4].wait()
    sum_of_b.second()
    loads[1].wait()
    weights = hidden_weights(wa_ref)
    normed_grad = hidden_backward(weights, na_ref[:, :OWN], gz[:, :OWN], acts, slice(0, OWN))
    move_gz.wait_recv()
    parts[...] = hidden_backward(
        weights, na_ref[:, OWN:], gz[:, OWN:], acts, slice(OWN, 2 * OWN)
    ).astype(BF16)
    move_gn = swap(place, parts, got, sem_z)
    shares = [
        share_n,
        share(place, acts.at[:, D:], acts_got, sem_act, 1),
        share(place, gz, gz_got, sem_act, 2),
    ]
    sum_of_b.third()
    gather_n3.relay()
    gather_n3.cross()
    for copy in shares:
        copy.wait_recv()
    hidden_weight_grads(acts, acts_got, ((na_ref, na_got), (na_ref, na_got), (gz, gz_got)), gmlp_a)
    for part in sums_of_a:
        part.first()
    move_gn.wait_recv()
    normed_grad = normed_grad + got[...].astype(F32)
    stream_grad, gain_grad = norm_backward(normed_grad, x1_ref[...], gain_a)
    ggain_ref[...] = gain_grads + jnp.where(lane == 0, gain_grad, 0.0)
    gy1_ref[:, half(me)] = (gx2 + stream_grad).astype(BF16)
    gather_gy1 = Gather(place, gy1_ref, sem_y)
    gather_gy1.begin()
    sum_of_b.back()
    for index in range(3):
        gather_n3.arrive(index)
    share_q.wait_recv()
    for index in range(-1, 3):
        gather_n3.joined(index)
    for index in range(CHIPS):
        q_rows[:, half(index * 2 + core)] = chip_sum[index, rows(core, 96), :]
        q_rows[:, half(index * 2 + 1 - core)] = row_got[index]
    gat[: 3 * CH] = nt(q_rows[...], n3_all[...]).astype(BF16)
    for copy in o_first:
        copy.wait_recv()
    loads[5].wait()
    value = gwo_own[...].astype(F32)
    for index in range(MP - 1):
        value = value + gwo_got[index].astype(F32)
    gat[3 * CH :] = value.astype(BF16)
    t_first = []
    for step in range(1, DP):
        there = place.along_dp(step)
        copy = remote(gat.at[rows(there, 16)], gat_got.at[step - 1], sem_t, step - 1, {"dp": there})
        copy.start()
        t_first.append(copy)
    sum_of_b.back_y()
    gather_gy1.relay()
    reverse_taps(taps_ref, reverse)

    def build(filter_index, slot):
        def store(block, value):
            table[slot, block * OWN : (block + 1) * OWN, :] = value

        toeplitz_down(reverse[pl.ds(filter_index, 1), :], store)

    def build_some(begin, end):
        @pl.loop(begin, end)
        def _(index):
            build(index, index)

    joint_sum[...] = jnp.zeros_like(joint_sum)

    def absorb(quarter):
        here = pl.ds(pl.multiple_of(quarter * 512, 512), 512)
        grads = gy1_ref[:, here]
        joint_sum[...] += nt(feat_ref[:, here], grads)
        feature_grad[:, here] = nn(weight_ref[: K * CH], grads).astype(BF16)

    loads[2].wait()
    loads[3].wait()
    build_some(0, 4)
    gather_gy1.joined(-1)
    gather_gy1.cross()
    absorb(place.z)
    gather_gy1.arrive(0)
    build_some(4, 8)
    gather_gy1.joined(0)
    absorb((place.z + 3) % 4)
    gather_gy1.arrive(1)
    build_some(8, K // 2)
    gather_gy1.joined(1)
    absorb((place.z + 1) % 4)
    gather_gy1.arrive(2)
    for part in sums_of_a:
        part.second()
    gather_gy1.joined(2)
    absorb((place.z + 2) % 4)
    joint[:FEAT] = joint_sum[...].astype(BF16)
    joint[FEAT:] = jnp.zeros((CH, D), BF16)
    j_first = []
    for step in range(1, DP):
        there = place.along_dp(step)
        copy = remote(joint.at[rows(there, 112)], joint_got.at[step - 1], sem_j, step - 1, {"dp": there})
        copy.start()
        j_first.append(copy)
    total[...] = jnp.zeros_like(total)
    shifted[...] = jnp.zeros_like(shifted)
    joined = jnp.full((CH, T // 2), (pick == 1).astype(F32)).astype(BF16)
    middle = CH * count // 2

    def convolve(filter_index, slot):
        mine = feature_grad[pl.ds(pl.multiple_of(filter_index * CH, CH), CH), :]
        for source in range(count):
            here = slice(source * CH, (source + 1) * CH)
            begin = source * wide
            if source < count // 2:
                near_end = T // 2 - begin
                shifted[here, :near_end] = mine[:, begin : T // 2]
                shifted[here, near_end : T - begin] = mine[:, T // 2 :] * joined
            else:
                shifted[here, : T - begin] = mine[:, begin:]
        total[:middle] += nn(shifted[:middle, :], table[slot])
        total[middle:] += nn(shifted[middle:, : T // 2], table[slot, : T // 2, :])


    @pl.loop(0, K // 2)
    def _(index):
        convolve(index, index)

    for part in sums_of_a:
        part.third()
    last = []
    for copy in t_first:
        copy.wait_recv()
    value = gat[rows(dp, 16), :].astype(F32)
    for index in range(DP - 1):
        value = value + gat_got[index].astype(F32)
    sum_t[rows(dp, 16), :] = value.astype(BF16)
    done_t = sum_t.at[rows(dp, 16)]
    for step in range(1, DP):
        copy = remote(done_t, done_t, sem_tg, step - 1, {"dp": place.along_dp(step)})
        copy.start()
        last.append(copy)

    @pl.loop(K // 2, K)
    def _(index):
        build(index, index - K // 2)
        convolve(index, index - K // 2)

    for source in range(count):
        gh_ref[:, source * wide : (source + 1) * wide] = total[source * CH : (source + 1) * CH]
    for shift in range(LAGS):
        begin = (K + shift) * CH
        value = nn(weight_ref[begin : begin + CH], gy1_ref[...])
        value = jnp.where(lag_mask(shift, pick), value, 0.0)
        if shift:
            value = pltpu.roll(value, T - shift, 1)
        gh_ref[...] += value
    stream = x_ref[...].astype(F32)
    scaled = gh_ref[...] * gains_ref[:, 3:4].astype(F32)
    partial = jnp.sum(scaled * stream, axis=0, keepdims=True)
    for index in range(4):
        inner[me, index : index + 1] = partial[:, index * 512 : (index + 1) * 512]
    inner[me, 4:] = ggain_ref[...].T[:4]
    sums = []
    for step in range(1, MP):
        copy = remote(inner.at[me], inner.at[me], sem_p, step - 1, place.around(step))
        copy.start()
        sums.append(copy)
    scaling = scale_ref[...]
    gain_grad = jnp.sum(gh_ref[...] * stream * scaling, axis=1, keepdims=True)
    gain_grad = jnp.concatenate(
        [jnp.broadcast_to(gain_grad, (CH, OWN)), jnp.zeros((OWN - CH, OWN), F32)], axis=0
    ).T
    for copy in j_first:
        copy.wait_recv()
    value = joint[rows(dp, 112), :].astype(F32)
    for index in range(DP - 1):
        value = value + joint_got[index].astype(F32)
    joint_ref[rows(dp, 112), :] = value.astype(BF16)
    done_j = joint_ref.at[rows(dp, 112)]
    for step in range(1, DP):
        copy = remote(done_j, done_j, sem_jg, step - 1, {"dp": place.along_dp(step)})
        copy.start()
        last.append(copy)
    for part in sums_of_a:
        part.back()
    for copy in sums:
        copy.wait()
    value = inner[0]
    for index in range(1, MP):
        value = value + inner[index]
    gain_own[...] = pltpu.roll(value, (D - CH * me) % D, 1)[:, :OWN]
    gain_own[7:] = gain_grad[:1]
    for step in range(1, DP):
        copy = remote(gain_own, gain_dp.at[step - 1], sem_gd, step - 1, {"dp": place.along_dp(step)})
        copy.start()
        last.append(copy)
    value = jnp.concatenate([value[index : index + 1] for index in range(4)], axis=1)
    stream_grad = scaled * scaling - stream * (scaling * scaling * scaling * value / D)
    gx_ref[...] = stream_grad + gy1_ref[rows(me, CH), :].astype(F32)
    for part in sums_of_a:
        part.back_y()
    for copy in last:
        copy.wait()
    value = gain_own[...]
    for index in range(DP - 1):
        value = value + gain_dp[index]
    gain_sum[...] = value
    for copy in first + second + [share_q] + shares + [move_gz, move_gn] + o_first + t_first + j_first:
        copy.wait_send()
    gather_n3.close()
    gather_gy1.close()
    for part in (sum_of_b, *sums_of_a):
        part.close()


def second(*operands):
    return pl.pallas_call(
        second_kernel,
        out_shape=(
            jax.ShapeDtypeStruct((CH, T), F32),
            jax.ShapeDtypeStruct((DP * 112, D), BF16),
            jax.ShapeDtypeStruct((OWN, D), BF16),
            jax.ShapeDtypeStruct((3 * OWN, D), BF16),
            jax.ShapeDtypeStruct((3 * OWN, D), BF16),
            jax.ShapeDtypeStruct((8, OWN), F32),
        ),
        in_specs=[SMEM, VMEM, VMEM, ANY, VMEM, VMEM, VMEM, VMEM, ANY, ANY]
        + [VMEM] * 6
        + [ANY, ANY]
        + [VMEM] * 3
        + [ANY],
        out_specs=(VMEM,) * 6,
        scratch_shapes=[
            pltpu.VMEM((FEAT, T), BF16),
            pltpu.VMEM((2, 4, 3 * OWN, D), BF16),
            pltpu.VMEM((CHIPS, 2, OWN, D), BF16),
            pltpu.VMEM((D, T), BF16),
            pltpu.VMEM((FEAT, D), BF16),
            pltpu.VMEM((4, 3 * OWN, D), BF16),
            pltpu.VMEM((CH, D), BF16),
            pltpu.VMEM((HD, T), BF16),
            pltpu.VMEM((HD, T), BF16),
            pltpu.VMEM((T, 2 * HD), F32),
            pltpu.VMEM((2, HD, 512), BF16),
            pltpu.VMEM((CHIPS, 2, 3 * HD, OWN), BF16),
            pltpu.VMEM((CHIPS, 3 * HD, OWN), BF16),
            pltpu.VMEM((CHIPS, 3 * HD, OWN), BF16),
            pltpu.VMEM((CHIPS, 3 * HD, OWN), BF16),
            pltpu.VMEM((D, 2 * OWN), BF16),
            pltpu.VMEM((D, 2 * OWN), BF16),
            pltpu.VMEM((D, 2 * OWN), BF16),
            pltpu.VMEM((D, OWN), BF16),
            pltpu.VMEM((D, OWN), BF16),
            pltpu.VMEM((3, 2 * D, 2 * OWN), BF16),
            pltpu.VMEM((3, D, 2 * OWN), BF16),
            pltpu.VMEM((D, T), BF16),
            pltpu.VMEM((CHIPS, 96, OWN), BF16),
            pltpu.VMEM((96, T), BF16),
            pltpu.VMEM((MP - 1, CH, D), BF16),
            *sum_buffers(48, False),
            pltpu.VMEM((4, 3 * OWN, D), BF16),
            *sum_buffers(32, False),
            *sum_buffers(16, True),
            pltpu.VMEM((OWN, D), BF16),
            pltpu.VMEM((DP - 1, 16, D), BF16),
            pltpu.VMEM((D, OWN), F32),
            pltpu.VMEM((8, OWN), F32),
            pltpu.VMEM((DP - 1, 8, OWN), F32),
            pltpu.VMEM((K, T + 2 * OWN), F32),
            pltpu.VMEM((K // 2, T, 2 * OWN), BF16),
            pltpu.VMEM((K * CH, T), BF16),
            pltpu.VMEM((CH * T // (2 * OWN), T), BF16),
            pltpu.VMEM((CH * T // (2 * OWN), 2 * OWN), F32),
            pltpu.VMEM((CH, T), F32),
            pltpu.VMEM((FEAT, D), F32),
            pltpu.VMEM((DP * 112, D), BF16),
            pltpu.VMEM((DP - 1, 112, D), BF16),
            pltpu.VMEM((MP, 8, D), F32),
            sems(15), sems(1), sems(1), sems(15), sems(15), sems(1), sems(14), sems(14), sems(14), sems(7), sems(7),
            sems(7), sems(7), sems(7), sems(15), sems(3), sems(15),
            pltpu.SemaphoreType.DMA((6,)),
        ],
        compiler_params=pltpu.CompilerParams(
            collective_id=1, has_side_effects=True, vmem_limit_bytes=LIMIT
        ),
        name="second",
    )(*operands)


def final_kernel(
    joint_ref, t_ref, a_ref, b_ref, gain_ref, out_in, gx_in,
    out_ref, gx_ref, gws, gate_ga, up_ga, down_ga, gqkv, gout, gate_gb, up_gb, down_gb, *gain_grads,
):
    out_ref[...] = out_in[...]
    gx_ref[...] = gx_in[...]
    gws[...] = joint_ref[:FEAT].astype(F32)
    gqkv[...] = t_ref[: 3 * CH].astype(F32)
    gout[...] = t_ref[3 * CH :].astype(F32)
    for ref, (gate, up, down) in ((a_ref, (gate_ga, up_ga, down_ga)), (b_ref, (gate_gb, up_gb, down_gb))):
        gate[...] = ref[:OWN].astype(F32).T
        up[...] = ref[OWN : 2 * OWN].astype(F32).T
        down[...] = ref[2 * OWN :].astype(F32)
    for index, grad in enumerate(gain_grads):
        grad[...] = gain_ref[4 + index : 5 + index, :CH]


def final(*operands):
    mlp = [jax.ShapeDtypeStruct(shape, F32) for shape in ((D, OWN), (D, OWN), (OWN, D))]
    return pl.pallas_call(
        final_kernel,
        out_shape=(
            jax.ShapeDtypeStruct((CH, T), BF16),
            jax.ShapeDtypeStruct((CH, T), F32),
            jax.ShapeDtypeStruct((FEAT, D), F32),
            *mlp,
            jax.ShapeDtypeStruct((3 * CH, D), F32),
            jax.ShapeDtypeStruct((CH, D), F32),
            *mlp,
            *[jax.ShapeDtypeStruct((1, CH), F32)] * 4,
        ),
        in_specs=[VMEM] * 7,
        out_specs=(VMEM,) * 15,
        compiler_params=pltpu.CompilerParams(vmem_limit_bytes=LIMIT),
        name="final",
    )(*operands)


def on_device(
    inputs, out_grad, shape_pick, filters, stu_gain, stu_weight,
    mlp_gain_a, gate_a, up_a, down_a, attn_gain, qkv_weight, out_weight,
    mlp_gain_b, gate_b, up_b, down_b,
):
    gains = [gain.reshape(1, CH) for gain in (mlp_gain_a, attn_gain, mlp_gain_b, stu_gain)]
    weight = stu_weight.reshape(FEAT, D)
    x = inputs.T
    (
        gains_own, scaling, features, x1, x2, na, qkv, wa, wat, gains_all,
        lse, of, go_heads, gx3, out, n3, gwo, gmlp_b, ggain_b,
    ) = first(
        shape_pick, x, out_grad.T, *gains, filters, weight,
        gate_a, up_a, down_a, qkv_weight.T, out_weight, gate_b, up_b, down_b,
    )
    gx, joint, gat, ga, gb, gain_sum = second(
        shape_pick, x, scaling, features, x1, x2, na, qkv, wa, wat, gains_all,
        lse, of, go_heads, gx3, n3, gwo, gmlp_b, ggain_b, gains_own, filters, weight,
    )
    out, gx, gws, gate_ga, up_ga, down_ga, gqkv, gout, gate_gb, up_gb, down_gb, *gain_grads = final(
        joint, gat, ga, gb, gain_sum, out, gx
    )
    gain_a, gain_n, gain_b, gain_s = (grad.reshape(CH) for grad in gain_grads)
    return (
        out.T, gx.T, gain_s, gws.reshape(K + LAGS, CH, D), gain_a, gate_ga, up_ga, down_ga,
        gain_n, gqkv.T, gout, gain_b, gate_gb, up_gb, down_gb,
    )


def solution(mesh):
    cols, mid, row = P(None, "mp"), P(None, "mp", None), P("mp", None)
    return jax.shard_map(
        on_device,
        mesh=mesh,
        in_specs=(
            P("dp", "mp"), P("dp", "mp"), P("dp"), P(), P("mp"), mid,
            P("mp"), cols, cols, row, P("mp"), cols, row, P("mp"), cols, cols, row,
        ),
        out_specs=(
            P("dp", "mp"), P("dp", "mp"), P("mp"), mid, P("mp"), cols, cols, row,
            P("mp"), cols, row, P("mp"), cols, cols, row,
        ),
        check_vma=False,
    )
```

```python
import jax
import jax.numpy as jnp
from jax import lax
from jax.experimental import pallas as pl
from jax.experimental.pallas import tpu as pltpu
from jax.sharding import PartitionSpec as P

D = 512
T = 2048
OWN = 128
CH = 32
K = 24
LAGS = 3
FEAT = (K + LAGS) * CH
HD = 64
MP = 16
DP = 8
CHIPS = 8
EPSILON = 1e-05
NEG = -1e30
F32 = jnp.float32
BF16 = jnp.bfloat16
MESH = pl.DeviceIdType.MESH
VMEM = pl.BlockSpec(memory_space=pltpu.VMEM)
SMEM = pl.BlockSpec(memory_space=pltpu.SMEM)
ANY = pl.BlockSpec(memory_space=pl.ANY)
LIMIT = 62 * 2**20
EARLY_TABLES = 4


def nn(left, right):
    return jnp.dot(left, right, preferred_element_type=F32)


def tn(left, right):
    return lax.dot_general(left, right, (((0,), (0,)), ((), ())), preferred_element_type=F32)


def tn_narrow(weights, right):
    return tn(right, weights).T


def nt(left, right):
    return lax.dot_general(left, right, (((1,), (1,)), ((), ())), preferred_element_type=F32)


class Place:
    def __init__(self):
        self.me = lax.axis_index("mp")
        self.z = self.me // 4
        self.chip = self.me // 2
        self.y = self.chip % 2
        self.core = self.me % 2
        self.dp = lax.axis_index("dp")
        self.x = self.dp % 4
        self.ylo = self.dp // 4
        self.partner = self.me + 1 - 2 * self.core
        self.beside = self.me + 2 - 4 * self.y
        self.across = self.me + 4 - 8 * (self.z % 2)
        self.query_core = ((self.z + 1) // 2) % 2
        self.quarters = (self.core, 3 - self.core)

    def around(self, step):
        return (self.me + step) % MP

    def chip_at(self, step):
        return (self.chip + step) % CHIPS

    def same_units(self, slot):
        return ((self.z + 2 * (slot // 2)) % 4) * 4 + ((self.y + slot % 2) % 2) * 2 + self.core

    def along_z(self, step):
        return ((self.z + step) % 4) * 4 + self.me % 4

    def along_x(self, step):
        return {"dp": self.dp - self.x + (self.x + step) % 4}

    def along_dp(self, step):
        return (self.dp + step) % DP


def half(index):
    return pl.ds(pl.multiple_of(index * OWN, OWN), OWN)


def rows(index, count):
    return pl.ds(pl.multiple_of(index * count, count), count)


def remote(src, dst, sems, slot, target):
    return pltpu.make_async_remote_copy(
        src_ref=src,
        dst_ref=dst,
        send_sem=sems.at[0, slot],
        recv_sem=sems.at[1, slot],
        device_id=target if isinstance(target, dict) else {"mp": target},
        device_id_type=MESH,
    )


def greet(targets):
    barrier = pltpu.get_barrier_semaphore()
    for target in targets:
        where = target if isinstance(target, dict) else {"mp": target}
        pl.semaphore_signal(barrier, inc=1, device_id=where, device_id_type=MESH)
    return lambda: pl.semaphore_wait(barrier, len(targets))


def sems(count):
    return pltpu.SemaphoreType.DMA((2, count))


def norm_forward(stream, gain):
    scaling = lax.rsqrt(jnp.sum(stream * stream, axis=0, keepdims=True) / D + EPSILON)
    return stream * scaling * gain, scaling


def norm_backward(upstream, stream, gain):
    scaling = lax.rsqrt(jnp.sum(stream * stream, axis=0, keepdims=True) / D + EPSILON)
    gain_grad = jnp.sum(upstream * stream * scaling, axis=1, keepdims=True)
    scaled = upstream * gain
    inner = jnp.sum(scaled * stream, axis=0, keepdims=True)
    return scaled * scaling - stream * (scaling * scaling * scaling * inner / D), gain_grad


def swap(place, src, dst, sem, slot=0):
    copy = remote(src, dst, sem, slot, place.across)
    copy.start()
    return copy


def share(place, src, dst, sem, slot):
    copy = remote(src, dst, sem, slot, place.partner)
    copy.start()
    return copy


def hidden_weights(ref):
    return [ref[:, :, group * OWN : (group + 1) * OWN].reshape(2 * D, D) for group in range(3)]


def hidden_backward(weights, normed, grad, acts, where):
    w_gate, w_up, w_down = weights
    gate = nn(w_gate, normed)
    up = nn(w_up, normed)
    sig = jax.nn.sigmoid(gate)
    hidden_grad = nn(w_down, grad)
    gate_grad = (hidden_grad * up * sig * (1.0 + gate * (1.0 - sig))).astype(BF16)
    up_grad = (hidden_grad * gate * sig).astype(BF16)
    acts[0, :, where] = gate_grad
    acts[1, :, where] = up_grad
    acts[2, :, where] = (gate * sig * up).astype(BF16)
    return (tn(gate_grad, w_gate) + tn(up_grad, w_up)).T


def hidden_weight_grads(acts, acts_got, inputs, out):
    for group, (right, right_got) in enumerate(inputs):
        value = (nt(acts[group, :D], right[...]) + nt(acts_got[group], right_got[...])).astype(BF16)
        for index in range(4):
            out[index, group * OWN : (group + 1) * OWN] = value[index * OWN : (index + 1) * OWN]


class Gather:
    steps = (1, 3, 2)

    def __init__(self, place, buf, sem):
        me = place.me
        own = buf.at[:, half(me)]
        beside = buf.at[:, half(place.beside)]
        self.to_beside = remote(own, own, sem, 0, place.beside)
        self.to_z = [remote(own, own, sem, step, place.along_z(step)) for step in self.steps]
        farthest = buf.at[:, half(((place.z + 2) % 4) * 4 + me % 4)]
        self.relays = [remote(beside, beside, sem, 3 + step, place.along_z(step)) for step in self.steps[:2]]
        self.relays.append(remote(farthest, farthest, sem, 5, place.beside))
        self.forwards = [remote(own, own, sem, 7, place.partner), remote(beside, beside, sem, 8, place.partner)]
        for step in self.steps:
            for shift, other in ((8, me), (11, place.beside)):
                index = ((place.z + 4 - step) % 4) * 4 + other % 4
                here = buf.at[:, half(index)]
                self.forwards.append(remote(here, here, sem, shift + step, place.partner))

    def begin(self):
        for copy in [self.to_beside, *self.to_z, self.forwards[0]]:
            copy.start()

    def relay(self):
        self.to_beside.wait_recv()
        for copy in [*self.relays[:2], self.forwards[1]]:
            copy.start()

    def cross(self):
        self.to_z[2].wait_recv()
        self.relays[2].start()
        self.forwards[6].start()

    def arrive(self, index):
        if index < 2:
            self.to_z[index].wait_recv()
            self.forwards[2 + 2 * index].start()
        self.relays[index].wait_recv()
        self.forwards[3 + 2 * index].start()

    def joined(self, index):
        for copy in self.forwards[2 + 2 * index : 4 + 2 * index]:
            copy.wait_recv()

    def close(self):
        for copy in [self.to_beside, *self.to_z, *self.relays, *self.forwards]:
            copy.wait_send()


def toeplitz(taps):
    wide = pltpu.roll(jnp.broadcast_to(taps, (OWN, T)), 0, 1, stride=1, stride_axis=0)
    lane = lax.broadcasted_iota(jnp.int32, (OWN, OWN), 1)
    row = lax.broadcasted_iota(jnp.int32, (OWN, OWN), 0)
    first = jnp.where(lane >= row, wide[:, :OWN], 0.0)
    return jnp.concatenate([first.astype(BF16), wide[:, OWN:].astype(BF16)], axis=1)


def reverse_taps(taps_ref, reverse):
    row = lax.broadcasted_iota(jnp.int32, (2 * OWN, OWN), 0)
    lane = lax.broadcasted_iota(jnp.int32, (2 * OWN, OWN), 1)
    inside = (lane >= 1) & (row == OWN - lane)
    edge = (lane == 0) & (row == OWN)
    flip = jnp.where(inside | edge, 1.0, 0.0).astype(BF16)
    for index in range(T // OWN):
        begin = T - (index + 1) * OWN
        piece = taps_ref[:, begin : begin + min(2 * OWN, T - begin)]
        reverse[:, index * OWN : (index + 1) * OWN] = nn(piece, flip[: piece.shape[1]])
    reverse[:, T : T + OWN] = nn(taps_ref[:, :OWN], flip[OWN:])
    reverse[:, T + OWN :] = jnp.zeros((K, OWN), F32)


def toeplitz_down(reverse, store):
    wide = pltpu.roll(jnp.broadcast_to(reverse, (OWN, T + 2 * OWN)), 0, 1, stride=1, stride_axis=0).astype(BF16)
    for block in range(T // OWN):
        begin = T - block * OWN
        store(block, wide[:, begin : begin + 2 * OWN])


def lag_mask(shift, pick):
    lane = lax.broadcasted_iota(jnp.int32, (CH, T), 1)
    inner = lane % (T // 2)
    return (lane >= shift) & ((inner >= shift) | (pick == 1))


def spread(qkv_ref, keys, values):
    for index in range(MP):
        keys[:, index * OWN : (index + 1) * OWN] = qkv_ref[index, HD : 2 * HD]
        values[:, index * OWN : (index + 1) * OWN] = qkv_ref[index, 2 * HD :]


def query_block(qkv_ref, quarter):
    parts = [qkv_ref[quarter * 4 + index, :HD] for index in range(4)]
    return jnp.concatenate(parts, axis=1) * jnp.asarray(HD**-0.5, BF16)


def score_mask(quarter, chunk, pick):
    query = quarter * 512 + lax.broadcasted_iota(jnp.int32, (512, 512), 1)
    key = chunk * 512 + lax.broadcasted_iota(jnp.int32, (512, 512), 0)
    same_half = (quarter // 2) == (chunk // 2)
    return (key <= query) & (same_half | (pick == 1))


class GradientSum:
    def __init__(self, place, parts, done, bufs, sem, begin, each, y_first, source=None):
        self.place, self.parts, self.done, self.sem = place, parts, done, sem
        self.source = parts if source is None else source
        self.got, self.sum_1, self.got_2, self.sum_2, self.z_got = bufs
        self.begin, self.each, self.y_first = begin, each, y_first
        self.copies = []
        self.to_y = [(1 - place.ylo, {"dp": place.dp + 4 - 8 * place.ylo})]
        self.to_x = [((place.x + step) % 4, place.along_x(step)) for step in range(1, 4)]

    def at(self, index, count, begin=0):
        return pl.ds(pl.multiple_of(begin + index * count, 16), count)

    def send(self, src, dst, target):
        copy = remote(src, dst, self.sem, len(self.copies), target)
        copy.start()
        self.copies.append(copy)

    def arrived(self, count):
        for copy in self.copies[-count:]:
            copy.wait_recv()

    def first(self):
        count = self.each * (4 if self.y_first else 2)
        for slot, (there, target) in enumerate(self.to_y if self.y_first else self.to_x):
            self.send(self.source.at[:, self.at(there, count, self.begin)], self.got.at[slot], target)

    def second(self):
        place, each = self.place, self.each
        here, peers, count = (place.ylo, 1, each * 4) if self.y_first else (place.x, 3, each * 2)
        self.arrived(peers)
        value = self.parts[:, self.at(here, count, self.begin)].astype(F32)
        for slot in range(peers):
            value = value + self.got[slot].astype(F32)
        self.sum_1[...] = value.astype(BF16)
        for slot, (there, target) in enumerate(self.to_x if self.y_first else self.to_y):
            self.send(self.sum_1.at[:, self.at(there, each)], self.got_2.at[slot], target)

    def third(self):
        place, each = self.place, self.each
        here, peers = (place.x, 3) if self.y_first else (place.ylo, 1)
        self.arrived(peers)
        value = self.sum_1[:, self.at(here, each)].astype(F32)
        for slot in range(peers):
            value = value + self.got_2[slot].astype(F32)
        self.sum_2[...] = value.astype(BF16)
        for step in range(1, 4):
            self.send(self.sum_2.at[step], self.z_got.at[step - 1], place.same_units(step))

    def back(self):
        place, each = self.place, self.each
        self.arrived(3)
        value = self.sum_2[0].astype(F32)
        for slot in range(3):
            value = value + self.z_got[slot].astype(F32)
        index = place.ylo * 4 + place.x if self.y_first else place.x * 2 + place.ylo
        mine = self.at(index, each, self.begin)
        self.done[mine, :] = value.astype(BF16)
        for _, target in self.to_x:
            self.send(self.done.at[mine], self.done.at[mine], target)

    def back_y(self):
        place, each = self.place, self.each
        self.arrived(3)
        for x in range(4):
            index = place.ylo * 4 + x if self.y_first else x * 2 + place.ylo
            part = self.done.at[self.at(index, each, self.begin)]
            self.send(part, part, self.to_y[0][1])

    def close(self):
        self.arrived(4)
        for copy in self.copies:
            copy.wait_send()


def sum_buffers(each, y_first):
    first, second = (1, 3) if y_first else (3, 1)
    wide = each * (4 if y_first else 2)
    return [
        pltpu.VMEM((first, 4, wide, D), BF16),
        pltpu.VMEM((4, wide, D), BF16),
        pltpu.VMEM((second, 4, each, D), BF16),
        pltpu.VMEM((4, each, D), BF16),
        pltpu.VMEM((3, each, D), BF16),
    ]


def first_kernel(
    pick_ref, x_ref, go_ref, gain_a, gain_n, gain_b_in, gain_s, taps_ref, weight_ref,
    gate_a, up_a, down_a, qkv_w, out_w, gate_b, up_b, down_b,
    gains_ref, scale_ref, feat_out, x1_ref, x2_ref, na_out, qkv_out, wa_out, wat_out, gains_all,
    lse_ref, of_ref, go_heads, gx3_ref, out_ref, n3_ref, gwo_ref, gmlp_ref, ggain_ref,
    feat_ref, na_ref, qkv_ref, wa_ref, wat_ref, streams, streams_own, go2, squares, taps, table, table_late, weight_t, blocks, y_ref,
    core_got, chip_got, parts, got, heads, wb_ref, keys, values, own_heads, all_heads, x3_ref, nb, nb_got, go_got,
    acts, acts_got, parts_n, got_n, parts_z, got_z, grad_heads, out_own,
    sem_s, sem_x, sem_wa, sem_wb, sem_wat, sem_y, sem_n, sem_g, sem_z, sem_q,
    sem_o, sem_nb, sem_gn, sem_zb, sem_h, sem_out, sem_act, sem_save,
):
    place = Place()
    me, chip, core, x = place.me, place.chip, place.core, place.x
    count = T // OWN
    pick = pick_ref[0]
    wat_ref[chip, core, : 3 * CH] = qkv_w[...]
    wat_ref[chip, core, 3 * CH :] = out_w[...]
    arrived = greet(
        [place.around(step) for step in range(1, MP)] + [place.along_x(step) for step in range(1, 4)]
    )
    stream = x_ref[...].astype(F32)
    squares[pl.ds(me, 1)] = jnp.sum(stream * stream, axis=0, keepdims=True)[None]
    for ref, (gate, up, down) in ((wa_ref, (gate_a, up_a, down_a)), (wb_ref, (gate_b, up_b, down_b))):
        ref[0, 0, :OWN] = gate[...].T
        ref[0, 0, OWN : 2 * OWN] = up[...].T
        ref[0, 0, 2 * OWN :] = down[...]
    lines = [ref[...].astype(F32) for ref in (gain_a, gain_n, gain_b_in, gain_s)]
    lines = jnp.concatenate(lines + [jnp.zeros((OWN - 4, CH), F32)], axis=0)
    lines = jnp.concatenate([lines, jnp.zeros((OWN, OWN - CH), F32)], axis=1)
    gains_ref[...] = lines.T[:CH].astype(BF16)
    streams[0] = x_ref[...]
    streams[1] = go_ref[...]
    for index in range(MP):
        streams[2, :, index * OWN : (index + 1) * OWN] = gains_ref[...]
    streams_own[:, rows(me, CH)] = streams[:, :, half(me)]
    taps[...] = taps_ref[...].astype(F32)

    def build(step, table, shift=0):
        for index in range(2):
            filter_table = toeplitz(taps[pl.ds((step + shift) * 2 + index, 1), :])
            for offset in range(count):
                table[step, offset * OWN : (offset + 1) * OWN, index * OWN : (index + 1) * OWN] = filter_table[
                    :, offset * OWN : (offset + 1) * OWN
                ]

    build_early = lambda step: build(step, table)
    pl.loop(0, EARLY_TABLES)(build_early)
    arrived()
    sums, late, fetch_a, fetch_b, fetch_t, rest_a, rest_b, rest_t = [], [], [], [], [], [], [], []
    for step in range(1, MP):
        there = place.around(step)
        copy = remote(squares.at[me], squares.at[me], sem_s, step - 1, there)
        copy.start()
        sums.append(copy)
    for step in range(1, 4):
        copy = remote(
            wa_ref.at[0, 0, rows(x, 96)], wa_ref.at[0, step, rows(x, 96)], sem_wa, step - 1, place.same_units(step)
        )
        copy.start()
        fetch_a.append(copy)
    mine_t = wat_ref.at[chip, core, rows(x, CH)]
    for step in range(1, CHIPS):
        copy = remote(mine_t, mine_t, sem_wat, step - 1, place.chip_at(step) * 2 + core)
        copy.start()
        fetch_t.append(copy)
    for step in range(1, MP):
        there = place.around(step)
        copy = remote(
            streams.at[:, :, half(there)], streams_own.at[:, rows(me, CH)], sem_x, step - 1, there
        )
        copy.start()
        late.append(copy)
    for step in range(1, 4):
        copy = remote(
            wb_ref.at[0, 0, rows(x, 96)], wb_ref.at[0, step, rows(x, 96)], sem_wb, step - 1, place.same_units(step)
        )
        copy.start()
        fetch_b.append(copy)
    share_a = [share(place, wa_ref.at[0, 0], wa_ref.at[1, 0], sem_wa, 6)]
    share_b = [share(place, wb_ref.at[0, 0], wb_ref.at[1, 0], sem_wb, 6)]
    weight_t[...] = weight_ref[...].T
    pl.loop(EARLY_TABLES, K // 4)(build_early)
    for copy in sums:
        copy.wait()
    total = squares[0]
    for index in range(1, MP):
        total = total + squares[index]
    scaling = lax.rsqrt(total / D + EPSILON)
    scale_ref[...] = scaling
    own = stream * scaling * gains_ref[:, 3:4].astype(F32)
    h = own.astype(BF16)
    own = h.astype(F32)
    joined = jnp.full((CH, OWN), (pick == 1).astype(F32)).astype(BF16)
    for target in range(count):
        for offset in range(count):
            here = (slice(target * CH, (target + 1) * CH), slice(offset * OWN, (offset + 1) * OWN))
            if offset > target:
                blocks[here] = jnp.zeros((CH, OWN), BF16)
                continue
            source = target - offset
            value = h[:, source * OWN : (source + 1) * OWN]
            if target >= count // 2 and source < count // 2:
                value = value * joined
            blocks[here] = value
    for shift in range(LAGS):
        moved = own if shift == 0 else pltpu.roll(own, shift, 1)
        moved = jnp.where(lag_mask(shift, pick), moved, 0.0).astype(BF16)
        feat_ref[(K + shift) * CH : (K + shift + 1) * CH, :] = moved

    def convolve(step, table, shift=0):
        early = nn(blocks[: CH * count // 2, : T // 2], table[step, : T // 2, :]).astype(BF16)
        late_half = nn(blocks[CH * count // 2 :, :], table[step]).astype(BF16)
        for index in range(2):
            base = pl.multiple_of(((step + shift) * 2 + index) * CH, CH)
            for target in range(count):
                part, at = (early, target) if target < count // 2 else (late_half, target - count // 2)
                feat_ref[pl.ds(base, CH), target * OWN : (target + 1) * OWN] = part[
                    at * CH : (at + 1) * CH, index * OWN : (index + 1) * OWN
                ]


    def pass_on(fetched, source, sem, done, rest):
        for copy in fetched:
            copy.wait_recv()
        for step in range(1, 4):
            copy = remote(source, source, sem, done + step - 1, place.along_x(step))
            copy.start()
            rest.append(copy)

    @pl.loop(0, K // 4)
    def _(step):
        build(step, table_late, K // 4)
        convolve(step, table)

    pass_on(fetch_a, wa_ref.at[0, 1:4, rows(x, 96)], sem_wa, 3, rest_a)

    @pl.loop(0, K // 4)
    def _(step):
        convolve(step, table_late, K // 4)

    saves = []

    def save(src, dst):
        copy = pltpu.make_async_copy(src, dst, sem_save.at[len(saves)])
        copy.start()
        saves.append(copy)

    save(feat_ref, feat_out)
    for group in range(4):
        y = nn(weight_t[...], feat_ref[:, group * 512 : (group + 1) * 512]).astype(BF16)
        for index in range(4):
            y_ref[group * 2 + index // 2, index % 2] = y[:, index * OWN : (index + 1) * OWN]
    order = list(range(1, CHIPS)) + [0]
    first, second = [], []
    for step in order:
        there = place.chip_at(step)
        copy = remote(y_ref.at[there, 1 - core], core_got.at[there], sem_y, step, place.partner)
        copy.start()
        first.append(copy)
    for copy, step in zip(first, order):
        there = place.chip_at(step)
        copy.wait_recv()
        total = y_ref[there, core].astype(F32) + core_got[there].astype(F32)
        if step == 0:
            x1_ref[...] = total
        else:
            y_ref[there, core] = total.astype(BF16)
            move = remote(y_ref.at[there, core], chip_got.at[step - 1], sem_y, 7 + step, there * 2 + core)
            move.start()
            second.append(move)
    pass_on(fetch_t, wat_ref.at[:, core, rows(x, CH)], sem_wat, 7, rest_t)
    for copy in late:
        copy.wait()
    go2[:, :OWN] = streams_own[1]
    move_go = swap(place, go2.at[:, :OWN], go2.at[:, OWN:], sem_g)
    gains_all[...] = streams_own[2]
    for copy in rest_a:
        copy.wait_recv()
    share_a.append(share(place, wa_ref.at[0, 1:], wa_ref.at[1, 1:], sem_wa, 7))
    for move in second:
        move.wait_recv()
    x1 = x1_ref[...] + streams_own[0].astype(F32)
    for index in range(CHIPS - 1):
        x1 = x1 + chip_got[index].astype(F32)
    x1_ref[...] = x1
    normed, _ = norm_forward(x1, gains_all[:, 0:1].astype(F32))
    na_ref[:, :OWN] = normed.astype(BF16)
    move_n = swap(place, na_ref.at[:, :OWN], na_ref.at[:, OWN:], sem_n)
    for copy in share_a:
        copy.wait_recv()
    save(wa_ref, wa_out)
    w_gate, w_up, w_down = hidden_weights(wa_ref)

    def forward(normed):
        gate = nn(w_gate, normed)
        hidden = (gate * jax.nn.sigmoid(gate) * nn(w_up, normed)).astype(BF16)
        return tn_narrow(w_down, hidden)

    z = forward(na_ref[:, :OWN])
    pass_on(fetch_b, wb_ref.at[0, 1:4, rows(x, 96)], sem_wb, 3, rest_b)
    move_n.wait_recv()
    parts[...] = forward(na_ref[:, OWN:]).astype(BF16)
    move_z = swap(place, parts, got, sem_z)
    save(na_ref, na_out)
    for copy in rest_t:
        copy.wait_recv()
    half_t = wat_ref.at[:, core]
    share_t = share(place, half_t, half_t, sem_wat, 10)
    move_z.wait_recv()
    x2 = x1 + z + got[...].astype(F32)
    x2_ref[...] = x2
    n3 = norm_forward(x2, gains_all[:, 1:2].astype(F32))[0].astype(BF16)
    n3_ref[...] = n3
    share_t.wait_recv()
    save(wat_ref, wat_out)
    w_qkv = wat_ref[:, :, : 3 * CH].reshape(3 * D, D)
    heads[...] = nn(w_qkv, n3).astype(BF16).reshape(CHIPS, 3 * HD, OWN)
    sends = []
    for step in range(1, CHIPS):
        there = place.chip_at(step)
        copy = remote(heads.at[there], qkv_ref.at[me], sem_q, step - 1, there * 2 + core)
        copy.start()
        sends.append(copy)
    qkv_ref[me] = heads[chip]
    forwards = [remote(qkv_ref.at[me], qkv_ref.at[me], sem_q, 7, place.partner)]
    forwards[0].start()
    for step in range(1, CHIPS):
        source = place.chip_at(CHIPS - step) * 2 + core
        sends[step - 1].wait_recv()
        copy = remote(qkv_ref.at[source], qkv_ref.at[source], sem_q, 7 + step, place.partner)
        copy.start()
        forwards.append(copy)
    for copy in forwards:
        copy.wait()
    save(qkv_ref, qkv_out)
    for copy in rest_b:
        copy.wait_recv()
    share_b.append(share(place, wb_ref.at[0, 1:], wb_ref.at[1, 1:], sem_wb, 7))
    for copy in fetch_a + fetch_b + fetch_t + rest_a + rest_t + share_a + [share_t] + first + second + sends:
        copy.wait_send()
    move_n.wait_send()
    move_z.wait_send()
    spread(qkv_ref, keys, values)
    targets = [place.quarters[slot // 4] * 4 + slot % 4 for slot in range(8)]
    copies = [
        pltpu.make_async_remote_copy(
            src_ref=own_heads.at[slot], dst_ref=all_heads.at[chip],
            send_sem=sem_o.at[0, slot], recv_sem=sem_o.at[1, chip],
            device_id={"mp": targets[slot]}, device_id_type=MESH,
        )
        for slot in range(8)
    ]
    for part in range(2):
        quarter = place.quarters[part]
        queries = query_block(qkv_ref, quarter)
        top = jnp.full((1, 512), NEG, F32)
        norm = jnp.zeros((1, 512), F32)
        total = jnp.zeros((HD, 512), F32)
        for chunk in range(2 + 2 * part):
            here = slice(chunk * 512, (chunk + 1) * 512)
            scores = jnp.where(score_mask(quarter, chunk, pick), tn(keys[:, here], queries), NEG)
            new_top = jnp.maximum(top, jnp.max(scores, axis=0, keepdims=True))
            weights = jnp.exp(scores - new_top)
            rescale = jnp.exp(top - new_top)
            norm = norm * rescale + jnp.sum(weights, axis=0, keepdims=True)
            total = total * rescale + nn(values[:, here], weights.astype(BF16))
            top = new_top
        total = total / norm
        lse_ref[part] = top + jnp.log(norm)
        of_ref[part] = total
        for index in range(4):
            own_heads[part * 4 + index] = total[:, index * OWN : (index + 1) * OWN].astype(BF16)
        for slot in range(part * 4, part * 4 + 4):
            pl.when(targets[slot] != me)(copies[slot].start)

            @pl.when(targets[slot] == me)
            def _():
                all_heads[chip] = own_heads[slot]
    arrivals = [
        remote(own_heads.at[0], all_heads.at[head], sem_o, head, place.partner) for head in range(CHIPS)
    ]
    for head in range(CHIPS):
        pl.when(head * 2 + place.query_core != me)(arrivals[head].wait_recv)
    w_out = wat_ref[:, :, 3 * CH :].reshape(D, D)
    outputs = all_heads[...].reshape(D, OWN)
    x3 = x2 + tn_narrow(w_out, outputs)
    x3_ref[...] = x3
    gain_b = gains_all[:, 2:3].astype(F32)
    nb[:, :OWN] = norm_forward(x3, gain_b)[0].astype(BF16)
    move_n = swap(place, nb.at[:, :OWN], nb.at[:, OWN:], sem_nb)
    for copy in share_b + [move_go]:
        copy.wait_recv()
    weights = hidden_weights(wb_ref)
    normed_grad = hidden_backward(weights, nb[:, :OWN], go2[:, :OWN], acts, slice(0, OWN))
    move_n.wait_recv()
    parts_n[...] = hidden_backward(
        weights, nb[:, OWN:], go2[:, OWN:], acts, slice(OWN, 2 * OWN)
    ).astype(BF16)
    move_gn = swap(place, parts_n, got_n, sem_gn)
    shares = [
        share(place, acts.at[:, D:], acts_got, sem_act, 0),
        share(place, nb, nb_got, sem_act, 1),
        share(place, go2, go_got, sem_act, 2),
    ]
    parts_z[...] = tn_narrow(weights[2], acts[2, :, OWN:]).astype(BF16)
    move_z = swap(place, parts_z, got_z, sem_zb)
    z = tn_narrow(weights[2], acts[2, :, :OWN])
    move_gn.wait_recv()
    normed_grad = normed_grad + got_n[...].astype(F32)
    stream_grad, gain_grad = norm_backward(normed_grad, x3_ref[...], gain_b)
    ggain_ref[...] = gain_grad
    gx3 = go2[:, :OWN].astype(F32) + stream_grad
    gx3_ref[...] = gx3
    gy = gx3.astype(BF16)
    grad_heads[...] = nn(w_out, gy).astype(BF16).reshape(CHIPS, HD, OWN)
    slot = (place.z // 2) * 4 + me % 4
    sends = [
        pltpu.make_async_remote_copy(
            src_ref=grad_heads.at[head], dst_ref=go_heads.at[slot],
            send_sem=sem_h.at[0, head], recv_sem=sem_h.at[1, slot],
            device_id={"mp": head * 2 + place.query_core}, device_id_type=MESH,
        )
        for head in range(CHIPS)
    ]
    for head in range(CHIPS):
        pl.when(head * 2 + place.query_core != me)(sends[head].start)

        @pl.when(head * 2 + place.query_core == me)
        def _():
            go_heads[slot] = grad_heads[head]

    move_z.wait_recv()
    out_own[...] = (x3_ref[...] + z + got_z[...].astype(F32)).astype(BF16)
    moves = []
    for step in range(1, MP):
        there = place.around(step)
        copy = remote(out_own.at[rows(there, CH)], out_ref.at[:, half(me)], sem_out, step - 1, there)
        copy.start()
        moves.append(copy)
    out_ref[:, half(me)] = out_own[rows(me, CH), :]
    gwo_ref[...] = nt(outputs, gy).astype(BF16).reshape(MP, CH, D)
    for copy in shares:
        copy.wait_recv()
    hidden_weight_grads(acts, acts_got, ((nb, nb_got), (nb, nb_got), (go2, go_got)), gmlp_ref)
    for slot_in in range(8):
        arrival = remote(grad_heads.at[0], go_heads.at[slot_in], sem_h, slot_in, place.partner)
        pl.when(targets[slot_in] != me)(arrival.wait_recv)
    for slot_out in range(8):
        pl.when(targets[slot_out] != me)(copies[slot_out].wait_send)
        pl.when(slot_out * 2 + place.query_core != me)(sends[slot_out].wait_send)
    for copy in moves:
        copy.wait()
    for copy in rest_b + share_b + shares + [move_go, move_n, move_gn, move_z]:
        copy.wait_send()
    for copy in saves:
        copy.wait()


def first(*operands):
    return pl.pallas_call(
        first_kernel,
        out_shape=(
            jax.ShapeDtypeStruct((CH, OWN), BF16),
            jax.ShapeDtypeStruct((1, T), F32),
            jax.ShapeDtypeStruct((FEAT, T), BF16),
            jax.ShapeDtypeStruct((D, OWN), F32),
            jax.ShapeDtypeStruct((D, OWN), F32),
            jax.ShapeDtypeStruct((D, 2 * OWN), BF16),
            jax.ShapeDtypeStruct((MP, 3 * HD, OWN), BF16),
            jax.ShapeDtypeStruct((2, 4, 3 * OWN, D), BF16),
            jax.ShapeDtypeStruct((CHIPS, 2, OWN, D), BF16),
            jax.ShapeDtypeStruct((D, OWN), BF16),
            jax.ShapeDtypeStruct((2, 1, 512), F32),
            jax.ShapeDtypeStruct((2, HD, 512), F32),
            jax.ShapeDtypeStruct((8, HD, OWN), BF16),
            jax.ShapeDtypeStruct((D, OWN), F32),
            jax.ShapeDtypeStruct((CH, T), BF16),
            jax.ShapeDtypeStruct((D, OWN), BF16),
            jax.ShapeDtypeStruct((MP, CH, D), BF16),
            jax.ShapeDtypeStruct((4, 3 * OWN, D), BF16),
            jax.ShapeDtypeStruct((D, 1), F32),
        ),
        in_specs=[SMEM] + [VMEM] * 16,
        out_specs=(VMEM, VMEM, ANY, VMEM, VMEM, ANY, ANY, ANY, ANY) + (VMEM,) * 10,
        scratch_shapes=[
            pltpu.VMEM((FEAT, T), BF16),
            pltpu.VMEM((D, 2 * OWN), BF16),
            pltpu.VMEM((MP, 3 * HD, OWN), BF16),
            pltpu.VMEM((2, 4, 3 * OWN, D), BF16),
            pltpu.VMEM((CHIPS, 2, OWN, D), BF16),
            pltpu.VMEM((3, CH, T), BF16),
            pltpu.VMEM((3, D, OWN), BF16),
            pltpu.VMEM((D, 2 * OWN), BF16),
            pltpu.VMEM((MP, 1, T), F32),
            pltpu.VMEM((K, T), F32),
            pltpu.VMEM((K // 4, T, 2 * OWN), BF16),
            pltpu.VMEM((K // 4, T, 2 * OWN), BF16),
            pltpu.VMEM((D, FEAT), BF16),
            pltpu.VMEM((CH * T // OWN, T), BF16),
            pltpu.VMEM((CHIPS, 2, D, OWN), BF16),
            pltpu.VMEM((CHIPS, D, OWN), BF16),
            pltpu.VMEM((CHIPS - 1, D, OWN), BF16),
            pltpu.VMEM((D, OWN), BF16),
            pltpu.VMEM((D, OWN), BF16),
            pltpu.VMEM((CHIPS, 3 * HD, OWN), BF16),
            pltpu.VMEM((2, 4, 3 * OWN, D), BF16),
            pltpu.VMEM((HD, T), BF16),
            pltpu.VMEM((HD, T), BF16),
            pltpu.VMEM((8, HD, OWN), BF16),
            pltpu.VMEM((8, HD, OWN), BF16),
            pltpu.VMEM((D, OWN), F32),
            pltpu.VMEM((D, 2 * OWN), BF16),
            pltpu.VMEM((D, 2 * OWN), BF16),
            pltpu.VMEM((D, 2 * OWN), BF16),
            pltpu.VMEM((3, 2 * D, 2 * OWN), BF16),
            pltpu.VMEM((3, D, 2 * OWN), BF16),
            pltpu.VMEM((D, OWN), BF16),
            pltpu.VMEM((D, OWN), BF16),
            pltpu.VMEM((D, OWN), BF16),
            pltpu.VMEM((D, OWN), BF16),
            pltpu.VMEM((CHIPS, HD, OWN), BF16),
            pltpu.VMEM((D, OWN), BF16),
            sems(15), sems(15), sems(8), sems(8), sems(11),
            sems(15), sems(1), sems(1), sems(1), sems(15),
            sems(8), sems(1), sems(1), sems(1), sems(8), sems(15), sems(3),
            pltpu.SemaphoreType.DMA((5,)),
        ],
        compiler_params=pltpu.CompilerParams(
            collective_id=0, has_side_effects=True, vmem_limit_bytes=LIMIT
        ),
        name="first",
    )(*operands)


def second_kernel(
    pick_ref, x_ref, scale_ref, feat_in, x1_ref, x2_ref, na_ref, qkv_ref, wa_in, wat_in, gains_all,
    lse_ref, of_ref, go_heads, gx3_ref, n3_ref, gwo_in, gmlp_in, ggain_b, gains_ref, taps_ref, weight_in,
    gx_ref, joint_ref, sum_t, sum_a, sum_b, gain_sum,
    feat_ref, wa_ref, wat_ref, n3_all, weight_ref, gmlp_b, gwo_own,
    keys, values, kv_grad, q_grad, mine, core_got, chip_sum, head_grads, gz, gz_got, na_got, parts, got,
    acts, acts_got, gy1_ref, row_got, q_rows, gwo_got,
    b_1, b_2, b_3, b_4, b_5, gmlp_a, a_1, a_2, a_3, a_4, a_5, a_6, a_7, a_8, a_9, a_10, gat, gat_got, ggain_ref, gain_own, gain_dp,
    reverse, table, feature_grad, shifted, total, gh_ref, joint_sum, joint, joint_got, inner,
    sem_q, sem_n, sem_z, sem_y, sem_gwo, sem_rows, sem_b, sem_a, sem_a2, sem_t, sem_tg, sem_gd, sem_j, sem_jg, sem_p, sem_act, sem_all, sem_load,
):
    place = Place()
    me, dp, chip, core = place.me, place.dp, place.chip, place.core
    wide = 2 * OWN
    count = T // wide
    n3_all[:, half(me)] = n3_ref[...]
    loads = []
    for src, dst in (
        (wat_in, wat_ref), (wa_in, wa_ref), (feat_in, feat_ref), (weight_in, weight_ref),
        (gmlp_in, gmlp_b), (gwo_in.at[me], gwo_own),
    ):
        copy = pltpu.make_async_copy(src, dst, sem_load.at[len(loads)])
        copy.start()
        loads.append(copy)
    arrived = greet(
        [place.around(step) for step in range(1, MP)]
        + [{"dp": place.along_dp(step)} for step in range(1, DP)]
    )
    gain_a = gains_all[:, 0:1].astype(F32)
    gain_n = gains_all[:, 1:2].astype(F32)
    sum_of_b = GradientSum(place, gmlp_b, sum_b, (b_1, b_2, b_3, b_4, b_5), sem_b, 0, 48, False, gmlp_in)
    sums_of_a = (
        GradientSum(place, gmlp_a, sum_a, (a_1, a_2, a_3, a_4, a_5), sem_a, 0, 32, False),
        GradientSum(place, gmlp_a, sum_a, (a_6, a_7, a_8, a_9, a_10), sem_a2, 256, 16, True),
    )
    pick = pick_ref[0]
    spread(qkv_ref, keys, values)
    for part in range(2):
        quarter = place.quarters[part]
        queries = query_block(qkv_ref, quarter)
        out_grad = jnp.concatenate([go_heads[part * 4 + index] for index in range(4)], axis=1)
        weighted = jnp.sum(of_ref[part] * out_grad.astype(F32), axis=0, keepdims=True)
        queries_t = queries.T
        out_grad_t = out_grad.T
        query_grad = jnp.zeros((HD, 512), F32)
        for chunk in range(2 + 2 * part):
            here = slice(chunk * 512, (chunk + 1) * 512)
            scores = tn(keys[:, here], queries) - lse_ref[part]
            probs = jnp.where(score_mask(quarter, chunk, pick), jnp.exp(scores), 0.0)
            score_grad = (probs * (tn(values[:, here], out_grad) - weighted)).astype(BF16)
            query_grad = query_grad + nn(keys[:, here], score_grad)
            key_part = nn(score_grad, queries_t)
            value_part = nn(probs.astype(BF16), out_grad_t)
            both = jnp.concatenate([key_part, value_part], axis=1)
            if part == 1 and chunk < 2:
                both = both + kv_grad[here]
            kv_grad[here] = both
        q_grad[part] = (query_grad * HD**-0.5).astype(BF16)
        if part == 0:
            arrived()
            gather_n3 = Gather(place, n3_all, sem_all)
            gather_n3.begin()
            share_n = share(place, na_ref, na_got, sem_act, 0)
            sum_of_b.first()
            o_first = []
            for step in range(1, MP):
                there = place.around(step)
                copy = remote(gwo_in.at[there], gwo_got.at[step - 1], sem_gwo, step - 1, there)
                copy.start()
                o_first.append(copy)
    for index in range(MP):
        mine[index // 2, index % 2, :HD] = jnp.zeros((HD, OWN), BF16)
        mine[index // 2, index % 2, HD:] = kv_grad[index * OWN : (index + 1) * OWN].T.astype(BF16)
    for part in range(2):
        quarter = place.quarters[part]
        for index in range(4):
            mine[quarter * 2 + index // 2, index % 2, :HD] = q_grad[part, :, index * OWN : (index + 1) * OWN]
    order = list(range(1, CHIPS)) + [0]
    first = []
    for step in order:
        there = place.chip_at(step)
        copy = remote(mine.at[there, 1 - core], core_got.at[there], sem_q, step, place.partner)
        copy.start()
        first.append(copy)
    second = []
    for copy, step in zip(first, order):
        there = place.chip_at(step)
        copy.wait_recv()
        amount = (mine[there, core].astype(F32) + core_got[there].astype(F32)).astype(BF16)
        chip_sum[there] = amount
        if step == 0:
            head_grads[chip] = amount
        else:
            move = remote(chip_sum.at[there], head_grads.at[chip], sem_q, 7 + step, there * 2 + core)
            move.start()
            second.append(move)
    share_q = share(place, chip_sum.at[:, rows(1 - core, 96)], row_got, sem_rows, 0)
    for move in second:
        move.wait_recv()
    loads[0].wait()
    w_qkv = wat_ref[:, :, : 3 * CH].reshape(3 * D, D)
    columns = head_grads[...].reshape(3 * D, OWN)
    stream_grad, gain_grad = norm_backward(tn_narrow(w_qkv, columns), x2_ref[...], gain_n)
    lane = lax.broadcasted_iota(jnp.int32, (D, OWN), 1)
    gain_grads = jnp.where(lane == 1, gain_grad, 0.0) + jnp.where(lane == 2, ggain_b[...], 0.0)
    gx2 = gx3_ref[...] + stream_grad
    gz[:, :OWN] = gx2.astype(BF16)
    move_gz = swap(place, gz.at[:, :OWN], gz.at[:, OWN:], sem_n)
    loads[4].wait()
    sum_of_b.second()
    loads[1].wait()
    weights = hidden_weights(wa_ref)
    normed_grad = hidden_backward(weights, na_ref[:, :OWN], gz[:, :OWN], acts, slice(0, OWN))
    move_gz.wait_recv()
    parts[...] = hidden_backward(
        weights, na_ref[:, OWN:], gz[:, OWN:], acts, slice(OWN, 2 * OWN)
    ).astype(BF16)
    move_gn = swap(place, parts, got, sem_z)
    shares = [
        share_n,
        share(place, acts.at[:, D:], acts_got, sem_act, 1),
        share(place, gz, gz_got, sem_act, 2),
    ]
    sum_of_b.third()
    gather_n3.relay()
    gather_n3.cross()
    for copy in shares:
        copy.wait_recv()
    hidden_weight_grads(acts, acts_got, ((na_ref, na_got), (na_ref, na_got), (gz, gz_got)), gmlp_a)
    for part in sums_of_a:
        part.first()
    move_gn.wait_recv()
    normed_grad = normed_grad + got[...].astype(F32)
    stream_grad, gain_grad = norm_backward(normed_grad, x1_ref[...], gain_a)
    ggain_ref[...] = gain_grads + jnp.where(lane == 0, gain_grad, 0.0)
    gy1_ref[:, half(me)] = (gx2 + stream_grad).astype(BF16)
    gather_gy1 = Gather(place, gy1_ref, sem_y)
    gather_gy1.begin()
    sum_of_b.back()
    for index in range(3):
        gather_n3.arrive(index)
    share_q.wait_recv()
    for index in range(-1, 3):
        gather_n3.joined(index)
    for index in range(CHIPS):
        q_rows[:, half(index * 2 + core)] = chip_sum[index, rows(core, 96), :]
        q_rows[:, half(index * 2 + 1 - core)] = row_got[index]
    gat[: 3 * CH] = nt(q_rows[...], n3_all[...]).astype(BF16)
    for copy in o_first:
        copy.wait_recv()
    loads[5].wait()
    value = gwo_own[...].astype(F32)
    for index in range(MP - 1):
        value = value + gwo_got[index].astype(F32)
    gat[3 * CH :] = value.astype(BF16)
    t_first = []
    for step in range(1, DP):
        there = place.along_dp(step)
        copy = remote(gat.at[rows(there, 16)], gat_got.at[step - 1], sem_t, step - 1, {"dp": there})
        copy.start()
        t_first.append(copy)
    gather_gy1.relay()
    reverse_taps(taps_ref, reverse)

    def build(filter_index, slot):
        def store(block, value):
            table[slot, block * OWN : (block + 1) * OWN, :] = value

        toeplitz_down(reverse[pl.ds(filter_index, 1), :], store)

    def build_some(begin, end):
        @pl.loop(begin, end)
        def _(index):
            build(index, index)

    joint_sum[...] = jnp.zeros_like(joint_sum)

    def absorb(quarter):
        here = pl.ds(pl.multiple_of(quarter * 512, 512), 512)
        grads = gy1_ref[:, here]
        joint_sum[...] += nt(feat_ref[:, here], grads)
        feature_grad[:, here] = nn(weight_ref[: K * CH], grads).astype(BF16)

    loads[2].wait()
    loads[3].wait()
    build_some(0, 4)
    gather_gy1.joined(-1)
    gather_gy1.cross()
    absorb(place.z)
    gather_gy1.arrive(0)
    sum_of_b.back_y()
    build_some(4, 8)
    gather_gy1.joined(0)
    absorb((place.z + 3) % 4)
    gather_gy1.arrive(1)
    build_some(8, K // 2)
    gather_gy1.joined(1)
    absorb((place.z + 1) % 4)
    gather_gy1.arrive(2)
    for part in sums_of_a:
        part.second()
    gather_gy1.joined(2)
    absorb((place.z + 2) % 4)
    joint[:FEAT] = joint_sum[...].astype(BF16)
    joint[FEAT:] = jnp.zeros((CH, D), BF16)
    j_first = []
    for step in range(1, DP):
        there = place.along_dp(step)
        copy = remote(joint.at[rows(there, 112)], joint_got.at[step - 1], sem_j, step - 1, {"dp": there})
        copy.start()
        j_first.append(copy)
    total[...] = jnp.zeros_like(total)
    shifted[...] = jnp.zeros_like(shifted)
    joined = jnp.full((CH, T // 2), (pick == 1).astype(F32)).astype(BF16)
    middle = CH * count // 2

    def convolve(filter_index, slot):
        mine = feature_grad[pl.ds(pl.multiple_of(filter_index * CH, CH), CH), :]
        for source in range(count):
            here = slice(source * CH, (source + 1) * CH)
            begin = source * wide
            if source < count // 2:
                near_end = T // 2 - begin
                shifted[here, :near_end] = mine[:, begin : T // 2]
                shifted[here, near_end : T - begin] = mine[:, T // 2 :] * joined
            else:
                shifted[here, : T - begin] = mine[:, begin:]
        total[:middle] += nn(shifted[:middle, :], table[slot])
        total[middle:] += nn(shifted[middle:, : T // 2], table[slot, : T // 2, :])


    @pl.loop(0, K // 2)
    def _(index):
        convolve(index, index)

    for part in sums_of_a:
        part.third()
    last = []
    for copy in t_first:
        copy.wait_recv()
    value = gat[rows(dp, 16), :].astype(F32)
    for index in range(DP - 1):
        value = value + gat_got[index].astype(F32)
    sum_t[rows(dp, 16), :] = value.astype(BF16)
    done_t = sum_t.at[rows(dp, 16)]
    for step in range(1, DP):
        copy = remote(done_t, done_t, sem_tg, step - 1, {"dp": place.along_dp(step)})
        copy.start()
        last.append(copy)

    @pl.loop(K // 2, K)
    def _(index):
        build(index, index - K // 2)
        convolve(index, index - K // 2)

    for source in range(count):
        gh_ref[:, source * wide : (source + 1) * wide] = total[source * CH : (source + 1) * CH]
    for shift in range(LAGS):
        begin = (K + shift) * CH
        value = nn(weight_ref[begin : begin + CH], gy1_ref[...])
        value = jnp.where(lag_mask(shift, pick), value, 0.0)
        if shift:
            value = pltpu.roll(value, T - shift, 1)
        gh_ref[...] += value
    stream = x_ref[...].astype(F32)
    scaled = gh_ref[...] * gains_ref[:, 3:4].astype(F32)
    partial = jnp.sum(scaled * stream, axis=0, keepdims=True)
    for index in range(4):
        inner[me, index : index + 1] = partial[:, index * 512 : (index + 1) * 512]
    inner[me, 4:] = ggain_ref[...].T[:4]
    sums = []
    for step in range(1, MP):
        copy = remote(inner.at[me], inner.at[me], sem_p, step - 1, place.around(step))
        copy.start()
        sums.append(copy)
    scaling = scale_ref[...]
    gain_grad = jnp.sum(gh_ref[...] * stream * scaling, axis=1, keepdims=True)
    gain_grad = jnp.concatenate(
        [jnp.broadcast_to(gain_grad, (CH, OWN)), jnp.zeros((OWN - CH, OWN), F32)], axis=0
    ).T
    for copy in j_first:
        copy.wait_recv()
    value = joint[rows(dp, 112), :].astype(F32)
    for index in range(DP - 1):
        value = value + joint_got[index].astype(F32)
    joint_ref[rows(dp, 112), :] = value.astype(BF16)
    done_j = joint_ref.at[rows(dp, 112)]
    for step in range(1, DP):
        copy = remote(done_j, done_j, sem_jg, step - 1, {"dp": place.along_dp(step)})
        copy.start()
        last.append(copy)
    for part in sums_of_a:
        part.back()
    for copy in sums:
        copy.wait()
    value = inner[0]
    for index in range(1, MP):
        value = value + inner[index]
    gain_own[...] = pltpu.roll(value, (D - CH * me) % D, 1)[:, :OWN]
    gain_own[7:] = gain_grad[:1]
    for step in range(1, DP):
        copy = remote(gain_own, gain_dp.at[step - 1], sem_gd, step - 1, {"dp": place.along_dp(step)})
        copy.start()
        last.append(copy)
    value = jnp.concatenate([value[index : index + 1] for index in range(4)], axis=1)
    stream_grad = scaled * scaling - stream * (scaling * scaling * scaling * value / D)
    gx_ref[...] = stream_grad + gy1_ref[rows(me, CH), :].astype(F32)
    for part in sums_of_a:
        part.back_y()
    for copy in last:
        copy.wait()
    value = gain_own[...]
    for index in range(DP - 1):
        value = value + gain_dp[index]
    gain_sum[...] = value
    for copy in first + second + [share_q] + shares + [move_gz, move_gn] + o_first + t_first + j_first:
        copy.wait_send()
    gather_n3.close()
    gather_gy1.close()
    for part in (sum_of_b, *sums_of_a):
        part.close()


def second(*operands):
    return pl.pallas_call(
        second_kernel,
        out_shape=(
            jax.ShapeDtypeStruct((CH, T), F32),
            jax.ShapeDtypeStruct((DP * 112, D), BF16),
            jax.ShapeDtypeStruct((OWN, D), BF16),
            jax.ShapeDtypeStruct((3 * OWN, D), BF16),
            jax.ShapeDtypeStruct((3 * OWN, D), BF16),
            jax.ShapeDtypeStruct((8, OWN), F32),
        ),
        in_specs=[SMEM, VMEM, VMEM, ANY, VMEM, VMEM, VMEM, VMEM, ANY, ANY]
        + [VMEM] * 6
        + [ANY, ANY]
        + [VMEM] * 3
        + [ANY],
        out_specs=(VMEM,) * 6,
        scratch_shapes=[
            pltpu.VMEM((FEAT, T), BF16),
            pltpu.VMEM((2, 4, 3 * OWN, D), BF16),
            pltpu.VMEM((CHIPS, 2, OWN, D), BF16),
            pltpu.VMEM((D, T), BF16),
            pltpu.VMEM((FEAT, D), BF16),
            pltpu.VMEM((4, 3 * OWN, D), BF16),
            pltpu.VMEM((CH, D), BF16),
            pltpu.VMEM((HD, T), BF16),
            pltpu.VMEM((HD, T), BF16),
            pltpu.VMEM((T, 2 * HD), F32),
            pltpu.VMEM((2, HD, 512), BF16),
            pltpu.VMEM((CHIPS, 2, 3 * HD, OWN), BF16),
            pltpu.VMEM((CHIPS, 3 * HD, OWN), BF16),
            pltpu.VMEM((CHIPS, 3 * HD, OWN), BF16),
            pltpu.VMEM((CHIPS, 3 * HD, OWN), BF16),
            pltpu.VMEM((D, 2 * OWN), BF16),
            pltpu.VMEM((D, 2 * OWN), BF16),
            pltpu.VMEM((D, 2 * OWN), BF16),
            pltpu.VMEM((D, OWN), BF16),
            pltpu.VMEM((D, OWN), BF16),
            pltpu.VMEM((3, 2 * D, 2 * OWN), BF16),
            pltpu.VMEM((3, D, 2 * OWN), BF16),
            pltpu.VMEM((D, T), BF16),
            pltpu.VMEM((CHIPS, 96, OWN), BF16),
            pltpu.VMEM((96, T), BF16),
            pltpu.VMEM((MP - 1, CH, D), BF16),
            *sum_buffers(48, False),
            pltpu.VMEM((4, 3 * OWN, D), BF16),
            *sum_buffers(32, False),
            *sum_buffers(16, True),
            pltpu.VMEM((OWN, D), BF16),
            pltpu.VMEM((DP - 1, 16, D), BF16),
            pltpu.VMEM((D, OWN), F32),
            pltpu.VMEM((8, OWN), F32),
            pltpu.VMEM((DP - 1, 8, OWN), F32),
            pltpu.VMEM((K, T + 2 * OWN), F32),
            pltpu.VMEM((K // 2, T, 2 * OWN), BF16),
            pltpu.VMEM((K * CH, T), BF16),
            pltpu.VMEM((CH * T // (2 * OWN), T), BF16),
            pltpu.VMEM((CH * T // (2 * OWN), 2 * OWN), F32),
            pltpu.VMEM((CH, T), F32),
            pltpu.VMEM((FEAT, D), F32),
            pltpu.VMEM((DP * 112, D), BF16),
            pltpu.VMEM((DP - 1, 112, D), BF16),
            pltpu.VMEM((MP, 8, D), F32),
            sems(15), sems(1), sems(1), sems(15), sems(15), sems(1), sems(14), sems(14), sems(14), sems(7), sems(7),
            sems(7), sems(7), sems(7), sems(15), sems(3), sems(15),
            pltpu.SemaphoreType.DMA((6,)),
        ],
        compiler_params=pltpu.CompilerParams(
            collective_id=1, has_side_effects=True, vmem_limit_bytes=LIMIT
        ),
        name="second",
    )(*operands)


def final_kernel(
    joint_ref, t_ref, a_ref, b_ref, gain_ref, out_in, gx_in,
    out_ref, gx_ref, gws, gate_ga, up_ga, down_ga, gqkv, gout, gate_gb, up_gb, down_gb, *gain_grads,
):
    out_ref[...] = out_in[...]
    gx_ref[...] = gx_in[...]
    gws[...] = joint_ref[:FEAT].astype(F32)
    gqkv[...] = t_ref[: 3 * CH].astype(F32)
    gout[...] = t_ref[3 * CH :].astype(F32)
    for ref, (gate, up, down) in ((a_ref, (gate_ga, up_ga, down_ga)), (b_ref, (gate_gb, up_gb, down_gb))):
        gate[...] = ref[:OWN].astype(F32).T
        up[...] = ref[OWN : 2 * OWN].astype(F32).T
        down[...] = ref[2 * OWN :].astype(F32)
    for index, grad in enumerate(gain_grads):
        grad[...] = gain_ref[4 + index : 5 + index, :CH]


def final(*operands):
    mlp = [jax.ShapeDtypeStruct(shape, F32) for shape in ((D, OWN), (D, OWN), (OWN, D))]
    return pl.pallas_call(
        final_kernel,
        out_shape=(
            jax.ShapeDtypeStruct((CH, T), BF16),
            jax.ShapeDtypeStruct((CH, T), F32),
            jax.ShapeDtypeStruct((FEAT, D), F32),
            *mlp,
            jax.ShapeDtypeStruct((3 * CH, D), F32),
            jax.ShapeDtypeStruct((CH, D), F32),
            *mlp,
            *[jax.ShapeDtypeStruct((1, CH), F32)] * 4,
        ),
        in_specs=[VMEM] * 7,
        out_specs=(VMEM,) * 15,
        compiler_params=pltpu.CompilerParams(vmem_limit_bytes=LIMIT),
        name="final",
    )(*operands)


def on_device(
    inputs, out_grad, shape_pick, filters, stu_gain, stu_weight,
    mlp_gain_a, gate_a, up_a, down_a, attn_gain, qkv_weight, out_weight,
    mlp_gain_b, gate_b, up_b, down_b,
):
    gains = [gain.reshape(1, CH) for gain in (mlp_gain_a, attn_gain, mlp_gain_b, stu_gain)]
    weight = stu_weight.reshape(FEAT, D)
    x = inputs.T
    (
        gains_own, scaling, features, x1, x2, na, qkv, wa, wat, gains_all,
        lse, of, go_heads, gx3, out, n3, gwo, gmlp_b, ggain_b,
    ) = first(
        shape_pick, x, out_grad.T, *gains, filters, weight,
        gate_a, up_a, down_a, qkv_weight.T, out_weight, gate_b, up_b, down_b,
    )
    gx, joint, gat, ga, gb, gain_sum = second(
        shape_pick, x, scaling, features, x1, x2, na, qkv, wa, wat, gains_all,
        lse, of, go_heads, gx3, n3, gwo, gmlp_b, ggain_b, gains_own, filters, weight,
    )
    out, gx, gws, gate_ga, up_ga, down_ga, gqkv, gout, gate_gb, up_gb, down_gb, *gain_grads = final(
        joint, gat, ga, gb, gain_sum, out, gx
    )
    gain_a, gain_n, gain_b, gain_s = (grad.reshape(CH) for grad in gain_grads)
    return (
        out.T, gx.T, gain_s, gws.reshape(K + LAGS, CH, D), gain_a, gate_ga, up_ga, down_ga,
        gain_n, gqkv.T, gout, gain_b, gate_gb, up_gb, down_gb,
    )


def solution(mesh):
    cols, mid, row = P(None, "mp"), P(None, "mp", None), P("mp", None)
    return jax.shard_map(
        on_device,
        mesh=mesh,
        in_specs=(
            P("dp", "mp"), P("dp", "mp"), P("dp"), P(), P("mp"), mid,
            P("mp"), cols, cols, row, P("mp"), cols, row, P("mp"), cols, cols, row,
        ),
        out_specs=(
            P("dp", "mp"), P("dp", "mp"), P("mp"), mid, P("mp"), cols, cols, row,
            P("mp"), cols, row, P("mp"), cols, cols, row,
        ),
        check_vma=False,
    )
```

```python
import jax
import jax.numpy as jnp
from jax import lax
from jax.experimental import pallas as pl
from jax.experimental.pallas import tpu as pltpu
from jax.sharding import PartitionSpec as P

D = 512
T = 2048
OWN = 128
CH = 32
K = 24
LAGS = 3
FEAT = (K + LAGS) * CH
HD = 64
MP = 16
DP = 8
CHIPS = 8
EPSILON = 1e-05
NEG = -1e30
F32 = jnp.float32
BF16 = jnp.bfloat16
MESH = pl.DeviceIdType.MESH
VMEM = pl.BlockSpec(memory_space=pltpu.VMEM)
SMEM = pl.BlockSpec(memory_space=pltpu.SMEM)
ANY = pl.BlockSpec(memory_space=pl.ANY)
LIMIT = 62 * 2**20
EARLY_TABLES = 4


def nn(left, right):
    return jnp.dot(left, right, preferred_element_type=F32)


def tn(left, right):
    return lax.dot_general(left, right, (((0,), (0,)), ((), ())), preferred_element_type=F32)


def tn_narrow(weights, right):
    return tn(right, weights).T


def nt(left, right):
    return lax.dot_general(left, right, (((1,), (1,)), ((), ())), preferred_element_type=F32)


class Place:
    def __init__(self):
        self.me = lax.axis_index("mp")
        self.z = self.me // 4
        self.chip = self.me // 2
        self.y = self.chip % 2
        self.core = self.me % 2
        self.dp = lax.axis_index("dp")
        self.x = self.dp % 4
        self.ylo = self.dp // 4
        self.partner = self.me + 1 - 2 * self.core
        self.beside = self.me + 2 - 4 * self.y
        self.across = self.me + 4 - 8 * (self.z % 2)
        self.query_core = ((self.z + 1) // 2) % 2
        self.quarters = (self.core, 3 - self.core)

    def around(self, step):
        return (self.me + step) % MP

    def chip_at(self, step):
        return (self.chip + step) % CHIPS

    def same_units(self, slot):
        return ((self.z + 2 * (slot // 2)) % 4) * 4 + ((self.y + slot % 2) % 2) * 2 + self.core

    def along_z(self, step):
        return ((self.z + step) % 4) * 4 + self.me % 4

    def along_x(self, step):
        return {"dp": self.dp - self.x + (self.x + step) % 4}

    def along_dp(self, step):
        return (self.dp + step) % DP


def half(index):
    return pl.ds(pl.multiple_of(index * OWN, OWN), OWN)


def rows(index, count):
    return pl.ds(pl.multiple_of(index * count, count), count)


def remote(src, dst, sems, slot, target):
    return pltpu.make_async_remote_copy(
        src_ref=src,
        dst_ref=dst,
        send_sem=sems.at[0, slot],
        recv_sem=sems.at[1, slot],
        device_id=target if isinstance(target, dict) else {"mp": target},
        device_id_type=MESH,
    )


def greet(targets):
    barrier = pltpu.get_barrier_semaphore()
    for target in targets:
        where = target if isinstance(target, dict) else {"mp": target}
        pl.semaphore_signal(barrier, inc=1, device_id=where, device_id_type=MESH)
    return lambda: pl.semaphore_wait(barrier, len(targets))


def sems(count):
    return pltpu.SemaphoreType.DMA((2, count))


def norm_forward(stream, gain):
    scaling = lax.rsqrt(jnp.sum(stream * stream, axis=0, keepdims=True) / D + EPSILON)
    return stream * scaling * gain, scaling


def norm_backward(upstream, stream, gain):
    scaling = lax.rsqrt(jnp.sum(stream * stream, axis=0, keepdims=True) / D + EPSILON)
    gain_grad = jnp.sum(upstream * stream * scaling, axis=1, keepdims=True)
    scaled = upstream * gain
    inner = jnp.sum(scaled * stream, axis=0, keepdims=True)
    return scaled * scaling - stream * (scaling * scaling * scaling * inner / D), gain_grad


def swap(place, src, dst, sem, slot=0):
    copy = remote(src, dst, sem, slot, place.across)
    copy.start()
    return copy


def share(place, src, dst, sem, slot):
    copy = remote(src, dst, sem, slot, place.partner)
    copy.start()
    return copy


def hidden_weights(ref):
    return [ref[:, :, group * OWN : (group + 1) * OWN].reshape(2 * D, D) for group in range(3)]


def hidden_backward(weights, normed, grad, acts, where):
    w_gate, w_up, w_down = weights
    gate = nn(w_gate, normed)
    up = nn(w_up, normed)
    sig = jax.nn.sigmoid(gate)
    hidden_grad = nn(w_down, grad)
    gate_grad = (hidden_grad * up * sig * (1.0 + gate * (1.0 - sig))).astype(BF16)
    up_grad = (hidden_grad * gate * sig).astype(BF16)
    acts[0, :, where] = gate_grad
    acts[1, :, where] = up_grad
    acts[2, :, where] = (gate * sig * up).astype(BF16)
    return (tn(gate_grad, w_gate) + tn(up_grad, w_up)).T


def hidden_weight_grads(acts, acts_got, inputs, out):
    for group, (right, right_got) in enumerate(inputs):
        value = (nt(acts[group, :D], right[...]) + nt(acts_got[group], right_got[...])).astype(BF16)
        for index in range(4):
            out[index, group * OWN : (group + 1) * OWN] = value[index * OWN : (index + 1) * OWN]


class Gather:
    steps = (1, 3, 2)

    def __init__(self, place, buf, sem):
        me = place.me
        own = buf.at[:, half(me)]
        beside = buf.at[:, half(place.beside)]
        self.to_beside = remote(own, own, sem, 0, place.beside)
        self.to_z = [remote(own, own, sem, step, place.along_z(step)) for step in self.steps]
        farthest = buf.at[:, half(((place.z + 2) % 4) * 4 + me % 4)]
        self.relays = [remote(beside, beside, sem, 3 + step, place.along_z(step)) for step in self.steps[:2]]
        self.relays.append(remote(farthest, farthest, sem, 5, place.beside))
        self.forwards = [remote(own, own, sem, 7, place.partner), remote(beside, beside, sem, 8, place.partner)]
        for step in self.steps:
            for shift, other in ((8, me), (11, place.beside)):
                index = ((place.z + 4 - step) % 4) * 4 + other % 4
                here = buf.at[:, half(index)]
                self.forwards.append(remote(here, here, sem, shift + step, place.partner))

    def begin(self):
        for copy in [self.to_beside, *self.to_z, self.forwards[0]]:
            copy.start()

    def relay(self):
        self.to_beside.wait_recv()
        for copy in [*self.relays[:2], self.forwards[1]]:
            copy.start()

    def cross(self):
        self.to_z[2].wait_recv()
        self.relays[2].start()
        self.forwards[6].start()

    def arrive(self, index):
        if index < 2:
            self.to_z[index].wait_recv()
            self.forwards[2 + 2 * index].start()
        self.relays[index].wait_recv()
        self.forwards[3 + 2 * index].start()

    def joined(self, index):
        for copy in self.forwards[2 + 2 * index : 4 + 2 * index]:
            copy.wait_recv()

    def close(self):
        for copy in [self.to_beside, *self.to_z, *self.relays, *self.forwards]:
            copy.wait_send()


def toeplitz(taps):
    wide = pltpu.roll(jnp.broadcast_to(taps, (OWN, T)), 0, 1, stride=1, stride_axis=0)
    lane = lax.broadcasted_iota(jnp.int32, (OWN, OWN), 1)
    row = lax.broadcasted_iota(jnp.int32, (OWN, OWN), 0)
    first = jnp.where(lane >= row, wide[:, :OWN], 0.0)
    return jnp.concatenate([first.astype(BF16), wide[:, OWN:].astype(BF16)], axis=1)


def reverse_taps(taps_ref, reverse):
    row = lax.broadcasted_iota(jnp.int32, (2 * OWN, OWN), 0)
    lane = lax.broadcasted_iota(jnp.int32, (2 * OWN, OWN), 1)
    inside = (lane >= 1) & (row == OWN - lane)
    edge = (lane == 0) & (row == OWN)
    flip = jnp.where(inside | edge, 1.0, 0.0).astype(BF16)
    for index in range(T // OWN):
        begin = T - (index + 1) * OWN
        piece = taps_ref[:, begin : begin + min(2 * OWN, T - begin)]
        reverse[:, index * OWN : (index + 1) * OWN] = nn(piece, flip[: piece.shape[1]])
    reverse[:, T : T + OWN] = nn(taps_ref[:, :OWN], flip[OWN:])
    reverse[:, T + OWN :] = jnp.zeros((K, OWN), F32)


def toeplitz_down(reverse, store):
    wide = pltpu.roll(jnp.broadcast_to(reverse, (OWN, T + 2 * OWN)), 0, 1, stride=1, stride_axis=0).astype(BF16)
    for block in range(T // OWN):
        begin = T - block * OWN
        store(block, wide[:, begin : begin + 2 * OWN])


def lag_mask(shift, pick):
    lane = lax.broadcasted_iota(jnp.int32, (CH, T), 1)
    inner = lane % (T // 2)
    return (lane >= shift) & ((inner >= shift) | (pick == 1))


def spread(qkv_ref, keys, values):
    for index in range(MP):
        keys[:, index * OWN : (index + 1) * OWN] = qkv_ref[index, HD : 2 * HD]
        values[:, index * OWN : (index + 1) * OWN] = qkv_ref[index, 2 * HD :]


def query_block(qkv_ref, quarter):
    parts = [qkv_ref[quarter * 4 + index, :HD] for index in range(4)]
    return jnp.concatenate(parts, axis=1) * jnp.asarray(HD**-0.5, BF16)


def score_mask(quarter, chunk, pick):
    query = quarter * 512 + lax.broadcasted_iota(jnp.int32, (512, 512), 1)
    key = chunk * 512 + lax.broadcasted_iota(jnp.int32, (512, 512), 0)
    same_half = (quarter // 2) == (chunk // 2)
    return (key <= query) & (same_half | (pick == 1))


class GradientSum:
    def __init__(self, place, parts, done, bufs, sem, begin, each, y_first, source=None):
        self.place, self.parts, self.done, self.sem = place, parts, done, sem
        self.source = parts if source is None else source
        self.got, self.sum_1, self.got_2, self.sum_2, self.z_got = bufs
        self.begin, self.each, self.y_first = begin, each, y_first
        self.copies = []
        self.to_y = [(1 - place.ylo, {"dp": place.dp + 4 - 8 * place.ylo})]
        self.to_x = [((place.x + step) % 4, place.along_x(step)) for step in range(1, 4)]

    def at(self, index, count, begin=0):
        return pl.ds(pl.multiple_of(begin + index * count, 16), count)

    def send(self, src, dst, target):
        copy = remote(src, dst, self.sem, len(self.copies), target)
        copy.start()
        self.copies.append(copy)

    def arrived(self, count):
        for copy in self.copies[-count:]:
            copy.wait_recv()

    def first(self):
        count = self.each * (4 if self.y_first else 2)
        for slot, (there, target) in enumerate(self.to_y if self.y_first else self.to_x):
            self.send(self.source.at[:, self.at(there, count, self.begin)], self.got.at[slot], target)

    def second(self):
        place, each = self.place, self.each
        here, peers, count = (place.ylo, 1, each * 4) if self.y_first else (place.x, 3, each * 2)
        self.arrived(peers)
        value = self.parts[:, self.at(here, count, self.begin)].astype(F32)
        for slot in range(peers):
            value = value + self.got[slot].astype(F32)
        self.sum_1[...] = value.astype(BF16)
        for slot, (there, target) in enumerate(self.to_x if self.y_first else self.to_y):
            self.send(self.sum_1.at[:, self.at(there, each)], self.got_2.at[slot], target)

    def third(self):
        place, each = self.place, self.each
        here, peers = (place.x, 3) if self.y_first else (place.ylo, 1)
        self.arrived(peers)
        value = self.sum_1[:, self.at(here, each)].astype(F32)
        for slot in range(peers):
            value = value + self.got_2[slot].astype(F32)
        self.sum_2[...] = value.astype(BF16)
        for step in range(1, 4):
            self.send(self.sum_2.at[step], self.z_got.at[step - 1], place.same_units(step))

    def back(self):
        place, each = self.place, self.each
        self.arrived(3)
        value = self.sum_2[0].astype(F32)
        for slot in range(3):
            value = value + self.z_got[slot].astype(F32)
        index = place.ylo * 4 + place.x if self.y_first else place.x * 2 + place.ylo
        mine = self.at(index, each, self.begin)
        self.done[mine, :] = value.astype(BF16)
        for _, target in self.to_x:
            self.send(self.done.at[mine], self.done.at[mine], target)

    def back_y(self):
        place, each = self.place, self.each
        self.arrived(3)
        for x in range(4):
            index = place.ylo * 4 + x if self.y_first else x * 2 + place.ylo
            part = self.done.at[self.at(index, each, self.begin)]
            self.send(part, part, self.to_y[0][1])

    def close(self):
        self.arrived(4)
        for copy in self.copies:
            copy.wait_send()


def sum_buffers(each, y_first):
    first, second = (1, 3) if y_first else (3, 1)
    wide = each * (4 if y_first else 2)
    return [
        pltpu.VMEM((first, 4, wide, D), BF16),
        pltpu.VMEM((4, wide, D), BF16),
        pltpu.VMEM((second, 4, each, D), BF16),
        pltpu.VMEM((4, each, D), BF16),
        pltpu.VMEM((3, each, D), BF16),
    ]


def first_kernel(
    pick_ref, x_ref, go_ref, gain_a, gain_n, gain_b_in, gain_s, taps_ref, weight_ref,
    gate_a, up_a, down_a, qkv_w, out_w, gate_b, up_b, down_b,
    gains_ref, scale_ref, feat_out, x1_ref, x2_ref, na_out, qkv_out, wa_out, wat_out, gains_all,
    lse_ref, of_ref, go_heads, gx3_ref, out_ref, n3_ref, gwo_ref, gmlp_ref, ggain_ref,
    feat_ref, na_ref, qkv_ref, wa_ref, wat_ref, streams, streams_own, go2, squares, taps, table, table_late, weight_t, blocks, y_ref,
    core_got, chip_got, parts, got, heads, wb_ref, keys, values, own_heads, all_heads, x3_ref, nb, nb_got, go_got,
    acts, acts_got, parts_n, got_n, parts_z, got_z, grad_heads, out_own,
    sem_s, sem_x, sem_wa, sem_wb, sem_wat, sem_y, sem_n, sem_g, sem_z, sem_q,
    sem_o, sem_nb, sem_gn, sem_zb, sem_h, sem_out, sem_act, sem_save,
):
    place = Place()
    me, chip, core, x = place.me, place.chip, place.core, place.x
    count = T // OWN
    pick = pick_ref[0]
    wat_ref[chip, core, : 3 * CH] = qkv_w[...]
    wat_ref[chip, core, 3 * CH :] = out_w[...]
    arrived = greet(
        [place.around(step) for step in range(1, MP)] + [place.along_x(step) for step in range(1, 4)]
    )
    stream = x_ref[...].astype(F32)
    squares[pl.ds(me, 1)] = jnp.sum(stream * stream, axis=0, keepdims=True)[None]
    for ref, (gate, up, down) in ((wa_ref, (gate_a, up_a, down_a)), (wb_ref, (gate_b, up_b, down_b))):
        ref[0, 0, :OWN] = gate[...].T
        ref[0, 0, OWN : 2 * OWN] = up[...].T
        ref[0, 0, 2 * OWN :] = down[...]
    lines = [ref[...].astype(F32) for ref in (gain_a, gain_n, gain_b_in, gain_s)]
    lines = jnp.concatenate(lines + [jnp.zeros((OWN - 4, CH), F32)], axis=0)
    lines = jnp.concatenate([lines, jnp.zeros((OWN, OWN - CH), F32)], axis=1)
    gains_ref[...] = lines.T[:CH].astype(BF16)
    streams[0] = x_ref[...]
    streams[1] = go_ref[...]
    for index in range(MP):
        streams[2, :, index * OWN : (index + 1) * OWN] = gains_ref[...]
    streams_own[:, rows(me, CH)] = streams[:, :, half(me)]
    taps[...] = taps_ref[...].astype(F32)

    def build(step, table, shift=0):
        for index in range(2):
            filter_table = toeplitz(taps[pl.ds((step + shift) * 2 + index, 1), :])
            for offset in range(count):
                table[step, offset * OWN : (offset + 1) * OWN, index * OWN : (index + 1) * OWN] = filter_table[
                    :, offset * OWN : (offset + 1) * OWN
                ]

    build_early = lambda step: build(step, table)
    pl.loop(0, EARLY_TABLES)(build_early)
    arrived()
    sums, late, fetch_a, fetch_b, fetch_t, rest_a, rest_b, rest_t = [], [], [], [], [], [], [], []
    for step in range(1, MP):
        there = place.around(step)
        copy = remote(squares.at[me], squares.at[me], sem_s, step - 1, there)
        copy.start()
        sums.append(copy)
    for step in range(1, 4):
        copy = remote(
            wa_ref.at[0, 0, rows(x, 96)], wa_ref.at[0, step, rows(x, 96)], sem_wa, step - 1, place.same_units(step)
        )
        copy.start()
        fetch_a.append(copy)
    mine_t = wat_ref.at[chip, core, rows(x, CH)]
    for step in range(1, CHIPS):
        copy = remote(mine_t, mine_t, sem_wat, step - 1, place.chip_at(step) * 2 + core)
        copy.start()
        fetch_t.append(copy)
    for step in range(1, MP):
        there = place.around(step)
        copy = remote(
            streams.at[:, :, half(there)], streams_own.at[:, rows(me, CH)], sem_x, step - 1, there
        )
        copy.start()
        late.append(copy)
    for step in range(1, 4):
        copy = remote(
            wb_ref.at[0, 0, rows(x, 96)], wb_ref.at[0, step, rows(x, 96)], sem_wb, step - 1, place.same_units(step)
        )
        copy.start()
        fetch_b.append(copy)
    share_a = [share(place, wa_ref.at[0, 0], wa_ref.at[1, 0], sem_wa, 6)]
    share_b = [share(place, wb_ref.at[0, 0], wb_ref.at[1, 0], sem_wb, 6)]
    weight_t[...] = weight_ref[...].T
    pl.loop(EARLY_TABLES, K // 4)(build_early)
    for copy in sums:
        copy.wait()
    total = squares[0]
    for index in range(1, MP):
        total = total + squares[index]
    scaling = lax.rsqrt(total / D + EPSILON)
    scale_ref[...] = scaling
    own = stream * scaling * gains_ref[:, 3:4].astype(F32)
    h = own.astype(BF16)
    own = h.astype(F32)
    joined = jnp.full((CH, OWN), (pick == 1).astype(F32)).astype(BF16)
    for target in range(count):
        for offset in range(count):
            here = (slice(target * CH, (target + 1) * CH), slice(offset * OWN, (offset + 1) * OWN))
            if offset > target:
                blocks[here] = jnp.zeros((CH, OWN), BF16)
                continue
            source = target - offset
            value = h[:, source * OWN : (source + 1) * OWN]
            if target >= count // 2 and source < count // 2:
                value = value * joined
            blocks[here] = value
    for shift in range(LAGS):
        moved = own if shift == 0 else pltpu.roll(own, shift, 1)
        moved = jnp.where(lag_mask(shift, pick), moved, 0.0).astype(BF16)
        feat_ref[(K + shift) * CH : (K + shift + 1) * CH, :] = moved

    def convolve(step, table, shift=0):
        early = nn(blocks[: CH * count // 2, : T // 2], table[step, : T // 2, :]).astype(BF16)
        late_half = nn(blocks[CH * count // 2 :, :], table[step]).astype(BF16)
        for index in range(2):
            base = pl.multiple_of(((step + shift) * 2 + index) * CH, CH)
            for target in range(count):
                part, at = (early, target) if target < count // 2 else (late_half, target - count // 2)
                feat_ref[pl.ds(base, CH), target * OWN : (target + 1) * OWN] = part[
                    at * CH : (at + 1) * CH, index * OWN : (index + 1) * OWN
                ]


    def pass_on(fetched, source, sem, done, rest):
        for copy in fetched:
            copy.wait_recv()
        for step in range(1, 4):
            copy = remote(source, source, sem, done + step - 1, place.along_x(step))
            copy.start()
            rest.append(copy)

    @pl.loop(0, K // 4)
    def _(step):
        build(step, table_late, K // 4)
        convolve(step, table)

    pass_on(fetch_a, wa_ref.at[0, 1:4, rows(x, 96)], sem_wa, 3, rest_a)

    @pl.loop(0, K // 4)
    def _(step):
        convolve(step, table_late, K // 4)

    saves = []

    def save(src, dst):
        copy = pltpu.make_async_copy(src, dst, sem_save.at[len(saves)])
        copy.start()
        saves.append(copy)

    save(feat_ref, feat_out)
    for group in range(4):
        y = nn(weight_t[...], feat_ref[:, group * 512 : (group + 1) * 512]).astype(BF16)
        for index in range(4):
            y_ref[group * 2 + index // 2, index % 2] = y[:, index * OWN : (index + 1) * OWN]
    order = list(range(1, CHIPS)) + [0]
    first, second = [], []
    for step in order:
        there = place.chip_at(step)
        copy = remote(y_ref.at[there, 1 - core], core_got.at[there], sem_y, step, place.partner)
        copy.start()
        first.append(copy)
    for copy, step in zip(first, order):
        there = place.chip_at(step)
        copy.wait_recv()
        total = y_ref[there, core].astype(F32) + core_got[there].astype(F32)
        if step == 0:
            x1_ref[...] = total
        else:
            y_ref[there, core] = total.astype(BF16)
            move = remote(y_ref.at[there, core], chip_got.at[step - 1], sem_y, 7 + step, there * 2 + core)
            move.start()
            second.append(move)
    pass_on(fetch_t, wat_ref.at[:, core, rows(x, CH)], sem_wat, 7, rest_t)
    for copy in late:
        copy.wait()
    go2[:, :OWN] = streams_own[1]
    move_go = swap(place, go2.at[:, :OWN], go2.at[:, OWN:], sem_g)
    gains_all[...] = streams_own[2]
    for copy in rest_a:
        copy.wait_recv()
    share_a.append(share(place, wa_ref.at[0, 1:], wa_ref.at[1, 1:], sem_wa, 7))
    for move in second:
        move.wait_recv()
    x1 = x1_ref[...] + streams_own[0].astype(F32)
    for index in range(CHIPS - 1):
        x1 = x1 + chip_got[index].astype(F32)
    x1_ref[...] = x1
    normed, _ = norm_forward(x1, gains_all[:, 0:1].astype(F32))
    na_ref[:, :OWN] = normed.astype(BF16)
    move_n = swap(place, na_ref.at[:, :OWN], na_ref.at[:, OWN:], sem_n)
    for copy in share_a:
        copy.wait_recv()
    save(wa_ref, wa_out)
    w_gate, w_up, w_down = hidden_weights(wa_ref)

    def forward(normed):
        gate = nn(w_gate, normed)
        hidden = (gate * jax.nn.sigmoid(gate) * nn(w_up, normed)).astype(BF16)
        return tn_narrow(w_down, hidden)

    z = forward(na_ref[:, :OWN])
    pass_on(fetch_b, wb_ref.at[0, 1:4, rows(x, 96)], sem_wb, 3, rest_b)
    move_n.wait_recv()
    parts[...] = forward(na_ref[:, OWN:]).astype(BF16)
    move_z = swap(place, parts, got, sem_z)
    save(na_ref, na_out)
    for copy in rest_t:
        copy.wait_recv()
    half_t = wat_ref.at[:, core]
    share_t = share(place, half_t, half_t, sem_wat, 10)
    move_z.wait_recv()
    x2 = x1 + z + got[...].astype(F32)
    x2_ref[...] = x2
    n3 = norm_forward(x2, gains_all[:, 1:2].astype(F32))[0].astype(BF16)
    n3_ref[...] = n3
    share_t.wait_recv()
    save(wat_ref, wat_out)
    w_qkv = wat_ref[:, :, : 3 * CH].reshape(3 * D, D)
    heads[...] = nn(w_qkv, n3).astype(BF16).reshape(CHIPS, 3 * HD, OWN)
    sends = []
    for step in range(1, CHIPS):
        there = place.chip_at(step)
        copy = remote(heads.at[there], qkv_ref.at[me], sem_q, step - 1, there * 2 + core)
        copy.start()
        sends.append(copy)
    qkv_ref[me] = heads[chip]
    forwards = [remote(qkv_ref.at[me], qkv_ref.at[me], sem_q, 7, place.partner)]
    forwards[0].start()
    for step in range(1, CHIPS):
        source = place.chip_at(CHIPS - step) * 2 + core
        sends[step - 1].wait_recv()
        copy = remote(qkv_ref.at[source], qkv_ref.at[source], sem_q, 7 + step, place.partner)
        copy.start()
        forwards.append(copy)
    for copy in forwards:
        copy.wait()
    save(qkv_ref, qkv_out)
    for copy in rest_b:
        copy.wait_recv()
    share_b.append(share(place, wb_ref.at[0, 1:], wb_ref.at[1, 1:], sem_wb, 7))
    for copy in fetch_a + fetch_b + fetch_t + rest_a + rest_t + share_a + [share_t] + first + second + sends:
        copy.wait_send()
    move_n.wait_send()
    move_z.wait_send()
    spread(qkv_ref, keys, values)
    targets = [place.quarters[slot // 4] * 4 + slot % 4 for slot in range(8)]
    copies = [
        pltpu.make_async_remote_copy(
            src_ref=own_heads.at[slot], dst_ref=all_heads.at[chip],
            send_sem=sem_o.at[0, slot], recv_sem=sem_o.at[1, chip],
            device_id={"mp": targets[slot]}, device_id_type=MESH,
        )
        for slot in range(8)
    ]
    for part in range(2):
        quarter = place.quarters[part]
        queries = query_block(qkv_ref, quarter)
        top = jnp.full((1, 512), NEG, F32)
        norm = jnp.zeros((1, 512), F32)
        total = jnp.zeros((HD, 512), F32)
        for chunk in range(2 + 2 * part):
            here = slice(chunk * 512, (chunk + 1) * 512)
            scores = jnp.where(score_mask(quarter, chunk, pick), tn(keys[:, here], queries), NEG)
            new_top = jnp.maximum(top, jnp.max(scores, axis=0, keepdims=True))
            weights = jnp.exp(scores - new_top)
            rescale = jnp.exp(top - new_top)
            norm = norm * rescale + jnp.sum(weights, axis=0, keepdims=True)
            total = total * rescale + nn(values[:, here], weights.astype(BF16))
            top = new_top
        total = total / norm
        lse_ref[part] = top + jnp.log(norm)
        of_ref[part] = total
        for index in range(4):
            own_heads[part * 4 + index] = total[:, index * OWN : (index + 1) * OWN].astype(BF16)
        for slot in range(part * 4, part * 4 + 4):
            pl.when(targets[slot] != me)(copies[slot].start)

            @pl.when(targets[slot] == me)
            def _():
                all_heads[chip] = own_heads[slot]
    arrivals = [
        remote(own_heads.at[0], all_heads.at[head], sem_o, head, place.partner) for head in range(CHIPS)
    ]
    for head in range(CHIPS):
        pl.when(head * 2 + place.query_core != me)(arrivals[head].wait_recv)
    w_out = wat_ref[:, :, 3 * CH :].reshape(D, D)
    outputs = all_heads[...].reshape(D, OWN)
    x3 = x2 + tn_narrow(w_out, outputs)
    x3_ref[...] = x3
    gain_b = gains_all[:, 2:3].astype(F32)
    nb[:, :OWN] = norm_forward(x3, gain_b)[0].astype(BF16)
    move_n = swap(place, nb.at[:, :OWN], nb.at[:, OWN:], sem_nb)
    for copy in share_b + [move_go]:
        copy.wait_recv()
    weights = hidden_weights(wb_ref)
    normed_grad = hidden_backward(weights, nb[:, :OWN], go2[:, :OWN], acts, slice(0, OWN))
    move_n.wait_recv()
    parts_n[...] = hidden_backward(
        weights, nb[:, OWN:], go2[:, OWN:], acts, slice(OWN, 2 * OWN)
    ).astype(BF16)
    move_gn = swap(place, parts_n, got_n, sem_gn)
    shares = [
        share(place, acts.at[:, D:], acts_got, sem_act, 0),
        share(place, nb, nb_got, sem_act, 1),
        share(place, go2, go_got, sem_act, 2),
    ]
    parts_z[...] = tn_narrow(weights[2], acts[2, :, OWN:]).astype(BF16)
    move_z = swap(place, parts_z, got_z, sem_zb)
    z = tn_narrow(weights[2], acts[2, :, :OWN])
    move_gn.wait_recv()
    normed_grad = normed_grad + got_n[...].astype(F32)
    stream_grad, gain_grad = norm_backward(normed_grad, x3_ref[...], gain_b)
    ggain_ref[...] = gain_grad
    gx3 = go2[:, :OWN].astype(F32) + stream_grad
    gx3_ref[...] = gx3
    gy = gx3.astype(BF16)
    grad_heads[...] = nn(w_out, gy).astype(BF16).reshape(CHIPS, HD, OWN)
    slot = (place.z // 2) * 4 + me % 4
    sends = [
        pltpu.make_async_remote_copy(
            src_ref=grad_heads.at[head], dst_ref=go_heads.at[slot],
            send_sem=sem_h.at[0, head], recv_sem=sem_h.at[1, slot],
            device_id={"mp": head * 2 + place.query_core}, device_id_type=MESH,
        )
        for head in range(CHIPS)
    ]
    for head in range(CHIPS):
        pl.when(head * 2 + place.query_core != me)(sends[head].start)

        @pl.when(head * 2 + place.query_core == me)
        def _():
            go_heads[slot] = grad_heads[head]

    move_z.wait_recv()
    out_own[...] = (x3_ref[...] + z + got_z[...].astype(F32)).astype(BF16)
    moves = []
    for step in range(1, MP):
        there = place.around(step)
        copy = remote(out_own.at[rows(there, CH)], out_ref.at[:, half(me)], sem_out, step - 1, there)
        copy.start()
        moves.append(copy)
    out_ref[:, half(me)] = out_own[rows(me, CH), :]
    gwo_ref[...] = nt(outputs, gy).astype(BF16).reshape(MP, CH, D)
    for copy in shares:
        copy.wait_recv()
    hidden_weight_grads(acts, acts_got, ((nb, nb_got), (nb, nb_got), (go2, go_got)), gmlp_ref)
    for slot_in in range(8):
        arrival = remote(grad_heads.at[0], go_heads.at[slot_in], sem_h, slot_in, place.partner)
        pl.when(targets[slot_in] != me)(arrival.wait_recv)
    for slot_out in range(8):
        pl.when(targets[slot_out] != me)(copies[slot_out].wait_send)
        pl.when(slot_out * 2 + place.query_core != me)(sends[slot_out].wait_send)
    for copy in moves:
        copy.wait()
    for copy in rest_b + share_b + shares + [move_go, move_n, move_gn, move_z]:
        copy.wait_send()
    for copy in saves:
        copy.wait()


def first(*operands):
    return pl.pallas_call(
        first_kernel,
        out_shape=(
            jax.ShapeDtypeStruct((CH, OWN), BF16),
            jax.ShapeDtypeStruct((1, T), F32),
            jax.ShapeDtypeStruct((FEAT, T), BF16),
            jax.ShapeDtypeStruct((D, OWN), F32),
            jax.ShapeDtypeStruct((D, OWN), F32),
            jax.ShapeDtypeStruct((D, 2 * OWN), BF16),
            jax.ShapeDtypeStruct((MP, 3 * HD, OWN), BF16),
            jax.ShapeDtypeStruct((2, 4, 3 * OWN, D), BF16),
            jax.ShapeDtypeStruct((CHIPS, 2, OWN, D), BF16),
            jax.ShapeDtypeStruct((D, OWN), BF16),
            jax.ShapeDtypeStruct((2, 1, 512), F32),
            jax.ShapeDtypeStruct((2, HD, 512), F32),
            jax.ShapeDtypeStruct((8, HD, OWN), BF16),
            jax.ShapeDtypeStruct((D, OWN), F32),
            jax.ShapeDtypeStruct((CH, T), BF16),
            jax.ShapeDtypeStruct((D, OWN), BF16),
            jax.ShapeDtypeStruct((MP, CH, D), BF16),
            jax.ShapeDtypeStruct((4, 3 * OWN, D), BF16),
            jax.ShapeDtypeStruct((D, 1), F32),
        ),
        in_specs=[SMEM] + [VMEM] * 16,
        out_specs=(VMEM, VMEM, ANY, VMEM, VMEM, ANY, ANY, ANY, ANY) + (VMEM,) * 10,
        scratch_shapes=[
            pltpu.VMEM((FEAT, T), BF16),
            pltpu.VMEM((D, 2 * OWN), BF16),
            pltpu.VMEM((MP, 3 * HD, OWN), BF16),
            pltpu.VMEM((2, 4, 3 * OWN, D), BF16),
            pltpu.VMEM((CHIPS, 2, OWN, D), BF16),
            pltpu.VMEM((3, CH, T), BF16),
            pltpu.VMEM((3, D, OWN), BF16),
            pltpu.VMEM((D, 2 * OWN), BF16),
            pltpu.VMEM((MP, 1, T), F32),
            pltpu.VMEM((K, T), F32),
            pltpu.VMEM((K // 4, T, 2 * OWN), BF16),
            pltpu.VMEM((K // 4, T, 2 * OWN), BF16),
            pltpu.VMEM((D, FEAT), BF16),
            pltpu.VMEM((CH * T // OWN, T), BF16),
            pltpu.VMEM((CHIPS, 2, D, OWN), BF16),
            pltpu.VMEM((CHIPS, D, OWN), BF16),
            pltpu.VMEM((CHIPS - 1, D, OWN), BF16),
            pltpu.VMEM((D, OWN), BF16),
            pltpu.VMEM((D, OWN), BF16),
            pltpu.VMEM((CHIPS, 3 * HD, OWN), BF16),
            pltpu.VMEM((2, 4, 3 * OWN, D), BF16),
            pltpu.VMEM((HD, T), BF16),
            pltpu.VMEM((HD, T), BF16),
            pltpu.VMEM((8, HD, OWN), BF16),
            pltpu.VMEM((8, HD, OWN), BF16),
            pltpu.VMEM((D, OWN), F32),
            pltpu.VMEM((D, 2 * OWN), BF16),
            pltpu.VMEM((D, 2 * OWN), BF16),
            pltpu.VMEM((D, 2 * OWN), BF16),
            pltpu.VMEM((3, 2 * D, 2 * OWN), BF16),
            pltpu.VMEM((3, D, 2 * OWN), BF16),
            pltpu.VMEM((D, OWN), BF16),
            pltpu.VMEM((D, OWN), BF16),
            pltpu.VMEM((D, OWN), BF16),
            pltpu.VMEM((D, OWN), BF16),
            pltpu.VMEM((CHIPS, HD, OWN), BF16),
            pltpu.VMEM((D, OWN), BF16),
            sems(15), sems(15), sems(8), sems(8), sems(11),
            sems(15), sems(1), sems(1), sems(1), sems(15),
            sems(8), sems(1), sems(1), sems(1), sems(8), sems(15), sems(3),
            pltpu.SemaphoreType.DMA((5,)),
        ],
        compiler_params=pltpu.CompilerParams(
            collective_id=0, has_side_effects=True, vmem_limit_bytes=LIMIT
        ),
        name="first",
    )(*operands)


def second_kernel(
    pick_ref, x_ref, scale_ref, feat_in, x1_ref, x2_ref, na_ref, qkv_ref, wa_in, wat_in, gains_all,
    lse_ref, of_ref, go_heads, gx3_ref, n3_ref, gwo_in, gmlp_in, ggain_b, gains_ref, taps_ref, weight_in,
    gx_ref, joint_ref, sum_t, sum_a, sum_b, gain_sum,
    feat_ref, wa_ref, wat_ref, n3_all, weight_ref, gmlp_b, gwo_own,
    keys, values, kv_grad, q_grad, mine, core_got, chip_sum, head_grads, gz, gz_got, na_got, parts, got,
    acts, acts_got, gy1_ref, row_got, q_rows, gwo_got,
    b_1, b_2, b_3, b_4, b_5, gmlp_a, a_1, a_2, a_3, a_4, a_5, a_6, a_7, a_8, a_9, a_10, gat, gat_got, ggain_ref, gain_own, gain_dp,
    reverse, table, feature_grad, shifted, total, gh_ref, joint_sum, joint, joint_got, inner,
    sem_q, sem_n, sem_z, sem_y, sem_gwo, sem_rows, sem_b, sem_a, sem_a2, sem_t, sem_tg, sem_gd, sem_j, sem_jg, sem_p, sem_act, sem_all, sem_load,
):
    place = Place()
    me, dp, chip, core = place.me, place.dp, place.chip, place.core
    wide = 2 * OWN
    count = T // wide
    n3_all[:, half(me)] = n3_ref[...]
    loads = []
    for src, dst in (
        (wat_in, wat_ref), (wa_in, wa_ref), (feat_in, feat_ref), (weight_in, weight_ref),
        (gmlp_in, gmlp_b), (gwo_in.at[me], gwo_own),
    ):
        copy = pltpu.make_async_copy(src, dst, sem_load.at[len(loads)])
        copy.start()
        loads.append(copy)
    arrived = greet(
        [place.around(step) for step in range(1, MP)]
        + [{"dp": place.along_dp(step)} for step in range(1, DP)]
    )
    gain_a = gains_all[:, 0:1].astype(F32)
    gain_n = gains_all[:, 1:2].astype(F32)
    sum_of_b = GradientSum(place, gmlp_b, sum_b, (b_1, b_2, b_3, b_4, b_5), sem_b, 0, 48, False, gmlp_in)
    sums_of_a = (
        GradientSum(place, gmlp_a, sum_a, (a_1, a_2, a_3, a_4, a_5), sem_a, 0, 32, False),
        GradientSum(place, gmlp_a, sum_a, (a_6, a_7, a_8, a_9, a_10), sem_a2, 256, 16, True),
    )
    pick = pick_ref[0]
    spread(qkv_ref, keys, values)
    arrived()
    gather_n3 = Gather(place, n3_all, sem_all)
    gather_n3.begin()
    share_n = share(place, na_ref, na_got, sem_act, 0)
    sum_of_b.first()
    o_first = []
    for step in range(1, MP):
        there = place.around(step)
        copy = remote(gwo_in.at[there], gwo_got.at[step - 1], sem_gwo, step - 1, there)
        copy.start()
        o_first.append(copy)
    for part in range(2):
        quarter = place.quarters[part]
        queries = query_block(qkv_ref, quarter)
        out_grad = jnp.concatenate([go_heads[part * 4 + index] for index in range(4)], axis=1)
        weighted = jnp.sum(of_ref[part] * out_grad.astype(F32), axis=0, keepdims=True)
        queries_t = queries.T
        out_grad_t = out_grad.T
        query_grad = jnp.zeros((HD, 512), F32)
        for chunk in range(2 + 2 * part):
            here = slice(chunk * 512, (chunk + 1) * 512)
            scores = tn(keys[:, here], queries) - lse_ref[part]
            probs = jnp.where(score_mask(quarter, chunk, pick), jnp.exp(scores), 0.0)
            score_grad = (probs * (tn(values[:, here], out_grad) - weighted)).astype(BF16)
            query_grad = query_grad + nn(keys[:, here], score_grad)
            key_part = nn(score_grad, queries_t)
            value_part = nn(probs.astype(BF16), out_grad_t)
            both = jnp.concatenate([key_part, value_part], axis=1)
            if part == 1 and chunk < 2:
                both = both + kv_grad[here]
            kv_grad[here] = both
        q_grad[part] = (query_grad * HD**-0.5).astype(BF16)
    for index in range(MP):
        mine[index // 2, index % 2, :HD] = jnp.zeros((HD, OWN), BF16)
        mine[index // 2, index % 2, HD:] = kv_grad[index * OWN : (index + 1) * OWN].T.astype(BF16)
    for part in range(2):
        quarter = place.quarters[part]
        for index in range(4):
            mine[quarter * 2 + index // 2, index % 2, :HD] = q_grad[part, :, index * OWN : (index + 1) * OWN]
    order = list(range(1, CHIPS)) + [0]
    first = []
    for step in order:
        there = place.chip_at(step)
        copy = remote(mine.at[there, 1 - core], core_got.at[there], sem_q, step, place.partner)
        copy.start()
        first.append(copy)
    second = []
    for copy, step in zip(first, order):
        there = place.chip_at(step)
        copy.wait_recv()
        amount = (mine[there, core].astype(F32) + core_got[there].astype(F32)).astype(BF16)
        chip_sum[there] = amount
        if step == 0:
            head_grads[chip] = amount
        else:
            move = remote(chip_sum.at[there], head_grads.at[chip], sem_q, 7 + step, there * 2 + core)
            move.start()
            second.append(move)
    share_q = share(place, chip_sum.at[:, rows(1 - core, 96)], row_got, sem_rows, 0)
    for move in second:
        move.wait_recv()
    loads[0].wait()
    w_qkv = wat_ref[:, :, : 3 * CH].reshape(3 * D, D)
    columns = head_grads[...].reshape(3 * D, OWN)
    stream_grad, gain_grad = norm_backward(tn_narrow(w_qkv, columns), x2_ref[...], gain_n)
    lane = lax.broadcasted_iota(jnp.int32, (D, OWN), 1)
    gain_grads = jnp.where(lane == 1, gain_grad, 0.0) + jnp.where(lane == 2, ggain_b[...], 0.0)
    gx2 = gx3_ref[...] + stream_grad
    gz[:, :OWN] = gx2.astype(BF16)
    move_gz = swap(place, gz.at[:, :OWN], gz.at[:, OWN:], sem_n)
    loads[4].wait()
    sum_of_b.second()
    loads[1].wait()
    weights = hidden_weights(wa_ref)
    normed_grad = hidden_backward(weights, na_ref[:, :OWN], gz[:, :OWN], acts, slice(0, OWN))
    move_gz.wait_recv()
    parts[...] = hidden_backward(
        weights, na_ref[:, OWN:], gz[:, OWN:], acts, slice(OWN, 2 * OWN)
    ).astype(BF16)
    move_gn = swap(place, parts, got, sem_z)
    shares = [
        share_n,
        share(place, acts.at[:, D:], acts_got, sem_act, 1),
        share(place, gz, gz_got, sem_act, 2),
    ]
    sum_of_b.third()
    gather_n3.relay()
    gather_n3.cross()
    for copy in shares:
        copy.wait_recv()
    hidden_weight_grads(acts, acts_got, ((na_ref, na_got), (na_ref, na_got), (gz, gz_got)), gmlp_a)
    for part in sums_of_a:
        part.first()
    move_gn.wait_recv()
    normed_grad = normed_grad + got[...].astype(F32)
    stream_grad, gain_grad = norm_backward(normed_grad, x1_ref[...], gain_a)
    ggain_ref[...] = gain_grads + jnp.where(lane == 0, gain_grad, 0.0)
    gy1_ref[:, half(me)] = (gx2 + stream_grad).astype(BF16)
    gather_gy1 = Gather(place, gy1_ref, sem_y)
    gather_gy1.begin()
    sum_of_b.back()
    for index in range(3):
        gather_n3.arrive(index)
    share_q.wait_recv()
    for index in range(-1, 3):
        gather_n3.joined(index)
    for index in range(CHIPS):
        q_rows[:, half(index * 2 + core)] = chip_sum[index, rows(core, 96), :]
        q_rows[:, half(index * 2 + 1 - core)] = row_got[index]
    gat[: 3 * CH] = nt(q_rows[...], n3_all[...]).astype(BF16)
    for copy in o_first:
        copy.wait_recv()
    loads[5].wait()
    value = gwo_own[...].astype(F32)
    for index in range(MP - 1):
        value = value + gwo_got[index].astype(F32)
    gat[3 * CH :] = value.astype(BF16)
    t_first = []
    for step in range(1, DP):
        there = place.along_dp(step)
        copy = remote(gat.at[rows(there, 16)], gat_got.at[step - 1], sem_t, step - 1, {"dp": there})
        copy.start()
        t_first.append(copy)
    gather_gy1.relay()
    reverse_taps(taps_ref, reverse)

    def build(filter_index, slot):
        def store(block, value):
            table[slot, block * OWN : (block + 1) * OWN, :] = value

        toeplitz_down(reverse[pl.ds(filter_index, 1), :], store)

    def build_some(begin, end):
        @pl.loop(begin, end)
        def _(index):
            build(index, index)

    joint_sum[...] = jnp.zeros_like(joint_sum)

    def absorb(quarter):
        here = pl.ds(pl.multiple_of(quarter * 512, 512), 512)
        grads = gy1_ref[:, here]
        joint_sum[...] += nt(feat_ref[:, here], grads)
        feature_grad[:, here] = nn(weight_ref[: K * CH], grads).astype(BF16)

    loads[2].wait()
    loads[3].wait()
    build_some(0, 4)
    gather_gy1.joined(-1)
    gather_gy1.cross()
    absorb(place.z)
    gather_gy1.arrive(0)
    sum_of_b.back_y()
    build_some(4, 8)
    gather_gy1.joined(0)
    absorb((place.z + 3) % 4)
    gather_gy1.arrive(1)
    build_some(8, K // 2)
    gather_gy1.joined(1)
    absorb((place.z + 1) % 4)
    gather_gy1.arrive(2)
    for part in sums_of_a:
        part.second()
    gather_gy1.joined(2)
    absorb((place.z + 2) % 4)
    joint[:FEAT] = joint_sum[...].astype(BF16)
    joint[FEAT:] = jnp.zeros((CH, D), BF16)
    j_first = []
    for step in range(1, DP):
        there = place.along_dp(step)
        copy = remote(joint.at[rows(there, 112)], joint_got.at[step - 1], sem_j, step - 1, {"dp": there})
        copy.start()
        j_first.append(copy)
    total[...] = jnp.zeros_like(total)
    shifted[...] = jnp.zeros_like(shifted)
    joined = jnp.full((CH, T // 2), (pick == 1).astype(F32)).astype(BF16)
    middle = CH * count // 2

    def convolve(filter_index, slot):
        mine = feature_grad[pl.ds(pl.multiple_of(filter_index * CH, CH), CH), :]
        for source in range(count):
            here = slice(source * CH, (source + 1) * CH)
            begin = source * wide
            if source < count // 2:
                near_end = T // 2 - begin
                shifted[here, :near_end] = mine[:, begin : T // 2]
                shifted[here, near_end : T - begin] = mine[:, T // 2 :] * joined
            else:
                shifted[here, : T - begin] = mine[:, begin:]
        total[:middle] += nn(shifted[:middle, :], table[slot])
        total[middle:] += nn(shifted[middle:, : T // 2], table[slot, : T // 2, :])


    @pl.loop(0, K // 2)
    def _(index):
        convolve(index, index)

    for part in sums_of_a:
        part.third()
    last = []
    for copy in t_first:
        copy.wait_recv()
    value = gat[rows(dp, 16), :].astype(F32)
    for index in range(DP - 1):
        value = value + gat_got[index].astype(F32)
    sum_t[rows(dp, 16), :] = value.astype(BF16)
    done_t = sum_t.at[rows(dp, 16)]
    for step in range(1, DP):
        copy = remote(done_t, done_t, sem_tg, step - 1, {"dp": place.along_dp(step)})
        copy.start()
        last.append(copy)

    @pl.loop(K // 2, K)
    def _(index):
        build(index, index - K // 2)
        convolve(index, index - K // 2)

    for source in range(count):
        gh_ref[:, source * wide : (source + 1) * wide] = total[source * CH : (source + 1) * CH]
    for shift in range(LAGS):
        begin = (K + shift) * CH
        value = nn(weight_ref[begin : begin + CH], gy1_ref[...])
        value = jnp.where(lag_mask(shift, pick), value, 0.0)
        if shift:
            value = pltpu.roll(value, T - shift, 1)
        gh_ref[...] += value
    stream = x_ref[...].astype(F32)
    scaled = gh_ref[...] * gains_ref[:, 3:4].astype(F32)
    partial = jnp.sum(scaled * stream, axis=0, keepdims=True)
    for index in range(4):
        inner[me, index : index + 1] = partial[:, index * 512 : (index + 1) * 512]
    inner[me, 4:] = ggain_ref[...].T[:4]
    sums = []
    for step in range(1, MP):
        copy = remote(inner.at[me], inner.at[me], sem_p, step - 1, place.around(step))
        copy.start()
        sums.append(copy)
    scaling = scale_ref[...]
    gain_grad = jnp.sum(gh_ref[...] * stream * scaling, axis=1, keepdims=True)
    gain_grad = jnp.concatenate(
        [jnp.broadcast_to(gain_grad, (CH, OWN)), jnp.zeros((OWN - CH, OWN), F32)], axis=0
    ).T
    for copy in j_first:
        copy.wait_recv()
    value = joint[rows(dp, 112), :].astype(F32)
    for index in range(DP - 1):
        value = value + joint_got[index].astype(F32)
    joint_ref[rows(dp, 112), :] = value.astype(BF16)
    done_j = joint_ref.at[rows(dp, 112)]
    for step in range(1, DP):
        copy = remote(done_j, done_j, sem_jg, step - 1, {"dp": place.along_dp(step)})
        copy.start()
        last.append(copy)
    for part in sums_of_a:
        part.back()
    for copy in sums:
        copy.wait()
    value = inner[0]
    for index in range(1, MP):
        value = value + inner[index]
    gain_own[...] = pltpu.roll(value, (D - CH * me) % D, 1)[:, :OWN]
    gain_own[7:] = gain_grad[:1]
    for step in range(1, DP):
        copy = remote(gain_own, gain_dp.at[step - 1], sem_gd, step - 1, {"dp": place.along_dp(step)})
        copy.start()
        last.append(copy)
    value = jnp.concatenate([value[index : index + 1] for index in range(4)], axis=1)
    stream_grad = scaled * scaling - stream * (scaling * scaling * scaling * value / D)
    gx_ref[...] = stream_grad + gy1_ref[rows(me, CH), :].astype(F32)
    for part in sums_of_a:
        part.back_y()
    for copy in last:
        copy.wait()
    value = gain_own[...]
    for index in range(DP - 1):
        value = value + gain_dp[index]
    gain_sum[...] = value
    for copy in first + second + [share_q] + shares + [move_gz, move_gn] + o_first + t_first + j_first:
        copy.wait_send()
    gather_n3.close()
    gather_gy1.close()
    for part in (sum_of_b, *sums_of_a):
        part.close()


def second(*operands):
    return pl.pallas_call(
        second_kernel,
        out_shape=(
            jax.ShapeDtypeStruct((CH, T), F32),
            jax.ShapeDtypeStruct((DP * 112, D), BF16),
            jax.ShapeDtypeStruct((OWN, D), BF16),
            jax.ShapeDtypeStruct((3 * OWN, D), BF16),
            jax.ShapeDtypeStruct((3 * OWN, D), BF16),
            jax.ShapeDtypeStruct((8, OWN), F32),
        ),
        in_specs=[SMEM, VMEM, VMEM, ANY, VMEM, VMEM, VMEM, VMEM, ANY, ANY]
        + [VMEM] * 6
        + [ANY, ANY]
        + [VMEM] * 3
        + [ANY],
        out_specs=(VMEM,) * 6,
        scratch_shapes=[
            pltpu.VMEM((FEAT, T), BF16),
            pltpu.VMEM((2, 4, 3 * OWN, D), BF16),
            pltpu.VMEM((CHIPS, 2, OWN, D), BF16),
            pltpu.VMEM((D, T), BF16),
            pltpu.VMEM((FEAT, D), BF16),
            pltpu.VMEM((4, 3 * OWN, D), BF16),
            pltpu.VMEM((CH, D), BF16),
            pltpu.VMEM((HD, T), BF16),
            pltpu.VMEM((HD, T), BF16),
            pltpu.VMEM((T, 2 * HD), F32),
            pltpu.VMEM((2, HD, 512), BF16),
            pltpu.VMEM((CHIPS, 2, 3 * HD, OWN), BF16),
            pltpu.VMEM((CHIPS, 3 * HD, OWN), BF16),
            pltpu.VMEM((CHIPS, 3 * HD, OWN), BF16),
            pltpu.VMEM((CHIPS, 3 * HD, OWN), BF16),
            pltpu.VMEM((D, 2 * OWN), BF16),
            pltpu.VMEM((D, 2 * OWN), BF16),
            pltpu.VMEM((D, 2 * OWN), BF16),
            pltpu.VMEM((D, OWN), BF16),
            pltpu.VMEM((D, OWN), BF16),
            pltpu.VMEM((3, 2 * D, 2 * OWN), BF16),
            pltpu.VMEM((3, D, 2 * OWN), BF16),
            pltpu.VMEM((D, T), BF16),
            pltpu.VMEM((CHIPS, 96, OWN), BF16),
            pltpu.VMEM((96, T), BF16),
            pltpu.VMEM((MP - 1, CH, D), BF16),
            *sum_buffers(48, False),
            pltpu.VMEM((4, 3 * OWN, D), BF16),
            *sum_buffers(32, False),
            *sum_buffers(16, True),
            pltpu.VMEM((OWN, D), BF16),
            pltpu.VMEM((DP - 1, 16, D), BF16),
            pltpu.VMEM((D, OWN), F32),
            pltpu.VMEM((8, OWN), F32),
            pltpu.VMEM((DP - 1, 8, OWN), F32),
            pltpu.VMEM((K, T + 2 * OWN), F32),
            pltpu.VMEM((K // 2, T, 2 * OWN), BF16),
            pltpu.VMEM((K * CH, T), BF16),
            pltpu.VMEM((CH * T // (2 * OWN), T), BF16),
            pltpu.VMEM((CH * T // (2 * OWN), 2 * OWN), F32),
            pltpu.VMEM((CH, T), F32),
            pltpu.VMEM((FEAT, D), F32),
            pltpu.VMEM((DP * 112, D), BF16),
            pltpu.VMEM((DP - 1, 112, D), BF16),
            pltpu.VMEM((MP, 8, D), F32),
            sems(15), sems(1), sems(1), sems(15), sems(15), sems(1), sems(14), sems(14), sems(14), sems(7), sems(7),
            sems(7), sems(7), sems(7), sems(15), sems(3), sems(15),
            pltpu.SemaphoreType.DMA((6,)),
        ],
        compiler_params=pltpu.CompilerParams(
            collective_id=1, has_side_effects=True, vmem_limit_bytes=LIMIT
        ),
        name="second",
    )(*operands)


def final_kernel(
    joint_ref, t_ref, a_ref, b_ref, gain_ref, out_in, gx_in,
    out_ref, gx_ref, gws, gate_ga, up_ga, down_ga, gqkv, gout, gate_gb, up_gb, down_gb, *gain_grads,
):
    out_ref[...] = out_in[...]
    gx_ref[...] = gx_in[...]
    gws[...] = joint_ref[:FEAT].astype(F32)
    gqkv[...] = t_ref[: 3 * CH].astype(F32)
    gout[...] = t_ref[3 * CH :].astype(F32)
    for ref, (gate, up, down) in ((a_ref, (gate_ga, up_ga, down_ga)), (b_ref, (gate_gb, up_gb, down_gb))):
        gate[...] = ref[:OWN].astype(F32).T
        up[...] = ref[OWN : 2 * OWN].astype(F32).T
        down[...] = ref[2 * OWN :].astype(F32)
    for index, grad in enumerate(gain_grads):
        grad[...] = gain_ref[4 + index : 5 + index, :CH]


def final(*operands):
    mlp = [jax.ShapeDtypeStruct(shape, F32) for shape in ((D, OWN), (D, OWN), (OWN, D))]
    return pl.pallas_call(
        final_kernel,
        out_shape=(
            jax.ShapeDtypeStruct((CH, T), BF16),
            jax.ShapeDtypeStruct((CH, T), F32),
            jax.ShapeDtypeStruct((FEAT, D), F32),
            *mlp,
            jax.ShapeDtypeStruct((3 * CH, D), F32),
            jax.ShapeDtypeStruct((CH, D), F32),
            *mlp,
            *[jax.ShapeDtypeStruct((1, CH), F32)] * 4,
        ),
        in_specs=[VMEM] * 7,
        out_specs=(VMEM,) * 15,
        compiler_params=pltpu.CompilerParams(vmem_limit_bytes=LIMIT),
        name="final",
    )(*operands)


def on_device(
    inputs, out_grad, shape_pick, filters, stu_gain, stu_weight,
    mlp_gain_a, gate_a, up_a, down_a, attn_gain, qkv_weight, out_weight,
    mlp_gain_b, gate_b, up_b, down_b,
):
    gains = [gain.reshape(1, CH) for gain in (mlp_gain_a, attn_gain, mlp_gain_b, stu_gain)]
    weight = stu_weight.reshape(FEAT, D)
    x = inputs.T
    (
        gains_own, scaling, features, x1, x2, na, qkv, wa, wat, gains_all,
        lse, of, go_heads, gx3, out, n3, gwo, gmlp_b, ggain_b,
    ) = first(
        shape_pick, x, out_grad.T, *gains, filters, weight,
        gate_a, up_a, down_a, qkv_weight.T, out_weight, gate_b, up_b, down_b,
    )
    gx, joint, gat, ga, gb, gain_sum = second(
        shape_pick, x, scaling, features, x1, x2, na, qkv, wa, wat, gains_all,
        lse, of, go_heads, gx3, n3, gwo, gmlp_b, ggain_b, gains_own, filters, weight,
    )
    out, gx, gws, gate_ga, up_ga, down_ga, gqkv, gout, gate_gb, up_gb, down_gb, *gain_grads = final(
        joint, gat, ga, gb, gain_sum, out, gx
    )
    gain_a, gain_n, gain_b, gain_s = (grad.reshape(CH) for grad in gain_grads)
    return (
        out.T, gx.T, gain_s, gws.reshape(K + LAGS, CH, D), gain_a, gate_ga, up_ga, down_ga,
        gain_n, gqkv.T, gout, gain_b, gate_gb, up_gb, down_gb,
    )


def solution(mesh):
    cols, mid, row = P(None, "mp"), P(None, "mp", None), P("mp", None)
    return jax.shard_map(
        on_device,
        mesh=mesh,
        in_specs=(
            P("dp", "mp"), P("dp", "mp"), P("dp"), P(), P("mp"), mid,
            P("mp"), cols, cols, row, P("mp"), cols, row, P("mp"), cols, cols, row,
        ),
        out_specs=(
            P("dp", "mp"), P("dp", "mp"), P("mp"), mid, P("mp"), cols, cols, row,
            P("mp"), cols, row, P("mp"), cols, cols, row,
        ),
        check_vma=False,
    )
```
